32 devices in a mesh: fsdp: 4 (over z), ctx: 4 (over x, core), tp: 2 (over y).
Axes of the slice: x: 2, y: 2, z: 4, core: 2. Of those that a mesh axis runs over, the one named last changes fastest.
Arguments:
- tokens: bfloat16 [8192, 1024], P(('fsdp', 'ctx'), 'tp'), may hold values from -6 to 6
- cotangent: bfloat16 [8192, 1024], P(('fsdp', 'ctx'), 'tp'), may hold values from -6 to 6
- slot_of: int32 [8192], replicated, may hold values from 0 to 8191, as said below
- lengths: int32 [4, 3], P('fsdp'), may hold values from 0 to 2048, as said below
- w_query: bfloat16 [1024, 1024], P(('fsdp', 'ctx'), 'tp'), may hold values from -0.1875 to 0.1875
- key_weight: bfloat16 [1024, 512], P(('fsdp', 'ctx'), 'tp'), may hold values from -0.1875 to 0.1875
- value_weight: bfloat16 [1024, 512], P(('fsdp', 'ctx'), 'tp'), may hold values from -0.1875 to 0.1875
- w_out: bfloat16 [1024, 1024], P('tp', ('fsdp', 'ctx')), may hold values from -3 to 3
- w_gate: bfloat16 [1024, 4608], P(('fsdp', 'ctx'), 'tp'), may hold values from -0.1875 to 0.1875
- w_up: bfloat16 [1024, 4608], P(('fsdp', 'ctx'), 'tp'), may hold values from -0.1875 to 0.1875
- w_down: bfloat16 [4608, 1024], P('tp', ('fsdp', 'ctx')), may hold values from -0.09375 to 0.09375
- gain_attn: float32 [1024], replicated, may hold values from 0.25 to 1.75
- gain_ffn: float32 [1024], replicated, may hold values from 0.25 to 1.75
- gain_query: float32 [64], replicated, may hold values from 0.25 to 1.75
- gain_key: float32 [64], replicated, may hold values from 0.25 to 1.75
Outputs:
- output: bfloat16 [8192, 1024], P(('fsdp', 'ctx'), 'tp')
- grad_tokens: bfloat16 [8192, 1024], P(('fsdp', 'ctx'), 'tp')
- grad_w_query: float32 [1024, 1024], P(('fsdp', 'ctx'), 'tp')
- grad_w_key: float32 [1024, 512], P(('fsdp', 'ctx'), 'tp')
- grad_w_value: float32 [1024, 512], P(('fsdp', 'ctx'), 'tp')
- grad_w_out: float32 [1024, 1024], P('tp', ('fsdp', 'ctx'))
- grad_w_gate: float32 [1024, 4608], P(('fsdp', 'ctx'), 'tp')
- grad_w_up: float32 [1024, 4608], P(('fsdp', 'ctx'), 'tp')
- grad_w_down: float32 [4608, 1024], P('tp', ('fsdp', 'ctx'))
- grad_gain_attn: float32 [1024], replicated
- grad_gain_ffn: float32 [1024], replicated
- grad_gain_query: float32 [64], replicated
- grad_gain_key: float32 [64], replicated
- rms_stats: float32 [3], replicated
The draws below stay inside these ranges and needn't reach their ends.
Inputs may be any that keep to these rules, and one draw needn't show every extreme that they name: slot_of is a permutation of the 8192 slots; the tokens of each index of fsdp+ctx go in equal shares to the slots held by every index of fsdp+ctx (each index holds one piece of 2048 / 4 slots of its row). Each row's lengths sum to 2048; its nonzero lengths come first and are at least 512; a row holds one to three sequences, and the first row holds one.
All inputs are finite; a program needn't handle non-finite values.
Results may differ from the reference program's by a relative error of at most 0.024.
Values may be sent and summed in bfloat16 or wider, within the bound.
A program may use at most 256 MiB of HBM per device.

```python
import jax
import jax.numpy as jnp
from jax import lax

MODEL_WIDTH = 1024
FF = 4608
QUERY_HEADS = 16
KEY_VALUE_HEADS = 8
HEAD_SIZE = 64
PACKED_ROW_SLOTS = 2048
MINLEN = 512
QUERY_BLOCK_ROWS = 512
ROWS_DEV = 1
NROWS = 4
TOKENS = 8192
N_FSDP = 4
N_CTX = 4


def draw_lengths(key, part):
    first_key, second_key, third_key = jax.random.split(key, 3)
    pieces = jax.random.randint(first_key, (NROWS,), 1, 4).astype(jnp.int32)
    pieces = pieces.at[0].set(1)
    spare_room = jnp.where(pieces == 3, PACKED_ROW_SLOTS - 3 * MINLEN, PACKED_ROW_SLOTS - 2 * MINLEN)
    cut_one = jax.random.randint(second_key, (NROWS,), 0, spare_room + 1)
    cut_two = jax.random.randint(third_key, (NROWS,), 0, spare_room + 1)
    lower_cut = jnp.minimum(cut_one, cut_two)
    upper_cut = jnp.maximum(cut_one, cut_two)
    zero_col = jnp.zeros_like(pieces)
    single = jnp.stack([zero_col + PACKED_ROW_SLOTS, zero_col, zero_col], axis=1)
    double = jnp.stack([MINLEN + cut_one, PACKED_ROW_SLOTS - MINLEN - cut_one, zero_col], axis=1)
    triple = jnp.stack([MINLEN + lower_cut, MINLEN + upper_cut - lower_cut, MINLEN + spare_room - upper_cut], axis=1)
    chosen = jnp.where((pieces == 1)[:, None], single, jnp.where((pieces == 2)[:, None], double, triple))
    return chosen.astype(jnp.int32)


def shuffled_rows(key, groups, count):

    def one_order(row_key):
        return jax.random.permutation(row_key, count)
    return jax.vmap(one_order)(jax.random.split(key, groups)).astype(jnp.int32)


def draw_slot_of(key, part):
    groups = N_FSDP * N_CTX
    local = TOKENS // groups
    share = local // groups
    piece = PACKED_ROW_SLOTS // N_CTX
    send_key, take_key = jax.random.split(jax.random.fold_in(key, 7))
    sender = shuffled_rows(send_key, groups, local)
    taker = shuffled_rows(take_key, groups, local)
    target_dev = sender // share
    arrival = jnp.arange(groups, dtype=jnp.int32)[:, None] * share + sender % share
    local_slot = taker[target_dev, arrival]
    row_index = target_dev // N_CTX * ROWS_DEV + local_slot // piece
    slot = row_index * PACKED_ROW_SLOTS + target_dev % N_CTX * piece + local_slot % piece
    return slot.reshape(TOKENS).astype(jnp.int32)


def shard_levels(own_key, dims, cuts, smallest, high):
    def one(dim, blocks):
        heights = jax.random.uniform(jax.random.fold_in(jax.random.fold_in(own_key, 6), dim), (blocks,), jnp.float32, smallest / len(cuts), high / len(cuts))
        return jnp.repeat(jnp.exp(heights), dims[dim] // blocks).reshape((-1,) + (1,) * (len(dims) - dim - 1))

    loudness = one(*cuts[0])
    for cut in cuts[1:]:
        loudness = loudness * one(*cut)
    return loudness


def bell_draw(key, shape, deviation, limit, cuts=(), kind=jnp.bfloat16):
    values = deviation * jax.random.normal(key, shape, jnp.float32)
    if cuts:
        values = values * shard_levels(key, shape, cuts, -0.22, 0.18)
    return jnp.clip(values, -limit, limit).astype(kind)


def setup_inputs(seed: int = 0) -> dict:
    key_list = jax.random.split(jax.random.key(seed), 16)
    tokens = bell_draw(key_list[0], (TOKENS, MODEL_WIDTH), 1.0, 6.0, ((0, 16), (1, 2)))
    cotangent = bell_draw(key_list[1], (TOKENS, MODEL_WIDTH), 1.0, 6.0, ((0, 16), (1, 2)))
    slot_of = draw_slot_of(jax.random.fold_in(key_list[15], 71), 0)
    lengths = draw_lengths(jax.random.fold_in(key_list[15], 71), 0)
    w_query = bell_draw(key_list[4], (MODEL_WIDTH, QUERY_HEADS * HEAD_SIZE), MODEL_WIDTH ** -0.5, 0.1875, ((0, 16), (1, 2)))
    key_weight = bell_draw(key_list[5], (MODEL_WIDTH, KEY_VALUE_HEADS * HEAD_SIZE), MODEL_WIDTH ** -0.5, 0.1875, ((0, 16), (1, 2)))
    value_weight = bell_draw(key_list[6], (MODEL_WIDTH, KEY_VALUE_HEADS * HEAD_SIZE), MODEL_WIDTH ** -0.5, 0.1875, ((0, 16), (1, 2)))
    w_out = bell_draw(key_list[7], (QUERY_HEADS * HEAD_SIZE, MODEL_WIDTH), 4 ** -0.5, 3.0, ((0, 2), (1, 16)))
    w_gate = bell_draw(key_list[8], (MODEL_WIDTH, FF), MODEL_WIDTH ** -0.5, 0.1875, ((0, 16), (1, 2)))
    w_up = bell_draw(key_list[9], (MODEL_WIDTH, FF), MODEL_WIDTH ** -0.5, 0.1875, ((0, 16), (1, 2)))
    w_down = bell_draw(key_list[10], (FF, MODEL_WIDTH), FF ** -0.5, 0.09375, ((0, 2), (1, 16)))
    gain_attn = jnp.clip(1.0 + 0.15 * jax.random.normal(key_list[11], (MODEL_WIDTH,), jnp.float32), 0.25, 1.75)
    gain_ffn = jnp.clip(1.0 + 0.15 * jax.random.normal(key_list[12], (MODEL_WIDTH,), jnp.float32), 0.25, 1.75)
    gain_query = jnp.clip(1.0 + 0.15 * jax.random.normal(key_list[13], (HEAD_SIZE,), jnp.float32), 0.25, 1.75)
    gain_key = jnp.clip(1.0 + 0.15 * jax.random.normal(key_list[14], (HEAD_SIZE,), jnp.float32), 0.25, 1.75)
    return dict(tokens=tokens, cotangent=cotangent, slot_of=slot_of, lengths=lengths, w_query=w_query, key_weight=key_weight, value_weight=value_weight, w_out=w_out, w_gate=w_gate, w_up=w_up, w_down=w_down, gain_attn=gain_attn, gain_ffn=gain_ffn, gain_query=gain_query, gain_key=gain_key)


EPSILON = 1e-05
ROPE_THETA = 1000000.0
HIGHEST_ACCURACY = lax.Precision.HIGHEST
NEG_FILL = -1e+30

@jax.custom_vjp
def lowered_input(v):
    return lax.optimization_barrier(v.astype(jnp.bfloat16)).astype(jnp.float32)

@jax.custom_vjp
def lowered_gradient(v):
    return v

def low_keep(v):
    return (lowered_input(v), None)

def low_pass(kept, grad):
    return (grad,)

def back_keep(v):
    return (v, None)

def back_low(kept, grad):
    return (lowered_input(grad),)
lowered_input.defvjp(low_keep, low_pass)
lowered_gradient.defvjp(back_keep, back_low)

def rms_scale(values, gain):
    return values * lax.rsqrt(lax.optimization_barrier(jnp.mean(values * values, axis=-1, keepdims=True)) + EPSILON) * gain

def rotate(values, cosines, sines):
    middle = values.shape[-1] // 2
    first_half = values[..., :middle]
    second_half = values[..., middle:]
    return jnp.concatenate([first_half * cosines - second_half * sines, second_half * cosines + first_half * sines], axis=-1)

def slot_tables(lengths, slot_ids):
    seg_ends = jnp.cumsum(lengths, dtype=jnp.int32)
    passed = (slot_ids[:, None] >= seg_ends[None, :]).astype(jnp.int32)
    segment = lax.optimization_barrier(jnp.sum(passed, axis=1, dtype=jnp.int32))
    position = slot_ids - lax.optimization_barrier(jnp.sum(passed * lengths[None, :], axis=1, dtype=jnp.int32))
    return (segment, position)

def angle_tables(position):
    frequency = ROPE_THETA ** (-jnp.arange(0, HEAD_SIZE, 2).astype(jnp.float32) / HEAD_SIZE)
    angles = position.astype(jnp.float32)[:, None] * frequency[None, :]
    return (jnp.cos(angles)[:, None, :], jnp.sin(angles)[:, None, :])

def layer_rows(inputs, w_query, key_weight, value_weight, w_out, w_gate, w_up, w_down, gain_attn, gain_ffn, gain_query, gain_key, segment, position):
    cosines, sines = angle_tables(position)
    first_normed = lowered_input(rms_scale(inputs, gain_attn))
    query_tensor = lowered_gradient(jnp.dot(first_normed, w_query, precision=HIGHEST_ACCURACY)).reshape(PACKED_ROW_SLOTS, QUERY_HEADS, HEAD_SIZE)
    key_projected = lowered_gradient(jnp.dot(first_normed, key_weight, precision=HIGHEST_ACCURACY)).reshape(PACKED_ROW_SLOTS, KEY_VALUE_HEADS, HEAD_SIZE)
    value_projected = lowered_input(lowered_gradient(jnp.dot(first_normed, value_weight, precision=HIGHEST_ACCURACY))).reshape(PACKED_ROW_SLOTS, KEY_VALUE_HEADS, HEAD_SIZE)
    query_tensor = lowered_input(rotate(rms_scale(query_tensor, gain_query), cosines, sines))
    key_projected = lowered_input(rotate(rms_scale(key_projected, gain_key), cosines, sines))
    query_group_width = QUERY_HEADS // KEY_VALUE_HEADS
    block_list = PACKED_ROW_SLOTS // QUERY_BLOCK_ROWS
    query_block_list = query_tensor.reshape(block_list, QUERY_BLOCK_ROWS, KEY_VALUE_HEADS, query_group_width, HEAD_SIZE)
    slot_ids = jnp.arange(PACKED_ROW_SLOTS, dtype=jnp.int32)

    def attend(packed):
        q_block, q_segment, q_slot = packed
        scores = lowered_gradient(0.125 * jnp.einsum('qhgd,khd->hgqk', q_block, key_projected, precision=HIGHEST_ACCURACY))
        allowed = (q_segment[:, None] == segment[None, :]) & (slot_ids[None, :] <= q_slot[:, None])
        masked = jnp.where(allowed, scores, NEG_FILL)
        log_total = jax.nn.logsumexp(masked, axis=-1, keepdims=True)
        probabilities = lowered_input(jnp.exp(masked - log_total))
        return jnp.einsum('hgqk,khd->qhgd', probabilities, value_projected, precision=HIGHEST_ACCURACY)
    head_out = lax.map(jax.checkpoint(attend), (query_block_list, segment.reshape(block_list, QUERY_BLOCK_ROWS), slot_ids.reshape(block_list, QUERY_BLOCK_ROWS)))
    attn_heads = lowered_input(lowered_gradient(head_out.reshape(PACKED_ROW_SLOTS, QUERY_HEADS * HEAD_SIZE)))
    attn_out = lowered_gradient(jnp.dot(attn_heads, w_out, precision=HIGHEST_ACCURACY))
    middle_sum = inputs + attn_out
    normed_two = lowered_input(rms_scale(lowered_input(middle_sum), gain_ffn))
    gate_act = lowered_gradient(jnp.dot(normed_two, w_gate, precision=HIGHEST_ACCURACY))
    up_proj = lowered_gradient(jnp.dot(normed_two, w_up, precision=HIGHEST_ACCURACY))
    hidden = lowered_input(jax.nn.silu(gate_act) * up_proj)
    ffn_out = lowered_gradient(jnp.dot(hidden, w_down, precision=HIGHEST_ACCURACY))
    squares = jnp.stack([jnp.sum(inputs * inputs), jnp.sum(attn_out * attn_out), jnp.sum(ffn_out * ffn_out)])
    return (middle_sum + ffn_out, squares)

def reference(tokens, cotangent, slot_of, lengths, w_query, key_weight, value_weight, w_out, w_gate, w_up, w_down, gain_attn, gain_ffn, gain_query, gain_key):
    params = tuple((weight.astype(jnp.float32) for weight in (w_query, key_weight, value_weight, w_out, w_gate, w_up, w_down, gain_attn, gain_ffn, gain_query, gain_key)))
    slot_ids = jnp.arange(PACKED_ROW_SLOTS, dtype=jnp.int32)
    source = jnp.argsort(slot_of)
    packed_tokens = tokens[source].reshape(NROWS, PACKED_ROW_SLOTS, MODEL_WIDTH)
    packed_cot = cotangent[source].reshape(NROWS, PACKED_ROW_SLOTS, MODEL_WIDTH)

    def one_row(carried, packed):
        inputs, upstream, row_lengths = packed
        segment, position = slot_tables(row_lengths, slot_ids)

        def forward(inputs_f, *weights):
            return layer_rows(inputs_f, *weights, segment, position)
        result, pullback, squares = jax.vjp(forward, inputs.astype(jnp.float32), *params, has_aux=True)
        gradients = pullback(upstream.astype(jnp.float32))
        grad_sums, square_sum = carried
        grad_sums = tuple((running + increment for running, increment in zip(grad_sums, gradients[1:])))
        return ((grad_sums, square_sum + squares), (result.astype(jnp.bfloat16), gradients[0].astype(jnp.bfloat16)))
    initial = (tuple((jnp.zeros_like(param) for param in params)), jnp.zeros((3,), jnp.float32))
    (grad_sums, square_sum), (outputs, input_grads) = lax.scan(one_row, initial, (packed_tokens, packed_cot, lengths))
    rms_stats = jnp.sqrt(square_sum / (NROWS * PACKED_ROW_SLOTS * MODEL_WIDTH))
    output = outputs.reshape(TOKENS, MODEL_WIDTH)[slot_of]
    grad_tokens = input_grads.reshape(TOKENS, MODEL_WIDTH)[slot_of]
    return (output, grad_tokens, grad_sums[0], grad_sums[1], grad_sums[2], grad_sums[3], grad_sums[4], grad_sums[5], grad_sums[6], grad_sums[7], grad_sums[8], grad_sums[9], grad_sums[10], rms_stats)
```

```python
import functools

import jax
import jax.numpy as jnp
from jax import lax
from jax.experimental import pallas as pl
from jax.experimental.pallas import tpu as pltpu
from jax.sharding import PartitionSpec as P

MODEL_WIDTH = 1024
QUERY_HEADS = 16
KEY_VALUE_HEADS = 8
HEAD_SIZE = 64
PACKED_ROW_SLOTS = 2048
QUERY_BLOCK_ROWS = 512

EPSILON = 1e-05
ROPE_THETA = 1000000.0
NEG_FILL = -1e30
BF = jnp.bfloat16
F32 = jnp.float32


def rms_scale(values, gain):
    return values * lax.rsqrt(jnp.mean(values * values, axis=-1, keepdims=True) + EPSILON) * gain


def rotate(values, cosines, sines):
    middle = values.shape[-1] // 2
    first_half = values[..., :middle]
    second_half = values[..., middle:]
    return jnp.concatenate(
        [first_half * cosines - second_half * sines, second_half * cosines + first_half * sines],
        axis=-1,
    )


def segment_ends(lengths):
    total, ends = lengths[0], []
    for i in range(lengths.shape[0]):
        ends.append(total)
        if i + 1 < lengths.shape[0]:
            total = total + lengths[i + 1]
    return ends


def slot_tables(lengths, slot_ids):
    segment = jnp.zeros_like(slot_ids)
    start = jnp.zeros_like(slot_ids)
    for i, end in enumerate(segment_ends(lengths)):
        passed = (slot_ids >= end).astype(jnp.int32)
        segment = segment + passed
        start = start + passed * lengths[i]
    return (segment, slot_ids - start)


def angle_tables(position):
    frequency = ROPE_THETA ** (-jnp.arange(0, HEAD_SIZE, 2).astype(F32) / HEAD_SIZE)
    angles = position.astype(F32)[:, None] * frequency[None, :]
    return (jnp.cos(angles)[:, None, :], jnp.sin(angles)[:, None, :])


def product(left_arr, right_arr, pattern):
    return jnp.einsum(pattern, left_arr, right_arr, preferred_element_type=F32)


def score_probs(q_block, key_rows, q_seg, q_slot, k_seg, k_slot, lse_block):
    raw_scores = product(q_block, key_rows, "qhgd,khd->hgqk") * 0.125
    allowed = (q_seg[:, None] == k_seg[None, :]) & (k_slot[None, :] <= q_slot[:, None])
    shifted = raw_scores - jnp.transpose(lse_block, (1, 2, 0))[..., None]
    return jnp.exp(jnp.where(allowed, shifted, NEG_FILL))


def attend_row(query_row, key_rows, value_rows, q_segment, q_slot, k_segment, k_slot):
    block_list = query_row.shape[0] // QUERY_BLOCK_ROWS

    def attend_one_block(packed):
        q_block, seg_block, slot_block = packed
        raw_scores = product(q_block, key_rows, "qhgd,khd->hgqk") * 0.125
        allowed = (seg_block[:, None] == k_segment[None, :]) & (
            k_slot[None, :] <= slot_block[:, None]
        )
        masked = jnp.where(allowed, raw_scores, NEG_FILL)
        row_peak = jnp.max(masked, axis=-1, keepdims=True)
        weights = jnp.exp(masked - row_peak)
        row_total = jnp.sum(weights, axis=-1, keepdims=True)
        probabilities = weights / row_total
        head_out = product(probabilities.astype(BF), value_rows, "hgqk,khd->qhgd")
        log_total = jnp.transpose((row_peak + jnp.log(row_total))[..., 0], (2, 0, 1))
        return (head_out, log_total)

    shaped = query_row.reshape((block_list, QUERY_BLOCK_ROWS) + query_row.shape[1:])
    return lax.map(
        attend_one_block,
        (
            shaped,
            q_segment.reshape(block_list, QUERY_BLOCK_ROWS),
            q_slot.reshape(block_list, QUERY_BLOCK_ROWS),
        ),
    )


def query_back(
    query_row, key_rows, value_rows, q_segment, q_slot, k_segment, k_slot, log_total, grad_heads
):
    block_list = query_row.shape[0] // QUERY_BLOCK_ROWS

    def query_one_block(carried, packed):
        q_block, seg_block, slot_block, lse_block, grad_block = packed
        probabilities = score_probs(
            q_block, key_rows, seg_block, slot_block, k_segment, k_slot, lse_block
        )
        d_prob = product(grad_block, value_rows, "qhgd,khd->hgqk")
        delta = jnp.sum(probabilities * d_prob, axis=-1, keepdims=True)
        d_score = (probabilities * (d_prob - delta)).astype(BF)
        q_grad = product(d_score, key_rows, "hgqk,khd->qhgd") * 0.125
        key_grad = carried[0] + product(d_score, q_block, "hgqk,qhgd->khd") * 0.125
        value_grad = carried[1] + product(probabilities.astype(BF), grad_block, "hgqk,qhgd->khd")
        carried = (key_grad, value_grad)
        return (carried, q_grad)

    block_shape = (block_list, QUERY_BLOCK_ROWS) + query_row.shape[1:]
    initial = (jnp.zeros(key_rows.shape, F32), jnp.zeros(key_rows.shape, F32))
    packed = (
        query_row.reshape(block_shape),
        q_segment.reshape(block_list, QUERY_BLOCK_ROWS),
        q_slot.reshape(block_list, QUERY_BLOCK_ROWS),
        log_total,
        grad_heads.reshape(block_shape),
    )
    return lax.scan(query_one_block, initial, packed)


class Grid:
    def __init__(self):
        self.n = lax.axis_size("fsdp")
        self.ctx = lax.axis_size("ctx")
        self.tp = lax.axis_size("tp")
        self.z = lax.axis_index("fsdp")
        self.c = lax.axis_index("ctx")
        self.t = lax.axis_index("tp")

    def ring(self, v):
        return lax.ppermute(v, "fsdp", [(i, (i + 1) % self.n) for i in range(self.n)])

    def flip(self, v, bit):
        return lax.ppermute(v, "ctx", [(i, i ^ bit) for i in range(self.ctx)])

    def order(self):
        return [
            lax.rem(self.z - k + self.n, self.n) * self.ctx + (self.c ^ d)
            for d in range(self.ctx)
            for k in range(self.n)
        ]

    def collect(self, shard):
        have = [shard]
        for _ in range(self.n - 1):
            have.append(self.ring(have[-1]))
        bits = []
        b = self.ctx // 2
        while b:
            bits.append(b)
            b //= 2
        got = {(0, k): v for k, v in enumerate(have)}
        for bit in bits:
            more = {(d | bit, k): self.flip(v, bit) for (d, k), v in got.items()}
            got.update(more)
        return [got[(d, k)] for d in range(self.ctx) for k in range(self.n)]

    def reduce_ctx(self, keep, send):
        total = (keep.astype(F32) + self.flip(send, 1).astype(F32)).astype(BF)
        bit = self.ctx // 2
        stride = keep.shape[0] // 2
        if bit >= 2:
            away = self.flip(total[stride:], bit)
            total = (total[:stride].astype(F32) + away.astype(F32)).astype(BF)
        return total

    def reduce_ring(self, total):
        run = total[1 % self.n]
        for k in range(2, self.n + 1):
            run = self.ring(run).astype(F32) + total[k % self.n].astype(F32)
            if k < self.n:
                run = run.astype(BF)
        return run

    def tp_pair(self, own, other, axis):
        first = jnp.where(self.t == 0, own, other)
        second = jnp.where(self.t == 0, other, own)
        return jnp.concatenate([first, second], axis=axis)

    def tp_gather(self, v):
        if self.tp == 2:
            other = lax.ppermute(v, "tp", [(0, 1), (1, 0)])
            return self.tp_pair(v, other, 1)
        return lax.all_gather(v, "tp", axis=1, tiled=True)

    def tp_sum(self, v):
        if self.tp == 2:
            other = lax.ppermute(v, "tp", [(0, 1), (1, 0)])
            return v.astype(F32) + other.astype(F32)
        return lax.psum(v, "tp").astype(F32)

    def tp_scatter(self, v):
        if self.tp == 2:
            half = v.shape[1] // 2
            own = lax.dynamic_slice_in_dim(v, self.t * half, half, 1)
            away = lax.dynamic_slice_in_dim(v, (1 - self.t) * half, half, 1)
            other = lax.ppermute(away, "tp", [(0, 1), (1, 0)])
            return own.astype(F32) + other.astype(F32)
        return lax.psum_scatter(v, "tp", scatter_dimension=1, tiled=True).astype(F32)


def dot(a, b, ca, cb):
    return lax.dot_general(a, b, (((ca,), (cb,)), ((), ())), preferred_element_type=F32)


def ffn_kernel(pieces, shard_rows, tile, group, offs, mid, dy, gain, *refs):
    wg_in = refs[:pieces]
    wu_in = refs[pieces : 2 * pieces]
    wd_in = refs[2 * pieces : 3 * pieces]
    ffn, dmid, dgain, gk, gs, uk, us, dk, ds = refs[3 * pieces : 3 * pieces + 9]
    (wg, wu, wd, nb, n_t, dy_t, turn, ffn_acc, dn_acc, sem) = refs[3 * pieces + 9 :]
    step = pl.program_id(0)
    steps = pl.num_programs(0)
    n_groups = wg.shape[1] // group
    per_group = group // tile
    half = mid.shape[1] // 2

    def copies(g):
        out = []
        cols = pl.ds(g * group, group)
        for m, (src, dst) in enumerate(((wg_in, wg), (wu_in, wu), (wd_in, wd))):
            for i in range(pieces):
                rows = pl.ds(pl.multiple_of(offs[i], shard_rows), shard_rows)
                out.append(
                    pltpu.make_async_copy(src[i].at[:, cols], dst.at[rows, cols], sem.at[g, m, i])
                )
        return out

    @pl.when(step == 0)
    def _():
        for g in range(n_groups):
            for c in copies(g):
                c.start()
        v = mid[...].astype(F32)
        scale = lax.rsqrt(jnp.mean(v * v, axis=1, keepdims=True) + EPSILON)
        normed = v * scale * gain[...]
        nb[...] = normed.astype(BF)
        ffn_acc[...] = jnp.zeros_like(ffn_acc)
        dn_acc[...] = jnp.zeros_like(dn_acc)
        for value, to in ((normed, n_t), (dy[...].astype(F32), dy_t)):
            turn[...] = value.T.astype(BF)
            for i in range(pieces):
                row = pl.multiple_of(offs[pieces + i], shard_rows)
                to[i * shard_rows : (i + 1) * shard_rows, :] = turn[pl.ds(row, shard_rows), :]

    for g in range(n_groups):

        @pl.when(step == g * per_group)
        def _(g=g):
            for c in copies(g):
                c.wait()

    cols = pl.ds(pl.multiple_of(step * tile, tile), tile)
    w_gate = wg[:, cols]
    w_up = wu[:, cols]
    w_down = wd[:, cols]
    normed = nb[...]
    dyb = dy[...]
    gate = dot(normed, w_gate, 1, 0)
    up = dot(normed, w_up, 1, 0)
    d_hidden = dot(dyb, w_down, 1, 0)
    sig = 1.0 / (1.0 + jnp.exp(-gate))
    silu = gate * sig
    hidden = (silu * up).astype(BF)
    d_gate = (d_hidden * up * (sig * (1.0 + gate * (1.0 - sig)))).astype(BF)
    d_up = (d_hidden * silu).astype(BF)
    ffn_acc[...] += dot(hidden, w_down, 1, 1)
    dn_acc[...] += dot(d_gate, w_gate, 1, 1) + dot(d_up, w_up, 1, 1)
    for left, right, keep, send in (
        (n_t, d_gate, gk, gs),
        (n_t, d_up, uk, us),
        (dy_t, hidden, dk, ds),
    ):
        keep[...] = dot(left[:half, :], right, 1, 0).astype(BF)
        send[...] = dot(left[half:, :], right, 1, 0).astype(BF)

    @pl.when(step == steps - 1)
    def _():
        v = mid[...].astype(F32)
        scale = lax.rsqrt(jnp.mean(v * v, axis=1, keepdims=True) + EPSILON)
        unit = v * scale
        dn = dn_acc[...]
        dgain[...] = jnp.sum(dn * unit, axis=0, keepdims=True)
        scaled = dn * gain[...]
        dmid[...] = (
            scale * (scaled - unit * jnp.mean(scaled * unit, axis=1, keepdims=True))
        ).astype(BF)
        ffn[...] = ffn_acc[...].astype(BF)


def ffn_pass(mid, dy, gain, gate_p, up_p, down_p, offsets):
    rows, width = mid.shape
    pieces = len(gate_p)
    shard_rows, ff = gate_p[0].shape
    tile = 256 if ff % 256 == 0 else 128
    group = 3 * tile if ff % (3 * tile) == 0 else tile
    half = width // 2
    whole = lambda shape: pl.BlockSpec(shape, lambda s, o: (0, 0))
    column = pl.BlockSpec((half, tile), lambda s, o: (0, s))
    grad = jax.ShapeDtypeStruct((half, ff), BF)
    return pl.pallas_call(
        functools.partial(ffn_kernel, pieces, shard_rows, tile, group),
        grid_spec=pltpu.PrefetchScalarGridSpec(
            num_scalar_prefetch=1,
            grid=(ff // tile,),
            in_specs=[whole((rows, width)), whole((rows, width)), whole((1, width))]
            + [pl.BlockSpec(memory_space=pl.ANY)] * (3 * pieces),
            out_specs=[whole((rows, width)), whole((rows, width)), whole((1, width))]
            + [column] * 6,
            scratch_shapes=[
                pltpu.VMEM((width, ff), BF),
                pltpu.VMEM((width, ff), BF),
                pltpu.VMEM((width, ff), BF),
                pltpu.VMEM((rows, width), BF),
                pltpu.VMEM((width, rows), BF),
                pltpu.VMEM((width, rows), BF),
                pltpu.VMEM((width, rows), BF),
                pltpu.VMEM((rows, width), F32),
                pltpu.VMEM((rows, width), F32),
                pltpu.SemaphoreType.DMA((ff // group, 3, pieces)),
            ],
        ),
        out_shape=[
            jax.ShapeDtypeStruct((rows, width), BF),
            jax.ShapeDtypeStruct((rows, width), BF),
            jax.ShapeDtypeStruct((1, width), F32),
        ]
        + [grad] * 6,
        compiler_params=pltpu.CompilerParams(vmem_limit_bytes=58 * 2**20),
        cost_estimate=pl.CostEstimate(
            flops=18 * rows * width * ff, bytes_accessed=12 * width * ff, transcendentals=rows * ff
        ),
    )(offsets, mid, dy, gain, *gate_p, *up_p, *down_p)


def pad_columns(v, to):
    return v if v.shape[1] == to else jnp.pad(v, ((0, 0), (0, to - v.shape[1])))


def pick_blocks(stack, order):
    return jnp.concatenate([lax.dynamic_slice_in_dim(stack, i, 1, 0) for i in order], axis=0)


def one_hot(rows, columns):
    return (rows == columns).astype(BF)


def local(
    tokens,
    cotangent,
    slot_of,
    lengths,
    w_query,
    key_weight,
    value_weight,
    w_out,
    w_gate,
    w_up,
    w_down,
    gain_attn,
    gain_ffn,
    gain_query,
    gain_key,
):
    grid = Grid()
    stream_len = tokens.shape[0]
    feat_len = tokens.shape[1]
    local_len = PACKED_ROW_SLOTS // grid.ctx
    row_count = stream_len // local_len
    groups = grid.n * grid.ctx
    share = stream_len // groups
    q_heads = QUERY_HEADS // grid.tp
    key_value_heads = KEY_VALUE_HEADS // grid.tp
    query_group_width = QUERY_HEADS // KEY_VALUE_HEADS
    q_width = q_heads * HEAD_SIZE
    kv_width = key_value_heads * HEAD_SIZE
    flat_len = row_count * local_len
    row_len = PACKED_ROW_SLOTS
    me = grid.z * grid.ctx + grid.c
    both = ("fsdp", "ctx")

    def home(slots):
        row, place = slots // row_len, slots % row_len
        return (
            row // row_count * grid.ctx + place // local_len,
            row % row_count * local_len + place % local_len,
        )

    my_slots = lax.dynamic_slice_in_dim(slot_of, me * stream_len, stream_len, 0)
    my_target = home(my_slots)[0]
    ahead = (my_target[:, None] == my_target[None, :]) & (my_slots[None, :] < my_slots[:, None])
    send_place = my_target * share + jnp.sum(ahead.astype(jnp.int32), axis=1)
    line = jnp.arange(stream_len, dtype=jnp.int32)
    send_pick = one_hot(line[:, None], send_place[None, :])
    all_dev, all_local = home(slot_of)
    low = 32
    high = flat_len // low
    sender = (jnp.arange(slot_of.shape[0], dtype=jnp.int32) // stream_len).astype(F32)
    mine = (all_dev == me)[None, :] & (
        (all_local // low)[None, :] == jnp.arange(high, dtype=jnp.int32)[:, None]
    )
    left = jnp.where(mine, sender[None, :], 0.0).astype(BF)
    right = one_hot((all_local % low)[:, None], jnp.arange(low, dtype=jnp.int32)[None, :])
    source = product(left, right, "ht,tl->hl").reshape(flat_len).astype(jnp.int32)
    slot_line = jnp.arange(flat_len, dtype=jnp.int32)
    before = (source[:, None] == source[None, :]) & (slot_line[None, :] < slot_line[:, None])
    arrival = source * share + jnp.sum(before.astype(jnp.int32), axis=1)
    take_pick = one_hot(arrival[:, None], line[None, :])

    def spread(v):
        sent = product(send_pick, v, "pt,tf->pf").astype(BF)
        got = lax.all_to_all(sent, both, split_axis=0, concat_axis=0, tiled=True)
        return product(take_pick, got, "ja,af->jf").astype(BF)

    def bring_back(v):
        sent = product(take_pick, v, "ja,jf->af").astype(BF)
        got = lax.all_to_all(sent, both, split_axis=0, concat_axis=0, tiled=True)
        return product(send_pick, got, "pt,pf->tf").astype(BF)

    ff = w_gate.shape[1]
    ff_pad = -(-ff // 128) * 128
    attn_shard = jnp.concatenate([w_query, key_weight, value_weight, w_out.T], axis=1)
    attn_pieces = grid.collect(attn_shard)
    gate_p, up_p, down_p = (
        grid.collect(pad_columns(v, ff_pad)) for v in (w_gate, w_up, w_down.T)
    )
    shard_rows = w_gate.shape[0]
    order = grid.order()
    grad_order = [d for d in range(0, grid.ctx, 2)] + [d for d in range(1, grid.ctx, 2)]
    grad_order = [order[d * grid.n + k] for d in grad_order for k in range(grid.n)]
    offsets = (jnp.stack(order + grad_order) * shard_rows).astype(jnp.int32)

    packed_tok = spread(tokens)
    packed_cot = spread(cotangent)
    own_slots = grid.c * local_len + jnp.arange(local_len, dtype=jnp.int32)
    row_slots = jnp.arange(row_len, dtype=jnp.int32)

    def tables(row_lengths):
        q_segment, q_position = slot_tables(row_lengths, own_slots)
        k_segment = slot_tables(row_lengths, row_slots)[0]
        return (q_segment, q_position, k_segment)

    q_segment, q_position, k_segment = jax.vmap(tables)(lengths)
    cosines, sines = angle_tables(q_position.reshape(flat_len))
    x_full = grid.tp_gather(packed_tok)
    dy_full = grid.tp_gather(packed_cot)
    x_float = x_full.astype(F32)
    normed_f, attn_norm_pull = jax.vjp(rms_scale, x_float, gain_attn)
    first_normed = normed_f.astype(BF)

    stack = jnp.stack(attn_pieces)
    inverse = [
        (i % grid.ctx ^ grid.c) * grid.n + lax.rem(grid.z - i // grid.ctx + grid.n, grid.n)
        for i in range(groups)
    ]
    attn_w = pick_blocks(stack, inverse).reshape(MODEL_WIDTH, attn_shard.shape[1])
    a, b, c = q_width, q_width + kv_width, q_width + 2 * kv_width
    query_w, key_w, value_w, out_t = attn_w[:, :a], attn_w[:, a:b], attn_w[:, b:c], attn_w[:, c:]

    query_raw = product(first_normed, query_w, "nd,de->ne")
    key_raw = product(first_normed, key_w, "nd,de->ne")
    value_b = product(first_normed, value_w, "nd,de->ne").astype(BF)

    def head_prep(query_in, key_in, gain_q, gain_k):
        query_out = rotate(
            rms_scale(query_in.reshape(flat_len, q_heads, HEAD_SIZE), gain_q), cosines, sines
        )
        key_out = rotate(
            rms_scale(key_in.reshape(flat_len, key_value_heads, HEAD_SIZE), gain_k), cosines, sines
        )
        return (query_out, key_out)

    (query_rot, key_rot), prep_pull = jax.vjp(head_prep, query_raw, key_raw, gain_query, gain_key)
    query_b = query_rot.astype(BF)
    key_b = key_rot.astype(BF).reshape(flat_len, kv_width)
    local_kv = jnp.concatenate([key_b, value_b], axis=1).reshape(row_count, local_len, 2 * kv_width)
    row_kv = lax.all_gather(local_kv, "ctx", axis=1, tiled=True)
    key_rows = row_kv[..., :kv_width].reshape(row_count, row_len, key_value_heads, HEAD_SIZE)
    value_rows = row_kv[..., kv_width:].reshape(row_count, row_len, key_value_heads, HEAD_SIZE)
    query_rows = query_b.reshape(
        row_count, local_len, key_value_heads, query_group_width, HEAD_SIZE
    )

    def row_forward(packed):
        q_row, k_row, v_row, qs_row, ks_row = packed
        return attend_row(q_row, k_row, v_row, qs_row, own_slots, ks_row, row_slots)

    head_out, log_total = lax.map(
        row_forward, (query_rows, key_rows, value_rows, q_segment, k_segment)
    )
    heads_b = head_out.reshape(flat_len, q_width).astype(BF)
    attn_part = product(heads_b, out_t, "nq,dq->nd")
    attn_full = grid.tp_sum(attn_part.astype(BF))
    middle_full = x_float + attn_full
    middle_b = middle_full.astype(BF)
    own_features = lambda v: lax.dynamic_slice_in_dim(v, grid.t * feat_len, feat_len, 1)
    attn_own = own_features(attn_full)
    token_f = packed_tok.astype(F32)
    middle_own = token_f + attn_own

    ffn_part, d_mid_part, d_gain_ffn, *grads = ffn_pass(
        middle_b, dy_full, gain_ffn[None, :], gate_p, up_p, down_p, offsets
    )
    ffn_out = grid.tp_scatter(ffn_part)
    d_back = grid.tp_sum(d_mid_part)
    d_middle_full = dy_full.astype(F32) + d_back
    d_middle = own_features(d_middle_full)
    d_attn = d_middle_full.astype(BF)

    def reduce_weight(keep, send):
        blocks = (keep.shape[0] // shard_rows, shard_rows, keep.shape[1])
        return grid.reduce_ring(grid.reduce_ctx(keep.reshape(blocks), send.reshape(blocks)))

    sum_gate = reduce_weight(grads[0], grads[1])[:, :ff]
    sum_up = reduce_weight(grads[2], grads[3])[:, :ff]
    sum_down = reduce_weight(grads[4], grads[5])[:, :ff].T

    g_out = product(d_attn, heads_b, "nd,nq->dq")
    d_heads = product(d_attn, out_t, "nd,dq->nq").astype(BF)
    grad_rows = d_heads.reshape(row_count, local_len, key_value_heads, query_group_width, HEAD_SIZE)

    def row_query_keys(packed):
        q_row, k_row, v_row, qs_row, ks_row, lse_row, g_row = packed
        return query_back(q_row, k_row, v_row, qs_row, own_slots, ks_row, row_slots, lse_row, g_row)

    (key_grads, value_grads), q_grads = lax.map(
        row_query_keys,
        (query_rows, key_rows, value_rows, q_segment, k_segment, log_total, grad_rows),
    )
    kv_grads = jnp.concatenate(
        [
            key_grads.reshape(row_count, row_len, kv_width),
            value_grads.reshape(row_count, row_len, kv_width),
        ],
        axis=2,
    )
    own_kv = lax.psum_scatter(
        kv_grads.astype(BF), "ctx", scatter_dimension=1, tiled=True
    ).astype(F32)
    d_key_rot = own_kv[..., :kv_width].reshape(flat_len, key_value_heads, HEAD_SIZE)
    d_value = own_kv[..., kv_width:].reshape(flat_len, kv_width).astype(BF)
    d_query_raw, d_key_raw, d_gain_q, d_gain_k = prep_pull(
        (q_grads.reshape(flat_len, q_heads, HEAD_SIZE), d_key_rot)
    )
    d_query = d_query_raw.astype(BF)
    d_key = d_key_raw.astype(BF)
    d_qkv = jnp.concatenate([d_query, d_key, d_value], axis=1)
    g_qkv = product(first_normed, d_qkv, "nd,ne->de")
    d_normed_one = product(d_qkv, attn_w[:, :c], "ne,de->nd")
    d_x_part, d_gain_attn = attn_norm_pull(d_normed_one)
    d_x = grid.tp_scatter(d_x_part.astype(BF))
    grad_packed = (d_middle + d_x).astype(BF)
    output_packed = (middle_own + ffn_out).astype(BF)

    g_attn = jnp.concatenate([g_qkv.astype(BF), g_out.astype(BF)], axis=1)
    g_blocks = pick_blocks(g_attn.reshape(groups, shard_rows, -1), grad_order)
    sum_attn = grid.reduce_ring(
        grid.reduce_ctx(g_blocks[: groups // 2], g_blocks[groups // 2 :])
    )
    squares = jnp.stack(
        [jnp.sum(token_f * token_f), jnp.sum(attn_own * attn_own), jnp.sum(ffn_out * ffn_out)]
    )
    small = jnp.concatenate([d_gain_attn, d_gain_ffn[0], d_gain_q, d_gain_k, squares])
    small = lax.psum(small, ("fsdp", "ctx", "tp"))
    w, h = MODEL_WIDTH, HEAD_SIZE
    gain_a, gain_f = small[:w], small[w : 2 * w]
    gain_qs, gain_ks = small[2 * w : 2 * w + h], small[2 * w + h : 2 * w + 2 * h]
    entry_count = flat_len * groups * MODEL_WIDTH
    rms_stats = jnp.sqrt(small[2 * w + 2 * h :] / entry_count)
    output = bring_back(output_packed)
    grad_tokens = bring_back(grad_packed)
    return (
        output,
        grad_tokens,
        sum_attn[:, :a],
        sum_attn[:, a:b],
        sum_attn[:, b:c],
        sum_attn[:, c:].T,
        sum_gate,
        sum_up,
        sum_down,
        gain_a,
        gain_f,
        gain_qs,
        gain_ks,
        rms_stats,
    )


def solution(mesh):
    row = P(("fsdp", "ctx"), "tp")
    column = P("tp", ("fsdp", "ctx"))
    in_specs = (row, row, P(), P("fsdp", None), row, row, row, column, row, row, column) + (P(),) * 4
    out_specs = (row, row, row, row, row, column, row, row, column) + (P(),) * 5
    return jax.shard_map(local, mesh=mesh, in_specs=in_specs, out_specs=out_specs, check_vma=False)
```

```python
import functools

import jax
import jax.numpy as jnp
from jax import lax
from jax.experimental import pallas as pl
from jax.experimental.pallas import tpu as pltpu
from jax.sharding import PartitionSpec as P

MODEL_WIDTH = 1024
QUERY_HEADS = 16
KEY_VALUE_HEADS = 8
HEAD_SIZE = 64
PACKED_ROW_SLOTS = 2048
QUERY_BLOCK_ROWS = 512

EPSILON = 1e-05
ROPE_THETA = 1000000.0
NEG_FILL = -1e30
BF = jnp.bfloat16
F32 = jnp.float32


def segment_ends(lengths):
    total, ends = lengths[0], []
    for i in range(lengths.shape[0]):
        ends.append(total)
        if i + 1 < lengths.shape[0]:
            total = total + lengths[i + 1]
    return ends


def slot_tables(lengths, slot_ids):
    segment = jnp.zeros_like(slot_ids)
    start = jnp.zeros_like(slot_ids)
    for i, end in enumerate(segment_ends(lengths)):
        passed = (slot_ids >= end).astype(jnp.int32)
        segment = segment + passed
        start = start + passed * lengths[i]
    return (segment, slot_ids - start)


def product(left_arr, right_arr, pattern):
    return jnp.einsum(pattern, left_arr, right_arr, preferred_element_type=F32)


class Grid:
    def __init__(self):
        self.n = lax.axis_size("fsdp")
        self.ctx = lax.axis_size("ctx")
        self.tp = lax.axis_size("tp")
        self.z = lax.axis_index("fsdp")
        self.c = lax.axis_index("ctx")
        self.t = lax.axis_index("tp")

    def ring(self, v):
        return lax.ppermute(v, "fsdp", [(i, (i + 1) % self.n) for i in range(self.n)])

    def flip(self, v, bit):
        return lax.ppermute(v, "ctx", [(i, i ^ bit) for i in range(self.ctx)])

    def order(self):
        return [
            lax.rem(self.z - k + self.n, self.n) * self.ctx + (self.c ^ d)
            for d in range(self.ctx)
            for k in range(self.n)
        ]

    def collect(self, shard):
        have = [shard]
        for _ in range(self.n - 1):
            have.append(self.ring(have[-1]))
        bits = []
        b = self.ctx // 2
        while b:
            bits.append(b)
            b //= 2
        got = {(0, k): v for k, v in enumerate(have)}
        for bit in bits:
            more = {(d | bit, k): self.flip(v, bit) for (d, k), v in got.items()}
            got.update(more)
        return [got[(d, k)] for d in range(self.ctx) for k in range(self.n)]

    def reduce_ctx(self, keep, send):
        total = (keep.astype(F32) + self.flip(send, 1).astype(F32)).astype(BF)
        bit = self.ctx // 2
        stride = keep.shape[0] // 2
        if bit >= 2:
            away = self.flip(total[stride:], bit)
            total = (total[:stride].astype(F32) + away.astype(F32)).astype(BF)
        return total

    def reduce_ring(self, total):
        run = total[1 % self.n]
        for k in range(2, self.n + 1):
            run = self.ring(run).astype(F32) + total[k % self.n].astype(F32)
            if k < self.n:
                run = run.astype(BF)
        return run

    def tp_pair(self, own, other, axis):
        first = jnp.where(self.t == 0, own, other)
        second = jnp.where(self.t == 0, other, own)
        return jnp.concatenate([first, second], axis=axis)

    def tp_gather(self, v):
        if self.tp == 2:
            other = lax.ppermute(v, "tp", [(0, 1), (1, 0)])
            return self.tp_pair(v, other, 1)
        return lax.all_gather(v, "tp", axis=1, tiled=True)

    def tp_sum(self, v):
        if self.tp == 2:
            other = lax.ppermute(v, "tp", [(0, 1), (1, 0)])
            return v.astype(F32) + other.astype(F32)
        return lax.psum(v, "tp").astype(F32)

    def tp_scatter(self, v):
        if self.tp == 2:
            half = v.shape[1] // 2
            own = lax.dynamic_slice_in_dim(v, self.t * half, half, 1)
            away = lax.dynamic_slice_in_dim(v, (1 - self.t) * half, half, 1)
            other = lax.ppermute(away, "tp", [(0, 1), (1, 0)])
            return own.astype(F32) + other.astype(F32)
        return lax.psum_scatter(v, "tp", scatter_dimension=1, tiled=True).astype(F32)

    def tp_parts(self, v):
        if self.tp == 2:
            return v, lax.ppermute(v, "tp", [(0, 1), (1, 0)])
        return lax.psum(v, "tp"), jnp.zeros_like(v)

    def sum_all(self, v):
        for axis, size in (("ctx", self.ctx), ("tp", self.tp), ("fsdp", self.n)):
            bit = 1
            while bit < size:
                v = v + lax.ppermute(v, axis, [(i, i ^ bit) for i in range(size)])
                bit *= 2
        return v


def dot(a, b, ca, cb, precision=None):
    return lax.dot_general(
        a, b, (((ca,), (cb,)), ((), ())), preferred_element_type=F32, precision=precision
    )


def lanes(shape):
    return lax.broadcasted_iota(jnp.int32, shape, 1)


def half_mean(v):
    low = lanes(v.shape) < HEAD_SIZE
    first = jnp.sum(jnp.where(low, v, 0.0), axis=1, keepdims=True)
    second = jnp.sum(jnp.where(low, 0.0, v), axis=1, keepdims=True)
    return jnp.where(low, first, second) * (1.0 / HEAD_SIZE)


def half_swap(v):
    quarter = HEAD_SIZE // 2
    left = pltpu.roll(v, 128 - quarter, 1)
    right = pltpu.roll(v, quarter, 1)
    return jnp.where(lanes(v.shape) % HEAD_SIZE < quarter, left, right)


def row_scale(v):
    return lax.rsqrt(jnp.mean(v * v, axis=1, keepdims=True) + EPSILON)


def norm_back(dn, v, gain):
    scale = row_scale(v)
    unit = v * scale
    scaled = dn * gain
    grad = scale * (scaled - unit * jnp.mean(scaled * unit, axis=1, keepdims=True))
    return grad, jnp.sum(dn * unit, axis=0, keepdims=True)


def qk_forward(raw, gain, cosines, sines, is_value):
    normed = raw * lax.rsqrt(half_mean(raw * raw) + EPSILON) * gain
    turned = normed * cosines + half_swap(normed) * sines
    return jnp.where(is_value, raw, turned)


def qk_backward(grad, raw, gain, cosines, sines, is_value):
    straight = grad * cosines - half_swap(grad) * sines
    scale = lax.rsqrt(half_mean(raw * raw) + EPSILON)
    unit = raw * scale
    scaled = straight * gain
    back = scale * (scaled - unit * half_mean(scaled * unit))
    gain_grad = jnp.sum(straight * unit, axis=0, keepdims=True)
    return jnp.where(is_value, grad, back), gain_grad


def two_heads(v):
    low = lanes(v.shape) < HEAD_SIZE
    zero = jnp.zeros_like(v)
    return jnp.concatenate([jnp.where(low, v, zero), jnp.where(low, zero, v)], axis=0)


def one_row(v):
    rows = v.shape[0] // 2
    return jnp.where(lanes((rows, v.shape[1])) < HEAD_SIZE, v[:rows], v[rows:])


def doubled(ref, rows, column):
    v = ref[rows, column : column + HEAD_SIZE]
    return jnp.concatenate([v, v], axis=1)


def qkv_kernel(q_width, kv_width, pieces, shard_rows, offs, x, gain, head_gain, cosines, sines, *refs):
    sources = refs[:pieces]
    qb, kv, raw, w, sem = refs[pieces:]
    copies = [
        pltpu.make_async_copy(
            sources[i], w.at[pl.ds(pl.multiple_of(offs[i], shard_rows), shard_rows), :], sem.at[i]
        )
        for i in range(pieces)
    ]
    for c in copies:
        c.start()
    v = x[...].astype(F32)
    normed = (v * row_scale(v) * gain[...]).astype(BF)
    for c in copies:
        c.wait()
    total = q_width + 2 * kv_width
    values_from = q_width + kv_width
    for b in range(0, total, 128):
        block = dot(normed, w[:, b : b + 128], 1, 0)
        is_value = lanes(block.shape) + b >= values_from
        done = qk_forward(block, head_gain[:, b : b + 128], cosines[...], sines[...], is_value)
        raw[:, b : b + 128] = block
        if b < q_width:
            qb[:, b : b + 128] = done.astype(BF)
        else:
            kv[:, b - q_width : b - q_width + 128] = done.astype(BF)


def attend_kernel(q_width, kv_width, piece, where, qb, kv, start_col, w, heads, sums, part, acc, total, bias):
    ctx = where[0]
    rows = qb.shape[0]
    q_slot = ctx * piece + lax.broadcasted_iota(jnp.int32, (rows, piece), 0)
    n_pairs = q_width // 128

    def one_piece(p, carry):
        k_slot = p * piece + lanes((rows, piece))
        open_ = (k_slot >= start_col[...]) & (k_slot <= q_slot)
        bias[...] = jnp.where(open_, 0.0, NEG_FILL)
        at = pl.ds(pl.multiple_of(p * piece, piece), piece)
        for g in range(n_pairs):
            q2 = two_heads(qb[:, 128 * g : 128 * g + 128])
            k2 = doubled(kv, at, HEAD_SIZE * g)
            v2 = doubled(kv, at, kv_width + HEAD_SIZE * g)
            s = dot(q2, k2, 1, 1)
            for h in range(2):
                e = jnp.exp(s[h * rows : (h + 1) * rows] * 0.125 + bias[...])
                part_sum = e[:, :128]
                for b in range(128, piece, 128):
                    part_sum = part_sum + e[:, b : b + 128]
                o = dot(e.astype(BF), v2, 1, 0)
                acc[g, h * rows : (h + 1) * rows, :] += o
                total[g, h * rows : (h + 1) * rows, :] += part_sum
        return carry

    acc[...] = jnp.zeros_like(acc)
    total[...] = jnp.zeros_like(total)
    lax.fori_loop(0, ctx + 1, one_piece, 0)
    ones = jnp.ones((8, 128), F32)
    for g in range(n_pairs):
        row_total = jnp.sum(total[g], axis=1, keepdims=True)
        heads[:, 128 * g : 128 * g + 128] = one_row(acc[g] / row_total)
        sums[g] = 1.0 / dot(ones, total[g], 1, 1, lax.Precision.HIGHEST)
    out_from = q_width + 2 * kv_width
    part[...] = dot(heads[...].astype(BF), w[:, out_from:], 1, 1).astype(BF)


def attend_back_kernel(
    q_width, kv_width, piece, where, qb, kv, heads, sums, start_row, w, d_attn,
    dq, dkv, g_out, dob, bias, dq_t, *more
):
    ctx = where[0]
    rows = qb.shape[0]
    n_pairs = q_width // 128
    out_from = q_width + 2 * kv_width
    d = d_attn[...]
    dob[...] = dot(d, w[:, out_from:], 1, 0).astype(BF)
    d_turned = d.astype(F32).T.astype(BF)
    g_out[...] = dot(d_turned, heads[...].astype(BF), 1, 0).astype(BF)
    q_slot = ctx * piece + lanes((piece, rows))
    dkv[...] = jnp.zeros_like(dkv)
    dq_t[...] = jnp.zeros_like(dq_t)
    ones = jnp.ones((8, 128), F32)

    def one_piece(p, carry):
        k_slot = p * piece + lax.broadcasted_iota(jnp.int32, (piece, rows), 0)
        open_ = (k_slot >= start_row[...]) & (k_slot <= q_slot)
        bias[...] = jnp.where(open_, 0.0, NEG_FILL)
        at = pl.ds(pl.multiple_of(p * piece, piece), piece)
        for g in range(n_pairs):
            block = slice(128 * g, 128 * g + 128)
            q2 = two_heads(qb[:, block])
            do = dob[:, block]
            do2 = two_heads(do)
            delta = dot(
                ones, two_heads(do.astype(F32) * heads[:, block]), 1, 1, lax.Precision.HIGHEST
            )
            k2 = doubled(kv, at, HEAD_SIZE * g)
            v2 = doubled(kv, at, kv_width + HEAD_SIZE * g)
            k_t = k2.astype(F32).T.astype(BF)
            s = dot(k2, q2, 1, 1)
            dp = dot(v2, do2, 1, 1)
            dk = jnp.zeros((piece, 128), F32)
            dv = jnp.zeros((piece, 128), F32)
            for h in range(2):
                part = slice(h * rows, (h + 1) * rows)
                pe = jnp.exp(s[:, part] * 0.125 + bias[...]) * sums[g, 0:1, part]
                ds = (pe * (dp[:, part] - delta[0:1, part])).astype(BF)
                dv = dv + dot(pe.astype(BF), do2[part], 1, 0)
                dk = dk + dot(ds, q2[part], 1, 0)
                dq_t[g, :, part] += dot(k_t, ds, 1, 0)
            dk = dk[:, :HEAD_SIZE] + dk[:, HEAD_SIZE:]
            dv = dv[:, :HEAD_SIZE] + dv[:, HEAD_SIZE:]
            c = HEAD_SIZE * g
            dkv[at, c : c + HEAD_SIZE] = (dk * 0.125).astype(BF)
            dkv[at, kv_width + c : kv_width + c + HEAD_SIZE] = dv.astype(BF)
        return carry

    lax.fori_loop(0, ctx + 1, one_piece, 0)
    for g in range(n_pairs):
        dq[:, 128 * g : 128 * g + 128] = one_row(dq_t[g].T) * 0.125


def qkv_back_kernel(
    q_width, kv_width, pieces, shard_rows, offs, x, gain, head_gain, cosines, sines, raw, w, dq, dkv,
    g_out, dx, d_gain, d_head_gain, keep, send, d_all, turned, g
):
    total = q_width + 2 * kv_width
    values_from = q_width + kv_width
    for b in range(0, total, 128):
        grad = dq[:, b : b + 128] if b < q_width else dkv[:, b - q_width : b - q_width + 128]
        is_value = lanes(grad.shape) + b >= values_from
        back, gain_grad = qk_backward(
            grad, raw[:, b : b + 128], head_gain[:, b : b + 128], cosines[...], sines[...], is_value
        )
        d_all[:, b : b + 128] = back.astype(BF)
        d_head_gain[:, b : b + 128] = gain_grad
    v = x[...].astype(F32)
    turned[...] = (v * row_scale(v) * gain[...]).T.astype(BF)
    g[:, :total] = dot(turned[...], d_all[...], 1, 0).astype(BF)
    g[:, total:] = g_out[...]
    half = pieces // 2
    for i in range(pieces):
        at = pl.ds(pl.multiple_of(offs[pieces + i], shard_rows), shard_rows)
        to = keep if i < half else send
        row = (i % half) * shard_rows
        to[row : row + shard_rows, :] = g[at, :]
    dn = dot(d_all[...], w[:, :total], 1, 1)
    grad, gain_sum = norm_back(dn, v, gain[...])
    dx[...] = grad.astype(BF)
    d_gain[...] = gain_sum


def ffn_kernel(pieces, shard_rows, tile, group, offs, x, att_a, att_b, dy, gain, *refs):
    wg_in = refs[:pieces]
    wu_in = refs[pieces : 2 * pieces]
    wd_in = refs[2 * pieces : 3 * pieces]
    ffn, dmid, dgain, squares, nb, hid, dgt, dup = refs[3 * pieces : 3 * pieces + 8]
    (wg, wu, wd, mid, ffn_acc, dn_acc, sem) = refs[3 * pieces + 8 :]
    step = pl.program_id(0)
    steps = pl.num_programs(0)
    n_groups = wg.shape[1] // group
    per_group = group // tile

    def copies(g):
        out = []
        cols = pl.ds(g * group, group)
        for m, (src, dst) in enumerate(((wg_in, wg), (wu_in, wu), (wd_in, wd))):
            for i in range(pieces):
                rows = pl.ds(pl.multiple_of(offs[i], shard_rows), shard_rows)
                out.append(
                    pltpu.make_async_copy(src[i].at[:, cols], dst.at[rows, cols], sem.at[g, m, i])
                )
        return out

    @pl.when(step == 0)
    def _():
        for g in range(n_groups):
            for c in copies(g):
                c.start()
        v = x[...].astype(F32)
        att = att_a[...].astype(F32) + att_b[...].astype(F32)
        squares[0:1, :] = jnp.sum(v * v, axis=0, keepdims=True)
        squares[1:2, :] = jnp.sum(att * att, axis=0, keepdims=True)
        mid[...] = (v + att).astype(BF)
        v = mid[...].astype(F32)
        nb[...] = (v * row_scale(v) * gain[...]).astype(BF)
        ffn_acc[...] = jnp.zeros_like(ffn_acc)
        dn_acc[...] = jnp.zeros_like(dn_acc)

    for g in range(n_groups):

        @pl.when(step == g * per_group)
        def _(g=g):
            for c in copies(g):
                c.wait()

    cols = pl.ds(pl.multiple_of(step * tile, tile), tile)
    w_gate = wg[:, cols]
    w_up = wu[:, cols]
    w_down = wd[:, cols]
    normed = nb[...]
    dyb = dy[...]
    gate = dot(normed, w_gate, 1, 0)
    up = dot(normed, w_up, 1, 0)
    d_hidden = dot(dyb, w_down, 1, 0)
    sig = 1.0 / (1.0 + jnp.exp(-gate))
    silu = gate * sig
    hidden = (silu * up).astype(BF)
    d_gate = (d_hidden * up * (sig * (1.0 + gate * (1.0 - sig)))).astype(BF)
    d_up = (d_hidden * silu).astype(BF)
    hid[...] = hidden
    dgt[...] = d_gate
    dup[...] = d_up
    ffn_acc[...] += dot(hidden, w_down, 1, 1)
    dn_acc[...] += dot(d_gate, w_gate, 1, 1) + dot(d_up, w_up, 1, 1)

    @pl.when(step == steps - 1)
    def _():
        grad, gain_sum = norm_back(dn_acc[...], mid[...].astype(F32), gain[...])
        dgain[...] = gain_sum
        dmid[...] = grad.astype(BF)
        ffn[...] = ffn_acc[...].astype(BF)


def weight_grad_kernel(pieces, shard_rows, offs, left, right, keep, send, turn, ordered):
    @pl.when(pl.program_id(0) == 0)
    def _():
        turn[...] = left[...].astype(F32).T.astype(BF)
        for i in range(pieces):
            at = pl.ds(pl.multiple_of(offs[pieces + i], shard_rows), shard_rows)
            ordered[i * shard_rows : (i + 1) * shard_rows, :] = turn[at, :]

    half = ordered.shape[0] // 2
    keep[...] = dot(ordered[:half, :], right[...], 1, 0).astype(BF)
    send[...] = dot(ordered[half:, :], right[...], 1, 0).astype(BF)


def shape(s, t):
    return jax.ShapeDtypeStruct(s, t)


VMEM_LIMIT = pltpu.CompilerParams(vmem_limit_bytes=58 * 2**20)
ANYWHERE = pl.BlockSpec(memory_space=pl.ANY)


def once(body, scalars, n_in, n_any, outs, scratch, flops):
    vm = pl.BlockSpec(memory_space=pltpu.VMEM)

    def call(scalar, *operands):
        return pl.pallas_call(
            body,
            grid_spec=pltpu.PrefetchScalarGridSpec(
                num_scalar_prefetch=scalars,
                grid=(1,),
                in_specs=[vm] * n_in + [ANYWHERE] * n_any,
                out_specs=[vm] * len(outs),
                scratch_shapes=scratch,
            ),
            out_shape=outs,
            compiler_params=VMEM_LIMIT,
            cost_estimate=pl.CostEstimate(flops=flops, bytes_accessed=8 * 2**20, transcendentals=0),
        )(scalar, *operands)

    return call


def ffn_pass(x, att_a, att_b, dy, gain, gate_p, up_p, down_p, offsets):
    rows, width = x.shape
    pieces = len(gate_p)
    shard_rows, ff = gate_p[0].shape
    tile = 256 if ff % 256 == 0 else 128
    group = 3 * tile if ff % (3 * tile) == 0 else tile
    whole = lambda shape: pl.BlockSpec(shape, lambda s, o: (0, 0))
    column = pl.BlockSpec((rows, tile), lambda s, o: (0, s))
    return pl.pallas_call(
        functools.partial(ffn_kernel, pieces, shard_rows, tile, group),
        grid_spec=pltpu.PrefetchScalarGridSpec(
            num_scalar_prefetch=1,
            grid=(ff // tile,),
            in_specs=[whole((rows, width))] * 4 + [whole((1, width))] + [ANYWHERE] * (3 * pieces),
            out_specs=[whole((rows, width))] * 2
            + [whole((1, width)), whole((2, width)), whole((rows, width))]
            + [column] * 3,
            scratch_shapes=[
                pltpu.VMEM((width, ff), BF),
                pltpu.VMEM((width, ff), BF),
                pltpu.VMEM((width, ff), BF),
                pltpu.VMEM((rows, width), BF),
                pltpu.VMEM((rows, width), F32),
                pltpu.VMEM((rows, width), F32),
                pltpu.SemaphoreType.DMA((ff // group, 3, pieces)),
            ],
        ),
        out_shape=[shape((rows, width), BF)] * 2
        + [shape((1, width), F32), shape((2, width), F32), shape((rows, width), BF)]
        + [shape((rows, ff), BF)] * 3,
        compiler_params=VMEM_LIMIT,
        cost_estimate=pl.CostEstimate(
            flops=12 * rows * width * ff, bytes_accessed=6 * width * ff, transcendentals=rows * ff
        ),
    )(offsets, x, att_a, att_b, dy, gain, *gate_p, *up_p, *down_p)


def weight_grad(left, right, offsets, pieces):
    rows, width = left.shape
    ff = right.shape[1]
    tile = 256 if ff % 256 == 0 else 128
    half = width // 2
    column = pl.BlockSpec((half, tile), lambda s, o: (0, s))
    return pl.pallas_call(
        functools.partial(weight_grad_kernel, pieces, width // pieces),
        grid_spec=pltpu.PrefetchScalarGridSpec(
            num_scalar_prefetch=1,
            grid=(ff // tile,),
            in_specs=[
                pl.BlockSpec((rows, width), lambda s, o: (0, 0)),
                pl.BlockSpec((rows, tile), lambda s, o: (0, s)),
            ],
            out_specs=[column, column],
            scratch_shapes=[pltpu.VMEM((width, rows), BF), pltpu.VMEM((width, rows), BF)],
        ),
        out_shape=[shape((half, ff), BF)] * 2,
        compiler_params=VMEM_LIMIT,
        cost_estimate=pl.CostEstimate(
            flops=2 * rows * width * ff, bytes_accessed=2 * width * ff, transcendentals=0
        ),
    )(offsets, left, right)


def pad_columns(v, to):
    return v if v.shape[1] == to else jnp.pad(v, ((0, 0), (0, to - v.shape[1])))


def one_hot(rows, columns):
    return (rows == columns).astype(BF)


def local(
    tokens,
    cotangent,
    slot_of,
    lengths,
    w_query,
    key_weight,
    value_weight,
    w_out,
    w_gate,
    w_up,
    w_down,
    gain_attn,
    gain_ffn,
    gain_query,
    gain_key,
):
    grid = Grid()
    stream_len = tokens.shape[0]
    feat_len = tokens.shape[1]
    local_len = PACKED_ROW_SLOTS // grid.ctx
    row_count = stream_len // local_len
    groups = grid.n * grid.ctx
    share = stream_len // groups
    q_heads = QUERY_HEADS // grid.tp
    key_value_heads = KEY_VALUE_HEADS // grid.tp
    query_group_width = QUERY_HEADS // KEY_VALUE_HEADS
    q_width = q_heads * HEAD_SIZE
    kv_width = key_value_heads * HEAD_SIZE
    flat_len = row_count * local_len
    row_len = PACKED_ROW_SLOTS
    me = grid.z * grid.ctx + grid.c
    both = ("fsdp", "ctx")

    def home(slots):
        row, place = slots // row_len, slots % row_len
        return (
            row // row_count * grid.ctx + place // local_len,
            row % row_count * local_len + place % local_len,
        )

    my_slots = lax.dynamic_slice_in_dim(slot_of, me * stream_len, stream_len, 0)
    my_target = home(my_slots)[0]
    ahead = (my_target[:, None] == my_target[None, :]) & (my_slots[None, :] < my_slots[:, None])
    send_place = my_target * share + jnp.sum(ahead.astype(jnp.int32), axis=1)
    line = jnp.arange(stream_len, dtype=jnp.int32)
    send_pick = one_hot(line[:, None], send_place[None, :])
    all_dev, all_local = home(slot_of)
    low = 32
    high = flat_len // low
    sender = (jnp.arange(slot_of.shape[0], dtype=jnp.int32) // stream_len).astype(F32)
    mine = (all_dev == me)[None, :] & (
        (all_local // low)[None, :] == jnp.arange(high, dtype=jnp.int32)[:, None]
    )
    left = jnp.where(mine, sender[None, :], 0.0).astype(BF)
    right = one_hot((all_local % low)[:, None], jnp.arange(low, dtype=jnp.int32)[None, :])
    source = product(left, right, "ht,tl->hl").reshape(flat_len).astype(jnp.int32)
    slot_line = jnp.arange(flat_len, dtype=jnp.int32)
    before = (source[:, None] == source[None, :]) & (slot_line[None, :] < slot_line[:, None])
    arrival = source * share + jnp.sum(before.astype(jnp.int32), axis=1)
    take_pick = one_hot(arrival[:, None], line[None, :])

    def spread(v):
        sent = product(send_pick, v, "pt,tf->pf").astype(BF)
        got = lax.all_to_all(sent, both, split_axis=0, concat_axis=0, tiled=True)
        return product(take_pick, got, "ja,af->jf").astype(BF)

    def bring_back(v):
        sent = product(take_pick, v, "ja,jf->af").astype(BF)
        got = lax.all_to_all(sent, both, split_axis=0, concat_axis=0, tiled=True)
        return product(send_pick, got, "pt,pf->tf").astype(BF)

    ff = w_gate.shape[1]
    ff_pad = -(-ff // 128) * 128
    attn_shard = jnp.concatenate([w_query, key_weight, value_weight, w_out.T], axis=1)
    attn_pieces = grid.collect(attn_shard)
    gate_p, up_p, down_p = (
        grid.collect(pad_columns(v, ff_pad)) for v in (w_gate, w_up, w_down.T)
    )
    shard_rows = w_gate.shape[0]
    order = grid.order()
    grad_order = [d for d in range(0, grid.ctx, 2)] + [d for d in range(1, grid.ctx, 2)]
    grad_order = [order[d * grid.n + k] for d in grad_order for k in range(grid.n)]
    offsets = (jnp.stack(order + grad_order) * shard_rows).astype(jnp.int32)

    packed_tok = spread(tokens)
    x_full = grid.tp_gather(packed_tok)
    packed_cot = spread(cotangent)
    dy_full = grid.tp_gather(packed_cot)
    own_slots = grid.c * local_len + jnp.arange(local_len, dtype=jnp.int32)
    position = slot_tables(lengths[0], own_slots)[1]
    start = own_slots - position
    frequency = ROPE_THETA ** (-jnp.arange(0, HEAD_SIZE, 2).astype(F32) / HEAD_SIZE)
    angles = position.astype(F32)[:, None] * frequency[None, :]
    cosines = jnp.tile(jnp.cos(angles), (1, 4))
    sin = jnp.sin(angles)
    sines = jnp.tile(jnp.concatenate([-sin, sin], axis=1), (1, 2))
    head_gain = jnp.concatenate(
        [
            jnp.tile(gain_query, q_heads),
            jnp.tile(gain_key, key_value_heads),
            jnp.ones((kv_width,), F32),
        ]
    )[None, :]
    place = grid.c.astype(jnp.int32)[None]
    pieces = groups
    qkv_width = q_width + 2 * kv_width
    attn_width = attn_shard.shape[1]
    n_pairs = q_width // 128
    rows = flat_len

    qb, kv, raw, attn_w = once(
        functools.partial(qkv_kernel, q_width, kv_width, pieces, shard_rows),
        1,
        5,
        pieces,
        [
            shape((rows, q_width), BF),
            shape((rows, 2 * kv_width), BF),
            shape((rows, qkv_width), F32),
            shape((MODEL_WIDTH, attn_width), BF),
        ],
        [pltpu.SemaphoreType.DMA((pieces,))],
        2 * rows * MODEL_WIDTH * qkv_width,
    )(offsets, x_full, gain_attn[None, :], head_gain, cosines, sines, *attn_pieces)
    row_kv = lax.all_gather(kv, "ctx", axis=0, tiled=True)
    attn_flops = 4 * 2 * rows * row_len * q_width
    heads, sums, attn_part = once(
        functools.partial(attend_kernel, q_width, kv_width, local_len),
        1,
        4,
        0,
        [
            shape((rows, q_width), F32),
            shape((n_pairs, 8, 2 * rows), F32),
            shape((rows, MODEL_WIDTH), BF),
        ],
        [
            pltpu.VMEM((n_pairs, 2 * rows, 128), F32),
            pltpu.VMEM((n_pairs, 2 * rows, 128), F32),
            pltpu.VMEM((rows, local_len), F32),
        ],
        attn_flops,
    )(place, qb, row_kv, start[:, None], attn_w)
    attn_a, attn_b = grid.tp_parts(attn_part)

    own_features = lambda v: lax.dynamic_slice_in_dim(v, grid.t * feat_len, feat_len, 1)
    middle_own = (
        packed_tok.astype(F32)
        + own_features(attn_a).astype(F32)
        + own_features(attn_b).astype(F32)
    )
    ffn_part, d_mid_part, d_gain_ffn, squares, normed_two, hidden, d_gate, d_up = ffn_pass(
        x_full, attn_a, attn_b, dy_full, gain_ffn[None, :], gate_p, up_p, down_p, offsets
    )
    d_middle_full = dy_full.astype(F32) + grid.tp_sum(d_mid_part)
    d_middle = own_features(d_middle_full)
    d_attn = d_middle_full.astype(BF)

    def reduce_weight(pair):
        keep, send = pair
        blocks = (keep.shape[0] // shard_rows, shard_rows, keep.shape[1])
        return grid.reduce_ring(grid.reduce_ctx(keep.reshape(blocks), send.reshape(blocks)))

    sum_down = reduce_weight(weight_grad(dy_full, hidden, offsets, pieces))[:, :ff].T
    sum_gate = reduce_weight(weight_grad(normed_two, d_gate, offsets, pieces))[:, :ff]
    sum_up = reduce_weight(weight_grad(normed_two, d_up, offsets, pieces))[:, :ff]
    ffn_out = grid.tp_scatter(ffn_part)

    dq, dkv, g_out = once(
        functools.partial(attend_back_kernel, q_width, kv_width, local_len),
        1,
        7,
        0,
        [
            shape((rows, q_width), F32),
            shape((row_len, 2 * kv_width), BF),
            shape((MODEL_WIDTH, q_width), BF),
        ],
        [
            pltpu.VMEM((rows, q_width), BF),
            pltpu.VMEM((local_len, rows), F32),
            pltpu.VMEM((n_pairs, 128, 2 * rows), F32),
        ],
        3 * attn_flops,
    )(place, qb, row_kv, heads, sums, start[None, :], attn_w, d_attn)
    own_kv = lax.psum_scatter(dkv, "ctx", scatter_dimension=0, tiled=True).astype(F32)
    own_kv = jnp.concatenate(
        [own_kv[:, :kv_width], own_kv[:, kv_width:].astype(BF).astype(F32)], axis=1
    )
    d_x_part, d_gain_attn, d_head_gain, keep, send = once(
        functools.partial(qkv_back_kernel, q_width, kv_width, pieces, shard_rows),
        1,
        10,
        0,
        [
            shape((rows, MODEL_WIDTH), BF),
            shape((1, MODEL_WIDTH), F32),
            shape((1, qkv_width), F32),
            shape((MODEL_WIDTH // 2, attn_width), BF),
            shape((MODEL_WIDTH // 2, attn_width), BF),
        ],
        [
            pltpu.VMEM((rows, qkv_width), BF),
            pltpu.VMEM((MODEL_WIDTH, rows), BF),
            pltpu.VMEM((MODEL_WIDTH, attn_width), BF),
        ],
        4 * rows * MODEL_WIDTH * qkv_width,
    )(
        offsets, x_full, gain_attn[None, :], head_gain, cosines, sines, raw, attn_w, dq, own_kv, g_out
    )
    d_x = grid.tp_scatter(d_x_part)
    grad_packed = (d_middle + d_x).astype(BF)
    output_packed = (middle_own + ffn_out).astype(BF)
    sum_attn = reduce_weight((keep, send))
    a, b, c = q_width, q_width + kv_width, q_width + 2 * kv_width

    per_head = d_head_gain[0].reshape(-1, HEAD_SIZE)
    d_gain_q = jnp.sum(per_head[:q_heads], axis=0)
    d_gain_k = jnp.sum(per_head[q_heads : q_heads + key_value_heads], axis=0)
    sums_of_squares = jnp.concatenate(
        [jnp.sum(squares, axis=1) / grid.tp, jnp.sum(ffn_out * ffn_out)[None]]
    )
    small = jnp.concatenate([d_gain_attn[0], d_gain_ffn[0], d_gain_q, d_gain_k, sums_of_squares])
    small = grid.sum_all(small)
    w, h = MODEL_WIDTH, HEAD_SIZE
    gain_a, gain_f = small[:w], small[w : 2 * w]
    gain_qs, gain_ks = small[2 * w : 2 * w + h], small[2 * w + h : 2 * w + 2 * h]
    entry_count = flat_len * groups * MODEL_WIDTH
    rms_stats = jnp.sqrt(small[2 * w + 2 * h :] / entry_count)
    output = bring_back(output_packed)
    grad_tokens = bring_back(grad_packed)
    return (
        output,
        grad_tokens,
        sum_attn[:, :a],
        sum_attn[:, a:b],
        sum_attn[:, b:c],
        sum_attn[:, c:].T,
        sum_gate,
        sum_up,
        sum_down,
        gain_a,
        gain_f,
        gain_qs,
        gain_ks,
        rms_stats,
    )


def solution(mesh):
    row = P(("fsdp", "ctx"), "tp")
    column = P("tp", ("fsdp", "ctx"))
    in_specs = (row, row, P(), P("fsdp", None), row, row, row, column, row, row, column) + (P(),) * 4
    out_specs = (row, row, row, row, row, column, row, row, column) + (P(),) * 5
    return jax.shard_map(local, mesh=mesh, in_specs=in_specs, out_specs=out_specs, check_vma=False)
```

```python
import functools

import jax
import jax.numpy as jnp
from jax import lax
from jax.experimental import pallas as pl
from jax.experimental.pallas import tpu as pltpu
from jax.sharding import PartitionSpec as P

MODEL_WIDTH = 1024
QUERY_HEADS = 16
KEY_VALUE_HEADS = 8
HEAD_SIZE = 64
PACKED_ROW_SLOTS = 2048
QUERY_BLOCK_ROWS = 512

EPSILON = 1e-05
ROPE_THETA = 1000000.0
NEG_FILL = -1e30
BF = jnp.bfloat16
F32 = jnp.float32


def segment_ends(lengths):
    total, ends = lengths[0], []
    for i in range(lengths.shape[0]):
        ends.append(total)
        if i + 1 < lengths.shape[0]:
            total = total + lengths[i + 1]
    return ends


def slot_tables(lengths, slot_ids):
    segment = jnp.zeros_like(slot_ids)
    start = jnp.zeros_like(slot_ids)
    for i, end in enumerate(segment_ends(lengths)):
        passed = (slot_ids >= end).astype(jnp.int32)
        segment = segment + passed
        start = start + passed * lengths[i]
    return (segment, slot_ids - start)


def product(left_arr, right_arr, pattern):
    return jnp.einsum(pattern, left_arr, right_arr, preferred_element_type=F32)


class Grid:
    def __init__(self):
        self.n = lax.axis_size("fsdp")
        self.ctx = lax.axis_size("ctx")
        self.tp = lax.axis_size("tp")
        self.z = lax.axis_index("fsdp")
        self.c = lax.axis_index("ctx")
        self.t = lax.axis_index("tp")

    def ring(self, v):
        return lax.ppermute(v, "fsdp", [(i, (i + 1) % self.n) for i in range(self.n)])

    def flip(self, v, bit):
        return lax.ppermute(v, "ctx", [(i, i ^ bit) for i in range(self.ctx)])

    def order(self):
        return [
            lax.rem(self.z - k + self.n, self.n) * self.ctx + (self.c ^ d)
            for d in range(self.ctx)
            for k in range(self.n)
        ]

    def reduce_ctx(self, keep, send):
        total = (keep.astype(F32) + self.flip(send, 1).astype(F32)).astype(BF)
        bit = self.ctx // 2
        stride = keep.shape[0] // 2
        if bit >= 2:
            away = self.flip(total[stride:], bit)
            total = (total[:stride].astype(F32) + away.astype(F32)).astype(BF)
        return total

    def reduce_ring(self, total):
        run = total[1 % self.n]
        for k in range(2, self.n + 1):
            run = self.ring(run).astype(F32) + total[k % self.n].astype(F32)
            if k < self.n:
                run = run.astype(BF)
        return run

    def tp_pair(self, own, other, axis):
        first = jnp.where(self.t == 0, own, other)
        second = jnp.where(self.t == 0, other, own)
        return jnp.concatenate([first, second], axis=axis)

    def tp_gather(self, v):
        if self.tp == 2:
            other = lax.ppermute(v, "tp", [(0, 1), (1, 0)])
            return self.tp_pair(v, other, 1)
        return lax.all_gather(v, "tp", axis=1, tiled=True)

    def tp_sum(self, v):
        if self.tp == 2:
            other = lax.ppermute(v, "tp", [(0, 1), (1, 0)])
            return v.astype(F32) + other.astype(F32)
        return lax.psum(v, "tp").astype(F32)

    def tp_scatter(self, v):
        if self.tp == 2:
            half = v.shape[1] // 2
            own = lax.dynamic_slice_in_dim(v, self.t * half, half, 1)
            away = lax.dynamic_slice_in_dim(v, (1 - self.t) * half, half, 1)
            other = lax.ppermute(away, "tp", [(0, 1), (1, 0)])
            return own.astype(F32) + other.astype(F32)
        return lax.psum_scatter(v, "tp", scatter_dimension=1, tiled=True).astype(F32)

    def tp_parts(self, v):
        if self.tp == 2:
            return v, lax.ppermute(v, "tp", [(0, 1), (1, 0)])
        return lax.psum(v, "tp"), jnp.zeros_like(v)

    def sum_all(self, v):
        for axis, size in (("ctx", self.ctx), ("tp", self.tp), ("fsdp", self.n)):
            bit = 1
            while bit < size:
                v = v + lax.ppermute(v, axis, [(i, i ^ bit) for i in range(size)])
                bit *= 2
        return v


def dot(a, b, ca, cb, precision=None):
    return lax.dot_general(
        a, b, (((ca,), (cb,)), ((), ())), preferred_element_type=F32, precision=precision
    )


def lanes(shape):
    return lax.broadcasted_iota(jnp.int32, shape, 1)


def half_mean(v):
    low = lanes(v.shape) < HEAD_SIZE
    first = jnp.sum(jnp.where(low, v, 0.0), axis=1, keepdims=True)
    second = jnp.sum(jnp.where(low, 0.0, v), axis=1, keepdims=True)
    return jnp.where(low, first, second) * (1.0 / HEAD_SIZE)


def half_swap(v):
    quarter = HEAD_SIZE // 2
    left = pltpu.roll(v, 128 - quarter, 1)
    right = pltpu.roll(v, quarter, 1)
    return jnp.where(lanes(v.shape) % HEAD_SIZE < quarter, left, right)


def row_scale(v):
    return lax.rsqrt(jnp.mean(v * v, axis=1, keepdims=True) + EPSILON)


def norm_back(dn, v, gain):
    scale = row_scale(v)
    unit = v * scale
    scaled = dn * gain
    grad = scale * (scaled - unit * jnp.mean(scaled * unit, axis=1, keepdims=True))
    return grad, jnp.sum(dn * unit, axis=0, keepdims=True)


def qk_forward(raw, gain, cosines, sines, is_value):
    normed = raw * lax.rsqrt(half_mean(raw * raw) + EPSILON) * gain
    turned = normed * cosines + half_swap(normed) * sines
    return jnp.where(is_value, raw, turned)


def qk_backward(grad, raw, gain, cosines, sines, is_value):
    straight = grad * cosines - half_swap(grad) * sines
    scale = lax.rsqrt(half_mean(raw * raw) + EPSILON)
    unit = raw * scale
    scaled = straight * gain
    back = scale * (scaled - unit * half_mean(scaled * unit))
    gain_grad = jnp.sum(straight * unit, axis=0, keepdims=True)
    return jnp.where(is_value, grad, back), gain_grad


def two_heads(v):
    low = lanes(v.shape) < HEAD_SIZE
    zero = jnp.zeros_like(v)
    return jnp.concatenate([jnp.where(low, v, zero), jnp.where(low, zero, v)], axis=0)


def one_row(v):
    rows = v.shape[0] // 2
    return jnp.where(lanes((rows, v.shape[1])) < HEAD_SIZE, v[:rows], v[rows:])


def doubled(ref, rows, column):
    v = ref[rows, column : column + HEAD_SIZE]
    return jnp.concatenate([v, v], axis=1)


def attend_back_kernel(
    q_width, kv_width, piece, where, qb, kv, heads, sums, start_row, w, d_attn,
    dq, dkv, g_out, dob, bias, dq_t, *more
):
    ctx = where[0]
    rows = qb.shape[0]
    n_pairs = q_width // 128
    out_from = q_width + 2 * kv_width
    d = d_attn[...]
    dob[...] = dot(d, w[:, out_from:], 1, 0).astype(BF)
    d_turned = d.astype(F32).T.astype(BF)
    g_out[...] = dot(d_turned, heads[...].astype(BF), 1, 0).astype(BF)
    q_slot = ctx * piece + lanes((piece, rows))
    dkv[...] = jnp.zeros_like(dkv)
    dq_t[...] = jnp.zeros_like(dq_t)
    ones = jnp.ones((8, 128), F32)

    def one_piece(p, carry):
        k_slot = p * piece + lax.broadcasted_iota(jnp.int32, (piece, rows), 0)
        open_ = (k_slot >= start_row[...]) & (k_slot <= q_slot)
        bias[...] = jnp.where(open_, 0.0, NEG_FILL)
        at = pl.ds(pl.multiple_of(p * piece, piece), piece)
        for g in range(n_pairs):
            block = slice(128 * g, 128 * g + 128)
            q2 = two_heads(qb[:, block])
            do = dob[:, block]
            do2 = two_heads(do)
            delta = dot(
                ones, two_heads(do.astype(F32) * heads[:, block]), 1, 1, lax.Precision.HIGHEST
            )
            k2 = doubled(kv, at, HEAD_SIZE * g)
            v2 = doubled(kv, at, kv_width + HEAD_SIZE * g)
            k_t = k2.astype(F32).T.astype(BF)
            s = dot(k2, q2, 1, 1)
            dp = dot(v2, do2, 1, 1)
            dk = jnp.zeros((piece, 128), F32)
            dv = jnp.zeros((piece, 128), F32)
            for h in range(2):
                part = slice(h * rows, (h + 1) * rows)
                pe = jnp.exp(s[:, part] * 0.125 + bias[...]) * sums[g, 0:1, part]
                ds = (pe * (dp[:, part] - delta[0:1, part])).astype(BF)
                dv = dv + dot(pe.astype(BF), do2[part], 1, 0)
                dk = dk + dot(ds, q2[part], 1, 0)
                dq_t[g, :, part] += dot(k_t, ds, 1, 0)
            dk = dk[:, :HEAD_SIZE] + dk[:, HEAD_SIZE:]
            dv = dv[:, :HEAD_SIZE] + dv[:, HEAD_SIZE:]
            c = HEAD_SIZE * g
            dkv[at, c : c + HEAD_SIZE] = (dk * 0.125).astype(BF)
            dkv[at, kv_width + c : kv_width + c + HEAD_SIZE] = dv.astype(BF)
        return carry

    lax.fori_loop(0, ctx + 1, one_piece, 0)
    for g in range(n_pairs):
        dq[:, 128 * g : 128 * g + 128] = one_row(dq_t[g].T) * 0.125


def qkv_back_kernel(
    q_width, kv_width, pieces, shard_rows, offs, x, gain, head_gain, cosines, sines, raw, w, dq, dkv,
    g_out, dx, d_gain, d_head_gain, keep, send, d_all, turned, g
):
    total = q_width + 2 * kv_width
    values_from = q_width + kv_width
    for b in range(0, total, 128):
        grad = dq[:, b : b + 128] if b < q_width else dkv[:, b - q_width : b - q_width + 128]
        is_value = lanes(grad.shape) + b >= values_from
        back, gain_grad = qk_backward(
            grad, raw[:, b : b + 128], head_gain[:, b : b + 128], cosines[...], sines[...], is_value
        )
        d_all[:, b : b + 128] = back.astype(BF)
        d_head_gain[:, b : b + 128] = gain_grad
    v = x[...].astype(F32)
    turned[...] = (v * row_scale(v) * gain[...]).T.astype(BF)
    g[:, :total] = dot(turned[...], d_all[...], 1, 0).astype(BF)
    g[:, total:] = g_out[...]
    half = pieces // 2
    for i in range(pieces):
        at = pl.ds(pl.multiple_of(offs[pieces + i], shard_rows), shard_rows)
        to = keep if i < half else send
        row = (i % half) * shard_rows
        to[row : row + shard_rows, :] = g[at, :]
    dn = dot(d_all[...], w[:, :total], 1, 1)
    grad, gain_sum = norm_back(dn, v, gain[...])
    dx[...] = grad.astype(BF)
    d_gain[...] = gain_sum


def ffn_kernel(mid, dy, gain, w_gate, w_up, w_down, ffn, dmid, dgain, nb, hid, dgt, dup, ffn_acc, dn_acc):
    step = pl.program_id(0)

    @pl.when(step == 0)
    def _():
        v = mid[...].astype(BF).astype(F32)
        nb[...] = (v * row_scale(v) * gain[...]).astype(BF)
        ffn_acc[...] = jnp.zeros_like(ffn_acc)
        dn_acc[...] = jnp.zeros_like(dn_acc)

    normed = nb[...]
    gate = dot(normed, w_gate[...], 1, 0)
    up = dot(normed, w_up[...], 1, 0)
    d_hidden = dot(dy[...], w_down[...], 1, 0)
    sig = 1.0 / (1.0 + jnp.exp(-gate))
    silu = gate * sig
    hidden = (silu * up).astype(BF)
    d_gate = (d_hidden * up * (sig * (1.0 + gate * (1.0 - sig)))).astype(BF)
    d_up = (d_hidden * silu).astype(BF)
    hid[...] = hidden
    dgt[...] = d_gate
    dup[...] = d_up
    ffn_acc[...] += dot(hidden, w_down[...], 1, 1)
    dn_acc[...] += dot(d_gate, w_gate[...], 1, 1) + dot(d_up, w_up[...], 1, 1)

    @pl.when(step == pl.num_programs(0) - 1)
    def _():
        v = mid[...].astype(BF).astype(F32)
        grad, gain_sum = norm_back(dn_acc[...], v, gain[...])
        dgain[...] = gain_sum
        dmid[...] = grad.astype(BF)
        ffn[...] = ffn_acc[...].astype(BF)


def weight_grad_kernel(pieces, shard_rows, offs, left, right, keep, send, turn, ordered):
    @pl.when(pl.program_id(0) == 0)
    def _():
        turn[...] = left[...].astype(F32).T.astype(BF)
        for i in range(pieces):
            at = pl.ds(pl.multiple_of(offs[pieces + i], shard_rows), shard_rows)
            ordered[i * shard_rows : (i + 1) * shard_rows, :] = turn[at, :]

    half = ordered.shape[0] // 2
    keep[...] = dot(ordered[:half, :], right[...], 1, 0).astype(BF)
    send[...] = dot(ordered[half:, :], right[...], 1, 0).astype(BF)


class Place:
    def __init__(self, n, ctx, tp):
        self.n, self.ctx, self.tp = n, ctx, tp
        self.z = lax.axis_index("fsdp")
        self.c = lax.axis_index("ctx")
        self.t = lax.axis_index("tp")
        self.me = self.z * ctx + self.c

    def at(self, z=None, c=None, t=None):
        return (
            self.z if z is None else z,
            self.c if c is None else c,
            self.t if t is None else t,
        )

    def peer(self, j):
        p = lax.rem(self.me + j, self.n * self.ctx)
        return self.at(p // self.ctx, lax.rem(p, self.ctx))

    def up(self, j):
        return self.at(z=lax.rem(self.z + j, self.n))

    def flip(self, bit):
        if bit == 1:
            return self.c + 1 - 2 * lax.rem(self.c, 2)
        return lax.rem(self.c + 2, 4)

    def side(self, j):
        return self.at(t=lax.rem(self.t + j, self.tp))

    def owner(self, k, c):
        return lax.rem(self.z - k + self.n, self.n) * self.ctx + c

    def greet(self):
        barrier = pltpu.get_barrier_semaphore()
        group = self.n * self.ctx
        for j in range(1, group):
            pl.semaphore_signal(barrier, inc=1, device_id=self.peer(j), device_id_type=MESH)
        for j in range(1, self.tp):
            pl.semaphore_signal(barrier, inc=1, device_id=self.side(j), device_id_type=MESH)
        pl.semaphore_wait(barrier, group + self.tp - 2)


MESH = pl.DeviceIdType.MESH


def remote(src, dst, send, recv, device):
    return pltpu.make_async_remote_copy(
        src_ref=src, dst_ref=dst, send_sem=send, recv_sem=recv, device_id=device, device_id_type=MESH
    )


def block_rows(index, size):
    return pl.ds(pl.multiple_of(index * size, size), size)


class Gather:
    def __init__(self, place, shard, whole, columns, number, sems):
        z_send, z_recv, x_send, x_recv, c_send, c_recv, own = sems
        h = shard.shape[0]
        n = place.n
        view = lambda index: whole.at[block_rows(index, h), columns]
        here, there = place.c, place.flip(2)
        mine = shard.at[:, columns]
        self.own = pltpu.make_async_copy(mine, view(place.me), own.at[number])
        self.line = [
            remote(mine, view(place.me), z_send.at[number, j], z_recv.at[number, j], place.up(j))
            for j in range(1, n)
        ]
        self.chip = [
            remote(
                mine if k == 0 else view(place.owner(k, here)),
                view(place.owner(k, here)),
                x_send.at[number, k],
                x_recv.at[number, k],
                place.at(c=there),
            )
            for k in range(n)
        ]
        self.core = [
            remote(
                mine if i == 0 else view(place.owner(i % n, here if i < n else there)),
                view(place.owner(i % n, here if i < n else there)),
                c_send.at[number, i],
                c_recv.at[number, i],
                place.at(c=place.flip(1)),
            )
            for i in range(2 * n)
        ]

    def begin(self):
        for copy in self.line:
            copy.start()
        self.chip[0].start()
        self.own.start()
        self.core[0].start()

    def pass_line(self, k):
        self.line[k - 1].wait_recv()
        self.chip[k].start()
        self.core[k].start()

    def pass_chip(self, k):
        self.chip[k].wait_recv()
        self.core[len(self.chip) + k].start()

    def finish(self):
        for copy in self.core:
            copy.wait_recv()
        self.own.wait()

    def drain(self):
        for copy in self.line + self.chip + self.core:
            copy.wait_send()


def forward_kernel(
    n, ctx, tp, q_width, kv_width, ff,
    sent_x, sent_y, pick, gain, head_gain, cosines, sines, start_col, attn_shard, ffn_shard,
    x, dy, qb, kv, raw, heads, sums, mid, squares, w_attn, w_ffn,
    got_x, got_y, own_x, own_y, x_land, y_land, w, kv_all, part, land, acc, total, bias,
    route_send, route_recv, tp_send, tp_recv, kv_send, kv_recv, out_sem, *gather_sems
):
    place = Place(n, ctx, tp)
    group = n * ctx
    rows = got_x.shape[0]
    share = rows // group
    feat = got_x.shape[1]
    width = x_land.shape[1]
    piece = rows
    every = pl.ds(0, attn_shard.shape[1])
    attn = Gather(place, attn_shard, w, every, 0, gather_sems)
    ffn = [
        Gather(place, ffn_shard, w_ffn, pl.ds(i * ff, ff), 1 + i, gather_sems) for i in range(3)
    ]

    def route(number, src, dst):
        return [
            remote(
                src.at[block_rows(lax.rem(place.me + j, group), share), :],
                dst.at[block_rows(place.me, share), :],
                route_send.at[number, j],
                route_recv.at[number, j],
                place.peer(j),
            )
            for j in range(1, group)
        ]

    def widen(number, src, dst):
        return [
            remote(
                src,
                dst.at[:, block_rows(place.t, feat)],
                tp_send.at[number, j],
                tp_recv.at[number, j],
                place.side(j),
            )
            for j in range(1, tp)
        ]

    def own_block(src, dst):
        at = block_rows(place.me, share)
        dst[at, :] = src[at, :]

    route_x, route_y = route(0, sent_x, got_x), route(1, sent_y, got_y)
    wide_x, wide_y = widen(0, own_x, x_land), widen(1, own_y, y_land)
    place.greet()
    for copy in route_x:
        copy.start()
    attn.begin()
    for g in ffn:
        g.begin()
    own_block(sent_x, got_x)
    for copy in route_x:
        copy.wait_recv()
    own_x[...] = dot(pick[...], got_x[...], 1, 0).astype(BF)
    for copy in wide_x:
        copy.start()
    x_land[:, block_rows(place.t, feat)] = own_x[...]
    for copy in route_y:
        copy.start()
    own_block(sent_y, got_y)
    for k in range(1, n):
        attn.pass_line(k)
    for k in range(n):
        attn.pass_chip(k)
    for copy in wide_x:
        copy.wait_recv()
    v = x_land[...].astype(F32)
    x[...] = x_land[...]
    normed = (v * row_scale(v) * gain[...]).astype(BF)
    attn.finish()
    write_w = pltpu.make_async_copy(w, w_attn, out_sem.at[0])
    write_w.start()

    own_rows = block_rows(place.c, piece)
    values_from = q_width + kv_width
    for b in list(range(q_width, q_width + 2 * kv_width, 128)) + list(range(0, q_width, 128)):
        if b == 0:
            later = start_keys(place, kv_all, own_rows, kv_send, kv_recv)
        block = dot(normed, w[:, b : b + 128], 1, 0)
        is_value = lanes(block.shape) + b >= values_from
        done = qk_forward(block, head_gain[:, b : b + 128], cosines[...], sines[...], is_value)
        raw[:, b : b + 128] = block
        if b < q_width:
            qb[:, b : b + 128] = done.astype(BF)
        else:
            kv_all[own_rows, b - q_width : b - q_width + 128] = done.astype(BF)
    for g in ffn:
        g.pass_line(1)
        g.pass_chip(0)

    q_slot = place.c * piece + lax.broadcasted_iota(jnp.int32, (rows, piece), 0)
    n_pairs = q_width // 128

    def one_piece(p):
        k_slot = p * piece + lanes((rows, piece))
        open_ = (k_slot >= start_col[...]) & (k_slot <= q_slot)
        bias[...] = jnp.where(open_, 0.0, NEG_FILL)
        at = block_rows(p, piece)

        for g in range(n_pairs):
            q2 = two_heads(qb[:, 128 * g : 128 * g + 128])
            k2 = doubled(kv_all, at, HEAD_SIZE * g)
            v2 = doubled(kv_all, at, kv_width + HEAD_SIZE * g)
            s = dot(q2, k2, 1, 1)
            for h in range(2):
                e = jnp.exp(s[h * rows : (h + 1) * rows] * 0.125 + bias[...])
                part_sum = e[:, :128]
                for b in range(128, piece, 128):
                    part_sum = part_sum + e[:, b : b + 128]
                o = dot(e.astype(BF), v2, 1, 0)
                acc[g, h * rows : (h + 1) * rows, :] += o
                total[g, h * rows : (h + 1) * rows, :] += part_sum

    acc[...] = jnp.zeros_like(acc)
    total[...] = jnp.zeros_like(total)
    one_piece(place.c)
    x_bit, core_bit = place.c // 2, lax.rem(place.c, 2)
    near, across, passed = later

    @pl.when(x_bit == 1)
    def _():
        across.wait_recv()
        passed.start()

    for g in ffn:
        g.pass_line(2)
        g.pass_chip(1)

    @pl.when(core_bit == 1)
    def _():
        near.wait_recv()
        one_piece(place.c - 1)

    for g in ffn:
        g.pass_line(3)

    @pl.when(x_bit == 1)
    def _():
        passed.wait_recv()

        def step(p, carry):
            one_piece(p)
            return carry

        lax.fori_loop(0, 2, step, 0)

    ones = jnp.ones((8, 128), F32)
    for g in range(n_pairs):
        row_total = jnp.sum(total[g], axis=1, keepdims=True)
        heads[:, 128 * g : 128 * g + 128] = one_row(acc[g] / row_total)
        sums[g] = 1.0 / dot(ones, total[g], 1, 1, lax.Precision.HIGHEST)
    part[...] = dot(heads[...].astype(BF), w[:, q_width + 2 * kv_width :], 1, 1).astype(BF)
    attention = [
        remote(part, land.at[j - 1], tp_send.at[2, j], tp_recv.at[2, j], place.side(j))
        for j in range(1, tp)
    ]
    for copy in attention:
        copy.start()
    write_kv = pltpu.make_async_copy(kv_all, kv, out_sem.at[1])
    for copy in route_y:
        copy.wait_recv()
    own_y[...] = dot(pick[...], got_y[...], 1, 0).astype(BF)
    for copy in wide_y:
        copy.start()
    y_land[:, block_rows(place.t, feat)] = own_y[...]
    for g in ffn:
        g.pass_chip(2)
    for copy in attention:
        copy.wait_recv()
    att = part[...].astype(F32)
    for j in range(1, tp):
        att = att + land[j - 1].astype(F32)
    v = x_land[...].astype(F32)
    squares[0:1, :] = jnp.sum(v * v, axis=0, keepdims=True)
    squares[1:2, :] = jnp.sum(att * att, axis=0, keepdims=True)
    mid[...] = v + att
    for copy in wide_y:
        copy.wait_recv()
    dy[...] = y_land[...]
    for g in ffn:
        g.pass_chip(3)

    @pl.when(core_bit == 0)
    def _():
        near.wait_send()

    @pl.when(x_bit == 0)
    def _():
        across.wait_send()

    @pl.when(x_bit == 1)
    def _():
        passed.wait_send()

    write_kv.start()
    for g in ffn:
        g.finish()
    for copy in route_x + route_y + wide_x + wide_y + attention:
        copy.wait_send()
    for g in [attn] + ffn:
        g.drain()
    write_w.wait()
    write_kv.wait()


def start_keys(place, kv_all, own_rows, send, recv):
    x_bit, core_bit = place.c // 2, lax.rem(place.c, 2)
    mine = kv_all.at[own_rows, :]
    near = remote(mine, mine, send.at[0], recv.at[0], place.at(c=place.flip(1)))
    across = remote(mine, mine, send.at[1], recv.at[1], place.at(c=place.flip(2)))
    from_chip = kv_all.at[block_rows(place.flip(2), own_rows.size), :]
    passed = remote(from_chip, from_chip, send.at[2], recv.at[2], place.at(c=place.flip(1)))

    @pl.when(x_bit == 0)
    def _():
        across.start()

    @pl.when(core_bit == 0)
    def _():
        near.start()

    return near, across, passed


def forward_pass(grid, q_width, kv_width, ff, *operands):
    sent_x, attn_shard = operands[0], operands[8]
    rows, feat = sent_x.shape
    n, ctx, tp = grid.n, grid.ctx, grid.tp
    width = feat * tp
    n_pairs = q_width // 128
    row_len = rows * ctx
    qkv_width = q_width + 2 * kv_width
    vm = pl.BlockSpec(memory_space=pltpu.VMEM)
    dma = pltpu.SemaphoreType.DMA
    group = n * ctx
    return pl.pallas_call(
        functools.partial(forward_kernel, n, ctx, tp, q_width, kv_width, ff),
        in_specs=[vm] * 8 + [ANYWHERE] * 2,
        out_specs=[vm] * 3 + [ANYWHERE] + [vm] * 5 + [ANYWHERE] * 2,
        out_shape=[
            shape((rows, width), BF),
            shape((rows, width), BF),
            shape((rows, q_width), BF),
            shape((row_len, 2 * kv_width), BF),
            shape((rows, qkv_width), F32),
            shape((rows, q_width), F32),
            shape((n_pairs, 8, 2 * rows), F32),
            shape((rows, width), F32),
            shape((2, width), F32),
            shape((width, attn_shard.shape[1]), BF),
            shape((width, 3 * ff), BF),
        ],
        scratch_shapes=[
            pltpu.VMEM((rows, feat), BF),
            pltpu.VMEM((rows, feat), BF),
            pltpu.VMEM((rows, feat), BF),
            pltpu.VMEM((rows, feat), BF),
            pltpu.VMEM((rows, width), BF),
            pltpu.VMEM((rows, width), BF),
            pltpu.VMEM((width, attn_shard.shape[1]), BF),
            pltpu.VMEM((row_len, 2 * kv_width), BF),
            pltpu.VMEM((rows, width), BF),
            pltpu.VMEM((tp - 1, rows, width), BF),
            pltpu.VMEM((n_pairs, 2 * rows, 128), F32),
            pltpu.VMEM((n_pairs, 2 * rows, 128), F32),
            pltpu.VMEM((rows, rows), F32),
            dma((2, group)),
            dma((2, group)),
            dma((3, tp)),
            dma((3, tp)),
            dma((3,)),
            dma((3,)),
            dma((2,)),
            dma((4, n)),
            dma((4, n)),
            dma((4, n)),
            dma((4, n)),
            dma((4, 2 * n)),
            dma((4, 2 * n)),
            dma((4,)),
        ],
        compiler_params=pltpu.CompilerParams(
            vmem_limit_bytes=58 * 2**20, collective_id=0, has_side_effects=True
        ),
        cost_estimate=pl.CostEstimate(
            flops=8 * rows * row_len * q_width, bytes_accessed=40 * 2**20, transcendentals=0
        ),
    )(*operands)


def shape(s, t):
    return jax.ShapeDtypeStruct(s, t)


VMEM_LIMIT = pltpu.CompilerParams(vmem_limit_bytes=58 * 2**20)
ANYWHERE = pl.BlockSpec(memory_space=pl.ANY)


def once(body, scalars, n_in, n_any, outs, scratch, flops):
    vm = pl.BlockSpec(memory_space=pltpu.VMEM)

    def call(scalar, *operands):
        return pl.pallas_call(
            body,
            grid_spec=pltpu.PrefetchScalarGridSpec(
                num_scalar_prefetch=scalars,
                grid=(1,),
                in_specs=[vm] * n_in + [ANYWHERE] * n_any,
                out_specs=[vm] * len(outs),
                scratch_shapes=scratch,
            ),
            out_shape=outs,
            compiler_params=VMEM_LIMIT,
            cost_estimate=pl.CostEstimate(flops=flops, bytes_accessed=8 * 2**20, transcendentals=0),
        )(scalar, *operands)

    return call


def ffn_pass(mid, dy, gain, w_ffn):
    rows, width = mid.shape
    ff = w_ffn.shape[1] // 3
    tile = 256 if ff % 256 == 0 else 128
    steps = ff // tile
    whole = lambda shape: pl.BlockSpec(shape, lambda s: (0, 0))
    column = pl.BlockSpec((rows, tile), lambda s: (0, s))
    weight = lambda i: pl.BlockSpec((width, tile), lambda s: (0, i * steps + s))
    return pl.pallas_call(
        ffn_kernel,
        grid=(steps,),
        in_specs=[whole((rows, width))] * 2 + [whole((1, width))] + [weight(i) for i in range(3)],
        out_specs=[whole((rows, width))] * 2
        + [whole((1, width)), whole((rows, width))]
        + [column] * 3,
        scratch_shapes=[pltpu.VMEM((rows, width), F32), pltpu.VMEM((rows, width), F32)],
        out_shape=[shape((rows, width), BF)] * 2
        + [shape((1, width), F32), shape((rows, width), BF)]
        + [shape((rows, ff), BF)] * 3,
        compiler_params=VMEM_LIMIT,
        cost_estimate=pl.CostEstimate(
            flops=12 * rows * width * ff, bytes_accessed=6 * width * ff, transcendentals=rows * ff
        ),
    )(mid, dy, gain, w_ffn, w_ffn, w_ffn)


def weight_grad(left, right, offsets, pieces):
    rows, width = left.shape
    ff = right.shape[1]
    tile = 256 if ff % 256 == 0 else 128
    half = width // 2
    column = pl.BlockSpec((half, tile), lambda s, o: (0, s))
    return pl.pallas_call(
        functools.partial(weight_grad_kernel, pieces, width // pieces),
        grid_spec=pltpu.PrefetchScalarGridSpec(
            num_scalar_prefetch=1,
            grid=(ff // tile,),
            in_specs=[
                pl.BlockSpec((rows, width), lambda s, o: (0, 0)),
                pl.BlockSpec((rows, tile), lambda s, o: (0, s)),
            ],
            out_specs=[column, column],
            scratch_shapes=[pltpu.VMEM((width, rows), BF), pltpu.VMEM((width, rows), BF)],
        ),
        out_shape=[shape((half, ff), BF)] * 2,
        compiler_params=VMEM_LIMIT,
        cost_estimate=pl.CostEstimate(
            flops=2 * rows * width * ff, bytes_accessed=2 * width * ff, transcendentals=0
        ),
    )(offsets, left, right)


def pad_columns(v, to):
    return v if v.shape[1] == to else jnp.pad(v, ((0, 0), (0, to - v.shape[1])))


def one_hot(rows, columns):
    return (rows == columns).astype(BF)


def local(
    tokens,
    cotangent,
    slot_of,
    lengths,
    w_query,
    key_weight,
    value_weight,
    w_out,
    w_gate,
    w_up,
    w_down,
    gain_attn,
    gain_ffn,
    gain_query,
    gain_key,
):
    grid = Grid()
    stream_len = tokens.shape[0]
    feat_len = tokens.shape[1]
    local_len = PACKED_ROW_SLOTS // grid.ctx
    row_count = stream_len // local_len
    groups = grid.n * grid.ctx
    share = stream_len // groups
    q_heads = QUERY_HEADS // grid.tp
    key_value_heads = KEY_VALUE_HEADS // grid.tp
    query_group_width = QUERY_HEADS // KEY_VALUE_HEADS
    q_width = q_heads * HEAD_SIZE
    kv_width = key_value_heads * HEAD_SIZE
    flat_len = row_count * local_len
    row_len = PACKED_ROW_SLOTS
    me = grid.z * grid.ctx + grid.c
    both = ("fsdp", "ctx")

    def home(slots):
        row, place = slots // row_len, slots % row_len
        return (
            row // row_count * grid.ctx + place // local_len,
            row % row_count * local_len + place % local_len,
        )

    my_slots = lax.dynamic_slice_in_dim(slot_of, me * stream_len, stream_len, 0)
    my_target = home(my_slots)[0]
    ahead = (my_target[:, None] == my_target[None, :]) & (my_slots[None, :] < my_slots[:, None])
    send_place = my_target * share + jnp.sum(ahead.astype(jnp.int32), axis=1)
    line = jnp.arange(stream_len, dtype=jnp.int32)
    send_pick = one_hot(line[:, None], send_place[None, :])
    all_dev, all_local = home(slot_of)
    low = 32
    high = flat_len // low
    sender = (jnp.arange(slot_of.shape[0], dtype=jnp.int32) // stream_len).astype(F32)
    mine = (all_dev == me)[None, :] & (
        (all_local // low)[None, :] == jnp.arange(high, dtype=jnp.int32)[:, None]
    )
    left = jnp.where(mine, sender[None, :], 0.0).astype(BF)
    right = one_hot((all_local % low)[:, None], jnp.arange(low, dtype=jnp.int32)[None, :])
    source = product(left, right, "ht,tl->hl").reshape(flat_len).astype(jnp.int32)
    slot_line = jnp.arange(flat_len, dtype=jnp.int32)
    before = (source[:, None] == source[None, :]) & (slot_line[None, :] < slot_line[:, None])
    arrival = source * share + jnp.sum(before.astype(jnp.int32), axis=1)
    take_pick = one_hot(arrival[:, None], line[None, :])

    def sent_order(v):
        return product(send_pick, v, "pt,tf->pf").astype(BF)

    def bring_back(v):
        sent = product(take_pick, v, "ja,jf->af").astype(BF)
        got = lax.all_to_all(sent, both, split_axis=0, concat_axis=0, tiled=True)
        return product(send_pick, got, "pt,pf->tf").astype(BF)

    ff = w_gate.shape[1]
    ff_pad = -(-ff // 128) * 128
    attn_shard = jnp.concatenate([w_query, key_weight, value_weight, w_out.T], axis=1)
    ffn_shard = jnp.concatenate(
        [pad_columns(v, ff_pad) for v in (w_gate, w_up, w_down.T)], axis=1
    )
    shard_rows = w_gate.shape[0]
    order = grid.order()
    grad_order = [d for d in range(0, grid.ctx, 2)] + [d for d in range(1, grid.ctx, 2)]
    grad_order = [order[d * grid.n + k] for d in grad_order for k in range(grid.n)]
    offsets = (jnp.stack(order + grad_order) * shard_rows).astype(jnp.int32)

    own_slots = grid.c * local_len + jnp.arange(local_len, dtype=jnp.int32)
    position = slot_tables(lengths[0], own_slots)[1]
    start = own_slots - position
    frequency = ROPE_THETA ** (-jnp.arange(0, HEAD_SIZE, 2).astype(F32) / HEAD_SIZE)
    angles = position.astype(F32)[:, None] * frequency[None, :]
    cosines = jnp.tile(jnp.cos(angles), (1, 4))
    sin = jnp.sin(angles)
    sines = jnp.tile(jnp.concatenate([-sin, sin], axis=1), (1, 2))
    head_gain = jnp.concatenate(
        [
            jnp.tile(gain_query, q_heads),
            jnp.tile(gain_key, key_value_heads),
            jnp.ones((kv_width,), F32),
        ]
    )[None, :]
    place = grid.c.astype(jnp.int32)[None]
    pieces = groups
    qkv_width = q_width + 2 * kv_width
    attn_width = attn_shard.shape[1]
    n_pairs = q_width // 128
    rows = flat_len

    attn_flops = 4 * 2 * rows * row_len * q_width
    x_full, dy_full, qb, row_kv, raw, heads, sums, middle, squares, attn_w, ffn_w = forward_pass(
        grid,
        q_width,
        kv_width,
        ff_pad,
        sent_order(tokens),
        sent_order(cotangent),
        take_pick,
        gain_attn[None, :],
        head_gain,
        cosines,
        sines,
        start[:, None],
        attn_shard,
        ffn_shard,
    )
    own_features = lambda v: lax.dynamic_slice_in_dim(v, grid.t * feat_len, feat_len, 1)
    middle_own = own_features(middle)
    ffn_part, d_mid_part, d_gain_ffn, normed_two, hidden, d_gate, d_up = ffn_pass(
        middle, dy_full, gain_ffn[None, :], ffn_w
    )
    d_middle_full = dy_full.astype(F32) + grid.tp_sum(d_mid_part)
    d_middle = own_features(d_middle_full)
    d_attn = d_middle_full.astype(BF)

    def reduce_weight(pair):
        keep, send = pair
        blocks = (keep.shape[0] // shard_rows, shard_rows, keep.shape[1])
        return grid.reduce_ring(grid.reduce_ctx(keep.reshape(blocks), send.reshape(blocks)))

    sum_down = reduce_weight(weight_grad(dy_full, hidden, offsets, pieces))[:, :ff].T
    sum_gate = reduce_weight(weight_grad(normed_two, d_gate, offsets, pieces))[:, :ff]
    sum_up = reduce_weight(weight_grad(normed_two, d_up, offsets, pieces))[:, :ff]
    ffn_out = grid.tp_scatter(ffn_part)

    dq, dkv, g_out = once(
        functools.partial(attend_back_kernel, q_width, kv_width, local_len),
        1,
        7,
        0,
        [
            shape((rows, q_width), F32),
            shape((row_len, 2 * kv_width), BF),
            shape((MODEL_WIDTH, q_width), BF),
        ],
        [
            pltpu.VMEM((rows, q_width), BF),
            pltpu.VMEM((local_len, rows), F32),
            pltpu.VMEM((n_pairs, 128, 2 * rows), F32),
        ],
        3 * attn_flops,
    )(place, qb, row_kv, heads, sums, start[None, :], attn_w, d_attn)
    own_kv = lax.psum_scatter(dkv, "ctx", scatter_dimension=0, tiled=True).astype(F32)
    own_kv = jnp.concatenate(
        [own_kv[:, :kv_width], own_kv[:, kv_width:].astype(BF).astype(F32)], axis=1
    )
    d_x_part, d_gain_attn, d_head_gain, keep, send = once(
        functools.partial(qkv_back_kernel, q_width, kv_width, pieces, shard_rows),
        1,
        10,
        0,
        [
            shape((rows, MODEL_WIDTH), BF),
            shape((1, MODEL_WIDTH), F32),
            shape((1, qkv_width), F32),
            shape((MODEL_WIDTH // 2, attn_width), BF),
            shape((MODEL_WIDTH // 2, attn_width), BF),
        ],
        [
            pltpu.VMEM((rows, qkv_width), BF),
            pltpu.VMEM((MODEL_WIDTH, rows), BF),
            pltpu.VMEM((MODEL_WIDTH, attn_width), BF),
        ],
        4 * rows * MODEL_WIDTH * qkv_width,
    )(
        offsets, x_full, gain_attn[None, :], head_gain, cosines, sines, raw, attn_w, dq, own_kv, g_out
    )
    d_x = grid.tp_scatter(d_x_part)
    grad_packed = (d_middle + d_x).astype(BF)
    output_packed = (middle_own + ffn_out).astype(BF)
    sum_attn = reduce_weight((keep, send))
    a, b, c = q_width, q_width + kv_width, q_width + 2 * kv_width

    per_head = d_head_gain[0].reshape(-1, HEAD_SIZE)
    d_gain_q = jnp.sum(per_head[:q_heads], axis=0)
    d_gain_k = jnp.sum(per_head[q_heads : q_heads + key_value_heads], axis=0)
    sums_of_squares = jnp.concatenate(
        [jnp.sum(squares, axis=1) / grid.tp, jnp.sum(ffn_out * ffn_out)[None]]
    )
    small = jnp.concatenate([d_gain_attn[0], d_gain_ffn[0], d_gain_q, d_gain_k, sums_of_squares])
    small = grid.sum_all(small)
    w, h = MODEL_WIDTH, HEAD_SIZE
    gain_a, gain_f = small[:w], small[w : 2 * w]
    gain_qs, gain_ks = small[2 * w : 2 * w + h], small[2 * w + h : 2 * w + 2 * h]
    entry_count = flat_len * groups * MODEL_WIDTH
    rms_stats = jnp.sqrt(small[2 * w + 2 * h :] / entry_count)
    output = bring_back(output_packed)
    grad_tokens = bring_back(grad_packed)
    return (
        output,
        grad_tokens,
        sum_attn[:, :a],
        sum_attn[:, a:b],
        sum_attn[:, b:c],
        sum_attn[:, c:].T,
        sum_gate,
        sum_up,
        sum_down,
        gain_a,
        gain_f,
        gain_qs,
        gain_ks,
        rms_stats,
    )


def solution(mesh):
    row = P(("fsdp", "ctx"), "tp")
    column = P("tp", ("fsdp", "ctx"))
    in_specs = (row, row, P(), P("fsdp", None), row, row, row, column, row, row, column) + (P(),) * 4
    out_specs = (row, row, row, row, row, column, row, row, column) + (P(),) * 5
    return jax.shard_map(local, mesh=mesh, in_specs=in_specs, out_specs=out_specs, check_vma=False)
```

```python
import functools

import jax
import jax.numpy as jnp
from jax import lax
from jax.experimental import pallas as pl
from jax.experimental.pallas import tpu as pltpu
from jax.sharding import PartitionSpec as P

MODEL_WIDTH = 1024
QUERY_HEADS = 16
KEY_VALUE_HEADS = 8
HEAD_SIZE = 64
PACKED_ROW_SLOTS = 2048
QUERY_BLOCK_ROWS = 512

EPSILON = 1e-05
ROPE_THETA = 1000000.0
NEG_FILL = -1e30
BF = jnp.bfloat16
F32 = jnp.float32


def segment_ends(lengths):
    total, ends = lengths[0], []
    for i in range(lengths.shape[0]):
        ends.append(total)
        if i + 1 < lengths.shape[0]:
            total = total + lengths[i + 1]
    return ends


def slot_tables(lengths, slot_ids):
    segment = jnp.zeros_like(slot_ids)
    start = jnp.zeros_like(slot_ids)
    for i, end in enumerate(segment_ends(lengths)):
        passed = (slot_ids >= end).astype(jnp.int32)
        segment = segment + passed
        start = start + passed * lengths[i]
    return (segment, slot_ids - start)


def product(left_arr, right_arr, pattern):
    return jnp.einsum(pattern, left_arr, right_arr, preferred_element_type=F32)


class Grid:
    def __init__(self):
        self.n = lax.axis_size("fsdp")
        self.ctx = lax.axis_size("ctx")
        self.tp = lax.axis_size("tp")
        self.z = lax.axis_index("fsdp")
        self.c = lax.axis_index("ctx")
        self.t = lax.axis_index("tp")


def dot(a, b, ca, cb, precision=None):
    return lax.dot_general(
        a, b, (((ca,), (cb,)), ((), ())), preferred_element_type=F32, precision=precision
    )


def lanes(shape):
    return lax.broadcasted_iota(jnp.int32, shape, 1)


def half_mean(v):
    low = lanes(v.shape) < HEAD_SIZE
    first = jnp.sum(jnp.where(low, v, 0.0), axis=1, keepdims=True)
    second = jnp.sum(jnp.where(low, 0.0, v), axis=1, keepdims=True)
    return jnp.where(low, first, second) * (1.0 / HEAD_SIZE)


def half_swap(v):
    quarter = HEAD_SIZE // 2
    left = pltpu.roll(v, 128 - quarter, 1)
    right = pltpu.roll(v, quarter, 1)
    return jnp.where(lanes(v.shape) % HEAD_SIZE < quarter, left, right)


def row_scale(v):
    return lax.rsqrt(jnp.mean(v * v, axis=1, keepdims=True) + EPSILON)


def norm_back(dn, v, gain):
    scale = row_scale(v)
    unit = v * scale
    scaled = dn * gain
    grad = scale * (scaled - unit * jnp.mean(scaled * unit, axis=1, keepdims=True))
    return grad, jnp.sum(dn * unit, axis=0, keepdims=True)


def qk_forward(raw, gain, cosines, sines, is_value):
    normed = raw * lax.rsqrt(half_mean(raw * raw) + EPSILON) * gain
    turned = normed * cosines + half_swap(normed) * sines
    return jnp.where(is_value, raw, turned)


def qk_backward(grad, raw, gain, cosines, sines, is_value):
    straight = grad * cosines - half_swap(grad) * sines
    scale = lax.rsqrt(half_mean(raw * raw) + EPSILON)
    unit = raw * scale
    scaled = straight * gain
    back = scale * (scaled - unit * half_mean(scaled * unit))
    gain_grad = jnp.sum(straight * unit, axis=0, keepdims=True)
    return jnp.where(is_value, grad, back), gain_grad


def two_heads(v):
    low = lanes(v.shape) < HEAD_SIZE
    zero = jnp.zeros_like(v)
    return jnp.concatenate([jnp.where(low, v, zero), jnp.where(low, zero, v)], axis=0)


def one_row(v):
    rows = v.shape[0] // 2
    return jnp.where(lanes((rows, v.shape[1])) < HEAD_SIZE, v[:rows], v[rows:])


def twice(v, which):
    half = v[:, which * HEAD_SIZE : (which + 1) * HEAD_SIZE]
    return jnp.concatenate([half, half], axis=1)


def both_halves(v):
    return v + jnp.concatenate([v[:, HEAD_SIZE:], v[:, :HEAD_SIZE]], axis=1)


def over_key_heads(n_heads, values_from, body):
    if n_heads % 2:
        for g in range(n_heads):
            body([(g, (g // 2, g % 2), ((values_from + g) // 2, (values_from + g) % 2))])
        return

    def step(i, carry):
        body([(2 * i + e, (i, e), (values_from // 2 + i, e)) for e in range(2)])
        return carry

    lax.fori_loop(0, n_heads // 2, step, 0)


def lane_block(i):
    return block_rows(i, 128)


def ffn_kernel(mid, dy, gain, w_gate, w_up, w_down, ffn, dmid, dgain, nb, hid, dgt, dup, ffn_acc, dn_acc):
    step = pl.program_id(0)

    @pl.when(step == 0)
    def _():
        v = mid[...].astype(BF).astype(F32)
        nb[...] = (v * row_scale(v) * gain[...]).astype(BF)
        ffn_acc[...] = jnp.zeros_like(ffn_acc)
        dn_acc[...] = jnp.zeros_like(dn_acc)

    normed = nb[...]
    gate = dot(normed, w_gate[...], 1, 0)
    up = dot(normed, w_up[...], 1, 0)
    d_hidden = dot(dy[...], w_down[...], 1, 0)
    sig = 1.0 / (1.0 + jnp.exp(-gate))
    silu = gate * sig
    hidden = (silu * up).astype(BF)
    d_gate = (d_hidden * up * (sig * (1.0 + gate * (1.0 - sig)))).astype(BF)
    d_up = (d_hidden * silu).astype(BF)
    hid[...] = hidden
    dgt[...] = d_gate
    dup[...] = d_up
    ffn_acc[...] += dot(hidden, w_down[...], 1, 1)
    dn_acc[...] += dot(d_gate, w_gate[...], 1, 1) + dot(d_up, w_up[...], 1, 1)

    @pl.when(step == pl.num_programs(0) - 1)
    def _():
        v = mid[...].astype(BF).astype(F32)
        grad, gain_sum = norm_back(dn_acc[...], v, gain[...])
        dgain[...] = gain_sum
        dmid[...] = grad.astype(BF)
        ffn[...] = ffn_acc[...].astype(BF)


class Place:
    def __init__(self, n, ctx, tp):
        self.n, self.ctx, self.tp = n, ctx, tp
        self.z = lax.axis_index("fsdp")
        self.c = lax.axis_index("ctx")
        self.t = lax.axis_index("tp")
        self.me = self.z * ctx + self.c

    def at(self, z=None, c=None, t=None):
        return (
            self.z if z is None else z,
            self.c if c is None else c,
            self.t if t is None else t,
        )

    def peer(self, j):
        p = lax.rem(self.me + j, self.n * self.ctx)
        return self.at(p // self.ctx, lax.rem(p, self.ctx))

    def up(self, j):
        return self.at(z=lax.rem(self.z + j, self.n))

    def flip(self, bit):
        if bit == 1:
            return self.c + 1 - 2 * lax.rem(self.c, 2)
        return lax.rem(self.c + 2, 4)

    def side(self, j):
        return self.at(t=lax.rem(self.t + j, self.tp))

    def owner(self, k, c):
        return lax.rem(self.z - k + self.n, self.n) * self.ctx + c

    def greet(self):
        barrier = pltpu.get_barrier_semaphore()
        group = self.n * self.ctx
        for j in range(1, group):
            pl.semaphore_signal(barrier, inc=1, device_id=self.peer(j), device_id_type=MESH)
        for j in range(1, self.tp):
            pl.semaphore_signal(barrier, inc=1, device_id=self.side(j), device_id_type=MESH)
        pl.semaphore_wait(barrier, group + self.tp - 2)


MESH = pl.DeviceIdType.MESH


def remote(src, dst, send, recv, device):
    return pltpu.make_async_remote_copy(
        src_ref=src, dst_ref=dst, send_sem=send, recv_sem=recv, device_id=device, device_id_type=MESH
    )


def block_rows(index, size):
    return pl.ds(pl.multiple_of(index * size, size), size)


class Gather:
    def __init__(self, place, shard, whole, columns, number, sems):
        z_send, z_recv, x_send, x_recv, c_send, c_recv, own = sems
        h = shard.shape[0]
        n = place.n
        view = lambda index: whole.at[block_rows(index, h), columns]
        here, there = place.c, place.flip(2)
        mine = shard.at[:, columns]
        self.own = pltpu.make_async_copy(mine, view(place.me), own.at[number])
        self.line = [
            remote(mine, view(place.me), z_send.at[number, j], z_recv.at[number, j], place.up(j))
            for j in range(1, n)
        ]
        self.chip = [
            remote(
                mine if k == 0 else view(place.owner(k, here)),
                view(place.owner(k, here)),
                x_send.at[number, k],
                x_recv.at[number, k],
                place.at(c=there),
            )
            for k in range(n)
        ]
        self.core = [
            remote(
                mine if i == 0 else view(place.owner(i % n, here if i < n else there)),
                view(place.owner(i % n, here if i < n else there)),
                c_send.at[number, i],
                c_recv.at[number, i],
                place.at(c=place.flip(1)),
            )
            for i in range(2 * n)
        ]

    def begin(self):
        for copy in self.line:
            copy.start()
        self.chip[0].start()
        self.own.start()
        self.core[0].start()

    def pass_line(self, k):
        self.line[k - 1].wait_recv()
        self.chip[k].start()
        self.core[k].start()

    def pass_chip(self, k):
        self.chip[k].wait_recv()
        self.core[len(self.chip) + k].start()

    def finish(self):
        for copy in self.core:
            copy.wait_recv()
        self.own.wait()

    def drain(self):
        for copy in self.line + self.chip + self.core:
            copy.wait_send()


def forward_kernel(
    n, ctx, tp, q_width, kv_width, ff,
    sent_x, sent_y, pick, gain, head_gain, cosines, sines, start_col, attn_shard, ffn_shard,
    x, dy, qb, kv, heads, sums, mid, squares, w_attn, w_ffn,
    got_x, got_y, own_x, own_y, x_land, y_land, w, kv_all, part, land, acc, total, bias,
    route_send, route_recv, tp_send, tp_recv, kv_send, kv_recv, out_sem, *gather_sems
):
    place = Place(n, ctx, tp)
    group = n * ctx
    rows = got_x.shape[0]
    share = rows // group
    feat = got_x.shape[1]
    width = x_land.shape[1]
    piece = rows
    every = pl.ds(0, attn_shard.shape[1])
    attn = Gather(place, attn_shard, w, every, 0, gather_sems)
    ffn = [
        Gather(place, ffn_shard, w_ffn, pl.ds(i * ff, ff), 1 + i, gather_sems) for i in range(3)
    ]

    def route(number, src, dst):
        return [
            remote(
                src.at[block_rows(lax.rem(place.me + j, group), share), :],
                dst.at[block_rows(place.me, share), :],
                route_send.at[number, j],
                route_recv.at[number, j],
                place.peer(j),
            )
            for j in range(1, group)
        ]

    def widen(number, src, dst):
        return [
            remote(
                src,
                dst.at[:, block_rows(place.t, feat)],
                tp_send.at[number, j],
                tp_recv.at[number, j],
                place.side(j),
            )
            for j in range(1, tp)
        ]

    def own_block(src, dst):
        at = block_rows(place.me, share)
        dst[at, :] = src[at, :]

    route_x, route_y = route(0, sent_x, got_x), route(1, sent_y, got_y)
    wide_x, wide_y = widen(0, own_x, x_land), widen(1, own_y, y_land)
    place.greet()
    for copy in route_x:
        copy.start()
    attn.begin()
    for g in ffn:
        g.begin()
    own_block(sent_x, got_x)
    for copy in route_x:
        copy.wait_recv()
    own_x[...] = dot(pick[...], got_x[...], 1, 0).astype(BF)
    for copy in wide_x:
        copy.start()
    x_land[:, block_rows(place.t, feat)] = own_x[...]
    for copy in route_y:
        copy.start()
    own_block(sent_y, got_y)
    for k in range(1, n):
        attn.pass_line(k)
    for k in range(n):
        attn.pass_chip(k)
    for copy in wide_x:
        copy.wait_recv()
    v = x_land[...].astype(F32)
    x[...] = x_land[...]
    normed = (v * row_scale(v) * gain[...]).astype(BF)
    attn.finish()
    write_w = pltpu.make_async_copy(w, w_attn, out_sem.at[0])
    write_w.start()

    own_rows = block_rows(place.c, piece)
    values_from = q_width + kv_width
    for b in list(range(q_width, q_width + 2 * kv_width, 128)) + list(range(0, q_width, 128)):
        if b == 0:
            later = start_keys(place, kv_all, own_rows, kv_send, kv_recv)
        block = dot(normed, w[:, b : b + 128], 1, 0)
        is_value = lanes(block.shape) + b >= values_from
        done = qk_forward(block, head_gain[:, b : b + 128], cosines[...], sines[...], is_value)
        if b < q_width:
            qb[:, b : b + 128] = done.astype(BF)
        else:
            kv_all[own_rows, b - q_width : b - q_width + 128] = done.astype(BF)
    for g in ffn:
        g.pass_line(1)
        g.pass_chip(0)

    q_slot = place.c * piece + lax.broadcasted_iota(jnp.int32, (rows, piece), 0)
    n_pairs = q_width // 128

    def one_piece(p):
        k_slot = p * piece + lanes((rows, piece))
        open_ = (k_slot >= start_col[...]) & (k_slot <= q_slot)
        bias[...] = jnp.where(open_, 0.0, NEG_FILL)
        at = block_rows(p, piece)

        def heads_of(members):
            for g, (kb, ke), (vb, ve) in members:
                q2 = two_heads(qb[:, lane_block(g)])
                k2 = twice(kv_all[at, lane_block(kb)], ke)
                v2 = twice(kv_all[at, lane_block(vb)], ve)
                for h in range(2):
                    part = slice(h * rows, (h + 1) * rows)
                    e = jnp.exp(dot(q2[part], k2, 1, 1) * 0.125 + bias[...])
                    part_sum = e[:, :128]
                    for b in range(128, piece, 128):
                        part_sum = part_sum + e[:, b : b + 128]
                    acc[g, part, :] += dot(e.astype(BF), v2, 1, 0)
                    total[g, part, :] += part_sum

        over_key_heads(n_pairs, kv_width // HEAD_SIZE, heads_of)

    acc[...] = jnp.zeros_like(acc)
    total[...] = jnp.zeros_like(total)
    one_piece(place.c)
    x_bit, core_bit = place.c // 2, lax.rem(place.c, 2)
    near, across, passed = later

    @pl.when(x_bit == 1)
    def _():
        across.wait_recv()
        passed.start()

    for g in ffn:
        g.pass_line(2)
        g.pass_chip(1)

    @pl.when(core_bit == 1)
    def _():
        near.wait_recv()
        one_piece(place.c - 1)

    for g in ffn:
        g.pass_line(3)

    @pl.when(x_bit == 1)
    def _():
        passed.wait_recv()

        def step(p, carry):
            one_piece(p)
            return carry

        lax.fori_loop(0, 2, step, 0)

    ones = jnp.ones((8, 128), F32)
    for g in range(n_pairs):
        row_total = jnp.sum(total[g], axis=1, keepdims=True)
        heads[:, 128 * g : 128 * g + 128] = one_row(acc[g] / row_total)
        sums[g] = 1.0 / dot(ones, total[g], 1, 1, lax.Precision.HIGHEST)
    part[...] = dot(heads[...].astype(BF), w[:, q_width + 2 * kv_width :], 1, 1).astype(BF)
    attention = [
        remote(part, land.at[j - 1], tp_send.at[2, j], tp_recv.at[2, j], place.side(j))
        for j in range(1, tp)
    ]
    for copy in attention:
        copy.start()
    write_kv = pltpu.make_async_copy(kv_all, kv, out_sem.at[1])
    for copy in route_y:
        copy.wait_recv()
    own_y[...] = dot(pick[...], got_y[...], 1, 0).astype(BF)
    for copy in wide_y:
        copy.start()
    y_land[:, block_rows(place.t, feat)] = own_y[...]
    for g in ffn:
        g.pass_chip(2)
    for copy in attention:
        copy.wait_recv()
    att = part[...].astype(F32)
    for j in range(1, tp):
        att = att + land[j - 1].astype(F32)
    v = x_land[...].astype(F32)
    squares[0:1, :] = jnp.sum(v * v, axis=0, keepdims=True)
    squares[1:2, :] = jnp.sum(att * att, axis=0, keepdims=True)
    mid[...] = v + att
    for copy in wide_y:
        copy.wait_recv()
    dy[...] = y_land[...]
    for g in ffn:
        g.pass_chip(3)

    @pl.when(core_bit == 0)
    def _():
        near.wait_send()

    @pl.when(x_bit == 0)
    def _():
        across.wait_send()

    @pl.when(x_bit == 1)
    def _():
        passed.wait_send()

    write_kv.start()
    for g in ffn:
        g.finish()
    for copy in route_x + route_y + wide_x + wide_y + attention:
        copy.wait_send()
    for g in [attn] + ffn:
        g.drain()
    write_w.wait()
    write_kv.wait()


def start_keys(place, kv_all, own_rows, send, recv):
    x_bit, core_bit = place.c // 2, lax.rem(place.c, 2)
    mine = kv_all.at[own_rows, :]
    near = remote(mine, mine, send.at[0], recv.at[0], place.at(c=place.flip(1)))
    across = remote(mine, mine, send.at[1], recv.at[1], place.at(c=place.flip(2)))
    from_chip = kv_all.at[block_rows(place.flip(2), own_rows.size), :]
    passed = remote(from_chip, from_chip, send.at[2], recv.at[2], place.at(c=place.flip(1)))

    @pl.when(x_bit == 0)
    def _():
        across.start()

    @pl.when(core_bit == 0)
    def _():
        near.start()

    return near, across, passed


def forward_pass(grid, q_width, kv_width, ff, *operands):
    sent_x, attn_shard = operands[0], operands[8]
    rows, feat = sent_x.shape
    n, ctx, tp = grid.n, grid.ctx, grid.tp
    width = feat * tp
    n_pairs = q_width // 128
    row_len = rows * ctx
    vm = pl.BlockSpec(memory_space=pltpu.VMEM)
    dma = pltpu.SemaphoreType.DMA
    group = n * ctx
    return pl.pallas_call(
        functools.partial(forward_kernel, n, ctx, tp, q_width, kv_width, ff),
        in_specs=[vm] * 8 + [ANYWHERE] * 2,
        out_specs=[vm] * 3 + [ANYWHERE] + [vm] * 4 + [ANYWHERE] * 2,
        out_shape=[
            shape((rows, width), BF),
            shape((rows, width), BF),
            shape((rows, q_width), BF),
            shape((row_len, 2 * kv_width), BF),
            shape((rows, q_width), F32),
            shape((n_pairs, 8, 2 * rows), F32),
            shape((rows, width), F32),
            shape((2, width), F32),
            shape((width, attn_shard.shape[1]), BF),
            shape((width, 3 * ff), BF),
        ],
        scratch_shapes=[
            pltpu.VMEM((rows, feat), BF),
            pltpu.VMEM((rows, feat), BF),
            pltpu.VMEM((rows, feat), BF),
            pltpu.VMEM((rows, feat), BF),
            pltpu.VMEM((rows, width), BF),
            pltpu.VMEM((rows, width), BF),
            pltpu.VMEM((width, attn_shard.shape[1]), BF),
            pltpu.VMEM((row_len, 2 * kv_width), BF),
            pltpu.VMEM((rows, width), BF),
            pltpu.VMEM((tp - 1, rows, width), BF),
            pltpu.VMEM((n_pairs, 2 * rows, 128), F32),
            pltpu.VMEM((n_pairs, 2 * rows, 128), F32),
            pltpu.VMEM((rows, rows), F32),
            dma((2, group)),
            dma((2, group)),
            dma((3, tp)),
            dma((3, tp)),
            dma((3,)),
            dma((3,)),
            dma((2,)),
            dma((4, n)),
            dma((4, n)),
            dma((4, n)),
            dma((4, n)),
            dma((4, 2 * n)),
            dma((4, 2 * n)),
            dma((4,)),
        ],
        compiler_params=pltpu.CompilerParams(
            vmem_limit_bytes=58 * 2**20, collective_id=0, has_side_effects=True
        ),
        cost_estimate=pl.CostEstimate(
            flops=8 * rows * row_len * q_width, bytes_accessed=40 * 2**20, transcendentals=0
        ),
    )(*operands)


def repeat(count, body):
    def step(i, carry):
        body(i)
        return carry

    lax.fori_loop(0, count, step, 0)


def add_into(to, more):
    step = 16

    def add(i):
        at = block_rows(i, step)
        to[at, :] = (to[at, :].astype(F32) + more[at, :].astype(F32)).astype(to.dtype)

    repeat(to.shape[0] // step, add)


def turn_blocks(place, source, turned):
    width = source.shape[1]
    n = place.n
    h = width // (n * place.ctx)
    first = lax.rem(place.c, 2) == 0

    def turn(i):
        chip = lax.rem(place.c // 2 + i // n, 2)
        pair = lax.rem(place.z - lax.rem(i, n) + n, n) * (place.ctx // 2) + chip
        block = source[:, block_rows(pair, 2 * h)].astype(F32).T.astype(turned.dtype)
        low, high = block[:h], block[h:]
        turned[block_rows(i, h), :] = jnp.where(first, low, high)
        turned[block_rows(i + 2 * n, h), :] = jnp.where(first, high, low)

    repeat(2 * n, turn)


class Scatter:
    def __init__(self, place, keep, send, core_land, chip_land, line_land, number, sems):
        c_send, c_recv, x_send, x_recv, z_send, z_recv = sems
        n = place.n
        self.keep, self.n = keep, n
        self.core_land, self.chip_land, self.line_land = core_land, chip_land, line_land
        self.h = h = keep.shape[0] // (2 * n)
        self.core = remote(
            send, core_land, c_send.at[number], c_recv.at[number], place.at(c=place.flip(1))
        )
        self.chip = remote(
            keep.at[pl.ds(n * h, n * h), :],
            chip_land,
            x_send.at[number],
            x_recv.at[number],
            place.at(c=place.flip(2)),
        )
        self.line = [
            remote(
                keep.at[pl.ds(k * h, h), :],
                line_land.at[k - 1],
                z_send.at[number, k],
                z_recv.at[number, k],
                place.at(z=lax.rem(place.z - k + n, n)),
            )
            for k in range(1, n)
        ]

    def start(self):
        self.core.start()

    def after_core(self):
        self.core.wait_recv()
        top = self.n * self.h
        add_into(self.keep.at[pl.ds(top, top), :], self.core_land.at[pl.ds(top, top), :])
        self.chip.start()
        add_into(self.keep.at[pl.ds(0, top), :], self.core_land.at[pl.ds(0, top), :])

    def after_chip(self):
        self.chip.wait_recv()
        h = self.h
        for k in list(range(1, self.n)) + [0]:
            at = pl.ds(k * h, h)
            add_into(self.keep.at[at, :], self.chip_land.at[at, :])
            if k:
                self.line[k - 1].start()

    def after_line(self, out):
        for copy in self.line:
            copy.wait_recv()
        step = 16

        def add(i):
            at = block_rows(i, step)
            total = self.keep[at, :].astype(F32)
            for k in range(self.n - 1):
                total = total + self.line_land[k, at, :].astype(F32)
            out[at, :] = total

        repeat(self.h // step, add)

    def drain(self, core=True):
        if core:
            self.core.wait_send()
        self.chip.wait_send()
        for copy in self.line:
            copy.wait_send()


def backward_kernel(
    n, ctx, tp, q_width, kv_width, stage_cols,
    ffn, dmid, qb, kv_all, heads, sums, w, cosines, sines, pick_t, gain, head_gain,
    start_row, gain_ffn_grad, squares, dy_in, x_in, mid_in, normed_two, hidden, d_gate, d_up,
    back_o, back_g, sum_gate, sum_up, sum_down, sum_out, sum_qkv, small,
    x, turned, stage, keep, send, core_land, chip_land, line_land,
    o_keep, o_send, o_core, o_chip, o_line, a_keep, a_send, a_core, a_chip, a_line,
    d_mid_own, d_attn, dob, delta, bias, dq_t, dkv, kv_land, tp_land, ffn_away, ffn_land, dx_away, dx_land,
    sent, small_mine, small_land, small_side,
    tp_send, tp_recv, route_send, route_recv, small_send, small_recv, kv_send, kv_recv, load_sem,
    free_sem, *scatter_sems
):
    place = Place(n, ctx, tp)
    group = n * ctx
    rows, width = dmid.shape
    feat = width // tp
    share = rows // group
    piece = rows
    ff = hidden.shape[1]
    half = width // 2
    n_pairs = q_width // 128
    qkv_width = q_width + 2 * kv_width
    values_from = q_width + kv_width
    x_bit, core_bit = place.c // 2, lax.rem(place.c, 2)
    own_cols = block_rows(place.t, feat)
    weights = [
        Scatter(
            place, keep.at[m], send.at[m % 2], core_land.at[m % 2], chip_land.at[m],
            line_land.at[m], m, scatter_sems,
        )
        for m in range(3)
    ]
    out_sum = Scatter(place, o_keep, o_send, o_core, o_chip, o_line, 3, scatter_sems)
    qkv_sum = Scatter(place, a_keep, a_send, a_core, a_chip, a_line, 4, scatter_sems)

    def to_sides(number, src, dst):
        return [
            remote(
                src(j), dst.at[j - 1], tp_send.at[number, j], tp_recv.at[number, j], place.side(j)
            )
            for j in range(1, tp)
        ]

    def away(buffer):
        return lambda j: buffer.at[j - 1]

    def fill_away(buffer, source):
        for j in range(1, tp):
            buffer[j - 1] = source[:, block_rows(lax.rem(place.t + j, tp), feat)]

    def route(number, src, dst):
        return [
            remote(
                src.at[block_rows(lax.rem(place.me + j, group), share), :],
                dst.at[block_rows(place.me, share), :],
                route_send.at[number, j],
                route_recv.at[number, j],
                place.peer(j),
            )
            for j in range(1, group)
        ]

    dmid_sum = to_sides(0, lambda j: dmid, tp_land)
    ffn_sum = to_sides(1, away(ffn_away), ffn_land)
    dx_sum = to_sides(2, away(dx_away), dx_land)
    route_o, route_g = route(0, sent, back_o), route(1, sent, back_g)

    place.greet()
    for copy in dmid_sum:
        copy.start()

    sources = (hidden, d_gate, d_up)
    tiles = [(m, b) for m in range(3) for b in range(0, ff, stage_cols)]
    loads = [
        pltpu.make_async_copy(
            sources[m].at[:, pl.ds(b, stage_cols)], stage.at[i % 2], load_sem.at[i]
        )
        for i, (m, b) in enumerate(tiles)
    ]
    load_n = pltpu.make_async_copy(normed_two, d_attn, load_sem.at[len(tiles)])
    dy, mid = x, d_mid_own
    load_dy = pltpu.make_async_copy(dy_in, dy, load_sem.at[len(tiles) + 1])
    load_x = pltpu.make_async_copy(x_in, x, load_sem.at[len(tiles) + 2])
    load_mid = pltpu.make_async_copy(mid_in, mid, load_sem.at[len(tiles) + 3])
    load_dy.start()
    loads[0].start()
    load_n.start()
    load_mid.start()
    fill_away(ffn_away, ffn)
    for copy in ffn_sum:
        copy.start()
    load_dy.wait()
    turn_blocks(place, dy, turned)
    sub = 256 if stage_cols % 256 == 0 else 128
    for i, (m, b) in enumerate(tiles):
        if i + 1 < len(tiles):
            loads[i + 1].start()
        if b == 0 and m == 1:
            load_n.wait()
            turn_blocks(place, d_attn, turned)
        if b == 0 and m == 2:
            weights[0].after_core()
            pl.semaphore_signal(
                free_sem, inc=1, device_id=place.at(c=place.flip(1)), device_id_type=MESH
            )
            weights[0].core.wait_send()
        loads[i].wait()
        for s in range(0, stage_cols, sub):
            right = stage[i % 2, :, s : s + sub]
            cols = slice(b + s, b + s + sub)
            keep[m, :, cols] = dot(turned[:half, :], right, 1, 0).astype(BF)
            send[m % 2, :, cols] = dot(turned[half:, :], right, 1, 0).astype(BF)
        if b + stage_cols == ff:
            if m == 2:
                pl.semaphore_wait(free_sem, 1)
            weights[m].start()
    weights[1].after_core()

    for copy in ffn_sum:
        copy.wait_recv()
    small_mine[...] = jnp.zeros_like(small_mine)
    load_mid.wait()

    def finish_output(i):
        r = block_rows(i, 128)
        ffn_out = ffn[r, own_cols].astype(F32)
        for j in range(1, tp):
            ffn_out = ffn_out + ffn_land[j - 1, r, :].astype(F32)
        small_mine[5:6, :feat] += jnp.sum(ffn_out * ffn_out, axis=0, keepdims=True)
        dx_away[0, r, :] = (mid[r, :] + ffn_out).astype(BF)

    repeat(rows // 128, finish_output)
    sent[...] = dot(pick_t[...], dx_away[0], 1, 0).astype(BF)
    weights[2].after_core()

    for copy in dmid_sum:
        copy.wait_recv()
    for copy in route_o:
        copy.start()
    own = block_rows(place.me, share)
    back_o[own, :] = sent[own, :]

    def sum_gradient(i):
        r = block_rows(i, 128)
        d_own = dy[r, own_cols].astype(F32) + dmid[r, own_cols].astype(F32)
        d_all = dy[r, :].astype(F32) + dmid[r, :].astype(F32)
        for j in range(1, tp):
            d_own = d_own + tp_land[j - 1, r, own_cols].astype(F32)
            d_all = d_all + tp_land[j - 1, r, :].astype(F32)
        d_mid_own[r, :] = d_own
        d_attn[r, :] = d_all.astype(BF)

    repeat(rows // 128, sum_gradient)
    load_x.start()
    dob[...] = dot(d_attn[...], w[:, qkv_width:], 1, 0).astype(BF)
    dq_t[...] = jnp.zeros_like(dq_t)
    ones = jnp.ones((8, 128), F32)

    def set_delta(g):
        both = dob[:, lane_block(g)].astype(F32) * heads[:, lane_block(g)]
        delta[g] = dot(ones, two_heads(both), 1, 1, lax.Precision.HIGHEST)

    repeat(n_pairs, set_delta)
    q_slot = place.c * piece + lanes((piece, rows))

    def one_piece(p):
        k_slot = p * piece + lax.broadcasted_iota(jnp.int32, (piece, rows), 0)
        open_ = (k_slot >= start_row[...]) & (k_slot <= q_slot)
        bias[...] = jnp.where(open_, 0.0, NEG_FILL)
        at = block_rows(p, piece)
        def heads_of(members):
            grads = []
            for g, (kb, ke), (vb, ve) in members:
                q2 = two_heads(qb[:, lane_block(g)])
                do2 = two_heads(dob[:, lane_block(g)])
                k2 = twice(kv_all[at, lane_block(kb)], ke)
                v2 = twice(kv_all[at, lane_block(vb)], ve)
                k_t = k2.astype(F32).T.astype(BF)
                dk = jnp.zeros((piece, 128), F32)
                dv = jnp.zeros((piece, 128), F32)
                for h in range(0, 2 * rows, 256):
                    part = slice(h, h + 256)
                    open_part = slice(h % rows, h % rows + 256)
                    s = dot(k2, q2[part], 1, 1)
                    dp = dot(v2, do2[part], 1, 1)
                    pe = jnp.exp(s * 0.125 + bias[:, open_part]) * sums[g, 0:1, part]
                    ds = (pe * (dp - delta[g, 0:1, part])).astype(BF)
                    dv = dv + dot(pe.astype(BF), do2[part], 1, 0)
                    dk = dk + dot(ds, q2[part], 1, 0)
                    dq_t[g, :, part] += dot(k_t, ds, 1, 0)
                grads.append((both_halves(dk) * 0.125, both_halves(dv)))
            low = lanes((piece, 128)) < HEAD_SIZE
            kb, vb = members[0][1][0], members[0][2][0]
            if len(members) == 2:
                dkv[at, lane_block(kb)] = jnp.where(low, grads[0][0], grads[1][0]).astype(BF)
                dkv[at, lane_block(vb)] = jnp.where(low, grads[0][1], grads[1][1]).astype(BF)
            else:
                for value, (b, e) in zip(grads[0], members[0][1:]):
                    c = 128 * b + HEAD_SIZE * e
                    dkv[at, c : c + HEAD_SIZE] = value[:, :HEAD_SIZE].astype(BF)

        over_key_heads(n_pairs, kv_width // HEAD_SIZE, heads_of)

    sibling = place.at(c=place.flip(1))
    other = 1 - core_bit
    to_passer = remote(
        dkv.at[block_rows(other, piece), :], kv_land.at[0], kv_send.at[0], kv_recv.at[0], sibling
    )
    to_chip = remote(
        dkv.at[block_rows(core_bit, piece), :],
        kv_land.at[0],
        kv_send.at[1],
        kv_recv.at[1],
        place.at(c=place.flip(2)),
    )
    to_core = remote(
        dkv.at[block_rows(2 * x_bit, piece), :], kv_land.at[1], kv_send.at[2], kv_recv.at[2], sibling
    )

    @pl.when(x_bit == 1)
    def _():
        def step(p, carry):
            one_piece(p)
            return carry

        lax.fori_loop(0, 2, step, 0)
        to_passer.start()

    turn_blocks(place, d_attn, turned)
    right = heads[...].astype(BF)
    o_keep[...] = dot(turned[:half, :], right, 1, 0).astype(BF)
    o_send[...] = dot(turned[half:, :], right, 1, 0).astype(BF)
    out_sum.start()

    @pl.when(x_bit == 1)
    def _():
        to_passer.wait_recv()
        mine = block_rows(core_bit, piece)
        dkv[mine, :] = (dkv[mine, :].astype(F32) + kv_land[0].astype(F32)).astype(BF)
        to_chip.start()

    weights[0].after_chip()

    @pl.when(core_bit == 1)
    def _():
        one_piece(place.c - 1)
        to_core.start()

    out_sum.after_core()
    one_piece(place.c)
    weights[1].after_chip()
    normed = tp_land.at[0]
    load_x.wait()

    def norm_again(i):
        v = x[block_rows(i, 128), :].astype(F32)
        normed[block_rows(i, 128), :] = (v * row_scale(v) * gain[...]).astype(BF)

    repeat(rows // 128, norm_again)
    turn_blocks(place, normed, turned)
    mine = block_rows(place.c, piece)

    @pl.when(core_bit == 0)
    def _():
        to_core.wait_recv()

    @pl.when(x_bit == 0)
    def _():
        to_chip.wait_recv()

    d_qkv = d_attn.at[:, pl.ds(0, qkv_width)]
    for b in range(0, qkv_width, 128):
        if b < q_width:
            g = b // 128
            grad = one_row(dq_t[g].T) * 0.125
        else:
            cols = slice(b - q_width, b - q_width + 128)
            grad = dkv[mine, cols].astype(F32)
            grad = jnp.where(x_bit == 0, grad + kv_land[0, :, cols].astype(F32), grad)
            grad = jnp.where(core_bit == 0, grad + kv_land[1, :, cols].astype(F32), grad)
        raw = dot(normed[...], w[:, b : b + 128], 1, 0)
        is_value = lanes(grad.shape) + b >= values_from
        back, gain_grad = qk_backward(
            grad, raw, head_gain[:, b : b + 128], cosines[...], sines[...], is_value
        )
        small_mine[2:3, b : b + 128] = gain_grad
        d_qkv[:, b : b + 128] = back.astype(BF)

    def finish_gradient(i):
        r = block_rows(i, 128)
        dn = dot(d_qkv[r, :], w[:, :qkv_width], 1, 1)
        dx, gain_grad = norm_back(dn, x[r, :].astype(F32), gain[...])
        normed[r, :] = dx.astype(BF)
        small_mine[0:1, :] += gain_grad

    repeat(rows // 128, finish_gradient)
    fill_away(dx_away, normed)
    for copy in dx_sum:
        copy.start()
    small_mine[1:2, :] = gain_ffn_grad[...]
    small_mine[3:5, :] = squares[...]
    for b in range(0, qkv_width, 256):
        cols = slice(b, b + 256)
        a_keep[:, cols] = dot(turned[:half, :], d_qkv[:, cols], 1, 0).astype(BF)
        a_send[:, cols] = dot(turned[half:, :], d_qkv[:, cols], 1, 0).astype(BF)
    qkv_sum.start()
    small_out = [
        remote(
            small_mine, small_land.at[place.me], small_send.at[0, j], small_recv.at[0, j], place.peer(j)
        )
        for j in range(1, group)
    ]
    for copy in small_out:
        copy.start()
    small_land[place.me] = small_mine[...]
    weights[2].after_chip()
    qkv_sum.after_core()
    out_sum.after_chip()

    for copy in dx_sum:
        copy.wait_recv()
    for copy in ffn_sum:
        copy.wait_send()

    def finish_input(i):
        r = block_rows(i, 128)
        total = d_mid_own[r, :] + normed[r, own_cols].astype(F32)
        for j in range(1, tp):
            total = total + dx_land[j - 1, r, :].astype(F32)
        ffn_away[0, r, :] = total.astype(BF)

    repeat(rows // 128, finish_input)
    for copy in route_o:
        copy.wait_send()
    sent[...] = dot(pick_t[...], ffn_away[0], 1, 0).astype(BF)
    for copy in route_g:
        copy.start()
    back_g[own, :] = sent[own, :]
    for copy in small_out:
        copy.wait_recv()
    total = small_land[0]
    for i in range(1, group):
        total = total + small_land[i]
    small_side[place.t] = total
    for copy in small_out:
        copy.wait_send()
    small_mine[...] = total
    sides = [
        remote(
            small_mine, small_side.at[place.t], small_send.at[1, j], small_recv.at[1, j], place.side(j)
        )
        for j in range(1, tp)
    ]
    for copy in sides:
        copy.start()
    for m, out in enumerate((sum_down, sum_gate, sum_up)):
        weights[m].after_line(out)
    qkv_sum.after_chip()
    out_sum.after_line(sum_out)
    for copy in sides:
        copy.wait_recv()
    total = small_side[0]
    for j in range(1, tp):
        total = total + small_side[j]
    small[...] = total
    for copy in route_o + route_g:
        copy.wait_recv()
    qkv_sum.after_line(sum_qkv)

    @pl.when(x_bit == 1)
    def _():
        to_passer.wait_send()
        to_chip.wait_send()

    @pl.when(core_bit == 1)
    def _():
        to_core.wait_send()

    for copy in dmid_sum + dx_sum + route_g + sides:
        copy.wait_send()
    weights[0].drain(core=False)
    for s in (weights[1], weights[2], out_sum, qkv_sum):
        s.drain()


def backward_pass(grid, q_width, kv_width, *operands):
    dmid, hidden = operands[1], operands[19]
    rows, width = dmid.shape
    ff = hidden.shape[1]
    n, ctx, tp = grid.n, grid.ctx, grid.tp
    group = n * ctx
    feat = width // tp
    half = width // 2
    h = width // group
    n_pairs = q_width // 128
    qkv_width = q_width + 2 * kv_width
    stage_cols = 256 if ff % 256 == 0 else 128
    vm = pl.BlockSpec(memory_space=pltpu.VMEM)
    dma = pltpu.SemaphoreType.DMA
    V = pltpu.VMEM

    def scatter_space(cols):
        return [
            V((half, cols), BF),
            V((half, cols), BF),
            V((half, cols), BF),
            V((half // 2, cols), BF),
            V((n - 1, h, cols), BF),
        ]

    return pl.pallas_call(
        functools.partial(backward_kernel, n, ctx, tp, q_width, kv_width, stage_cols),
        in_specs=[vm] * 15 + [ANYWHERE] * 7,
        out_specs=[vm] * 8,
        out_shape=[
            shape((rows, feat), BF),
            shape((rows, feat), BF),
            shape((h, ff), F32),
            shape((h, ff), F32),
            shape((h, ff), F32),
            shape((h, q_width), F32),
            shape((h, qkv_width), F32),
            shape((8, width), F32),
        ],
        scratch_shapes=[
            V((rows, width), BF),
            V((width, rows), BF),
            V((2, rows, stage_cols), BF),
            V((3, half, ff), BF),
            V((2, half, ff), BF),
            V((2, half, ff), BF),
            V((3, half // 2, ff), BF),
            V((3, n - 1, h, ff), BF),
        ]
        + scatter_space(q_width)
        + scatter_space(qkv_width)
        + [
            V((rows, feat), F32),
            V((rows, width), BF),
            V((rows, q_width), BF),
            V((n_pairs, 8, 2 * rows), F32),
            V((rows, rows), F32),
            V((n_pairs, 128, 2 * rows), F32),
            V((rows * ctx, 2 * kv_width), BF),
            V((2, rows, 2 * kv_width), BF),
            V((tp - 1, rows, width), BF),
            V((tp - 1, rows, feat), BF),
            V((tp - 1, rows, feat), BF),
            V((tp - 1, rows, feat), BF),
            V((tp - 1, rows, feat), BF),
            V((rows, feat), BF),
            V((8, width), F32),
            V((group, 8, width), F32),
            V((tp, 8, width), F32),
            dma((3, tp)),
            dma((3, tp)),
            dma((2, group)),
            dma((2, group)),
            dma((2, max(group, tp))),
            dma((2, max(group, tp))),
            dma((3,)),
            dma((3,)),
            dma((3 * (ff // stage_cols) + 4,)),
            pltpu.SemaphoreType.REGULAR,
            dma((5,)),
            dma((5,)),
            dma((5,)),
            dma((5,)),
            dma((5, n)),
            dma((5, n)),
        ],
        compiler_params=pltpu.CompilerParams(
            vmem_limit_bytes=61 * 2**20, collective_id=1, has_side_effects=True
        ),
        cost_estimate=pl.CostEstimate(
            flops=20 * rows * rows * ctx * q_width, bytes_accessed=40 * 2**20, transcendentals=0
        ),
    )(*operands)


def shape(s, t):
    return jax.ShapeDtypeStruct(s, t)


VMEM_LIMIT = pltpu.CompilerParams(vmem_limit_bytes=58 * 2**20)
ANYWHERE = pl.BlockSpec(memory_space=pl.ANY)


def ffn_pass(mid, dy, gain, w_ffn):
    rows, width = mid.shape
    ff = w_ffn.shape[1] // 3
    tile = 256 if ff % 256 == 0 else 128
    steps = ff // tile
    whole = lambda shape: pl.BlockSpec(shape, lambda s: (0, 0))
    column = pl.BlockSpec((rows, tile), lambda s: (0, s))
    weight = lambda i: pl.BlockSpec((width, tile), lambda s: (0, i * steps + s))
    return pl.pallas_call(
        ffn_kernel,
        grid=(steps,),
        in_specs=[whole((rows, width))] * 2 + [whole((1, width))] + [weight(i) for i in range(3)],
        out_specs=[whole((rows, width))] * 2
        + [whole((1, width)), whole((rows, width))]
        + [column] * 3,
        scratch_shapes=[pltpu.VMEM((rows, width), F32), pltpu.VMEM((rows, width), F32)],
        out_shape=[shape((rows, width), BF)] * 2
        + [shape((1, width), F32), shape((rows, width), BF)]
        + [shape((rows, ff), BF)] * 3,
        compiler_params=VMEM_LIMIT,
        cost_estimate=pl.CostEstimate(
            flops=12 * rows * width * ff, bytes_accessed=6 * width * ff, transcendentals=rows * ff
        ),
    )(mid, dy, gain, w_ffn, w_ffn, w_ffn)


def pad_columns(v, to):
    return v if v.shape[1] == to else jnp.pad(v, ((0, 0), (0, to - v.shape[1])))


def one_hot(rows, columns):
    return (rows == columns).astype(BF)


def local(
    tokens,
    cotangent,
    slot_of,
    lengths,
    w_query,
    key_weight,
    value_weight,
    w_out,
    w_gate,
    w_up,
    w_down,
    gain_attn,
    gain_ffn,
    gain_query,
    gain_key,
):
    grid = Grid()
    stream_len = tokens.shape[0]
    feat_len = tokens.shape[1]
    local_len = PACKED_ROW_SLOTS // grid.ctx
    row_count = stream_len // local_len
    groups = grid.n * grid.ctx
    share = stream_len // groups
    q_heads = QUERY_HEADS // grid.tp
    key_value_heads = KEY_VALUE_HEADS // grid.tp
    query_group_width = QUERY_HEADS // KEY_VALUE_HEADS
    q_width = q_heads * HEAD_SIZE
    kv_width = key_value_heads * HEAD_SIZE
    flat_len = row_count * local_len
    row_len = PACKED_ROW_SLOTS
    me = grid.z * grid.ctx + grid.c
    both = ("fsdp", "ctx")

    def home(slots):
        row, place = slots // row_len, slots % row_len
        return (
            row // row_count * grid.ctx + place // local_len,
            row % row_count * local_len + place % local_len,
        )

    my_slots = lax.dynamic_slice_in_dim(slot_of, me * stream_len, stream_len, 0)
    my_target = home(my_slots)[0]
    ahead = (my_target[:, None] == my_target[None, :]) & (my_slots[None, :] < my_slots[:, None])
    send_place = my_target * share + jnp.sum(ahead.astype(jnp.int32), axis=1)
    line = jnp.arange(stream_len, dtype=jnp.int32)
    send_pick = one_hot(line[:, None], send_place[None, :])
    all_dev, all_local = home(slot_of)
    low = 32
    high = flat_len // low
    sender = (jnp.arange(slot_of.shape[0], dtype=jnp.int32) // stream_len).astype(F32)
    mine = (all_dev == me)[None, :] & (
        (all_local // low)[None, :] == jnp.arange(high, dtype=jnp.int32)[:, None]
    )
    left = jnp.where(mine, sender[None, :], 0.0).astype(BF)
    right = one_hot((all_local % low)[:, None], jnp.arange(low, dtype=jnp.int32)[None, :])
    source = product(left, right, "ht,tl->hl").reshape(flat_len).astype(jnp.int32)
    slot_line = jnp.arange(flat_len, dtype=jnp.int32)
    before = (source[:, None] == source[None, :]) & (slot_line[None, :] < slot_line[:, None])
    arrival = source * share + jnp.sum(before.astype(jnp.int32), axis=1)
    take_pick = one_hot(arrival[:, None], line[None, :])

    def sent_order(v):
        return product(send_pick, v, "pt,tf->pf").astype(BF)

    take_back = one_hot(line[:, None], arrival[None, :])
    send_back = one_hot(send_place[:, None], line[None, :])

    ff = w_gate.shape[1]
    ff_pad = -(-ff // 128) * 128
    attn_shard = jnp.concatenate([w_query, key_weight, value_weight, w_out.T], axis=1)
    ffn_shard = jnp.concatenate(
        [pad_columns(v, ff_pad) for v in (w_gate, w_up, w_down.T)], axis=1
    )
    own_slots = grid.c * local_len + jnp.arange(local_len, dtype=jnp.int32)
    position = slot_tables(lengths[0], own_slots)[1]
    start = own_slots - position
    frequency = ROPE_THETA ** (-jnp.arange(0, HEAD_SIZE, 2).astype(F32) / HEAD_SIZE)
    angles = position.astype(F32)[:, None] * frequency[None, :]
    cosines = jnp.tile(jnp.cos(angles), (1, 4))
    sin = jnp.sin(angles)
    sines = jnp.tile(jnp.concatenate([-sin, sin], axis=1), (1, 2))
    head_gain = jnp.concatenate(
        [
            jnp.tile(gain_query, q_heads),
            jnp.tile(gain_key, key_value_heads),
            jnp.ones((kv_width,), F32),
        ]
    )[None, :]
    x_full, dy_full, qb, row_kv, heads, sums, middle, squares, attn_w, ffn_w = forward_pass(
        grid,
        q_width,
        kv_width,
        ff_pad,
        sent_order(tokens),
        sent_order(cotangent),
        take_pick,
        gain_attn[None, :],
        head_gain,
        cosines,
        sines,
        start[:, None],
        attn_shard,
        ffn_shard,
    )
    own_features = lambda v: lax.dynamic_slice_in_dim(v, grid.t * feat_len, feat_len, 1)
    middle_own = own_features(middle)
    ffn_part, d_mid_part, d_gain_ffn, normed_two, hidden, d_gate, d_up = ffn_pass(
        middle, dy_full, gain_ffn[None, :], ffn_w
    )
    back_o, back_g, sum_gate, sum_up, sum_down, sum_out, sum_qkv, small = backward_pass(
        grid,
        q_width,
        kv_width,
        ffn_part,
        d_mid_part,
        qb,
        row_kv,
        heads,
        sums,
        attn_w,
        cosines,
        sines,
        take_back,
        gain_attn[None, :],
        head_gain,
        start[None, :],
        d_gain_ffn,
        squares,
        dy_full,
        x_full,
        middle_own,
        normed_two,
        hidden,
        d_gate,
        d_up,
    )
    a, b = q_width, q_width + kv_width
    per_head = small[2, : b + kv_width].reshape(-1, HEAD_SIZE)
    entry_count = flat_len * groups * MODEL_WIDTH
    square_sums = jnp.sum(small[3:6], axis=1) / jnp.stack([grid.tp, grid.tp, 1]).astype(F32)

    def bring_back(v):
        return product(send_back, v, "tp,pf->tf").astype(BF)

    return (
        bring_back(back_o),
        bring_back(back_g),
        sum_qkv[:, :a],
        sum_qkv[:, a:b],
        sum_qkv[:, b:],
        sum_out.T,
        sum_gate[:, :ff],
        sum_up[:, :ff],
        sum_down[:, :ff].T,
        small[0],
        small[1],
        jnp.sum(per_head[:q_heads], axis=0),
        jnp.sum(per_head[q_heads : q_heads + key_value_heads], axis=0),
        jnp.sqrt(square_sums / entry_count),
    )


def solution(mesh):
    row = P(("fsdp", "ctx"), "tp")
    column = P("tp", ("fsdp", "ctx"))
    in_specs = (row, row, P(), P("fsdp", None), row, row, row, column, row, row, column) + (P(),) * 4
    out_specs = (row, row, row, row, row, column, row, row, column) + (P(),) * 5
    return jax.shard_map(local, mesh=mesh, in_specs=in_specs, out_specs=out_specs, check_vma=False)
```

```python
import functools

import jax
import jax.numpy as jnp
from jax import lax
from jax.experimental import pallas as pl
from jax.experimental.pallas import tpu as pltpu
from jax.sharding import PartitionSpec as P

MODEL_WIDTH = 1024
QUERY_HEADS = 16
KEY_VALUE_HEADS = 8
HEAD_SIZE = 64
PACKED_ROW_SLOTS = 2048
QUERY_BLOCK_ROWS = 512

EPSILON = 1e-05
ROPE_THETA = 1000000.0
NEG_FILL = -1e30
BF = jnp.bfloat16
F32 = jnp.float32


def segment_ends(lengths):
    total, ends = lengths[0], []
    for i in range(lengths.shape[0]):
        ends.append(total)
        if i + 1 < lengths.shape[0]:
            total = total + lengths[i + 1]
    return ends


def slot_tables(lengths, slot_ids):
    segment = jnp.zeros_like(slot_ids)
    start = jnp.zeros_like(slot_ids)
    for i, end in enumerate(segment_ends(lengths)):
        passed = (slot_ids >= end).astype(jnp.int32)
        segment = segment + passed
        start = start + passed * lengths[i]
    return (segment, slot_ids - start)


def product(left_arr, right_arr, pattern):
    return jnp.einsum(pattern, left_arr, right_arr, preferred_element_type=F32)


class Grid:
    def __init__(self):
        self.n = lax.axis_size("fsdp")
        self.ctx = lax.axis_size("ctx")
        self.tp = lax.axis_size("tp")
        self.z = lax.axis_index("fsdp")
        self.c = lax.axis_index("ctx")
        self.t = lax.axis_index("tp")


def dot(a, b, ca, cb, precision=None):
    return lax.dot_general(
        a, b, (((ca,), (cb,)), ((), ())), preferred_element_type=F32, precision=precision
    )


def lanes(shape):
    return lax.broadcasted_iota(jnp.int32, shape, 1)


def half_mean(v):
    low = lanes(v.shape) < HEAD_SIZE
    first = jnp.sum(jnp.where(low, v, 0.0), axis=1, keepdims=True)
    second = jnp.sum(jnp.where(low, 0.0, v), axis=1, keepdims=True)
    return jnp.where(low, first, second) * (1.0 / HEAD_SIZE)


def half_swap(v):
    quarter = HEAD_SIZE // 2
    left = pltpu.roll(v, 128 - quarter, 1)
    right = pltpu.roll(v, quarter, 1)
    return jnp.where(lanes(v.shape) % HEAD_SIZE < quarter, left, right)


def row_scale(v):
    return lax.rsqrt(jnp.mean(v * v, axis=1, keepdims=True) + EPSILON)


def norm_back(dn, v, gain):
    scale = row_scale(v)
    unit = v * scale
    scaled = dn * gain
    grad = scale * (scaled - unit * jnp.mean(scaled * unit, axis=1, keepdims=True))
    return grad, jnp.sum(dn * unit, axis=0, keepdims=True)


def qk_forward(raw, gain, cosines, sines, is_value):
    normed = raw * lax.rsqrt(half_mean(raw * raw) + EPSILON) * gain
    turned = normed * cosines + half_swap(normed) * sines
    return jnp.where(is_value, raw, turned)


def qk_backward(grad, raw, gain, cosines, sines, is_value):
    straight = grad * cosines - half_swap(grad) * sines
    scale = lax.rsqrt(half_mean(raw * raw) + EPSILON)
    unit = raw * scale
    scaled = straight * gain
    back = scale * (scaled - unit * half_mean(scaled * unit))
    gain_grad = jnp.sum(straight * unit, axis=0, keepdims=True)
    return jnp.where(is_value, grad, back), gain_grad


def two_heads(v):
    low = lanes(v.shape) < HEAD_SIZE
    zero = jnp.zeros_like(v)
    return jnp.concatenate([jnp.where(low, v, zero), jnp.where(low, zero, v)], axis=0)


def one_row(v):
    rows = v.shape[0] // 2
    return jnp.where(lanes((rows, v.shape[1])) < HEAD_SIZE, v[:rows], v[rows:])


def twice(v, which):
    half = v[:, which * HEAD_SIZE : (which + 1) * HEAD_SIZE]
    return jnp.concatenate([half, half], axis=1)


def both_halves(v):
    return v + jnp.concatenate([v[:, HEAD_SIZE:], v[:, :HEAD_SIZE]], axis=1)


def over_key_heads(n_heads, values_from, body):
    if n_heads % 2:
        for g in range(n_heads):
            body([(g, (g // 2, g % 2), ((values_from + g) // 2, (values_from + g) % 2))])
        return

    def step(i, carry):
        body([(2 * i + e, (i, e), (values_from // 2 + i, e)) for e in range(2)])
        return carry

    lax.fori_loop(0, n_heads // 2, step, 0)


def lane_block(i):
    return block_rows(i, 128)


def ffn_kernel(mid, dy, gain, w_gate, w_up, w_down, ffn, dmid, dgain, nb, hid, dgt, dup, ffn_acc, dn_acc):
    step = pl.program_id(0)

    @pl.when(step == 0)
    def _():
        v = mid[...].astype(BF).astype(F32)
        nb[...] = (v * row_scale(v) * gain[...]).astype(BF)
        ffn_acc[...] = jnp.zeros_like(ffn_acc)
        dn_acc[...] = jnp.zeros_like(dn_acc)

    normed = nb[...]
    gate = dot(normed, w_gate[...], 1, 0)
    up = dot(normed, w_up[...], 1, 0)
    d_hidden = dot(dy[...], w_down[...], 1, 0)
    sig = 1.0 / (1.0 + jnp.exp(-gate))
    silu = gate * sig
    hidden = (silu * up).astype(BF)
    d_gate = (d_hidden * up * (sig * (1.0 + gate * (1.0 - sig)))).astype(BF)
    d_up = (d_hidden * silu).astype(BF)
    hid[...] = hidden
    dgt[...] = d_gate
    dup[...] = d_up
    ffn_acc[...] += dot(hidden, w_down[...], 1, 1)
    dn_acc[...] += dot(d_gate, w_gate[...], 1, 1) + dot(d_up, w_up[...], 1, 1)

    @pl.when(step == pl.num_programs(0) - 1)
    def _():
        v = mid[...].astype(BF).astype(F32)
        grad, gain_sum = norm_back(dn_acc[...], v, gain[...])
        dgain[...] = gain_sum
        dmid[...] = grad.astype(BF)
        ffn[...] = ffn_acc[...].astype(BF)


class Place:
    def __init__(self, n, ctx, tp):
        self.n, self.ctx, self.tp = n, ctx, tp
        self.z = lax.axis_index("fsdp")
        self.c = lax.axis_index("ctx")
        self.t = lax.axis_index("tp")
        self.me = self.z * ctx + self.c

    def at(self, z=None, c=None, t=None):
        return (
            self.z if z is None else z,
            self.c if c is None else c,
            self.t if t is None else t,
        )

    def peer(self, j):
        p = lax.rem(self.me + j, self.n * self.ctx)
        return self.at(p // self.ctx, lax.rem(p, self.ctx))

    def up(self, j):
        return self.at(z=lax.rem(self.z + j, self.n))

    def flip(self, bit):
        if bit == 1:
            return self.c + 1 - 2 * lax.rem(self.c, 2)
        return lax.rem(self.c + 2, 4)

    def side(self, j):
        return self.at(t=lax.rem(self.t + j, self.tp))

    def owner(self, k, c):
        return lax.rem(self.z - k + self.n, self.n) * self.ctx + c

    def greet(self):
        barrier = pltpu.get_barrier_semaphore()
        group = self.n * self.ctx
        for j in range(1, group):
            pl.semaphore_signal(barrier, inc=1, device_id=self.peer(j), device_id_type=MESH)
        for j in range(1, self.tp):
            pl.semaphore_signal(barrier, inc=1, device_id=self.side(j), device_id_type=MESH)
        pl.semaphore_wait(barrier, group + self.tp - 2)


MESH = pl.DeviceIdType.MESH


def remote(src, dst, send, recv, device):
    return pltpu.make_async_remote_copy(
        src_ref=src, dst_ref=dst, send_sem=send, recv_sem=recv, device_id=device, device_id_type=MESH
    )


def block_rows(index, size):
    return pl.ds(pl.multiple_of(index * size, size), size)


class Gather:
    def __init__(self, place, shard, whole, columns, number, sems, chip_first=False):
        z_send, z_recv, x_send, x_recv, c_send, c_recv, own = sems
        h = shard.shape[0]
        n = place.n
        self.n, self.chip_first = n, chip_first
        view = lambda index: whole.at[block_rows(index, h), columns]
        here, there = place.c, place.flip(2)
        mine = shard.at[:, columns]
        self.own = pltpu.make_async_copy(mine, view(place.me), own.at[number])

        def ring(lane, row):
            return [
                remote(
                    mine if k == 1 and row == number else view(place.owner(k - 1, lane)),
                    view(place.owner(k - 1, lane)),
                    z_send.at[row, k],
                    z_recv.at[row, k],
                    place.up(1),
                )
                for k in range(1, n)
            ]

        self.rings = [ring(here, number)] + ([ring(there, number + 1)] if chip_first else [])
        self.chip = [
            remote(
                mine if k == 0 else view(place.owner(k, here)),
                view(place.owner(k, here)),
                x_send.at[number, k],
                x_recv.at[number, k],
                place.at(c=there),
            )
            for k in range(1 if chip_first else n)
        ]
        self.core = [
            remote(
                mine if i == 0 else view(place.owner(i % n, here if i < n else there)),
                view(place.owner(i % n, here if i < n else there)),
                c_send.at[number, i],
                c_recv.at[number, i],
                place.at(c=place.flip(1)),
            )
            for i in range(2 * n)
        ]

    def begin(self):
        if self.n > 1:
            self.rings[0][0].start()
        self.own.start()
        self.core[0].start()

    def begin_other(self):
        if self.n > 1:
            self.rings[1][0].start()

    def advance(self, k):
        if k >= self.n:
            return
        for r, ring in enumerate(self.rings):
            ring[k - 1].wait_recv()
            if k + 1 < self.n:
                ring[k].start()
            self.core[r * self.n + k].start()

    def to_chip(self, k):
        if k < len(self.chip):
            self.chip[k].start()

    def from_chip(self, k):
        if k < len(self.chip):
            self.chip[k].wait_recv()
            self.core[self.n + k].start()

    def finish(self):
        for copy in self.core:
            copy.wait_recv()
        self.own.wait()

    def drain(self):
        for copy in sum(self.rings, []) + self.chip + self.core:
            copy.wait_send()


def forward_kernel(
    n, ctx, tp, q_width, kv_width, ff,
    sent_x, sent_y, pick, gain, head_gain, cosines, sines, start_col, attn_shard, ffn_shard,
    x, dy, qb, kv, heads, sums, mid, squares, w_attn, w_ffn,
    got_x, got_y, own_x, own_y, x_land, y_land, w, kv_all, part, land, acc, total, bias,
    route_send, route_recv, tp_send, tp_recv, kv_send, kv_recv, out_sem, *gather_sems
):
    place = Place(n, ctx, tp)
    group = n * ctx
    rows = got_x.shape[0]
    share = rows // group
    feat = got_x.shape[1]
    width = x_land.shape[1]
    piece = rows
    every = pl.ds(0, attn_shard.shape[1])
    attn = Gather(place, attn_shard, w, every, 0, gather_sems)
    units = 3 * ff // 128
    last = -(-units // 6)
    cuts = [(units - last) * i // 3 * 128 for i in range(4)]
    groups = [
        Gather(
            place, ffn_shard, w_ffn, pl.ds(cuts[i], cuts[i + 1] - cuts[i]), 1 + i, gather_sems
        )
        for i in range(3)
    ]
    first, second, third = groups
    tail = Gather(
        place, ffn_shard, w_ffn, pl.ds(cuts[3], last * 128), 4, gather_sems, chip_first=True
    )

    def route(number, src, dst):
        return [
            remote(
                src.at[block_rows(lax.rem(place.me + j, group), share), :],
                dst.at[block_rows(place.me, share), :],
                route_send.at[number, j],
                route_recv.at[number, j],
                place.peer(j),
            )
            for j in range(1, group)
        ]

    def widen(number, src, dst):
        return [
            remote(
                src,
                dst.at[:, block_rows(place.t, feat)],
                tp_send.at[number, j],
                tp_recv.at[number, j],
                place.side(j),
            )
            for j in range(1, tp)
        ]

    def own_block(src, dst):
        at = block_rows(place.me, share)
        dst[at, :] = src[at, :]

    route_x, route_y = route(0, sent_x, got_x), route(1, sent_y, got_y)
    wide_x, wide_y = widen(0, own_x, x_land), widen(1, own_y, y_land)
    place.greet()
    for copy in route_x:
        copy.start()
    attn.begin()
    attn.to_chip(0)
    own_block(sent_x, got_x)
    own_block(sent_y, got_y)
    attn.advance(1)
    attn.to_chip(1)
    for copy in route_x:
        copy.wait_recv()
    own_x[...] = dot(pick[...], got_x[...], 1, 0).astype(BF)
    for copy in wide_x:
        copy.start()
    x_land[:, block_rows(place.t, feat)] = own_x[...]
    attn.from_chip(0)
    attn.advance(2)
    attn.to_chip(2)
    attn.from_chip(1)
    attn.advance(3)
    attn.to_chip(3)
    for g in groups:
        g.begin()
    attn.from_chip(2)
    attn.from_chip(3)
    first.to_chip(0)
    for copy in wide_x:
        copy.wait_recv()
    v = x_land[...].astype(F32)
    x[...] = x_land[...]
    normed = (v * row_scale(v) * gain[...]).astype(BF)
    attn.finish()
    write_w = pltpu.make_async_copy(w, w_attn, out_sem.at[0])
    write_w.start()

    own_rows = block_rows(place.c, piece)
    values_from = q_width + kv_width
    for b in list(range(q_width, q_width + 2 * kv_width, 128)) + list(range(0, q_width, 128)):
        if b == 0:
            later = start_keys(place, kv_all, own_rows, kv_send, kv_recv)
        block = dot(normed, w[:, b : b + 128], 1, 0)
        is_value = lanes(block.shape) + b >= values_from
        done = qk_forward(block, head_gain[:, b : b + 128], cosines[...], sines[...], is_value)
        if b < q_width:
            qb[:, b : b + 128] = done.astype(BF)
        else:
            kv_all[own_rows, b - q_width : b - q_width + 128] = done.astype(BF)

    q_slot = place.c * piece + lax.broadcasted_iota(jnp.int32, (rows, piece), 0)
    n_pairs = q_width // 128

    def one_piece(p):
        k_slot = p * piece + lanes((rows, piece))
        open_ = (k_slot >= start_col[...]) & (k_slot <= q_slot)
        bias[...] = jnp.where(open_, 0.0, NEG_FILL)
        at = block_rows(p, piece)

        def heads_of(members):
            for g, (kb, ke), (vb, ve) in members:
                q2 = two_heads(qb[:, lane_block(g)])
                k2 = twice(kv_all[at, lane_block(kb)], ke)
                v2 = twice(kv_all[at, lane_block(vb)], ve)
                for h in range(2):
                    part = slice(h * rows, (h + 1) * rows)
                    e = jnp.exp(dot(q2[part], k2, 1, 1) * 0.125 + bias[...])
                    part_sum = e[:, :128]
                    for b in range(128, piece, 128):
                        part_sum = part_sum + e[:, b : b + 128]
                    acc[g, part, :] += dot(e.astype(BF), v2, 1, 0)
                    total[g, part, :] += part_sum

        over_key_heads(n_pairs, kv_width // HEAD_SIZE, heads_of)

    acc[...] = jnp.zeros_like(acc)
    total[...] = jnp.zeros_like(total)
    one_piece(place.c)
    x_bit, core_bit = place.c // 2, lax.rem(place.c, 2)
    near, across, passed = later
    for g in groups:
        g.advance(1)
    second.to_chip(0)
    tail.to_chip(0)

    @pl.when(x_bit == 1)
    def _():
        across.wait_recv()
        passed.start()

    first.from_chip(0)
    third.to_chip(0)
    first.to_chip(1)

    @pl.when(core_bit == 1)
    def _():
        near.wait_recv()
        one_piece(place.c - 1)

    @pl.when(x_bit == 1)
    def _():
        passed.wait_recv()

        def step(p, carry):
            one_piece(p)
            return carry

        lax.fori_loop(0, 2, step, 0)

    second.from_chip(0)
    second.to_chip(1)
    tail.from_chip(0)
    tail.begin()
    tail.begin_other()
    for g in groups:
        g.advance(2)
    ones = jnp.ones((8, 128), F32)
    for g in range(n_pairs):
        row_total = jnp.sum(total[g], axis=1, keepdims=True)
        heads[:, 128 * g : 128 * g + 128] = one_row(acc[g] / row_total)
        sums[g] = 1.0 / dot(ones, total[g], 1, 1, lax.Precision.HIGHEST)
    part[...] = dot(heads[...].astype(BF), w[:, q_width + 2 * kv_width :], 1, 1).astype(BF)
    attention = [
        remote(part, land.at[j - 1], tp_send.at[2, j], tp_recv.at[2, j], place.side(j))
        for j in range(1, tp)
    ]
    for copy in attention:
        copy.start()
    write_kv = pltpu.make_async_copy(kv_all, kv, out_sem.at[1])
    for copy in route_y:
        copy.start()
    third.from_chip(0)
    third.to_chip(1)
    first.from_chip(1)
    first.to_chip(2)
    second.from_chip(1)
    second.to_chip(2)
    tail.advance(1)
    for g in groups:
        g.advance(3)
    third.from_chip(1)
    third.to_chip(2)
    for copy in route_y:
        copy.wait_recv()
    own_y[...] = dot(pick[...], got_y[...], 1, 0).astype(BF)
    for copy in attention:
        copy.wait_recv()
    for copy in wide_y:
        copy.start()
    y_land[:, block_rows(place.t, feat)] = own_y[...]
    tail.advance(2)
    first.from_chip(2)
    first.to_chip(3)
    att = part[...].astype(F32)
    for j in range(1, tp):
        att = att + land[j - 1].astype(F32)
    v = x_land[...].astype(F32)
    squares[0:1, :] = jnp.sum(v * v, axis=0, keepdims=True)
    squares[1:2, :] = jnp.sum(att * att, axis=0, keepdims=True)
    mid[...] = v + att
    second.from_chip(2)
    second.to_chip(3)
    third.from_chip(2)
    third.to_chip(3)
    tail.advance(3)
    for copy in wide_y:
        copy.wait_recv()
    dy[...] = y_land[...]
    for g in groups:
        g.from_chip(3)

    @pl.when(core_bit == 0)
    def _():
        near.wait_send()

    @pl.when(x_bit == 0)
    def _():
        across.wait_send()

    @pl.when(x_bit == 1)
    def _():
        passed.wait_send()

    write_kv.start()
    for g in groups + [tail]:
        g.finish()
    for copy in route_x + route_y + wide_x + wide_y + attention:
        copy.wait_send()
    for g in [attn, tail] + groups:
        g.drain()
    write_w.wait()
    write_kv.wait()


def start_keys(place, kv_all, own_rows, send, recv):
    x_bit, core_bit = place.c // 2, lax.rem(place.c, 2)
    mine = kv_all.at[own_rows, :]
    near = remote(mine, mine, send.at[0], recv.at[0], place.at(c=place.flip(1)))
    across = remote(mine, mine, send.at[1], recv.at[1], place.at(c=place.flip(2)))
    from_chip = kv_all.at[block_rows(place.flip(2), own_rows.size), :]
    passed = remote(from_chip, from_chip, send.at[2], recv.at[2], place.at(c=place.flip(1)))

    @pl.when(x_bit == 0)
    def _():
        across.start()

    @pl.when(core_bit == 0)
    def _():
        near.start()

    return near, across, passed


def forward_pass(grid, q_width, kv_width, ff, *operands):
    sent_x, attn_shard = operands[0], operands[8]
    rows, feat = sent_x.shape
    n, ctx, tp = grid.n, grid.ctx, grid.tp
    width = feat * tp
    n_pairs = q_width // 128
    row_len = rows * ctx
    vm = pl.BlockSpec(memory_space=pltpu.VMEM)
    dma = pltpu.SemaphoreType.DMA
    group = n * ctx
    return pl.pallas_call(
        functools.partial(forward_kernel, n, ctx, tp, q_width, kv_width, ff),
        in_specs=[vm] * 8 + [ANYWHERE] * 2,
        out_specs=[vm] * 3 + [ANYWHERE] + [vm] * 4 + [ANYWHERE] * 2,
        out_shape=[
            shape((rows, width), BF),
            shape((rows, width), BF),
            shape((rows, q_width), BF),
            shape((row_len, 2 * kv_width), BF),
            shape((rows, q_width), F32),
            shape((n_pairs, 8, 2 * rows), F32),
            shape((rows, width), F32),
            shape((2, width), F32),
            shape((width, attn_shard.shape[1]), BF),
            shape((width, 3 * ff), BF),
        ],
        scratch_shapes=[
            pltpu.VMEM((rows, feat), BF),
            pltpu.VMEM((rows, feat), BF),
            pltpu.VMEM((rows, feat), BF),
            pltpu.VMEM((rows, feat), BF),
            pltpu.VMEM((rows, width), BF),
            pltpu.VMEM((rows, width), BF),
            pltpu.VMEM((width, attn_shard.shape[1]), BF),
            pltpu.VMEM((row_len, 2 * kv_width), BF),
            pltpu.VMEM((rows, width), BF),
            pltpu.VMEM((tp - 1, rows, width), BF),
            pltpu.VMEM((n_pairs, 2 * rows, 128), F32),
            pltpu.VMEM((n_pairs, 2 * rows, 128), F32),
            pltpu.VMEM((rows, rows), F32),
            dma((2, group)),
            dma((2, group)),
            dma((3, tp)),
            dma((3, tp)),
            dma((3,)),
            dma((3,)),
            dma((2,)),
            dma((6, n)),
            dma((6, n)),
            dma((5, n)),
            dma((5, n)),
            dma((5, 2 * n)),
            dma((5, 2 * n)),
            dma((5,)),
        ],
        compiler_params=pltpu.CompilerParams(
            vmem_limit_bytes=58 * 2**20, collective_id=0, has_side_effects=True
        ),
        cost_estimate=pl.CostEstimate(
            flops=8 * rows * row_len * q_width, bytes_accessed=40 * 2**20, transcendentals=0
        ),
    )(*operands)


def repeat(count, body):
    def step(i, carry):
        body(i)
        return carry

    lax.fori_loop(0, count, step, 0)


def add_into(to, more):
    step = 16

    def add(i):
        at = block_rows(i, step)
        to[at, :] = (to[at, :].astype(F32) + more[at, :].astype(F32)).astype(to.dtype)

    repeat(to.shape[0] // step, add)


def turn_blocks(place, source, turned):
    width = source.shape[1]
    n = place.n
    h = width // (n * place.ctx)
    first = lax.rem(place.c, 2) == 0

    def turn(i):
        chip = lax.rem(place.c // 2 + i // n, 2)
        pair = lax.rem(place.z - lax.rem(i, n) + n, n) * (place.ctx // 2) + chip
        block = source[:, block_rows(pair, 2 * h)].astype(F32).T.astype(turned.dtype)
        low, high = block[:h], block[h:]
        turned[block_rows(i, h), :] = jnp.where(first, low, high)
        turned[block_rows(i + 2 * n, h), :] = jnp.where(first, high, low)

    repeat(2 * n, turn)


class Scatter:
    def __init__(
        self, place, keep, columns, chip_land, line_land, number, sems, line_first=False
    ):
        x_send, x_recv, z_send, z_recv = sems
        n = place.n
        self.n, self.line_first = n, line_first
        self.h = h = keep.shape[0] // (2 * n)
        self.keep = [keep.at[pl.ds(k * h, h), columns] for k in range(2 * n)]
        land = [chip_land.at[pl.ds(k * h, h), columns] for k in range(n)]
        line = [line_land.at[k, :, columns] for k in range(n - 1)]
        there = place.at(c=place.flip(2))

        def ring(blocks, lands, row):
            return [
                remote(blocks[k], lands[k - 1], z_send.at[row, k], z_recv.at[row, k], place.up(1))
                for k in range(1, n)
            ]

        self.rings = [(ring(self.keep[:n], line, number), self.keep[:n], line)]
        if line_first:
            self.rings.append((ring(self.keep[n:], land[1:], number + 1), self.keep[n:], land[1:]))
            self.chip = remote(
                self.keep[n], land[0], x_send.at[number], x_recv.at[number], there
            )
            self.chip_land = land[:1]
        else:
            self.chip = remote(
                keep.at[pl.ds(n * h, n * h), columns],
                chip_land.at[:, columns],
                x_send.at[number],
                x_recv.at[number],
                there,
            )
            self.chip_land = land

    def to_chip(self):
        self.chip.start()

    def from_chip(self):
        self.chip.wait_recv()
        if self.line_first:
            return
        for k in list(range(1, self.n)) + [0]:
            add_into(self.keep[k], self.chip_land[k])
            if k == 1:
                self.begin()

    def begin(self):
        for ring, _, _ in self.rings:
            if ring:
                ring[0].start()

    def advance(self, k):
        if k >= self.n:
            return
        for ring, blocks, lands in self.rings:
            ring[k - 1].wait_recv()
            if k + 1 < self.n:
                add_into(blocks[k + 1], lands[k - 1])
                ring[k].start()
            elif self.line_first:
                add_into(blocks[0], lands[k - 1])

    def finish(self, out):
        last = self.chip_land[0] if self.line_first else self.rings[0][2][self.n - 2]
        step = 16

        def add(i):
            at = block_rows(i, step)
            out[at, :] = self.keep[0][at, :].astype(F32) + last[at, :].astype(F32)

        repeat(self.h // step, add)

    def drain(self):
        self.chip.wait_send()
        for ring, _, _ in self.rings:
            for copy in ring:
                copy.wait_send()


def core_sum(keep, core_land, copy):
    copy.wait_recv()
    add_into(keep, core_land)


def backward_kernel(
    n, ctx, tp, q_width, kv_width, stage_cols,
    ffn, dmid, qb, kv_all, heads, sums, w, cosines, sines, pick_t, gain, head_gain,
    start_row, gain_ffn_grad, squares, dy_in, x_in, mid_in, normed_two, hidden, d_gate, d_up,
    back_o, back_g, sum_gate, sum_up, sum_down, sum_out, sum_qkv, small,
    x, turned, stage, keep, send, core_land, chip_land, line_land,
    o_keep, o_send, o_core, o_chip, o_line, a_keep, a_send, a_core, a_chip, a_line,
    d_mid_own, d_attn, dob, delta, bias, dq_t, dkv, kv_land, tp_land, ffn_away, ffn_land, dx_away, dx_land,
    sent, small_mine, small_land, small_side,
    tp_send, tp_recv, route_send, route_recv, small_send, small_recv, kv_send, kv_recv, load_sem,
    free_sem, *scatter_sems
):
    place = Place(n, ctx, tp)
    group = n * ctx
    rows, width = dmid.shape
    feat = width // tp
    share = rows // group
    piece = rows
    ff = hidden.shape[1]
    half = width // 2
    n_pairs = q_width // 128
    qkv_width = q_width + 2 * kv_width
    values_from = q_width + kv_width
    x_bit, core_bit = place.c // 2, lax.rem(place.c, 2)
    own_cols = block_rows(place.t, feat)
    c_send, c_recv, *ring_sems = scatter_sems
    everything = pl.ds(0, ff)
    cut = ff // 256 * 128
    lands = lambda m: (chip_land.at[m], line_land.at[m])
    down = Scatter(place, keep.at[0], everything, *lands(0), 0, ring_sems)
    gate = Scatter(place, keep.at[1], everything, *lands(1), 1, ring_sems)
    up = Scatter(place, keep.at[2], pl.ds(0, cut), *lands(2), 2, ring_sems)
    up_ring = Scatter(place, keep.at[2], pl.ds(cut, ff - cut), *lands(2), 3, ring_sems, True)
    out_sum = Scatter(place, o_keep, pl.ds(0, q_width), o_chip, o_line, 5, ring_sems)
    qkv_sum = Scatter(place, a_keep, pl.ds(0, qkv_width), a_chip, a_line, 6, ring_sems)
    across_cores = [
        remote(src, dst, c_send.at[i], c_recv.at[i], place.at(c=place.flip(1)))
        for i, (src, dst) in enumerate(
            [(send.at[m % 2], core_land.at[m % 2]) for m in range(3)]
            + [(o_send, o_core), (a_send, a_core)]
        )
    ]

    def to_sides(number, src, dst):
        return [
            remote(
                src(j), dst.at[j - 1], tp_send.at[number, j], tp_recv.at[number, j], place.side(j)
            )
            for j in range(1, tp)
        ]

    def away(buffer):
        return lambda j: buffer.at[j - 1]

    def fill_away(buffer, source):
        for j in range(1, tp):
            buffer[j - 1] = source[:, block_rows(lax.rem(place.t + j, tp), feat)]

    def route(number, src, dst):
        return [
            remote(
                src.at[block_rows(lax.rem(place.me + j, group), share), :],
                dst.at[block_rows(place.me, share), :],
                route_send.at[number, j],
                route_recv.at[number, j],
                place.peer(j),
            )
            for j in range(1, group)
        ]

    dmid_sum = to_sides(0, lambda j: dmid, tp_land)
    ffn_sum = to_sides(1, away(ffn_away), ffn_land)
    dx_sum = to_sides(2, away(dx_away), dx_land)
    route_o, route_g = route(0, sent, back_o), route(1, sent, back_g)

    place.greet()
    for copy in dmid_sum:
        copy.start()

    sources = (hidden, d_gate, d_up)
    tiles = [(m, b) for m in range(3) for b in range(0, ff, stage_cols)]
    loads = [
        pltpu.make_async_copy(
            sources[m].at[:, pl.ds(b, stage_cols)], stage.at[i % 2], load_sem.at[i]
        )
        for i, (m, b) in enumerate(tiles)
    ]
    load_n = pltpu.make_async_copy(normed_two, d_attn, load_sem.at[len(tiles)])
    dy, mid = x, d_mid_own
    load_dy = pltpu.make_async_copy(dy_in, dy, load_sem.at[len(tiles) + 1])
    load_x = pltpu.make_async_copy(x_in, x, load_sem.at[len(tiles) + 2])
    load_mid = pltpu.make_async_copy(mid_in, mid, load_sem.at[len(tiles) + 3])
    load_dy.start()
    loads[0].start()
    load_n.start()
    load_mid.start()
    fill_away(ffn_away, ffn)
    load_dy.wait()
    turn_blocks(place, dy, turned)
    sub = 256 if stage_cols % 256 == 0 else 128
    for i, (m, b) in enumerate(tiles):
        if i + 1 < len(tiles):
            loads[i + 1].start()
        if b == 0 and m == 1:
            load_n.wait()
            turn_blocks(place, d_attn, turned)
        if m == 1 and b == ff // 2 // stage_cols * stage_cols:
            core_sum(keep.at[0], core_land.at[0], across_cores[0])
            down.to_chip()
            pl.semaphore_signal(
                free_sem, inc=1, device_id=place.at(c=place.flip(1)), device_id_type=MESH
            )
        if b == 0 and m == 2:
            across_cores[0].wait_send()
        loads[i].wait()
        for s in range(0, stage_cols, sub):
            right = stage[i % 2, :, s : s + sub]
            cols = slice(b + s, b + s + sub)
            keep[m, :, cols] = dot(turned[:half, :], right, 1, 0).astype(BF)
            send[m % 2, :, cols] = dot(turned[half:, :], right, 1, 0).astype(BF)
        if b + stage_cols == ff:
            if m == 2:
                pl.semaphore_wait(free_sem, 1)
            across_cores[m].start()
    core_sum(keep.at[1], core_land.at[1], across_cores[1])
    core_sum(keep.at[2], core_land.at[0], across_cores[2])
    up_ring.begin()

    for copy in dmid_sum:
        copy.wait_recv()
    for copy in ffn_sum:
        copy.start()

    def sum_gradient(i):
        r = block_rows(i, 128)
        d_all = dy[r, :].astype(F32) + dmid[r, :].astype(F32)
        for j in range(1, tp):
            d_all = d_all + tp_land[j - 1, r, :].astype(F32)
        d_attn[r, :] = d_all.astype(BF)

    repeat(rows // 128, sum_gradient)
    dob[...] = dot(d_attn[...], w[:, qkv_width:], 1, 0).astype(BF)
    dq_t[...] = jnp.zeros_like(dq_t)
    ones = jnp.ones((8, 128), F32)

    def set_delta(g):
        both = dob[:, lane_block(g)].astype(F32) * heads[:, lane_block(g)]
        delta[g] = dot(ones, two_heads(both), 1, 1, lax.Precision.HIGHEST)

    repeat(n_pairs, set_delta)
    q_slot = place.c * piece + lanes((piece, rows))

    def one_piece(p):
        k_slot = p * piece + lax.broadcasted_iota(jnp.int32, (piece, rows), 0)
        open_ = (k_slot >= start_row[...]) & (k_slot <= q_slot)
        bias[...] = jnp.where(open_, 0.0, NEG_FILL)
        at = block_rows(p, piece)
        def heads_of(members):
            grads = []
            for g, (kb, ke), (vb, ve) in members:
                q2 = two_heads(qb[:, lane_block(g)])
                do2 = two_heads(dob[:, lane_block(g)])
                k2 = twice(kv_all[at, lane_block(kb)], ke)
                v2 = twice(kv_all[at, lane_block(vb)], ve)
                k_t = k2.astype(F32).T.astype(BF)
                dk = jnp.zeros((piece, 128), F32)
                dv = jnp.zeros((piece, 128), F32)
                for h in range(0, 2 * rows, 256):
                    part = slice(h, h + 256)
                    open_part = slice(h % rows, h % rows + 256)
                    s = dot(k2, q2[part], 1, 1)
                    dp = dot(v2, do2[part], 1, 1)
                    pe = jnp.exp(s * 0.125 + bias[:, open_part]) * sums[g, 0:1, part]
                    ds = (pe * (dp - delta[g, 0:1, part])).astype(BF)
                    dv = dv + dot(pe.astype(BF), do2[part], 1, 0)
                    dk = dk + dot(ds, q2[part], 1, 0)
                    dq_t[g, :, part] += dot(k_t, ds, 1, 0)
                grads.append((both_halves(dk) * 0.125, both_halves(dv)))
            low = lanes((piece, 128)) < HEAD_SIZE
            kb, vb = members[0][1][0], members[0][2][0]
            if len(members) == 2:
                dkv[at, lane_block(kb)] = jnp.where(low, grads[0][0], grads[1][0]).astype(BF)
                dkv[at, lane_block(vb)] = jnp.where(low, grads[0][1], grads[1][1]).astype(BF)
            else:
                for value, (b, e) in zip(grads[0], members[0][1:]):
                    c = 128 * b + HEAD_SIZE * e
                    dkv[at, c : c + HEAD_SIZE] = value[:, :HEAD_SIZE].astype(BF)

        over_key_heads(n_pairs, kv_width // HEAD_SIZE, heads_of)

    sibling = place.at(c=place.flip(1))
    other = 1 - core_bit
    to_passer = remote(
        dkv.at[block_rows(other, piece), :], kv_land.at[0], kv_send.at[0], kv_recv.at[0], sibling
    )
    to_chip = remote(
        dkv.at[block_rows(core_bit, piece), :],
        kv_land.at[0],
        kv_send.at[1],
        kv_recv.at[1],
        place.at(c=place.flip(2)),
    )
    to_core = remote(
        dkv.at[block_rows(2 * x_bit, piece), :], kv_land.at[1], kv_send.at[2], kv_recv.at[2], sibling
    )

    @pl.when(x_bit == 1)
    def _():
        def step(p, carry):
            one_piece(p)
            return carry

        lax.fori_loop(0, 2, step, 0)
        to_passer.start()

    turn_blocks(place, d_attn, turned)
    right = heads[...].astype(BF)
    o_keep[...] = dot(turned[:half, :], right, 1, 0).astype(BF)
    o_send[...] = dot(turned[half:, :], right, 1, 0).astype(BF)
    across_cores[3].start()
    down.from_chip()
    gate.to_chip()
    up_ring.advance(1)

    @pl.when(x_bit == 1)
    def _():
        to_passer.wait_recv()
        mine = block_rows(core_bit, piece)
        dkv[mine, :] = (dkv[mine, :].astype(F32) + kv_land[0].astype(F32)).astype(BF)
        to_chip.start()

    core_sum(o_keep, o_core, across_cores[3])

    @pl.when(core_bit == 1)
    def _():
        one_piece(place.c - 1)
        to_core.start()

    for copy in ffn_sum:
        copy.wait_recv()
    small_mine[...] = jnp.zeros_like(small_mine)
    load_mid.wait()

    def finish_output(i):
        r = block_rows(i, 128)
        ffn_out = ffn[r, own_cols].astype(F32)
        for j in range(1, tp):
            ffn_out = ffn_out + ffn_land[j - 1, r, :].astype(F32)
        small_mine[5:6, :feat] += jnp.sum(ffn_out * ffn_out, axis=0, keepdims=True)
        dx_away[0, r, :] = (mid[r, :] + ffn_out).astype(BF)

    repeat(rows // 128, finish_output)
    sent[...] = dot(pick_t[...], dx_away[0], 1, 0).astype(BF)
    for copy in route_o:
        copy.start()
    own = block_rows(place.me, share)
    back_o[own, :] = sent[own, :]


    def own_gradient(i):
        r = block_rows(i, 128)
        d_own = dy[r, own_cols].astype(F32) + dmid[r, own_cols].astype(F32)
        for j in range(1, tp):
            d_own = d_own + tp_land[j - 1, r, own_cols].astype(F32)
        d_mid_own[r, :] = d_own

    repeat(rows // 128, own_gradient)
    load_x.start()
    down.advance(1)
    up_ring.advance(2)
    one_piece(place.c)
    down.advance(2)
    gate.from_chip()
    up.to_chip()
    out_sum.to_chip()
    up_ring.advance(3)
    up_ring.to_chip()
    normed = tp_land.at[0]
    load_x.wait()

    def norm_again(i):
        v = x[block_rows(i, 128), :].astype(F32)
        normed[block_rows(i, 128), :] = (v * row_scale(v) * gain[...]).astype(BF)

    repeat(rows // 128, norm_again)
    turn_blocks(place, normed, turned)
    mine = block_rows(place.c, piece)

    @pl.when(core_bit == 0)
    def _():
        to_core.wait_recv()

    @pl.when(x_bit == 0)
    def _():
        to_chip.wait_recv()

    d_qkv = d_attn.at[:, pl.ds(0, qkv_width)]
    for b in range(0, qkv_width, 128):
        if b < q_width:
            g = b // 128
            grad = one_row(dq_t[g].T) * 0.125
        else:
            cols = slice(b - q_width, b - q_width + 128)
            grad = dkv[mine, cols].astype(F32)
            grad = jnp.where(x_bit == 0, grad + kv_land[0, :, cols].astype(F32), grad)
            grad = jnp.where(core_bit == 0, grad + kv_land[1, :, cols].astype(F32), grad)
        raw = dot(normed[...], w[:, b : b + 128], 1, 0)
        is_value = lanes(grad.shape) + b >= values_from
        back, gain_grad = qk_backward(
            grad, raw, head_gain[:, b : b + 128], cosines[...], sines[...], is_value
        )
        small_mine[2:3, b : b + 128] = gain_grad
        d_qkv[:, b : b + 128] = back.astype(BF)

    def finish_gradient(i):
        r = block_rows(i, 128)
        dn = dot(d_qkv[r, :], w[:, :qkv_width], 1, 1)
        dx, gain_grad = norm_back(dn, x[r, :].astype(F32), gain[...])
        normed[r, :] = dx.astype(BF)
        small_mine[0:1, :] += gain_grad

    repeat(rows // 128, finish_gradient)
    fill_away(dx_away, normed)
    for copy in dx_sum:
        copy.start()
    small_mine[1:2, :] = gain_ffn_grad[...]
    small_mine[3:5, :] = squares[...]
    for b in range(0, qkv_width, 256):
        cols = slice(b, b + 256)
        a_keep[:, cols] = dot(turned[:half, :], d_qkv[:, cols], 1, 0).astype(BF)
        a_send[:, cols] = dot(turned[half:, :], d_qkv[:, cols], 1, 0).astype(BF)
    across_cores[4].start()
    down.advance(3)
    small_out = [
        remote(
            small_mine, small_land.at[place.me], small_send.at[0, j], small_recv.at[0, j], place.peer(j)
        )
        for j in range(1, group)
    ]
    for copy in small_out:
        copy.start()
    small_land[place.me] = small_mine[...]
    core_sum(a_keep, a_core, across_cores[4])
    qkv_sum.to_chip()
    gate.advance(1)
    up.from_chip()
    out_sum.from_chip()

    for copy in dx_sum:
        copy.wait_recv()
    for copy in ffn_sum:
        copy.wait_send()

    def finish_input(i):
        r = block_rows(i, 128)
        total = d_mid_own[r, :] + normed[r, own_cols].astype(F32)
        for j in range(1, tp):
            total = total + dx_land[j - 1, r, :].astype(F32)
        ffn_away[0, r, :] = total.astype(BF)

    repeat(rows // 128, finish_input)
    for copy in route_o:
        copy.wait_send()
    sent[...] = dot(pick_t[...], ffn_away[0], 1, 0).astype(BF)
    for copy in route_g:
        copy.start()
    back_g[own, :] = sent[own, :]
    gate.advance(2)
    up.advance(1)
    out_sum.advance(1)
    qkv_sum.from_chip()
    gate.advance(3)
    up.advance(2)
    out_sum.advance(2)
    qkv_sum.advance(1)
    down.finish(sum_down)
    gate.finish(sum_gate)
    up_ring.from_chip()
    up_ring.finish(sum_up.at[:, pl.ds(cut, ff - cut)])
    up.advance(3)
    out_sum.advance(3)
    qkv_sum.advance(2)
    for copy in small_out:
        copy.wait_recv()
    total = small_land[0]
    for i in range(1, group):
        total = total + small_land[i]
    small_side[place.t] = total
    for copy in small_out:
        copy.wait_send()
    small_mine[...] = total
    sides = [
        remote(
            small_mine, small_side.at[place.t], small_send.at[1, j], small_recv.at[1, j], place.side(j)
        )
        for j in range(1, tp)
    ]
    for copy in sides:
        copy.start()
    up.finish(sum_up.at[:, pl.ds(0, cut)])
    out_sum.finish(sum_out)
    for copy in sides:
        copy.wait_recv()
    total = small_side[0]
    for j in range(1, tp):
        total = total + small_side[j]
    small[...] = total
    for copy in route_o + route_g:
        copy.wait_recv()
    qkv_sum.advance(3)
    qkv_sum.finish(sum_qkv)

    @pl.when(x_bit == 1)
    def _():
        to_passer.wait_send()
        to_chip.wait_send()

    @pl.when(core_bit == 1)
    def _():
        to_core.wait_send()

    for copy in dmid_sum + dx_sum + route_g + sides:
        copy.wait_send()
    for copy in across_cores[1:]:
        copy.wait_send()
    for s in (down, gate, up, up_ring, out_sum, qkv_sum):
        s.drain()


def backward_pass(grid, q_width, kv_width, *operands):
    dmid, hidden = operands[1], operands[19]
    rows, width = dmid.shape
    ff = hidden.shape[1]
    n, ctx, tp = grid.n, grid.ctx, grid.tp
    group = n * ctx
    feat = width // tp
    half = width // 2
    h = width // group
    n_pairs = q_width // 128
    qkv_width = q_width + 2 * kv_width
    stage_cols = 256 if ff % 256 == 0 else 128
    vm = pl.BlockSpec(memory_space=pltpu.VMEM)
    dma = pltpu.SemaphoreType.DMA
    V = pltpu.VMEM

    def scatter_space(cols):
        return [
            V((half, cols), BF),
            V((half, cols), BF),
            V((half, cols), BF),
            V((half // 2, cols), BF),
            V((n - 1, h, cols), BF),
        ]

    return pl.pallas_call(
        functools.partial(backward_kernel, n, ctx, tp, q_width, kv_width, stage_cols),
        in_specs=[vm] * 15 + [ANYWHERE] * 7,
        out_specs=[vm] * 8,
        out_shape=[
            shape((rows, feat), BF),
            shape((rows, feat), BF),
            shape((h, ff), F32),
            shape((h, ff), F32),
            shape((h, ff), F32),
            shape((h, q_width), F32),
            shape((h, qkv_width), F32),
            shape((8, width), F32),
        ],
        scratch_shapes=[
            V((rows, width), BF),
            V((width, rows), BF),
            V((2, rows, stage_cols), BF),
            V((3, half, ff), BF),
            V((2, half, ff), BF),
            V((2, half, ff), BF),
            V((3, half // 2, ff), BF),
            V((3, n - 1, h, ff), BF),
        ]
        + scatter_space(q_width)
        + scatter_space(qkv_width)
        + [
            V((rows, feat), F32),
            V((rows, width), BF),
            V((rows, q_width), BF),
            V((n_pairs, 8, 2 * rows), F32),
            V((rows, rows), F32),
            V((n_pairs, 128, 2 * rows), F32),
            V((rows * ctx, 2 * kv_width), BF),
            V((2, rows, 2 * kv_width), BF),
            V((tp - 1, rows, width), BF),
            V((tp - 1, rows, feat), BF),
            V((tp - 1, rows, feat), BF),
            V((tp - 1, rows, feat), BF),
            V((tp - 1, rows, feat), BF),
            V((rows, feat), BF),
            V((8, width), F32),
            V((group, 8, width), F32),
            V((tp, 8, width), F32),
            dma((3, tp)),
            dma((3, tp)),
            dma((2, group)),
            dma((2, group)),
            dma((2, max(group, tp))),
            dma((2, max(group, tp))),
            dma((3,)),
            dma((3,)),
            dma((3 * (ff // stage_cols) + 4,)),
            pltpu.SemaphoreType.REGULAR,
            dma((5,)),
            dma((5,)),
            dma((7,)),
            dma((7,)),
            dma((7, n)),
            dma((7, n)),
        ],
        compiler_params=pltpu.CompilerParams(
            vmem_limit_bytes=61 * 2**20, collective_id=1, has_side_effects=True
        ),
        cost_estimate=pl.CostEstimate(
            flops=20 * rows * rows * ctx * q_width, bytes_accessed=40 * 2**20, transcendentals=0
        ),
    )(*operands)


def shape(s, t):
    return jax.ShapeDtypeStruct(s, t)


VMEM_LIMIT = pltpu.CompilerParams(vmem_limit_bytes=58 * 2**20)
ANYWHERE = pl.BlockSpec(memory_space=pl.ANY)


def ffn_pass(mid, dy, gain, w_ffn):
    rows, width = mid.shape
    ff = w_ffn.shape[1] // 3
    tile = 256 if ff % 256 == 0 else 128
    steps = ff // tile
    whole = lambda shape: pl.BlockSpec(shape, lambda s: (0, 0))
    column = pl.BlockSpec((rows, tile), lambda s: (0, s))
    weight = lambda i: pl.BlockSpec((width, tile), lambda s: (0, i * steps + s))
    return pl.pallas_call(
        ffn_kernel,
        grid=(steps,),
        in_specs=[whole((rows, width))] * 2 + [whole((1, width))] + [weight(i) for i in range(3)],
        out_specs=[whole((rows, width))] * 2
        + [whole((1, width)), whole((rows, width))]
        + [column] * 3,
        scratch_shapes=[pltpu.VMEM((rows, width), F32), pltpu.VMEM((rows, width), F32)],
        out_shape=[shape((rows, width), BF)] * 2
        + [shape((1, width), F32), shape((rows, width), BF)]
        + [shape((rows, ff), BF)] * 3,
        compiler_params=VMEM_LIMIT,
        cost_estimate=pl.CostEstimate(
            flops=12 * rows * width * ff, bytes_accessed=6 * width * ff, transcendentals=rows * ff
        ),
    )(mid, dy, gain, w_ffn, w_ffn, w_ffn)


def pad_columns(v, to):
    return v if v.shape[1] == to else jnp.pad(v, ((0, 0), (0, to - v.shape[1])))


def one_hot(rows, columns):
    return (rows == columns).astype(BF)


def local(
    tokens,
    cotangent,
    slot_of,
    lengths,
    w_query,
    key_weight,
    value_weight,
    w_out,
    w_gate,
    w_up,
    w_down,
    gain_attn,
    gain_ffn,
    gain_query,
    gain_key,
):
    grid = Grid()
    stream_len = tokens.shape[0]
    feat_len = tokens.shape[1]
    local_len = PACKED_ROW_SLOTS // grid.ctx
    row_count = stream_len // local_len
    groups = grid.n * grid.ctx
    share = stream_len // groups
    q_heads = QUERY_HEADS // grid.tp
    key_value_heads = KEY_VALUE_HEADS // grid.tp
    query_group_width = QUERY_HEADS // KEY_VALUE_HEADS
    q_width = q_heads * HEAD_SIZE
    kv_width = key_value_heads * HEAD_SIZE
    flat_len = row_count * local_len
    row_len = PACKED_ROW_SLOTS
    me = grid.z * grid.ctx + grid.c
    both = ("fsdp", "ctx")

    def home(slots):
        row, place = slots // row_len, slots % row_len
        return (
            row // row_count * grid.ctx + place // local_len,
            row % row_count * local_len + place % local_len,
        )

    my_slots = lax.dynamic_slice_in_dim(slot_of, me * stream_len, stream_len, 0)
    my_target = home(my_slots)[0]
    ahead = (my_target[:, None] == my_target[None, :]) & (my_slots[None, :] < my_slots[:, None])
    send_place = my_target * share + jnp.sum(ahead.astype(jnp.int32), axis=1)
    line = jnp.arange(stream_len, dtype=jnp.int32)
    send_pick = one_hot(line[:, None], send_place[None, :])
    all_dev, all_local = home(slot_of)
    low = 32
    high = flat_len // low
    sender = (jnp.arange(slot_of.shape[0], dtype=jnp.int32) // stream_len).astype(F32)
    mine = (all_dev == me)[None, :] & (
        (all_local // low)[None, :] == jnp.arange(high, dtype=jnp.int32)[:, None]
    )
    left = jnp.where(mine, sender[None, :], 0.0).astype(BF)
    right = one_hot((all_local % low)[:, None], jnp.arange(low, dtype=jnp.int32)[None, :])
    source = product(left, right, "ht,tl->hl").reshape(flat_len).astype(jnp.int32)
    slot_line = jnp.arange(flat_len, dtype=jnp.int32)
    before = (source[:, None] == source[None, :]) & (slot_line[None, :] < slot_line[:, None])
    arrival = source * share + jnp.sum(before.astype(jnp.int32), axis=1)
    take_pick = one_hot(arrival[:, None], line[None, :])

    def sent_order(v):
        return product(send_pick, v, "pt,tf->pf").astype(BF)

    take_back = one_hot(line[:, None], arrival[None, :])
    send_back = one_hot(send_place[:, None], line[None, :])

    ff = w_gate.shape[1]
    ff_pad = -(-ff // 128) * 128
    attn_shard = jnp.concatenate([w_query, key_weight, value_weight, w_out.T], axis=1)
    ffn_shard = jnp.concatenate(
        [pad_columns(v, ff_pad) for v in (w_gate, w_up, w_down.T)], axis=1
    )
    own_slots = grid.c * local_len + jnp.arange(local_len, dtype=jnp.int32)
    position = slot_tables(lengths[0], own_slots)[1]
    start = own_slots - position
    frequency = ROPE_THETA ** (-jnp.arange(0, HEAD_SIZE, 2).astype(F32) / HEAD_SIZE)
    angles = position.astype(F32)[:, None] * frequency[None, :]
    cosines = jnp.tile(jnp.cos(angles), (1, 4))
    sin = jnp.sin(angles)
    sines = jnp.tile(jnp.concatenate([-sin, sin], axis=1), (1, 2))
    head_gain = jnp.concatenate(
        [
            jnp.tile(gain_query, q_heads),
            jnp.tile(gain_key, key_value_heads),
            jnp.ones((kv_width,), F32),
        ]
    )[None, :]
    x_full, dy_full, qb, row_kv, heads, sums, middle, squares, attn_w, ffn_w = forward_pass(
        grid,
        q_width,
        kv_width,
        ff_pad,
        sent_order(tokens),
        sent_order(cotangent),
        take_pick,
        gain_attn[None, :],
        head_gain,
        cosines,
        sines,
        start[:, None],
        attn_shard,
        ffn_shard,
    )
    own_features = lambda v: lax.dynamic_slice_in_dim(v, grid.t * feat_len, feat_len, 1)
    middle_own = own_features(middle)
    ffn_part, d_mid_part, d_gain_ffn, normed_two, hidden, d_gate, d_up = ffn_pass(
        middle, dy_full, gain_ffn[None, :], ffn_w
    )
    back_o, back_g, sum_gate, sum_up, sum_down, sum_out, sum_qkv, small = backward_pass(
        grid,
        q_width,
        kv_width,
        ffn_part,
        d_mid_part,
        qb,
        row_kv,
        heads,
        sums,
        attn_w,
        cosines,
        sines,
        take_back,
        gain_attn[None, :],
        head_gain,
        start[None, :],
        d_gain_ffn,
        squares,
        dy_full,
        x_full,
        middle_own,
        normed_two,
        hidden,
        d_gate,
        d_up,
    )
    a, b = q_width, q_width + kv_width
    per_head = small[2, : b + kv_width].reshape(-1, HEAD_SIZE)
    entry_count = flat_len * groups * MODEL_WIDTH
    square_sums = jnp.sum(small[3:6], axis=1) / jnp.stack([grid.tp, grid.tp, 1]).astype(F32)

    def bring_back(v):
        return product(send_back, v, "tp,pf->tf").astype(BF)

    return (
        bring_back(back_o),
        bring_back(back_g),
        sum_qkv[:, :a],
        sum_qkv[:, a:b],
        sum_qkv[:, b:],
        sum_out.T,
        sum_gate[:, :ff],
        sum_up[:, :ff],
        sum_down[:, :ff].T,
        small[0],
        small[1],
        jnp.sum(per_head[:q_heads], axis=0),
        jnp.sum(per_head[q_heads : q_heads + key_value_heads], axis=0),
        jnp.sqrt(square_sums / entry_count),
    )


def solution(mesh):
    row = P(("fsdp", "ctx"), "tp")
    column = P("tp", ("fsdp", "ctx"))
    in_specs = (row, row, P(), P("fsdp", None), row, row, row, column, row, row, column) + (P(),) * 4
    out_specs = (row, row, row, row, row, column, row, row, column) + (P(),) * 5
    return jax.shard_map(local, mesh=mesh, in_specs=in_specs, out_specs=out_specs, check_vma=False)
```

```python
import functools

import jax
import jax.numpy as jnp
import numpy as np
from jax import lax
from jax.experimental import pallas as pl
from jax.experimental.pallas import tpu as pltpu
from jax.sharding import PartitionSpec as P

MODEL_WIDTH = 1024
QUERY_HEADS = 16
KEY_VALUE_HEADS = 8
HEAD_SIZE = 64

EPSILON = 1e-05
ROPE_THETA = 1000000.0
NEG_FILL = -1e30
BF = jnp.bfloat16
F32 = jnp.float32


class Grid:
    def __init__(self):
        self.n = lax.axis_size("fsdp")
        self.ctx = lax.axis_size("ctx")
        self.tp = lax.axis_size("tp")
        self.z = lax.axis_index("fsdp")
        self.c = lax.axis_index("ctx")
        self.t = lax.axis_index("tp")


def shape(s, t):
    return jax.ShapeDtypeStruct(s, t)


ANYWHERE = pl.BlockSpec(memory_space=pl.ANY)


def dot(a, b, ca, cb, precision=None):
    return lax.dot_general(
        a, b, (((ca,), (cb,)), ((), ())), preferred_element_type=F32, precision=precision
    )


def lanes(shape):
    return lax.broadcasted_iota(jnp.int32, shape, 1)


def half_mean(v):
    low = lanes(v.shape) < HEAD_SIZE
    first = jnp.sum(jnp.where(low, v, 0.0), axis=1, keepdims=True)
    second = jnp.sum(jnp.where(low, 0.0, v), axis=1, keepdims=True)
    return jnp.where(low, first, second) * (1.0 / HEAD_SIZE)


def half_swap(v):
    quarter = HEAD_SIZE // 2
    left = pltpu.roll(v, 128 - quarter, 1)
    right = pltpu.roll(v, quarter, 1)
    return jnp.where(lanes(v.shape) % HEAD_SIZE < quarter, left, right)


def row_scale(v):
    return lax.rsqrt(jnp.mean(v * v, axis=1, keepdims=True) + EPSILON)


def norm_back(dn, v, gain):
    scale = row_scale(v)
    unit = v * scale
    scaled = dn * gain
    grad = scale * (scaled - unit * jnp.mean(scaled * unit, axis=1, keepdims=True))
    return grad, jnp.sum(dn * unit, axis=0, keepdims=True)


def qk_forward(raw, gain, cosines, sines, is_value):
    normed = raw * lax.rsqrt(half_mean(raw * raw) + EPSILON) * gain
    turned = normed * cosines + half_swap(normed) * sines
    return jnp.where(is_value, raw, turned)


def qk_backward(grad, raw, gain, cosines, sines, is_value):
    straight = grad * cosines - half_swap(grad) * sines
    scale = lax.rsqrt(half_mean(raw * raw) + EPSILON)
    unit = raw * scale
    scaled = straight * gain
    back = scale * (scaled - unit * half_mean(scaled * unit))
    gain_grad = jnp.sum(straight * unit, axis=0, keepdims=True)
    return jnp.where(is_value, grad, back), gain_grad


def two_heads(v):
    low = lanes(v.shape) < HEAD_SIZE
    zero = jnp.zeros_like(v)
    return jnp.concatenate([jnp.where(low, v, zero), jnp.where(low, zero, v)], axis=0)


def one_row(v):
    rows = v.shape[0] // 2
    return jnp.where(lanes((rows, v.shape[1])) < HEAD_SIZE, v[:rows], v[rows:])


def twice(v, which):
    half = v[:, which * HEAD_SIZE : (which + 1) * HEAD_SIZE]
    return jnp.concatenate([half, half], axis=1)


def both_halves(v):
    return v + jnp.concatenate([v[:, HEAD_SIZE:], v[:, :HEAD_SIZE]], axis=1)


def over_key_heads(n_heads, values_from, body):
    if n_heads % 2:
        for g in range(n_heads):
            body([(g, (g // 2, g % 2), ((values_from + g) // 2, (values_from + g) % 2))])
        return

    def step(i, carry):
        body([(2 * i + e, (i, e), (values_from // 2 + i, e)) for e in range(2)])
        return carry

    lax.fori_loop(0, n_heads // 2, step, 0)


def lane_block(i):
    return block_rows(i, 128)


def segment_start(lengths, slots):
    end = lengths[0, 0]
    start = jnp.where(slots >= end, end, 0)
    for i in range(1, lengths.shape[1] - 1):
        end = end + lengths[0, i]
        start = jnp.where(slots >= end, end, start)
    return start


def sublanes(shape):
    return lax.broadcasted_iota(jnp.int32, shape, 0)


def count(mask, axis):
    return jnp.sum(mask.astype(F32), axis=axis, keepdims=True).astype(jnp.int32)


def routing(place, slots, rows, share):
    groups = slots.shape[0]
    square = (rows, rows)
    row = slots[pl.ds(place.me, 1), :]
    column = jnp.broadcast_to(row.astype(F32), (128, rows)).T[:, :1].astype(jnp.int32)
    base = row // rows * rows
    rank = count((column < row) & (column >= base), 0)
    sent_row = row // rows * share + rank
    base = column // rows * rows
    rank = count((row < column) & (row >= base), 1)
    sent_column = column // rows * share + rank
    low = 32
    high = rows // low
    table = jnp.zeros((high, low), F32)
    for s in range(groups):
        r = slots[s : s + 1, :]
        left = (r // low - place.me * high) == sublanes((high, rows))
        right = r % low == sublanes((low, rows))
        table = table + dot(left.astype(BF), right.astype(BF), 1, 1) * float(s)
    spread = (lanes((low, rows)) % low == sublanes((low, rows))).astype(F32)
    pick = lanes((high, rows)) // low == sublanes((high, rows))
    from_row = jnp.sum(jnp.where(pick, dot(table, spread, 1, 0), 0.0), axis=0, keepdims=True)
    spread = (sublanes((rows, low)) % low == lanes((rows, low))).astype(F32)
    pick = sublanes((rows, high)) // low == lanes((rows, high))
    from_column = jnp.sum(jnp.where(pick, dot(spread, table, 1, 1), 0.0), axis=1, keepdims=True)
    from_row, from_column = from_row.astype(jnp.int32), from_column.astype(jnp.int32)
    same = from_row == from_column
    got_column = from_column * share + count(same & (lanes(square) < sublanes(square)), 1)
    got_row = from_row * share + count(same & (sublanes(square) < lanes(square)), 0)
    return sent_row, sent_column, got_row, got_column


class Place:
    def __init__(self, n, ctx, tp):
        self.n, self.ctx, self.tp = n, ctx, tp
        self.z = lax.axis_index("fsdp")
        self.c = lax.axis_index("ctx")
        self.t = lax.axis_index("tp")
        self.me = self.z * ctx + self.c

    def at(self, z=None, c=None, t=None):
        return (
            self.z if z is None else z,
            self.c if c is None else c,
            self.t if t is None else t,
        )

    def peer(self, j):
        p = lax.rem(self.me + j, self.n * self.ctx)
        return self.at(p // self.ctx, lax.rem(p, self.ctx))

    def up(self, j):
        return self.at(z=lax.rem(self.z + j, self.n))

    def flip(self, bit):
        if bit == 1:
            return self.c + 1 - 2 * lax.rem(self.c, 2)
        return lax.rem(self.c + 2, 4)

    def side(self, j):
        return self.at(t=lax.rem(self.t + j, self.tp))

    def owner(self, k, c):
        return lax.rem(self.z - k + self.n, self.n) * self.ctx + c

    def greet(self):
        barrier = pltpu.get_barrier_semaphore()
        group = self.n * self.ctx
        for j in range(1, group):
            pl.semaphore_signal(barrier, inc=1, device_id=self.peer(j), device_id_type=MESH)
        for j in range(1, self.tp):
            pl.semaphore_signal(barrier, inc=1, device_id=self.side(j), device_id_type=MESH)
        pl.semaphore_wait(barrier, group + self.tp - 2)


MESH = pl.DeviceIdType.MESH


def remote(src, dst, send, recv, device):
    return pltpu.make_async_remote_copy(
        src_ref=src, dst_ref=dst, send_sem=send, recv_sem=recv, device_id=device, device_id_type=MESH
    )


def block_rows(index, size):
    return pl.ds(pl.multiple_of(index * size, size), size)


class Gather:
    def __init__(self, place, shard, whole, columns, number, sems, chip_first=False):
        z_send, z_recv, x_send, x_recv, c_send, c_recv, own = sems
        h = shard.shape[0]
        n = place.n
        self.n, self.chip_first = n, chip_first
        view = lambda index: whole.at[block_rows(index, h), columns]
        here, there = place.c, place.flip(2)
        mine = shard.at[:, columns]
        self.own = pltpu.make_async_copy(mine, view(place.me), own.at[number])

        def ring(lane, row):
            return [
                remote(
                    mine if k == 1 and row == number else view(place.owner(k - 1, lane)),
                    view(place.owner(k - 1, lane)),
                    z_send.at[row, k],
                    z_recv.at[row, k],
                    place.up(1),
                )
                for k in range(1, n)
            ]

        self.rings = [ring(here, number)] + ([ring(there, number + 1)] if chip_first else [])
        self.chip = [
            remote(
                mine if k == 0 else view(place.owner(k, here)),
                view(place.owner(k, here)),
                x_send.at[number, k],
                x_recv.at[number, k],
                place.at(c=there),
            )
            for k in range(1 if chip_first else n)
        ]
        self.core = [
            remote(
                mine if i == 0 else view(place.owner(i % n, here if i < n else there)),
                view(place.owner(i % n, here if i < n else there)),
                c_send.at[number, i],
                c_recv.at[number, i],
                place.at(c=place.flip(1)),
            )
            for i in range(2 * n)
        ]

    def begin(self):
        if self.n > 1:
            self.rings[0][0].start()
        self.own.start()
        self.core[0].start()

    def begin_other(self):
        if self.n > 1:
            self.rings[1][0].start()

    def advance(self, k):
        if k >= self.n:
            return
        for r, ring in enumerate(self.rings):
            ring[k - 1].wait_recv()
            if k + 1 < self.n:
                ring[k].start()
            self.core[r * self.n + k].start()

    def to_chip(self, k):
        if k < len(self.chip):
            self.chip[k].start()

    def from_chip(self, k):
        if k < len(self.chip):
            self.chip[k].wait_recv()
            self.core[self.n + k].start()

    def finish(self):
        for copy in self.core:
            copy.wait_recv()
        self.own.wait()

    def drain(self):
        for copy in sum(self.rings, []) + self.chip + self.core:
            copy.wait_send()


def forward_kernel(
    n, ctx, tp, q_width, kv_width, tile,
    lengths, tokens, cotangent, slots, gain, head_gain, gain_ffn, frequency, attn_shard, ffn_shard,
    sums, squares, ffn_out, dmid, dgain, take_back, send_back, cosines, sines,
    x, dy, qb_out, kv, heads_out, mid_own, w_attn, normed_two, hidden, d_gate, d_up,
    sent_x, sent_y, got_x, got_y, own_x, own_y, x_land, y_land, pick, qb, heads, mid, nb,
    w, w_ffn, kv_all, part, land, acc, total, bias, ffn_acc, dn_acc, acts,
    route_send, route_recv, tp_send, tp_recv, kv_send, kv_recv, out_sem, act_sem, *gather_sems
):
    place = Place(n, ctx, tp)
    group = n * ctx
    rows = got_x.shape[0]
    share = rows // group
    feat = got_x.shape[1]
    width = x_land.shape[1]
    piece = rows
    every = pl.ds(0, attn_shard.shape[1])
    attn = Gather(place, attn_shard, w, every, 0, gather_sems)
    tiles = ffn_shard.shape[1] // (3 * tile)
    last = max(1, tiles * 2 // 9)
    cuts = [(tiles - last) * i // 3 for i in range(3)] + [tiles - last, tiles]
    first, second, third, tail = (
        Gather(
            place,
            ffn_shard,
            w_ffn,
            pl.ds(cuts[i] * 3 * tile, (cuts[i + 1] - cuts[i]) * 3 * tile),
            1 + i,
            gather_sems,
            chip_first=i == 3,
        )
        for i in range(4)
    )
    groups = [first, second, third]
    stores = []

    def store(src, dst):
        copy = pltpu.make_async_copy(src, dst, out_sem.at[len(stores)])
        copy.start()
        stores.append(copy)

    def route(number, src, dst):
        return [
            remote(
                src.at[block_rows(lax.rem(place.me + j, group), share), :],
                dst.at[block_rows(place.me, share), :],
                route_send.at[number, j],
                route_recv.at[number, j],
                place.peer(j),
            )
            for j in range(1, group)
        ]

    def widen(number, src, dst):
        return [
            remote(
                src,
                dst.at[:, block_rows(place.t, feat)],
                tp_send.at[number, j],
                tp_recv.at[number, j],
                place.side(j),
            )
            for j in range(1, tp)
        ]

    def own_block(src, dst):
        at = block_rows(place.me, share)
        dst[at, :] = src[at, :]

    route_x, route_y = route(0, sent_x, got_x), route(1, sent_y, got_y)
    wide_x, wide_y = widen(0, own_x, x_land), widen(1, own_y, y_land)
    place.greet()
    attn.begin()
    attn.to_chip(0)
    sent_row, sent_column, got_row, got_column = routing(place, slots, rows, share)
    square = (rows, rows)
    send_pick = (sublanes(square) == sent_row).astype(BF)
    sent_x[...] = dot(send_pick, tokens[...], 1, 0).astype(BF)
    for copy in route_x:
        copy.start()
    own_block(sent_x, got_x)
    attn.advance(1)
    attn.to_chip(1)
    sent_y[...] = dot(send_pick, cotangent[...], 1, 0).astype(BF)
    own_block(sent_y, got_y)
    pick[...] = (lanes(square) == got_column).astype(BF)
    take_back[...] = (sublanes(square) == got_row).astype(BF)
    send_back[...] = (lanes(square) == sent_column).astype(BF)
    slot = place.c * piece + sublanes((rows, 128))
    start_col = segment_start(lengths, slot)
    angle = (slot - start_col).astype(F32) * frequency[...]
    start_col = start_col[:, :1]
    cosines[...] = jnp.cos(angle)
    turned_lane = lanes((rows, 128)) % HEAD_SIZE < HEAD_SIZE // 2
    sines[...] = jnp.where(turned_lane, -1.0, 1.0) * jnp.sin(angle)
    attn.from_chip(0)
    attn.advance(2)
    attn.to_chip(2)
    first.begin()
    for copy in route_x:
        copy.wait_recv()
    own_x[...] = dot(pick[...], got_x[...], 1, 0).astype(BF)
    for copy in wide_x:
        copy.start()
    x_land[:, block_rows(place.t, feat)] = own_x[...]
    attn.from_chip(1)
    attn.advance(3)
    attn.to_chip(3)
    for copy in route_y:
        copy.start()
    second.begin()
    first.to_chip(0)
    attn.from_chip(2)
    attn.from_chip(3)
    second.to_chip(0)
    for copy in wide_x:
        copy.wait_recv()
    store(x_land, x)
    v = x_land[...].astype(F32)
    normed = (v * row_scale(v) * gain[...]).astype(BF)
    attn.finish()
    store(w, w_attn)

    own_rows = block_rows(place.c, piece)
    values_from = q_width + kv_width
    for b in list(range(q_width, q_width + 2 * kv_width, 128)) + list(range(0, q_width, 128)):
        if b == 0:
            later = start_keys(place, kv_all, own_rows, kv_send, kv_recv)
        block = dot(normed, w[:, b : b + 128], 1, 0)
        is_value = lanes(block.shape) + b >= values_from
        done = qk_forward(block, head_gain[:, b : b + 128], cosines[...], sines[...], is_value)
        if b < q_width:
            qb[:, b : b + 128] = done.astype(BF)
        else:
            kv_all[own_rows, b - q_width : b - q_width + 128] = done.astype(BF)

    q_slot = place.c * piece + lax.broadcasted_iota(jnp.int32, (rows, piece), 0)
    n_pairs = q_width // 128

    def one_piece(p):
        k_slot = p * piece + lanes((rows, piece))
        open_ = (k_slot >= start_col) & (k_slot <= q_slot)
        bias[...] = jnp.where(open_, 0.0, NEG_FILL)
        at = block_rows(p, piece)

        def heads_of(members):
            for g, (kb, ke), (vb, ve) in members:
                q2 = two_heads(qb[:, lane_block(g)])
                k2 = twice(kv_all[at, lane_block(kb)], ke)
                v2 = twice(kv_all[at, lane_block(vb)], ve)
                for h in range(2):
                    part = slice(h * rows, (h + 1) * rows)
                    e = jnp.exp(dot(q2[part], k2, 1, 1) * 0.125 + bias[...])
                    part_sum = e[:, :128]
                    for b in range(128, piece, 128):
                        part_sum = part_sum + e[:, b : b + 128]
                    acc[g, part, :] += dot(e.astype(BF), v2, 1, 0)
                    total[g, part, :] += part_sum

        over_key_heads(n_pairs, kv_width // HEAD_SIZE, heads_of)

    acc[...] = jnp.zeros_like(acc)
    total[...] = jnp.zeros_like(total)
    one_piece(place.c)
    x_bit, core_bit = place.c // 2, lax.rem(place.c, 2)
    near, across, passed = later
    first.advance(1)
    second.advance(1)

    @pl.when(x_bit == 1)
    def _():
        across.wait_recv()
        passed.start()

    first.from_chip(0)
    second.from_chip(0)
    tail.to_chip(0)
    first.to_chip(1)
    for copy in route_y:
        copy.wait_recv()
    own_y[...] = dot(pick[...], got_y[...], 1, 0).astype(BF)
    for copy in wide_y:
        copy.start()
    y_land[:, block_rows(place.t, feat)] = own_y[...]

    @pl.when(core_bit == 1)
    def _():
        near.wait_recv()
        one_piece(place.c - 1)

    first.advance(2)
    second.advance(2)
    second.to_chip(1)

    @pl.when(x_bit == 1)
    def _():
        passed.wait_recv()

        def step(p, carry):
            one_piece(p)
            return carry

        lax.fori_loop(0, 2, step, 0)

    ones = jnp.ones((8, 128), F32)
    for g in range(n_pairs):
        row_total = jnp.sum(total[g], axis=1, keepdims=True)
        heads[:, 128 * g : 128 * g + 128] = one_row(acc[g] / row_total)
        sums[g] = 1.0 / dot(ones, total[g], 1, 1, lax.Precision.HIGHEST)
    part[...] = dot(heads[...].astype(BF), w[:, q_width + 2 * kv_width :], 1, 1).astype(BF)
    attention = [
        remote(part, land.at[j - 1], tp_send.at[2, j], tp_recv.at[2, j], place.side(j))
        for j in range(1, tp)
    ]
    for copy in attention:
        copy.start()
    store(qb, qb_out)
    store(heads, heads_out)
    first.from_chip(1)
    first.to_chip(2)
    first.advance(3)
    second.advance(3)
    third.begin()
    tail.from_chip(0)
    tail.begin()
    tail.begin_other()
    second.from_chip(1)
    second.to_chip(2)
    first.from_chip(2)
    first.to_chip(3)
    third.advance(1)
    second.from_chip(2)
    second.to_chip(3)
    third.to_chip(0)
    tail.advance(1)
    third.advance(2)
    first.from_chip(3)
    third.to_chip(1)
    for copy in attention:
        copy.wait_recv()
    att = part[...].astype(F32)
    for j in range(1, tp):
        att = att + land[j - 1].astype(F32)
    v = x_land[...].astype(F32)
    squares[0:1, :] = jnp.sum(v * v, axis=0, keepdims=True)
    squares[1:2, :] = jnp.sum(att * att, axis=0, keepdims=True)
    mid[...] = v + att
    store(mid.at[:, block_rows(place.t, feat)], mid_own)
    v = (v + att).astype(BF).astype(F32)
    nb[...] = (v * row_scale(v) * gain_ffn[...]).astype(BF)
    store(nb, normed_two)
    ffn_acc[...] = jnp.zeros_like(ffn_acc)
    dn_acc[...] = jnp.zeros_like(dn_acc)
    tail.advance(2)
    second.from_chip(3)
    third.to_chip(2)
    third.advance(3)
    third.from_chip(0)
    third.to_chip(3)
    for copy in wide_y:
        copy.wait_recv()
    store(y_land, dy)

    def one_tile(i):
        at = lambda m: block_rows(3 * i + m, tile)
        w_gate, w_up, w_down = w_ffn[:, at(0)], w_ffn[:, at(1)], w_ffn[:, at(2)]
        gate = dot(nb[...], w_gate, 1, 0)
        up = dot(nb[...], w_up, 1, 0)
        d_hidden = dot(y_land[...], w_down, 1, 0)
        sig = 1.0 / (1.0 + jnp.exp(-gate))
        silu = gate * sig
        out = block_rows(i, tile)
        acts[0, :, out] = (silu * up).astype(BF)
        acts[1, :, out] = (d_hidden * up * (sig * (1.0 + gate * (1.0 - sig)))).astype(BF)
        acts[2, :, out] = (d_hidden * silu).astype(BF)
        ffn_acc[...] += dot(acts[0, :, out], w_down, 1, 1)
        dn_acc[...] += dot(acts[1, :, out], w_gate, 1, 1) + dot(acts[2, :, out], w_up, 1, 1)

    act_stores = []
    for i, g in enumerate(groups + [tail]):
        if i == 1:
            tail.advance(3)
            third.from_chip(1)
        if i == 2:
            third.from_chip(2)
            third.from_chip(3)
        g.finish()
        repeat(cuts[i + 1] - cuts[i], lambda k, i=i: one_tile(cuts[i] + k))
        cols = pl.ds(cuts[i] * tile, (cuts[i + 1] - cuts[i]) * tile)
        for m, out in enumerate((hidden, d_gate, d_up)):
            copy = pltpu.make_async_copy(acts.at[m, :, cols], out.at[:, cols], act_sem.at[m, i])
            copy.start()
            act_stores.append(copy)
    dgain[...] = jnp.zeros_like(dgain)

    def finish_rows(i):
        r = block_rows(i, 128)
        v = mid[r, :].astype(BF).astype(F32)
        grad, gain_sum = norm_back(dn_acc[r, :], v, gain_ffn[...])
        dgain[...] += gain_sum
        dmid[r, :] = grad.astype(BF)
        ffn_out[r, :] = ffn_acc[r, :].astype(BF)

    repeat(rows // 128, finish_rows)

    @pl.when(core_bit == 0)
    def _():
        near.wait_send()

    @pl.when(x_bit == 0)
    def _():
        across.wait_send()

    @pl.when(x_bit == 1)
    def _():
        passed.wait_send()

    store(kv_all, kv)
    for copy in route_x + route_y + wide_x + wide_y + attention:
        copy.wait_send()
    for g in [attn, tail] + groups:
        g.drain()
    for copy in stores + act_stores:
        copy.wait()


def start_keys(place, kv_all, own_rows, send, recv):
    x_bit, core_bit = place.c // 2, lax.rem(place.c, 2)
    mine = kv_all.at[own_rows, :]
    near = remote(mine, mine, send.at[0], recv.at[0], place.at(c=place.flip(1)))
    across = remote(mine, mine, send.at[1], recv.at[1], place.at(c=place.flip(2)))
    from_chip = kv_all.at[block_rows(place.flip(2), own_rows.size), :]
    passed = remote(from_chip, from_chip, send.at[2], recv.at[2], place.at(c=place.flip(1)))

    @pl.when(x_bit == 0)
    def _():
        across.start()

    @pl.when(core_bit == 0)
    def _():
        near.start()

    return near, across, passed


def forward_pass(grid, q_width, kv_width, tile, *operands):
    tokens, attn_shard, ffn_shard = operands[1], operands[8], operands[9]
    rows, feat = tokens.shape
    n, ctx, tp = grid.n, grid.ctx, grid.tp
    width = feat * tp
    n_pairs = q_width // 128
    row_len = rows * ctx
    ff = ffn_shard.shape[1] // 3
    vm = pl.BlockSpec(memory_space=pltpu.VMEM)
    dma = pltpu.SemaphoreType.DMA
    V = pltpu.VMEM
    group = n * ctx
    attn_width = attn_shard.shape[1]
    return pl.pallas_call(
        functools.partial(forward_kernel, n, ctx, tp, q_width, kv_width, tile),
        in_specs=[pl.BlockSpec(memory_space=pltpu.SMEM)] + [vm] * 7 + [ANYWHERE] * 2,
        out_specs=[vm] * 9 + [ANYWHERE] * 11,
        out_shape=[
            shape((n_pairs, 8, 2 * rows), F32),
            shape((2, width), F32),
            shape((rows, width), BF),
            shape((rows, width), BF),
            shape((1, width), F32),
            shape((rows, rows), BF),
            shape((rows, rows), BF),
            shape((rows, 128), F32),
            shape((rows, 128), F32),
            shape((rows, width), BF),
            shape((rows, width), BF),
            shape((rows, q_width), BF),
            shape((row_len, 2 * kv_width), BF),
            shape((rows, q_width), F32),
            shape((rows, feat), F32),
            shape((width, attn_width), BF),
            shape((rows, width), BF),
            shape((rows, ff), BF),
            shape((rows, ff), BF),
            shape((rows, ff), BF),
        ],
        scratch_shapes=[V((rows, feat), BF)] * 6
        + [
            V((rows, width), BF),
            V((rows, width), BF),
            V((rows, rows), BF),
            V((rows, q_width), BF),
            V((rows, q_width), F32),
            V((rows, width), F32),
            V((rows, width), BF),
            V((width, attn_width), BF),
            V((width, 3 * ff), BF),
            V((row_len, 2 * kv_width), BF),
            V((rows, width), BF),
            V((tp - 1, rows, width), BF),
            V((n_pairs, 2 * rows, 128), F32),
            V((n_pairs, 2 * rows, 128), F32),
            V((rows, rows), F32),
            V((rows, width), F32),
            V((rows, width), F32),
            V((3, rows, ff), BF),
            dma((2, group)),
            dma((2, group)),
            dma((3, tp)),
            dma((3, tp)),
            dma((3,)),
            dma((3,)),
            dma((8,)),
            dma((3, 4)),
            dma((6, n)),
            dma((6, n)),
            dma((5, n)),
            dma((5, n)),
            dma((5, 2 * n)),
            dma((5, 2 * n)),
            dma((5,)),
        ],
        compiler_params=pltpu.CompilerParams(
            vmem_limit_bytes=61 * 2**20, collective_id=0, has_side_effects=True
        ),
        cost_estimate=pl.CostEstimate(
            flops=12 * rows * width * ff, bytes_accessed=40 * 2**20, transcendentals=0
        ),
    )(*operands)


def repeat(count, body):
    def step(i, carry):
        body(i)
        return carry

    lax.fori_loop(0, count, step, 0)


def add_into(to, more):
    step = 16

    def add(i):
        at = block_rows(i, step)
        to[at, :] = (to[at, :].astype(F32) + more[at, :].astype(F32)).astype(to.dtype)

    repeat(to.shape[0] // step, add)


def turn_blocks(place, source, turned):
    width = source.shape[1]
    n = place.n
    h = width // (n * place.ctx)
    first = lax.rem(place.c, 2) == 0

    def turn(i):
        chip = lax.rem(place.c // 2 + i // n, 2)
        pair = lax.rem(place.z - lax.rem(i, n) + n, n) * (place.ctx // 2) + chip
        block = source[:, block_rows(pair, 2 * h)].astype(F32).T.astype(turned.dtype)
        low, high = block[:h], block[h:]
        turned[block_rows(i, h), :] = jnp.where(first, low, high)
        turned[block_rows(i + 2 * n, h), :] = jnp.where(first, high, low)

    repeat(2 * n, turn)


class Scatter:
    def __init__(
        self, place, keep, columns, chip_land, line_land, number, sems, line_first=False
    ):
        x_send, x_recv, z_send, z_recv = sems
        n = place.n
        self.n, self.line_first = n, line_first
        self.h = h = keep.shape[0] // (2 * n)
        self.keep = [keep.at[pl.ds(k * h, h), columns] for k in range(2 * n)]
        land = [chip_land.at[pl.ds(k * h, h), columns] for k in range(n)]
        line = [line_land.at[k, :, columns] for k in range(n - 1)]
        there = place.at(c=place.flip(2))

        def ring(blocks, lands, row):
            return [
                remote(blocks[k], lands[k - 1], z_send.at[row, k], z_recv.at[row, k], place.up(1))
                for k in range(1, n)
            ]

        self.rings = [(ring(self.keep[:n], line, number), self.keep[:n], line)]
        if line_first:
            self.rings.append((ring(self.keep[n:], land[1:], number + 1), self.keep[n:], land[1:]))
            self.chip = remote(
                self.keep[n], land[0], x_send.at[number], x_recv.at[number], there
            )
            self.chip_land = land[:1]
        else:
            self.chip = remote(
                keep.at[pl.ds(n * h, n * h), columns],
                chip_land.at[:, columns],
                x_send.at[number],
                x_recv.at[number],
                there,
            )
            self.chip_land = land

    def to_chip(self):
        self.chip.start()

    def from_chip(self):
        self.chip.wait_recv()
        if self.line_first:
            return
        for k in list(range(1, self.n)) + [0]:
            add_into(self.keep[k], self.chip_land[k])
            if k == 1:
                self.begin()

    def begin(self):
        for ring, _, _ in self.rings:
            if ring:
                ring[0].start()

    def advance(self, k):
        if k >= self.n:
            return
        for ring, blocks, lands in self.rings:
            ring[k - 1].wait_recv()
            if k + 1 < self.n:
                add_into(blocks[k + 1], lands[k - 1])
                ring[k].start()
            elif self.line_first:
                add_into(blocks[0], lands[k - 1])

    def finish(self, out):
        last = self.chip_land[0] if self.line_first else self.rings[0][2][self.n - 2]
        step = 16

        def add(i):
            at = block_rows(i, step)
            out[at, :] = self.keep[0][at, :].astype(F32) + last[at, :].astype(F32)

        repeat(self.h // step, add)

    def drain(self):
        self.chip.wait_send()
        for ring, _, _ in self.rings:
            for copy in ring:
                copy.wait_send()


def core_sum(keep, core_land, copy):
    copy.wait_recv()
    add_into(keep, core_land)


def backward_kernel(
    n, ctx, tp, q_width, kv_width, stage_cols,
    lengths, ffn, dmid, qb, kv_all, heads, sums, w, cosines, sines, pick_t, gain, head_gain,
    gain_ffn_grad, squares, dy_in, x_in, mid_in, send_back, normed_two, hidden, d_gate, d_up,
    out_o, out_g, sum_gate, sum_up, sum_down, sum_out, sum_qkv, small,
    x, turned, stage, keep, send, core_land, chip_land, line_land,
    o_keep, o_send, o_core, o_chip, o_line, a_keep, a_send, a_core, a_chip, a_line,
    d_mid_own, d_attn, dob, delta, bias, dq_t, dkv, kv_land, tp_land, ffn_away, ffn_land, dx_away, dx_land,
    sent, back_o, back_g, small_mine, small_land, small_side,
    tp_send, tp_recv, route_send, route_recv, small_send, small_recv, kv_send, kv_recv, load_sem,
    free_sem, *scatter_sems
):
    place = Place(n, ctx, tp)
    group = n * ctx
    rows, width = dmid.shape
    feat = width // tp
    share = rows // group
    piece = rows
    ff = hidden.shape[1]
    half = width // 2
    n_pairs = q_width // 128
    qkv_width = q_width + 2 * kv_width
    values_from = q_width + kv_width
    x_bit, core_bit = place.c // 2, lax.rem(place.c, 2)
    own_cols = block_rows(place.t, feat)
    c_send, c_recv, *ring_sems = scatter_sems
    everything = pl.ds(0, ff)
    lands = lambda m: (chip_land.at[m], line_land.at[m])
    down = Scatter(place, keep.at[0], everything, *lands(0), 0, ring_sems, True)
    gate = Scatter(place, keep.at[1], everything, *lands(1), 2, ring_sems)
    up = Scatter(place, keep.at[2], everything, *lands(2), 3, ring_sems)
    out_sum = Scatter(place, o_keep, pl.ds(0, q_width), o_chip, o_line, 4, ring_sems)
    qkv_sum = Scatter(place, a_keep, pl.ds(0, qkv_width), a_chip, a_line, 5, ring_sems)
    across_cores = [
        remote(src, dst, c_send.at[i], c_recv.at[i], place.at(c=place.flip(1)))
        for i, (src, dst) in enumerate(
            [(send.at[m % 2], core_land.at[m % 2]) for m in range(3)]
            + [(o_send, o_core), (a_send, a_core)]
        )
    ]

    def to_sides(number, src, dst):
        return [
            remote(
                src(j), dst.at[j - 1], tp_send.at[number, j], tp_recv.at[number, j], place.side(j)
            )
            for j in range(1, tp)
        ]

    def away(buffer):
        return lambda j: buffer.at[j - 1]

    def fill_away(buffer, source):
        for j in range(1, tp):
            buffer[j - 1] = source[:, block_rows(lax.rem(place.t + j, tp), feat)]

    def route(number, src, dst):
        return [
            remote(
                src.at[block_rows(lax.rem(place.me + j, group), share), :],
                dst.at[block_rows(place.me, share), :],
                route_send.at[number, j],
                route_recv.at[number, j],
                place.peer(j),
            )
            for j in range(1, group)
        ]

    dmid_sum = to_sides(0, lambda j: dmid, tp_land)
    ffn_sum = to_sides(1, away(ffn_away), ffn_land)
    dx_sum = to_sides(2, away(dx_away), dx_land)
    route_o, route_g = route(0, sent, back_o), route(1, sent, back_g)

    place.greet()
    for copy in dmid_sum:
        copy.start()

    sources = (hidden, d_gate, d_up)
    tiles = [(m, b) for m in range(3) for b in range(0, ff, stage_cols)]
    loads = [
        pltpu.make_async_copy(
            sources[m].at[:, pl.ds(b, stage_cols)], stage.at[i % 2], load_sem.at[i]
        )
        for i, (m, b) in enumerate(tiles)
    ]
    load_n = pltpu.make_async_copy(normed_two, d_attn, load_sem.at[len(tiles)])
    dy, mid = x, d_mid_own
    load_dy = pltpu.make_async_copy(dy_in, dy, load_sem.at[len(tiles) + 1])
    load_x = pltpu.make_async_copy(x_in, x, load_sem.at[len(tiles) + 2])
    load_mid = pltpu.make_async_copy(mid_in, mid, load_sem.at[len(tiles) + 3])
    load_dy.start()
    loads[0].start()
    load_n.start()
    load_mid.start()
    fill_away(ffn_away, ffn)
    load_dy.wait()
    turn_blocks(place, dy, turned)
    sub = 256 if stage_cols % 256 == 0 else 128
    for i, (m, b) in enumerate(tiles):
        if i + 1 < len(tiles):
            loads[i + 1].start()
        if b == 0 and m == 1:
            load_n.wait()
            turn_blocks(place, d_attn, turned)
        if m == 1 and b == ff // 2 // stage_cols * stage_cols:
            core_sum(keep.at[0], core_land.at[0], across_cores[0])
            down.begin()
            pl.semaphore_signal(
                free_sem, inc=1, device_id=place.at(c=place.flip(1)), device_id_type=MESH
            )
        if b == 0 and m == 2:
            across_cores[0].wait_send()
        loads[i].wait()
        for s in range(0, stage_cols, sub):
            right = stage[i % 2, :, s : s + sub]
            cols = slice(b + s, b + s + sub)
            keep[m, :, cols] = dot(turned[:half, :], right, 1, 0).astype(BF)
            send[m % 2, :, cols] = dot(turned[half:, :], right, 1, 0).astype(BF)
        if b + stage_cols == ff:
            if m == 2:
                pl.semaphore_wait(free_sem, 1)
            across_cores[m].start()
    core_sum(keep.at[1], core_land.at[1], across_cores[1])
    gate.to_chip()
    core_sum(keep.at[2], core_land.at[0], across_cores[2])

    for copy in dmid_sum:
        copy.wait_recv()
    for copy in ffn_sum:
        copy.start()

    def sum_gradient(i):
        r = block_rows(i, 128)
        d_all = dy[r, :].astype(F32) + dmid[r, :].astype(F32)
        for j in range(1, tp):
            d_all = d_all + tp_land[j - 1, r, :].astype(F32)
        d_attn[r, :] = d_all.astype(BF)

    repeat(rows // 128, sum_gradient)
    dob[...] = dot(d_attn[...], w[:, qkv_width:], 1, 0).astype(BF)
    dq_t[...] = jnp.zeros_like(dq_t)
    ones = jnp.ones((8, 128), F32)

    def set_delta(g):
        both = dob[:, lane_block(g)].astype(F32) * heads[:, lane_block(g)]
        delta[g] = dot(ones, two_heads(both), 1, 1, lax.Precision.HIGHEST)

    repeat(n_pairs, set_delta)
    q_slot = place.c * piece + lanes((piece, rows))
    start_row = segment_start(lengths, place.c * piece + lanes((8, rows)))[:1]

    def one_piece(p):
        k_slot = p * piece + lax.broadcasted_iota(jnp.int32, (piece, rows), 0)
        open_ = (k_slot >= start_row) & (k_slot <= q_slot)
        bias[...] = jnp.where(open_, 0.0, NEG_FILL)
        at = block_rows(p, piece)
        def heads_of(members):
            grads = []
            for g, (kb, ke), (vb, ve) in members:
                q2 = two_heads(qb[:, lane_block(g)])
                do2 = two_heads(dob[:, lane_block(g)])
                k2 = twice(kv_all[at, lane_block(kb)], ke)
                v2 = twice(kv_all[at, lane_block(vb)], ve)
                k_t = k2.astype(F32).T.astype(BF)
                dk = jnp.zeros((piece, 128), F32)
                dv = jnp.zeros((piece, 128), F32)
                for h in range(0, 2 * rows, 256):
                    part = slice(h, h + 256)
                    open_part = slice(h % rows, h % rows + 256)
                    s = dot(k2, q2[part], 1, 1)
                    dp = dot(v2, do2[part], 1, 1)
                    pe = jnp.exp(s * 0.125 + bias[:, open_part]) * sums[g, 0:1, part]
                    ds = (pe * (dp - delta[g, 0:1, part])).astype(BF)
                    dv = dv + dot(pe.astype(BF), do2[part], 1, 0)
                    dk = dk + dot(ds, q2[part], 1, 0)
                    dq_t[g, :, part] += dot(k_t, ds, 1, 0)
                grads.append((both_halves(dk) * 0.125, both_halves(dv)))
            low = lanes((piece, 128)) < HEAD_SIZE
            kb, vb = members[0][1][0], members[0][2][0]
            if len(members) == 2:
                dkv[at, lane_block(kb)] = jnp.where(low, grads[0][0], grads[1][0]).astype(BF)
                dkv[at, lane_block(vb)] = jnp.where(low, grads[0][1], grads[1][1]).astype(BF)
            else:
                for value, (b, e) in zip(grads[0], members[0][1:]):
                    c = 128 * b + HEAD_SIZE * e
                    dkv[at, c : c + HEAD_SIZE] = value[:, :HEAD_SIZE].astype(BF)

        over_key_heads(n_pairs, kv_width // HEAD_SIZE, heads_of)

    down.advance(1)

    sibling = place.at(c=place.flip(1))
    other = 1 - core_bit
    to_passer = remote(
        dkv.at[block_rows(other, piece), :], kv_land.at[0], kv_send.at[0], kv_recv.at[0], sibling
    )
    to_chip = remote(
        dkv.at[block_rows(core_bit, piece), :],
        kv_land.at[0],
        kv_send.at[1],
        kv_recv.at[1],
        place.at(c=place.flip(2)),
    )
    to_core = remote(
        dkv.at[block_rows(2 * x_bit, piece), :], kv_land.at[1], kv_send.at[2], kv_recv.at[2], sibling
    )

    @pl.when(x_bit == 1)
    def _():
        def step(p, carry):
            one_piece(p)
            return carry

        lax.fori_loop(0, 2, step, 0)
        to_passer.start()

    turn_blocks(place, d_attn, turned)
    right = heads[...].astype(BF)
    o_keep[...] = dot(turned[:half, :], right, 1, 0).astype(BF)
    o_send[...] = dot(turned[half:, :], right, 1, 0).astype(BF)
    across_cores[3].start()
    down.advance(2)

    @pl.when(x_bit == 1)
    def _():
        to_passer.wait_recv()
        mine = block_rows(core_bit, piece)
        dkv[mine, :] = (dkv[mine, :].astype(F32) + kv_land[0].astype(F32)).astype(BF)
        to_chip.start()

    gate.from_chip()
    up.to_chip()
    core_sum(o_keep, o_core, across_cores[3])

    @pl.when(core_bit == 1)
    def _():
        one_piece(place.c - 1)
        to_core.start()

    for copy in ffn_sum:
        copy.wait_recv()
    small_mine[...] = jnp.zeros_like(small_mine)
    load_mid.wait()

    def finish_output(i):
        r = block_rows(i, 128)
        ffn_out = ffn[r, own_cols].astype(F32)
        for j in range(1, tp):
            ffn_out = ffn_out + ffn_land[j - 1, r, :].astype(F32)
        small_mine[5:6, :feat] += jnp.sum(ffn_out * ffn_out, axis=0, keepdims=True)
        dx_away[0, r, :] = (mid[r, :] + ffn_out).astype(BF)

    repeat(rows // 128, finish_output)
    sent[...] = dot(pick_t[...], dx_away[0], 1, 0).astype(BF)
    for copy in route_o:
        copy.start()
    own = block_rows(place.me, share)
    back_o[own, :] = sent[own, :]


    def own_gradient(i):
        r = block_rows(i, 128)
        d_own = dy[r, own_cols].astype(F32) + dmid[r, own_cols].astype(F32)
        for j in range(1, tp):
            d_own = d_own + tp_land[j - 1, r, own_cols].astype(F32)
        d_mid_own[r, :] = d_own

    repeat(rows // 128, own_gradient)
    load_x.start()
    down.advance(3)
    down.to_chip()
    gate.advance(1)
    one_piece(place.c)
    gate.advance(2)
    normed = tp_land.at[0]
    load_x.wait()

    def norm_again(i):
        v = x[block_rows(i, 128), :].astype(F32)
        normed[block_rows(i, 128), :] = (v * row_scale(v) * gain[...]).astype(BF)

    repeat(rows // 128, norm_again)
    turn_blocks(place, normed, turned)
    mine = block_rows(place.c, piece)

    @pl.when(core_bit == 0)
    def _():
        to_core.wait_recv()

    @pl.when(x_bit == 0)
    def _():
        to_chip.wait_recv()

    d_qkv = d_attn.at[:, pl.ds(0, qkv_width)]
    for b in range(0, qkv_width, 128):
        if b < q_width:
            g = b // 128
            grad = one_row(dq_t[g].T) * 0.125
        else:
            cols = slice(b - q_width, b - q_width + 128)
            grad = dkv[mine, cols].astype(F32)
            grad = jnp.where(x_bit == 0, grad + kv_land[0, :, cols].astype(F32), grad)
            grad = jnp.where(core_bit == 0, grad + kv_land[1, :, cols].astype(F32), grad)
        raw = dot(normed[...], w[:, b : b + 128], 1, 0)
        is_value = lanes(grad.shape) + b >= values_from
        back, gain_grad = qk_backward(
            grad, raw, head_gain[:, b : b + 128], cosines[...], sines[...], is_value
        )
        small_mine[2:3, b : b + 128] = gain_grad
        d_qkv[:, b : b + 128] = back.astype(BF)

    def finish_gradient(i):
        r = block_rows(i, 128)
        dn = dot(d_qkv[r, :], w[:, :qkv_width], 1, 1)
        dx, gain_grad = norm_back(dn, x[r, :].astype(F32), gain[...])
        normed[r, :] = dx.astype(BF)
        small_mine[0:1, :] += gain_grad

    repeat(rows // 128, finish_gradient)
    fill_away(dx_away, normed)
    for copy in dx_sum:
        copy.start()
    small_mine[1:2, :] = gain_ffn_grad[...]
    small_mine[3:5, :] = squares[...]
    for b in range(0, qkv_width, 256):
        cols = slice(b, b + 256)
        a_keep[:, cols] = dot(turned[:half, :], d_qkv[:, cols], 1, 0).astype(BF)
        a_send[:, cols] = dot(turned[half:, :], d_qkv[:, cols], 1, 0).astype(BF)
    across_cores[4].start()
    load_back = pltpu.make_async_copy(
        send_back, turned.at[pl.ds(0, rows), :], load_sem.at[len(tiles) + 4]
    )
    load_back.start()
    small_out = [
        remote(
            small_mine, small_land.at[place.me], small_send.at[0, j], small_recv.at[0, j], place.peer(j)
        )
        for j in range(1, group)
    ]
    for copy in small_out:
        copy.start()
    small_land[place.me] = small_mine[...]
    up.from_chip()
    core_sum(a_keep, a_core, across_cores[4])
    qkv_sum.to_chip()
    out_sum.to_chip()
    gate.advance(3)

    for copy in dx_sum:
        copy.wait_recv()
    for copy in ffn_sum:
        copy.wait_send()

    def finish_input(i):
        r = block_rows(i, 128)
        total = d_mid_own[r, :] + normed[r, own_cols].astype(F32)
        for j in range(1, tp):
            total = total + dx_land[j - 1, r, :].astype(F32)
        ffn_away[0, r, :] = total.astype(BF)

    repeat(rows // 128, finish_input)
    for copy in route_o:
        copy.wait_send()
    sent[...] = dot(pick_t[...], ffn_away[0], 1, 0).astype(BF)
    for copy in route_g:
        copy.start()
    back_g[own, :] = sent[own, :]
    down.from_chip()
    down.finish(sum_down)
    gate.finish(sum_gate)
    up.advance(1)
    qkv_sum.from_chip()
    out_sum.from_chip()
    up.advance(2)
    qkv_sum.advance(1)
    out_sum.advance(1)
    up.advance(3)
    qkv_sum.advance(2)
    out_sum.advance(2)
    up.finish(sum_up)
    for copy in small_out:
        copy.wait_recv()
    total = small_land[0]
    for i in range(1, group):
        total = total + small_land[i]
    small_side[place.t] = total
    for copy in small_out:
        copy.wait_send()
    small_mine[...] = total
    sides = [
        remote(
            small_mine, small_side.at[place.t], small_send.at[1, j], small_recv.at[1, j], place.side(j)
        )
        for j in range(1, tp)
    ]
    for copy in sides:
        copy.start()
    out_sum.advance(3)
    out_sum.finish(sum_out)
    for copy in sides:
        copy.wait_recv()
    total = small_side[0]
    for j in range(1, tp):
        total = total + small_side[j]
    small[...] = total
    load_back.wait()
    for copy in route_o:
        copy.wait_recv()
    out_o[...] = dot(turned[:rows, :], back_o[...], 1, 0).astype(BF)
    qkv_sum.advance(3)
    qkv_sum.finish(sum_qkv)
    for copy in route_g:
        copy.wait_recv()
    out_g[...] = dot(turned[:rows, :], back_g[...], 1, 0).astype(BF)

    @pl.when(x_bit == 1)
    def _():
        to_passer.wait_send()
        to_chip.wait_send()

    @pl.when(core_bit == 1)
    def _():
        to_core.wait_send()

    for copy in dmid_sum + dx_sum + route_g + sides:
        copy.wait_send()
    for copy in across_cores[1:]:
        copy.wait_send()
    for s in (down, gate, up, out_sum, qkv_sum):
        s.drain()


def backward_pass(grid, q_width, kv_width, *operands):
    dmid, hidden = operands[2], operands[20]
    rows, width = dmid.shape
    ff = hidden.shape[1]
    n, ctx, tp = grid.n, grid.ctx, grid.tp
    group = n * ctx
    feat = width // tp
    half = width // 2
    h = width // group
    n_pairs = q_width // 128
    qkv_width = q_width + 2 * kv_width
    stage_cols = 256 if ff % 256 == 0 else 128
    vm = pl.BlockSpec(memory_space=pltpu.VMEM)
    dma = pltpu.SemaphoreType.DMA
    V = pltpu.VMEM

    def scatter_space(cols):
        return [
            V((half, cols), BF),
            V((half, cols), BF),
            V((half, cols), BF),
            V((half // 2, cols), BF),
            V((n - 1, h, cols), BF),
        ]

    return pl.pallas_call(
        functools.partial(backward_kernel, n, ctx, tp, q_width, kv_width, stage_cols),
        in_specs=[pl.BlockSpec(memory_space=pltpu.SMEM)] + [vm] * 14 + [ANYWHERE] * 8,
        out_specs=[vm] * 8,
        out_shape=[
            shape((rows, feat), BF),
            shape((rows, feat), BF),
            shape((h, ff), F32),
            shape((h, ff), F32),
            shape((h, ff), F32),
            shape((h, q_width), F32),
            shape((h, qkv_width), F32),
            shape((8, width), F32),
        ],
        scratch_shapes=[
            V((rows, width), BF),
            V((width, rows), BF),
            V((2, rows, stage_cols), BF),
            V((3, half, ff), BF),
            V((2, half, ff), BF),
            V((2, half, ff), BF),
            V((3, half // 2, ff), BF),
            V((3, n - 1, h, ff), BF),
        ]
        + scatter_space(q_width)
        + scatter_space(qkv_width)
        + [
            V((rows, feat), F32),
            V((rows, width), BF),
            V((rows, q_width), BF),
            V((n_pairs, 8, 2 * rows), F32),
            V((rows, rows), F32),
            V((n_pairs, 128, 2 * rows), F32),
            V((rows * ctx, 2 * kv_width), BF),
            V((2, rows, 2 * kv_width), BF),
            V((tp - 1, rows, width), BF),
            V((tp - 1, rows, feat), BF),
            V((tp - 1, rows, feat), BF),
            V((tp - 1, rows, feat), BF),
            V((tp - 1, rows, feat), BF),
            V((rows, feat), BF),
            V((rows, feat), BF),
            V((rows, feat), BF),
            V((8, width), F32),
            V((group, 8, width), F32),
            V((tp, 8, width), F32),
            dma((3, tp)),
            dma((3, tp)),
            dma((2, group)),
            dma((2, group)),
            dma((2, max(group, tp))),
            dma((2, max(group, tp))),
            dma((3,)),
            dma((3,)),
            dma((3 * (ff // stage_cols) + 5,)),
            pltpu.SemaphoreType.REGULAR,
            dma((5,)),
            dma((5,)),
            dma((6,)),
            dma((6,)),
            dma((6, n)),
            dma((6, n)),
        ],
        compiler_params=pltpu.CompilerParams(
            vmem_limit_bytes=61 * 2**20, collective_id=1, has_side_effects=True
        ),
        cost_estimate=pl.CostEstimate(
            flops=20 * rows * rows * ctx * q_width, bytes_accessed=40 * 2**20, transcendentals=0
        ),
    )(*operands)


def pad_columns(v, to):
    return v if v.shape[1] == to else jnp.pad(v, ((0, 0), (0, to - v.shape[1])))


def local(
    tokens,
    cotangent,
    slot_of,
    lengths,
    w_query,
    key_weight,
    value_weight,
    w_out,
    w_gate,
    w_up,
    w_down,
    gain_attn,
    gain_ffn,
    gain_query,
    gain_key,
):
    grid = Grid()
    rows, feat_len = tokens.shape
    groups = grid.n * grid.ctx
    q_heads = QUERY_HEADS // grid.tp
    key_value_heads = KEY_VALUE_HEADS // grid.tp
    q_width = q_heads * HEAD_SIZE
    kv_width = key_value_heads * HEAD_SIZE
    ff = w_gate.shape[1]
    tile = 256 if ff % 256 == 0 else 128
    tiles = -(-ff // tile)
    attn_shard = jnp.concatenate([w_query, key_weight, value_weight, w_out.T], axis=1)
    by_tile = [
        pad_columns(v, tiles * tile).reshape(-1, tiles, 1, tile) for v in (w_gate, w_up, w_down.T)
    ]
    ffn_shard = jnp.concatenate(by_tile, axis=2).reshape(-1, 3 * tiles * tile)
    head_gain = jnp.concatenate(
        [
            jnp.tile(gain_query, q_heads),
            jnp.tile(gain_key, key_value_heads),
            jnp.ones((kv_width,), F32),
        ]
    )[None, :]
    frequency = ROPE_THETA ** (-np.arange(0, HEAD_SIZE, 2, dtype=np.float64) / HEAD_SIZE)
    frequency = jnp.asarray(np.tile(frequency, 4)[None, :], F32)
    (
        sums, squares, ffn_part, d_mid_part, d_gain_ffn, take_back, send_back, cosines, sines,
        x_full, dy_full, qb, row_kv, heads, middle_own, attn_w, normed_two, hidden, d_gate, d_up,
    ) = forward_pass(
        grid,
        q_width,
        kv_width,
        tile,
        lengths,
        tokens,
        cotangent,
        slot_of.reshape(groups, rows),
        gain_attn[None, :],
        head_gain,
        gain_ffn[None, :],
        frequency,
        attn_shard,
        ffn_shard,
    )
    output, grad_tokens, sum_gate, sum_up, sum_down, sum_out, sum_qkv, small = backward_pass(
        grid,
        q_width,
        kv_width,
        lengths,
        ffn_part,
        d_mid_part,
        qb,
        row_kv,
        heads,
        sums,
        attn_w,
        cosines,
        sines,
        take_back,
        gain_attn[None, :],
        head_gain,
        d_gain_ffn,
        squares,
        dy_full,
        x_full,
        middle_own,
        send_back,
        normed_two,
        hidden,
        d_gate,
        d_up,
    )
    a, b = q_width, q_width + kv_width
    per_head = small[2, : b + kv_width].reshape(-1, HEAD_SIZE)
    entry_count = rows * groups * MODEL_WIDTH
    square_sums = jnp.sum(small[3:6], axis=1) / jnp.stack([grid.tp, grid.tp, 1]).astype(F32)

    return (
        output,
        grad_tokens,
        sum_qkv[:, :a],
        sum_qkv[:, a:b],
        sum_qkv[:, b:],
        sum_out.T,
        sum_gate[:, :ff],
        sum_up[:, :ff],
        sum_down[:, :ff].T,
        small[0],
        small[1],
        jnp.sum(per_head[:q_heads], axis=0),
        jnp.sum(per_head[q_heads : q_heads + key_value_heads], axis=0),
        jnp.sqrt(square_sums / entry_count),
    )


def solution(mesh):
    row = P(("fsdp", "ctx"), "tp")
    column = P("tp", ("fsdp", "ctx"))
    in_specs = (row, row, P(), P("fsdp", None), row, row, row, column, row, row, column) + (P(),) * 4
    out_specs = (row, row, row, row, row, column, row, row, column) + (P(),) * 5
    return jax.shard_map(local, mesh=mesh, in_specs=in_specs, out_specs=out_specs, check_vma=False)
```

```python
import functools

import jax
import jax.numpy as jnp
import numpy as np
from jax import lax
from jax.experimental import pallas as pl
from jax.experimental.pallas import tpu as pltpu
from jax.sharding import PartitionSpec as P

MODEL_WIDTH = 1024
QUERY_HEADS = 16
KEY_VALUE_HEADS = 8
HEAD_SIZE = 64

EPSILON = 1e-05
ROPE_THETA = 1000000.0
NEG_FILL = -1e30
BF = jnp.bfloat16
F32 = jnp.float32


class Grid:
    def __init__(self):
        self.n = lax.axis_size("fsdp")
        self.ctx = lax.axis_size("ctx")
        self.tp = lax.axis_size("tp")
        self.z = lax.axis_index("fsdp")
        self.c = lax.axis_index("ctx")
        self.t = lax.axis_index("tp")


def shape(s, t):
    return jax.ShapeDtypeStruct(s, t)


ANYWHERE = pl.BlockSpec(memory_space=pl.ANY)


def dot(a, b, ca, cb, precision=None):
    return lax.dot_general(
        a, b, (((ca,), (cb,)), ((), ())), preferred_element_type=F32, precision=precision
    )


def lanes(shape):
    return lax.broadcasted_iota(jnp.int32, shape, 1)


def half_mean(v):
    low = lanes(v.shape) < HEAD_SIZE
    first = jnp.sum(jnp.where(low, v, 0.0), axis=1, keepdims=True)
    second = jnp.sum(jnp.where(low, 0.0, v), axis=1, keepdims=True)
    return jnp.where(low, first, second) * (1.0 / HEAD_SIZE)


def half_swap(v):
    quarter = HEAD_SIZE // 2
    left = pltpu.roll(v, 128 - quarter, 1)
    right = pltpu.roll(v, quarter, 1)
    return jnp.where(lanes(v.shape) % HEAD_SIZE < quarter, left, right)


def row_scale(v):
    return lax.rsqrt(jnp.mean(v * v, axis=1, keepdims=True) + EPSILON)


def norm_back(dn, v, gain):
    scale = row_scale(v)
    unit = v * scale
    scaled = dn * gain
    grad = scale * (scaled - unit * jnp.mean(scaled * unit, axis=1, keepdims=True))
    return grad, jnp.sum(dn * unit, axis=0, keepdims=True)


def qk_forward(raw, gain, cosines, sines, is_value):
    normed = raw * lax.rsqrt(half_mean(raw * raw) + EPSILON) * gain
    turned = normed * cosines + half_swap(normed) * sines
    return jnp.where(is_value, raw, turned)


def qk_backward(grad, raw, gain, cosines, sines, is_value):
    straight = grad * cosines - half_swap(grad) * sines
    scale = lax.rsqrt(half_mean(raw * raw) + EPSILON)
    unit = raw * scale
    scaled = straight * gain
    back = scale * (scaled - unit * half_mean(scaled * unit))
    gain_grad = jnp.sum(straight * unit, axis=0, keepdims=True)
    return jnp.where(is_value, grad, back), gain_grad


def two_heads(v):
    low = lanes(v.shape) < HEAD_SIZE
    zero = jnp.zeros_like(v)
    return jnp.concatenate([jnp.where(low, v, zero), jnp.where(low, zero, v)], axis=0)


def one_row(v):
    rows = v.shape[0] // 2
    return jnp.where(lanes((rows, v.shape[1])) < HEAD_SIZE, v[:rows], v[rows:])


def twice(v, which):
    half = v[:, which * HEAD_SIZE : (which + 1) * HEAD_SIZE]
    return jnp.concatenate([half, half], axis=1)


def both_halves(v):
    return v + jnp.concatenate([v[:, HEAD_SIZE:], v[:, :HEAD_SIZE]], axis=1)


def over_key_heads(n_heads, values_from, body):
    if n_heads % 2:
        for g in range(n_heads):
            body([(g, (g // 2, g % 2), ((values_from + g) // 2, (values_from + g) % 2))])
        return

    def step(i, carry):
        body([(2 * i + e, (i, e), (values_from // 2 + i, e)) for e in range(2)])
        return carry

    lax.fori_loop(0, n_heads // 2, step, 0)


def lane_block(i):
    return block_rows(i, 128)


def segment_start(lengths, slots):
    end = lengths[0, 0]
    start = jnp.where(slots >= end, end, 0)
    for i in range(1, lengths.shape[1] - 1):
        end = end + lengths[0, i]
        start = jnp.where(slots >= end, end, start)
    return start


def sublanes(shape):
    return lax.broadcasted_iota(jnp.int32, shape, 0)


def count(mask, axis):
    return jnp.sum(mask.astype(F32), axis=axis, keepdims=True).astype(jnp.int32)


def routing(place, slots, rows, share):
    lines = rows // 128
    groups = slots.shape[0] // lines
    square = (rows, rows)

    def line(s):
        return jnp.concatenate([slots[pl.ds(s * lines + i, 1), :] for i in range(lines)], axis=1)

    row = line(place.me)
    column = jnp.broadcast_to(row.astype(F32), (128, rows)).T[:, :1].astype(jnp.int32)
    base = row // rows * rows
    rank = count((column < row) & (column >= base), 0)
    sent_row = row // rows * share + rank
    base = column // rows * rows
    rank = count((row < column) & (row >= base), 1)
    sent_column = column // rows * share + rank
    low = 32
    high = rows // low
    table = jnp.zeros((high, low), F32)
    for s in range(groups):
        r = line(s)
        left = (r // low - place.me * high) == sublanes((high, rows))
        right = r % low == sublanes((low, rows))
        table = table + dot(left.astype(BF), right.astype(BF), 1, 1) * float(s)
    spread = (lanes((low, rows)) % low == sublanes((low, rows))).astype(F32)
    pick = lanes((high, rows)) // low == sublanes((high, rows))
    from_row = jnp.sum(jnp.where(pick, dot(table, spread, 1, 0), 0.0), axis=0, keepdims=True)
    spread = (sublanes((rows, low)) % low == lanes((rows, low))).astype(F32)
    pick = sublanes((rows, high)) // low == lanes((rows, high))
    from_column = jnp.sum(jnp.where(pick, dot(spread, table, 1, 1), 0.0), axis=1, keepdims=True)
    from_row, from_column = from_row.astype(jnp.int32), from_column.astype(jnp.int32)
    same = from_row == from_column
    got_column = from_column * share + count(same & (lanes(square) < sublanes(square)), 1)
    got_row = from_row * share + count(same & (sublanes(square) < lanes(square)), 0)
    return sent_row, sent_column, got_row, got_column


class Place:
    def __init__(self, n, ctx, tp):
        self.n, self.ctx, self.tp = n, ctx, tp
        self.z = lax.axis_index("fsdp")
        self.c = lax.axis_index("ctx")
        self.t = lax.axis_index("tp")
        self.me = self.z * ctx + self.c

    def at(self, z=None, c=None, t=None):
        return (
            self.z if z is None else z,
            self.c if c is None else c,
            self.t if t is None else t,
        )

    def peer(self, j):
        p = lax.rem(self.me + j, self.n * self.ctx)
        return self.at(p // self.ctx, lax.rem(p, self.ctx))

    def up(self, j):
        return self.at(z=lax.rem(self.z + j, self.n))

    def flip(self, bit):
        if bit == 1:
            return self.c + 1 - 2 * lax.rem(self.c, 2)
        return lax.rem(self.c + 2, 4)

    def side(self, j):
        return self.at(t=lax.rem(self.t + j, self.tp))

    def owner(self, k, c):
        return lax.rem(self.z - k + self.n, self.n) * self.ctx + c

    def greet(self):
        barrier = pltpu.get_barrier_semaphore()
        group = self.n * self.ctx
        for j in range(1, group):
            pl.semaphore_signal(barrier, inc=1, device_id=self.peer(j), device_id_type=MESH)
        for j in range(1, self.tp):
            pl.semaphore_signal(barrier, inc=1, device_id=self.side(j), device_id_type=MESH)
        pl.semaphore_wait(barrier, group + self.tp - 2)


MESH = pl.DeviceIdType.MESH


def remote(src, dst, send, recv, device):
    return pltpu.make_async_remote_copy(
        src_ref=src, dst_ref=dst, send_sem=send, recv_sem=recv, device_id=device, device_id_type=MESH
    )


def block_rows(index, size):
    return pl.ds(pl.multiple_of(index * size, size), size)


class Gather:
    def __init__(self, place, whole, columns, number, sems, chip_first=False):
        z_send, z_recv, x_send, x_recv, c_send, c_recv = sems
        h = whole.shape[0] // (place.n * place.ctx)
        n = place.n
        self.n, self.chip_first = n, chip_first
        view = lambda index: whole.at[block_rows(index, h), columns]
        here, there = place.c, place.flip(2)

        def ring(lane, row):
            return [
                remote(
                    view(place.owner(k - 1, lane)),
                    view(place.owner(k - 1, lane)),
                    z_send.at[row, k],
                    z_recv.at[row, k],
                    place.up(1),
                )
                for k in range(1, n)
            ]

        self.rings = [ring(here, number)] + ([ring(there, number + 1)] if chip_first else [])
        self.chip = [
            remote(
                view(place.owner(k, here)),
                view(place.owner(k, here)),
                x_send.at[number, k],
                x_recv.at[number, k],
                place.at(c=there),
            )
            for k in range(1 if chip_first else n)
        ]
        self.core = [
            remote(
                view(place.owner(i % n, here if i < n else there)),
                view(place.owner(i % n, here if i < n else there)),
                c_send.at[number, i],
                c_recv.at[number, i],
                place.at(c=place.flip(1)),
            )
            for i in range(2 * n)
        ]

    def begin(self):
        if self.n > 1:
            self.rings[0][0].start()
        self.core[0].start()

    def begin_other(self):
        if self.n > 1:
            self.rings[1][0].start()

    def advance(self, k):
        if k >= self.n:
            return
        for r, ring in enumerate(self.rings):
            ring[k - 1].wait_recv()
            if k + 1 < self.n:
                ring[k].start()
            self.core[r * self.n + k].start()

    def to_chip(self, k):
        if k < len(self.chip):
            self.chip[k].start()

    def from_chip(self, k):
        if k < len(self.chip):
            self.chip[k].wait_recv()
            self.core[self.n + k].start()

    def finish(self):
        for copy in self.core:
            copy.wait_recv()

    def drain(self):
        for copy in sum(self.rings, []) + self.chip + self.core:
            copy.wait_send()


def forward_kernel(
    n, ctx, tp, q_width, kv_width, tile,
    lengths, tokens, cotangent, slots, gain, head_gain, gain_ffn, frequency,
    w_query, w_key, w_value, w_out, w_gate, w_up, w_down,
    sums, squares, ffn_out, dmid, dgain, take_back, send_back, cosines, sines,
    x, dy, qb_out, kv, heads_out, mid_own, w_attn, normed_two, hidden, d_gate, d_up,
    sent_x, sent_y, got_x, got_y, own_x, own_y, x_land, y_land, pick, qb, heads, mid, nb,
    w, w_ffn, kv_all, part, land, acc, total, bias, ffn_acc, dn_acc, acts,
    route_send, route_recv, tp_send, tp_recv, kv_send, kv_recv, out_sem, act_sem, *gather_sems
):
    place = Place(n, ctx, tp)
    group = n * ctx
    rows = got_x.shape[0]
    share = rows // group
    feat = got_x.shape[1]
    width = x_land.shape[1]
    piece = rows
    attn = Gather(place, w, pl.ds(0, w.shape[1]), 0, gather_sems)
    tiles = w_ffn.shape[1] // (3 * tile)
    last = max(1, tiles // 9)
    cuts = [(tiles - last) * i // 3 for i in range(3)] + [tiles - last, tiles]
    first, second, third, tail = (
        Gather(
            place,
            w_ffn,
            pl.ds(cuts[i] * 3 * tile, (cuts[i + 1] - cuts[i]) * 3 * tile),
            1 + i,
            gather_sems,
            chip_first=i == 3,
        )
        for i in range(4)
    )
    groups = [first, second, third]
    stores = []

    def store(src, dst):
        copy = pltpu.make_async_copy(src, dst, out_sem.at[len(stores)])
        copy.start()
        stores.append(copy)

    def route(number, src, dst):
        return [
            remote(
                src.at[block_rows(lax.rem(place.me + j, group), share), :],
                dst.at[block_rows(place.me, share), :],
                route_send.at[number, j],
                route_recv.at[number, j],
                place.peer(j),
            )
            for j in range(1, group)
        ]

    def widen(number, src, dst):
        return [
            remote(
                src,
                dst.at[:, block_rows(place.t, feat)],
                tp_send.at[number, j],
                tp_recv.at[number, j],
                place.side(j),
            )
            for j in range(1, tp)
        ]

    def own_block(src, dst):
        at = block_rows(place.me, share)
        dst[at, :] = src[at, :]

    route_x, route_y = route(0, sent_x, got_x), route(1, sent_y, got_y)
    wide_x, wide_y = widen(0, own_x, x_land), widen(1, own_y, y_land)
    shard_rows = w_query.shape[0]
    own_shard = block_rows(place.me, shard_rows)
    column = 0
    for part_w in (w_query, w_key, w_value):
        w[own_shard, column : column + part_w.shape[1]] = part_w[...]
        column += part_w.shape[1]
    w[own_shard, column:] = w_out[...]
    place.greet()
    attn.begin()
    attn.to_chip(0)
    sent_row, sent_column, got_row, got_column = routing(place, slots, rows, share)
    for i in range(tiles):
        used = min(tile, w_gate.shape[1] - i * tile)
        cols = slice(i * tile, i * tile + used)
        for m, value in enumerate((w_gate[:, cols], w_up[:, cols], w_down[:, cols])):
            if used < tile:
                value = jnp.concatenate(
                    [value, jnp.zeros((shard_rows, tile - used), BF)], axis=1
                )
            c = (3 * i + m) * tile
            w_ffn[own_shard, c : c + tile] = value
    square = (rows, rows)
    send_pick = (sublanes(square) == sent_row).astype(BF)
    sent_x[...] = dot(send_pick, tokens[...], 1, 0).astype(BF)
    for copy in route_x:
        copy.start()
    own_block(sent_x, got_x)
    attn.advance(1)
    attn.to_chip(1)
    sent_y[...] = dot(send_pick, cotangent[...], 1, 0).astype(BF)
    own_block(sent_y, got_y)
    pick[...] = (lanes(square) == got_column).astype(BF)
    take_back[...] = (sublanes(square) == got_row).astype(BF)
    send_back[...] = (lanes(square) == sent_column).astype(BF)
    slot = place.c * piece + sublanes((rows, 128))
    start_col = segment_start(lengths, slot)
    angle = (slot - start_col).astype(F32) * frequency[...]
    start_col = start_col[:, :1]
    cosines[...] = jnp.cos(angle)
    turned_lane = lanes((rows, 128)) % HEAD_SIZE < HEAD_SIZE // 2
    sines[...] = jnp.where(turned_lane, -1.0, 1.0) * jnp.sin(angle)
    attn.from_chip(0)
    attn.advance(2)
    attn.to_chip(2)
    first.begin()
    for copy in route_x:
        copy.wait_recv()
    own_x[...] = dot(pick[...], got_x[...], 1, 0).astype(BF)
    for copy in wide_x:
        copy.start()
    x_land[:, block_rows(place.t, feat)] = own_x[...]
    attn.from_chip(1)
    attn.advance(3)
    attn.to_chip(3)
    for copy in route_y:
        copy.start()
    second.begin()
    first.to_chip(0)
    attn.from_chip(2)
    attn.from_chip(3)
    second.to_chip(0)
    for copy in wide_x:
        copy.wait_recv()
    store(x_land, x)
    v = x_land[...].astype(F32)
    normed = (v * row_scale(v) * gain[...]).astype(BF)
    attn.finish()
    store(w, w_attn)

    own_rows = block_rows(place.c, piece)
    values_from = q_width + kv_width
    for b in list(range(q_width, q_width + 2 * kv_width, 128)) + list(range(0, q_width, 128)):
        if b == 0:
            later = start_keys(place, kv_all, own_rows, kv_send, kv_recv)
        block = dot(normed, w[:, b : b + 128], 1, 0)
        is_value = lanes(block.shape) + b >= values_from
        done = qk_forward(block, head_gain[:, b : b + 128], cosines[...], sines[...], is_value)
        if b < q_width:
            qb[:, b : b + 128] = done.astype(BF)
        else:
            kv_all[own_rows, b - q_width : b - q_width + 128] = done.astype(BF)

    q_slot = place.c * piece + lax.broadcasted_iota(jnp.int32, (rows, piece), 0)
    n_pairs = q_width // 128

    def one_piece(p):
        k_slot = p * piece + lanes((rows, piece))
        open_ = (k_slot >= start_col) & (k_slot <= q_slot)
        bias[...] = jnp.where(open_, 0.0, NEG_FILL)
        at = block_rows(p, piece)

        def heads_of(members):
            for g, (kb, ke), (vb, ve) in members:
                q2 = two_heads(qb[:, lane_block(g)])
                k2 = twice(kv_all[at, lane_block(kb)], ke)
                v2 = twice(kv_all[at, lane_block(vb)], ve)
                for h in range(2):
                    part = slice(h * rows, (h + 1) * rows)
                    e = jnp.exp(dot(q2[part], k2, 1, 1) * 0.125 + bias[...])
                    part_sum = e[:, :128]
                    for b in range(128, piece, 128):
                        part_sum = part_sum + e[:, b : b + 128]
                    acc[g, part, :] += dot(e.astype(BF), v2, 1, 0)
                    total[g, part, :] += part_sum

        over_key_heads(n_pairs, kv_width // HEAD_SIZE, heads_of)

    acc[...] = jnp.zeros_like(acc)
    total[...] = jnp.zeros_like(total)
    one_piece(place.c)
    x_bit, core_bit = place.c // 2, lax.rem(place.c, 2)
    near, across, passed = later
    first.advance(1)
    second.advance(1)

    @pl.when(x_bit == 1)
    def _():
        across.wait_recv()
        passed.start()

    first.from_chip(0)
    second.from_chip(0)
    tail.to_chip(0)
    first.to_chip(1)
    for copy in route_y:
        copy.wait_recv()
    own_y[...] = dot(pick[...], got_y[...], 1, 0).astype(BF)
    for copy in wide_y:
        copy.start()
    y_land[:, block_rows(place.t, feat)] = own_y[...]

    @pl.when(core_bit == 1)
    def _():
        near.wait_recv()
        one_piece(place.c - 1)

    first.advance(2)
    second.advance(2)
    second.to_chip(1)

    @pl.when(x_bit == 1)
    def _():
        passed.wait_recv()

        def step(p, carry):
            one_piece(p)
            return carry

        lax.fori_loop(0, 2, step, 0)

    ones = jnp.ones((8, 128), F32)
    for g in range(n_pairs):
        row_total = jnp.sum(total[g], axis=1, keepdims=True)
        heads[:, 128 * g : 128 * g + 128] = one_row(acc[g] / row_total)
        sums[g] = 1.0 / dot(ones, total[g], 1, 1, lax.Precision.HIGHEST)
    part[...] = dot(heads[...].astype(BF), w[:, q_width + 2 * kv_width :], 1, 1).astype(BF)
    attention = [
        remote(part, land.at[j - 1], tp_send.at[2, j], tp_recv.at[2, j], place.side(j))
        for j in range(1, tp)
    ]
    for copy in attention:
        copy.start()
    store(qb, qb_out)
    store(heads, heads_out)
    first.from_chip(1)
    first.to_chip(2)
    first.advance(3)
    second.advance(3)
    third.begin()
    tail.from_chip(0)
    tail.begin()
    tail.begin_other()
    second.from_chip(1)
    second.to_chip(2)
    first.from_chip(2)
    first.to_chip(3)
    third.advance(1)
    second.from_chip(2)
    second.to_chip(3)
    third.to_chip(0)
    tail.advance(1)
    third.advance(2)
    first.from_chip(3)
    third.to_chip(1)
    for copy in attention:
        copy.wait_recv()
    att = part[...].astype(F32)
    for j in range(1, tp):
        att = att + land[j - 1].astype(F32)
    v = x_land[...].astype(F32)
    squares[0:1, :] = jnp.sum(v * v, axis=0, keepdims=True)
    squares[1:2, :] = jnp.sum(att * att, axis=0, keepdims=True)
    mid[...] = v + att
    store(mid.at[:, block_rows(place.t, feat)], mid_own)
    v = (v + att).astype(BF).astype(F32)
    nb[...] = (v * row_scale(v) * gain_ffn[...]).astype(BF)
    store(nb, normed_two)
    ffn_acc[...] = jnp.zeros_like(ffn_acc)
    dn_acc[...] = jnp.zeros_like(dn_acc)
    third.to_chip(2)
    third.from_chip(0)
    for copy in wide_y:
        copy.wait_recv()
    store(y_land, dy)

    def one_tile(i):
        at = lambda m: block_rows(3 * i + m, tile)
        w_gate, w_up, w_down = w_ffn[:, at(0)], w_ffn[:, at(1)], w_ffn[:, at(2)]
        gate = dot(nb[...], w_gate, 1, 0)
        up = dot(nb[...], w_up, 1, 0)
        d_hidden = dot(y_land[...], w_down, 1, 0)
        sig = 1.0 / (1.0 + jnp.exp(-gate))
        silu = gate * sig
        out = block_rows(i, tile)
        acts[0, :, out] = (silu * up).astype(BF)
        acts[1, :, out] = (d_hidden * up * (sig * (1.0 + gate * (1.0 - sig)))).astype(BF)
        acts[2, :, out] = (d_hidden * silu).astype(BF)
        ffn_acc[...] += dot(acts[0, :, out], w_down, 1, 1)
        dn_acc[...] += dot(acts[1, :, out], w_gate, 1, 1) + dot(acts[2, :, out], w_up, 1, 1)

    act_stores = []
    for i, g in enumerate(groups + [tail]):
        if i == 1:
            tail.advance(2)
            third.advance(3)
            third.to_chip(3)
            second.from_chip(3)
            third.from_chip(1)
        if i == 2:
            tail.advance(3)
            third.from_chip(2)
            third.from_chip(3)
        g.finish()
        repeat(cuts[i + 1] - cuts[i], lambda k, i=i: one_tile(cuts[i] + k))
        cols = pl.ds(cuts[i] * tile, (cuts[i + 1] - cuts[i]) * tile)
        for m, out in enumerate((hidden, d_gate, d_up)):
            copy = pltpu.make_async_copy(acts.at[m, :, cols], out.at[:, cols], act_sem.at[m, i])
            copy.start()
            act_stores.append(copy)
    dgain[...] = jnp.zeros_like(dgain)

    def finish_rows(i):
        r = block_rows(i, 128)
        v = mid[r, :].astype(BF).astype(F32)
        grad, gain_sum = norm_back(dn_acc[r, :], v, gain_ffn[...])
        dgain[...] += gain_sum
        dmid[r, :] = grad.astype(BF)
        ffn_out[r, :] = ffn_acc[r, :].astype(BF)

    repeat(rows // 128, finish_rows)

    @pl.when(core_bit == 0)
    def _():
        near.wait_send()

    @pl.when(x_bit == 0)
    def _():
        across.wait_send()

    @pl.when(x_bit == 1)
    def _():
        passed.wait_send()

    store(kv_all, kv)
    for copy in route_x + route_y + wide_x + wide_y + attention:
        copy.wait_send()
    for g in [attn, tail] + groups:
        g.drain()
    for copy in stores + act_stores:
        copy.wait()


def start_keys(place, kv_all, own_rows, send, recv):
    x_bit, core_bit = place.c // 2, lax.rem(place.c, 2)
    mine = kv_all.at[own_rows, :]
    near = remote(mine, mine, send.at[0], recv.at[0], place.at(c=place.flip(1)))
    across = remote(mine, mine, send.at[1], recv.at[1], place.at(c=place.flip(2)))
    from_chip = kv_all.at[block_rows(place.flip(2), own_rows.size), :]
    passed = remote(from_chip, from_chip, send.at[2], recv.at[2], place.at(c=place.flip(1)))

    @pl.when(x_bit == 0)
    def _():
        across.start()

    @pl.when(core_bit == 0)
    def _():
        near.start()

    return near, across, passed


def forward_pass(grid, q_width, kv_width, tile, *operands):
    tokens, w_query, w_key, w_gate = operands[1], operands[8], operands[9], operands[12]
    rows, feat = tokens.shape
    n, ctx, tp = grid.n, grid.ctx, grid.tp
    width = feat * tp
    n_pairs = q_width // 128
    row_len = rows * ctx
    ff = -(-w_gate.shape[1] // tile) * tile
    vm = pl.BlockSpec(memory_space=pltpu.VMEM)
    dma = pltpu.SemaphoreType.DMA
    V = pltpu.VMEM
    group = n * ctx
    attn_width = 2 * w_query.shape[1] + 2 * w_key.shape[1]
    return pl.pallas_call(
        functools.partial(forward_kernel, n, ctx, tp, q_width, kv_width, tile),
        in_specs=[pl.BlockSpec(memory_space=pltpu.SMEM)] + [vm] * 14,
        out_specs=[vm] * 9 + [ANYWHERE] * 11,
        out_shape=[
            shape((n_pairs, 8, 2 * rows), F32),
            shape((2, width), F32),
            shape((rows, width), BF),
            shape((rows, width), BF),
            shape((1, width), F32),
            shape((rows, rows), BF),
            shape((rows, rows), BF),
            shape((rows, 128), F32),
            shape((rows, 128), F32),
            shape((rows, width), BF),
            shape((rows, width), BF),
            shape((rows, q_width), BF),
            shape((row_len, 2 * kv_width), BF),
            shape((rows, q_width), F32),
            shape((rows, feat), F32),
            shape((width, attn_width), BF),
            shape((rows, width), BF),
            shape((rows, ff), BF),
            shape((rows, ff), BF),
            shape((rows, ff), BF),
        ],
        scratch_shapes=[V((rows, feat), BF)] * 6
        + [
            V((rows, width), BF),
            V((rows, width), BF),
            V((rows, rows), BF),
            V((rows, q_width), BF),
            V((rows, q_width), F32),
            V((rows, width), F32),
            V((rows, width), BF),
            V((width, attn_width), BF),
            V((width, 3 * ff), BF),
            V((row_len, 2 * kv_width), BF),
            V((rows, width), BF),
            V((tp - 1, rows, width), BF),
            V((n_pairs, 2 * rows, 128), F32),
            V((n_pairs, 2 * rows, 128), F32),
            V((rows, rows), F32),
            V((rows, width), F32),
            V((rows, width), F32),
            V((3, rows, ff), BF),
            dma((2, group)),
            dma((2, group)),
            dma((3, tp)),
            dma((3, tp)),
            dma((3,)),
            dma((3,)),
            dma((8,)),
            dma((3, 4)),
            dma((6, n)),
            dma((6, n)),
            dma((5, n)),
            dma((5, n)),
            dma((5, 2 * n)),
            dma((5, 2 * n)),
        ],
        compiler_params=pltpu.CompilerParams(
            vmem_limit_bytes=61 * 2**20, collective_id=0, has_side_effects=True
        ),
        cost_estimate=pl.CostEstimate(
            flops=12 * rows * width * ff, bytes_accessed=40 * 2**20, transcendentals=0
        ),
    )(*operands)


def repeat(count, body):
    def step(i, carry):
        body(i)
        return carry

    lax.fori_loop(0, count, step, 0)


def add_into(to, more):
    step = 16

    def add(i):
        at = block_rows(i, step)
        to[at, :] = (to[at, :].astype(F32) + more[at, :].astype(F32)).astype(to.dtype)

    repeat(to.shape[0] // step, add)


def turn_blocks(place, source, turned):
    width = source.shape[1]
    n = place.n
    h = width // (n * place.ctx)
    first = lax.rem(place.c, 2) == 0

    def turn(i):
        chip = lax.rem(place.c // 2 + i // n, 2)
        pair = lax.rem(place.z - lax.rem(i, n) + n, n) * (place.ctx // 2) + chip
        block = source[:, block_rows(pair, 2 * h)].astype(F32).T.astype(turned.dtype)
        low, high = block[:h], block[h:]
        turned[block_rows(i, h), :] = jnp.where(first, low, high)
        turned[block_rows(i + 2 * n, h), :] = jnp.where(first, high, low)

    repeat(2 * n, turn)


class Scatter:
    def __init__(
        self, place, keep, columns, chip_land, line_land, number, sems, line_first=False
    ):
        x_send, x_recv, z_send, z_recv = sems
        n = place.n
        self.n, self.line_first = n, line_first
        self.h = h = keep.shape[0] // (2 * n)
        self.keep = [keep.at[pl.ds(k * h, h), columns] for k in range(2 * n)]
        land = [chip_land.at[pl.ds(k * h, h), columns] for k in range(n)]
        line = [line_land.at[k, :, columns] for k in range(n - 1)]
        there = place.at(c=place.flip(2))

        def ring(blocks, lands, row):
            return [
                remote(blocks[k], lands[k - 1], z_send.at[row, k], z_recv.at[row, k], place.up(1))
                for k in range(1, n)
            ]

        self.rings = [(ring(self.keep[:n], line, number), self.keep[:n], line)]
        if line_first:
            self.rings.append((ring(self.keep[n:], land[1:], number + 1), self.keep[n:], land[1:]))
            self.chip = remote(
                self.keep[n], land[0], x_send.at[number], x_recv.at[number], there
            )
            self.chip_land = land[:1]
        else:
            self.chip = remote(
                keep.at[pl.ds(n * h, n * h), columns],
                chip_land.at[:, columns],
                x_send.at[number],
                x_recv.at[number],
                there,
            )
            self.chip_land = land

    def to_chip(self):
        self.chip.start()

    def from_chip(self):
        self.chip.wait_recv()
        if self.line_first:
            return
        for k in list(range(1, self.n)) + [0]:
            add_into(self.keep[k], self.chip_land[k])
            if k == 1:
                self.begin()

    def begin(self):
        for ring, _, _ in self.rings:
            if ring:
                ring[0].start()

    def advance(self, k):
        if k >= self.n:
            return
        for ring, blocks, lands in self.rings:
            ring[k - 1].wait_recv()
            if k + 1 < self.n:
                add_into(blocks[k + 1], lands[k - 1])
                ring[k].start()
            elif self.line_first:
                add_into(blocks[0], lands[k - 1])

    def finish(self, out):
        last = self.chip_land[0] if self.line_first else self.rings[0][2][self.n - 2]
        step = 16

        def add(i):
            at = block_rows(i, step)
            out[at, :] = self.keep[0][at, :].astype(F32) + last[at, :].astype(F32)

        repeat(self.h // step, add)

    def drain(self):
        self.chip.wait_send()
        for ring, _, _ in self.rings:
            for copy in ring:
                copy.wait_send()


def core_sum(keep, core_land, copy):
    copy.wait_recv()
    add_into(keep, core_land)


def backward_kernel(
    n, ctx, tp, q_width, kv_width, stage_cols,
    lengths, ffn, dmid, sums, cosines, sines, pick_t, gain, head_gain,
    gain_ffn_grad, squares, qb_in, kv_in, heads_in, w_in, dy_in, x_in, mid_in, normed_two, hidden, d_gate, d_up,
    back_o, back_g, sum_gate, sum_up, sum_down, sum_out, sum_qkv, small,
    qb, kv_all, heads, w, x, turned, stage, keep, send, core_land, chip_land, line_land,
    o_keep, o_send, o_core, o_chip, o_line, a_keep, a_send, a_core, a_chip, a_line,
    d_mid_own, d_attn, dob, delta, bias, dq_t, dkv, kv_land, tp_land, ffn_away, ffn_land, dx_away, dx_land,
    sent, small_mine, small_land, small_side,
    tp_send, tp_recv, route_send, route_recv, small_send, small_recv, kv_send, kv_recv, load_sem,
    free_sem, *scatter_sems
):
    place = Place(n, ctx, tp)
    group = n * ctx
    rows, width = dmid.shape
    feat = width // tp
    share = rows // group
    piece = rows
    ff = hidden.shape[1]
    half = width // 2
    n_pairs = q_width // 128
    qkv_width = q_width + 2 * kv_width
    values_from = q_width + kv_width
    x_bit, core_bit = place.c // 2, lax.rem(place.c, 2)
    own_cols = block_rows(place.t, feat)
    c_send, c_recv, *ring_sems = scatter_sems
    everything = pl.ds(0, ff)
    lands = lambda m: (chip_land.at[m], line_land.at[m])
    cut = ff // 128 * 11 // 18 * 128
    down = Scatter(place, keep.at[0], pl.ds(0, cut), *lands(0), 0, ring_sems, True)
    down_x = Scatter(place, keep.at[0], pl.ds(cut, ff - cut), *lands(0), 6, ring_sems)
    gate = Scatter(place, keep.at[1], everything, *lands(1), 2, ring_sems)
    up = Scatter(place, keep.at[2], everything, *lands(2), 3, ring_sems)
    out_sum = Scatter(place, o_keep, pl.ds(0, q_width), o_chip, o_line, 4, ring_sems)
    qkv_sum = Scatter(place, a_keep, pl.ds(0, qkv_width), a_chip, a_line, 5, ring_sems)
    across_cores = [
        remote(src, dst, c_send.at[i], c_recv.at[i], place.at(c=place.flip(1)))
        for i, (src, dst) in enumerate(
            [(send.at[m % 2], core_land.at[m % 2]) for m in range(3)]
            + [(o_send, o_core), (a_send, a_core)]
        )
    ]

    def to_sides(number, src, dst):
        return [
            remote(
                src(j), dst.at[j - 1], tp_send.at[number, j], tp_recv.at[number, j], place.side(j)
            )
            for j in range(1, tp)
        ]

    def away(buffer):
        return lambda j: buffer.at[j - 1]

    def fill_away(buffer, source):
        for j in range(1, tp):
            buffer[j - 1] = source[:, block_rows(lax.rem(place.t + j, tp), feat)]

    def route(number, src, dst):
        return [
            remote(
                src.at[block_rows(lax.rem(place.me + j, group), share), :],
                dst.at[block_rows(place.me, share), :],
                route_send.at[number, j],
                route_recv.at[number, j],
                place.peer(j),
            )
            for j in range(1, group)
        ]

    dmid_sum = to_sides(0, lambda j: dmid, tp_land)
    ffn_sum = to_sides(1, away(ffn_away), ffn_land)
    dx_sum = to_sides(2, away(dx_away), dx_land)
    route_o, route_g = route(0, sent, back_o), route(1, dob, back_g)

    place.greet()
    for copy in dmid_sum:
        copy.start()

    sources = (hidden, d_gate, d_up)
    tiles = [(m, b) for m in range(3) for b in range(0, ff, stage_cols)]
    loads = [
        pltpu.make_async_copy(
            sources[m].at[:, pl.ds(b, stage_cols)], stage.at[i % 2], load_sem.at[i]
        )
        for i, (m, b) in enumerate(tiles)
    ]
    load_n = pltpu.make_async_copy(normed_two, d_attn, load_sem.at[len(tiles)])
    dy, mid = x, d_mid_own
    load_dy = pltpu.make_async_copy(dy_in, dy, load_sem.at[len(tiles) + 1])
    load_x = pltpu.make_async_copy(x_in, x, load_sem.at[len(tiles) + 2])
    load_mid = pltpu.make_async_copy(mid_in, mid, load_sem.at[len(tiles) + 3])
    load_dy.start()
    loads[0].start()
    load_n.start()
    load_mid.start()
    more_loads = [
        pltpu.make_async_copy(src, dst, load_sem.at[len(tiles) + 5 + i])
        for i, (src, dst) in enumerate(((w_in, w), (qb_in, qb), (kv_in, kv_all), (heads_in, heads)))
    ]
    for copy in more_loads:
        copy.start()
    fill_away(ffn_away, ffn)
    load_dy.wait()
    turn_blocks(place, dy, turned)
    sub = 256 if stage_cols % 256 == 0 else 128
    for i, (m, b) in enumerate(tiles):
        if i + 1 < len(tiles):
            loads[i + 1].start()
        if b == 0 and m == 1:
            load_n.wait()
            turn_blocks(place, d_attn, turned)
        if m == 1 and b == ff // 2 // stage_cols * stage_cols:
            core_sum(keep.at[0], core_land.at[0], across_cores[0])
            down.begin()
            down_x.to_chip()
            pl.semaphore_signal(
                free_sem, inc=1, device_id=place.at(c=place.flip(1)), device_id_type=MESH
            )
        if b == 0 and m == 2:
            across_cores[0].wait_send()
        if m == 2 and b == ff // 2 // stage_cols * stage_cols:
            core_sum(keep.at[1], core_land.at[1], across_cores[1])
            gate.to_chip()
        loads[i].wait()
        for s in range(0, stage_cols, sub):
            right = stage[i % 2, :, s : s + sub]
            cols = slice(b + s, b + s + sub)
            keep[m, :, cols] = dot(turned[:half, :], right, 1, 0).astype(BF)
            send[m % 2, :, cols] = dot(turned[half:, :], right, 1, 0).astype(BF)
        if b + stage_cols == ff:
            if m == 2:
                pl.semaphore_wait(free_sem, 1)
            across_cores[m].start()
    core_sum(keep.at[2], core_land.at[0], across_cores[2])

    for copy in more_loads:
        copy.wait()
    for copy in dmid_sum:
        copy.wait_recv()
    for copy in ffn_sum:
        copy.start()

    def sum_gradient(i):
        r = block_rows(i, 128)
        d_all = dy[r, :].astype(F32) + dmid[r, :].astype(F32)
        for j in range(1, tp):
            d_all = d_all + tp_land[j - 1, r, :].astype(F32)
        d_attn[r, :] = d_all.astype(BF)

    repeat(rows // 128, sum_gradient)
    dob[...] = dot(d_attn[...], w[:, qkv_width:], 1, 0).astype(BF)
    dq_t[...] = jnp.zeros_like(dq_t)
    ones = jnp.ones((8, 128), F32)

    def set_delta(g):
        both = dob[:, lane_block(g)].astype(F32) * heads[:, lane_block(g)]
        delta[g] = dot(ones, two_heads(both), 1, 1, lax.Precision.HIGHEST)

    repeat(n_pairs, set_delta)
    q_slot = place.c * piece + lanes((piece, rows))
    start_row = segment_start(lengths, place.c * piece + lanes((8, rows)))[:1]

    def one_piece(p):
        k_slot = p * piece + lax.broadcasted_iota(jnp.int32, (piece, rows), 0)
        open_ = (k_slot >= start_row) & (k_slot <= q_slot)
        bias[...] = jnp.where(open_, 0.0, NEG_FILL)
        at = block_rows(p, piece)
        def heads_of(members):
            grads = []
            for g, (kb, ke), (vb, ve) in members:
                q2 = two_heads(qb[:, lane_block(g)])
                do2 = two_heads(dob[:, lane_block(g)])
                k2 = twice(kv_all[at, lane_block(kb)], ke)
                v2 = twice(kv_all[at, lane_block(vb)], ve)
                k_t = k2.astype(F32).T.astype(BF)
                dk = jnp.zeros((piece, 128), F32)
                dv = jnp.zeros((piece, 128), F32)
                for h in range(0, 2 * rows, 256):
                    part = slice(h, h + 256)
                    open_part = slice(h % rows, h % rows + 256)
                    s = dot(k2, q2[part], 1, 1)
                    dp = dot(v2, do2[part], 1, 1)
                    pe = jnp.exp(s * 0.125 + bias[:, open_part]) * sums[g, 0:1, part]
                    ds = (pe * (dp - delta[g, 0:1, part])).astype(BF)
                    dv = dv + dot(pe.astype(BF), do2[part], 1, 0)
                    dk = dk + dot(ds, q2[part], 1, 0)
                    dq_t[g, :, part] += dot(k_t, ds, 1, 0)
                grads.append((both_halves(dk) * 0.125, both_halves(dv)))
            low = lanes((piece, 128)) < HEAD_SIZE
            kb, vb = members[0][1][0], members[0][2][0]
            if len(members) == 2:
                dkv[at, lane_block(kb)] = jnp.where(low, grads[0][0], grads[1][0]).astype(BF)
                dkv[at, lane_block(vb)] = jnp.where(low, grads[0][1], grads[1][1]).astype(BF)
            else:
                for value, (b, e) in zip(grads[0], members[0][1:]):
                    c = 128 * b + HEAD_SIZE * e
                    dkv[at, c : c + HEAD_SIZE] = value[:, :HEAD_SIZE].astype(BF)

        over_key_heads(n_pairs, kv_width // HEAD_SIZE, heads_of)

    down.advance(1)
    down_x.from_chip()

    sibling = place.at(c=place.flip(1))
    other = 1 - core_bit
    to_passer = remote(
        dkv.at[block_rows(other, piece), :], kv_land.at[0], kv_send.at[0], kv_recv.at[0], sibling
    )
    to_chip = remote(
        dkv.at[block_rows(core_bit, piece), :],
        kv_land.at[0],
        kv_send.at[1],
        kv_recv.at[1],
        place.at(c=place.flip(2)),
    )
    to_core = remote(
        dkv.at[block_rows(2 * x_bit, piece), :], kv_land.at[1], kv_send.at[2], kv_recv.at[2], sibling
    )

    @pl.when(x_bit == 1)
    def _():
        def step(p, carry):
            one_piece(p)
            return carry

        lax.fori_loop(0, 2, step, 0)
        to_passer.start()

    turn_blocks(place, d_attn, turned)
    right = heads[...].astype(BF)
    o_keep[...] = dot(turned[:half, :], right, 1, 0).astype(BF)
    o_send[...] = dot(turned[half:, :], right, 1, 0).astype(BF)
    across_cores[3].start()
    down.advance(2)
    down_x.advance(1)

    @pl.when(x_bit == 1)
    def _():
        to_passer.wait_recv()
        mine = block_rows(core_bit, piece)
        dkv[mine, :] = (dkv[mine, :].astype(F32) + kv_land[0].astype(F32)).astype(BF)
        to_chip.start()

    gate.from_chip()

    @pl.when(x_bit == 0)
    def _():
        up.to_chip()

    core_sum(o_keep, o_core, across_cores[3])
    out_sum.to_chip()

    @pl.when(core_bit == 1)
    def _():
        one_piece(place.c - 1)
        to_core.start()

    for copy in ffn_sum:
        copy.wait_recv()
    small_mine[...] = jnp.zeros_like(small_mine)
    load_mid.wait()

    def finish_output(i):
        r = block_rows(i, 128)
        ffn_out = ffn[r, own_cols].astype(F32)
        for j in range(1, tp):
            ffn_out = ffn_out + ffn_land[j - 1, r, :].astype(F32)
        small_mine[5:6, :feat] += jnp.sum(ffn_out * ffn_out, axis=0, keepdims=True)
        dx_away[0, r, :] = (mid[r, :] + ffn_out).astype(BF)

    repeat(rows // 128, finish_output)
    sent[...] = dot(pick_t[...], dx_away[0], 1, 0).astype(BF)
    for copy in route_o:
        copy.start()
    own = block_rows(place.me, share)
    back_o[own, :] = sent[own, :]


    def own_gradient(i):
        r = block_rows(i, 128)
        d_own = dy[r, own_cols].astype(F32) + dmid[r, own_cols].astype(F32)
        for j in range(1, tp):
            d_own = d_own + tp_land[j - 1, r, own_cols].astype(F32)
        d_mid_own[r, :] = d_own

    repeat(rows // 128, own_gradient)
    load_x.start()

    @pl.when(x_bit == 1)
    def _():
        to_chip.wait_send()
        up.to_chip()

    one_piece(place.c)
    down.advance(3)
    down.to_chip()
    down_x.advance(2)
    gate.advance(1)
    normed = tp_land.at[0]
    load_x.wait()

    def norm_again(i):
        v = x[block_rows(i, 128), :].astype(F32)
        normed[block_rows(i, 128), :] = (v * row_scale(v) * gain[...]).astype(BF)

    repeat(rows // 128, norm_again)
    turn_blocks(place, normed, turned)
    mine = block_rows(place.c, piece)

    @pl.when(core_bit == 0)
    def _():
        to_core.wait_recv()

    @pl.when(x_bit == 0)
    def _():
        to_chip.wait_recv()

    d_qkv = d_attn.at[:, pl.ds(0, qkv_width)]
    for b in range(0, qkv_width, 128):
        if b < q_width:
            g = b // 128
            grad = one_row(dq_t[g].T) * 0.125
        else:
            cols = slice(b - q_width, b - q_width + 128)
            grad = dkv[mine, cols].astype(F32)
            grad = jnp.where(x_bit == 0, grad + kv_land[0, :, cols].astype(F32), grad)
            grad = jnp.where(core_bit == 0, grad + kv_land[1, :, cols].astype(F32), grad)
        raw = dot(normed[...], w[:, b : b + 128], 1, 0)
        is_value = lanes(grad.shape) + b >= values_from
        back, gain_grad = qk_backward(
            grad, raw, head_gain[:, b : b + 128], cosines[...], sines[...], is_value
        )
        small_mine[2:3, b : b + 128] = gain_grad
        d_qkv[:, b : b + 128] = back.astype(BF)

    def finish_gradient(i):
        r = block_rows(i, 128)
        dn = dot(d_qkv[r, :], w[:, :qkv_width], 1, 1)
        dx, gain_grad = norm_back(dn, x[r, :].astype(F32), gain[...])
        normed[r, :] = dx.astype(BF)
        small_mine[0:1, :] += gain_grad

    repeat(rows // 128, finish_gradient)
    fill_away(dx_away, normed)
    for copy in dx_sum:
        copy.start()
    small_mine[1:2, :] = gain_ffn_grad[...]
    small_mine[3:5, :] = squares[...]
    for b in range(0, qkv_width, 256):
        cols = slice(b, b + 256)
        a_keep[:, cols] = dot(turned[:half, :], d_qkv[:, cols], 1, 0).astype(BF)
        a_send[:, cols] = dot(turned[half:, :], d_qkv[:, cols], 1, 0).astype(BF)
    across_cores[4].start()
    down_x.advance(3)
    gate.advance(2)
    small_out = [
        remote(
            small_mine, small_land.at[place.me], small_send.at[0, j], small_recv.at[0, j], place.peer(j)
        )
        for j in range(1, group)
    ]
    for copy in small_out:
        copy.start()
    small_land[place.me] = small_mine[...]
    core_sum(a_keep, a_core, across_cores[4])
    qkv_sum.to_chip()
    out_sum.from_chip()
    up.from_chip()

    for copy in dx_sum:
        copy.wait_recv()
    for copy in ffn_sum:
        copy.wait_send()

    def finish_input(i):
        r = block_rows(i, 128)
        total = d_mid_own[r, :] + normed[r, own_cols].astype(F32)
        for j in range(1, tp):
            total = total + dx_land[j - 1, r, :].astype(F32)
        ffn_away[0, r, :] = total.astype(BF)

    repeat(rows // 128, finish_input)
    dob[...] = dot(pick_t[...], ffn_away[0], 1, 0).astype(BF)
    for copy in route_g:
        copy.start()
    back_g[own, :] = dob[own, :]
    gate.advance(3)
    out_sum.advance(1)
    up.advance(1)
    qkv_sum.from_chip()
    gate.finish(sum_gate)
    out_sum.advance(2)
    up.advance(2)
    qkv_sum.advance(1)
    down.from_chip()
    down.finish(sum_down.at[:, pl.ds(0, cut)])
    down_x.finish(sum_down.at[:, pl.ds(cut, ff - cut)])
    out_sum.advance(3)
    up.advance(3)
    qkv_sum.advance(2)
    out_sum.finish(sum_out)
    up.finish(sum_up)
    for copy in small_out:
        copy.wait_recv()
    total = small_land[0]
    for i in range(1, group):
        total = total + small_land[i]
    small_side[place.t] = total
    for copy in small_out:
        copy.wait_send()
    small_mine[...] = total
    sides = [
        remote(
            small_mine, small_side.at[place.t], small_send.at[1, j], small_recv.at[1, j], place.side(j)
        )
        for j in range(1, tp)
    ]
    for copy in sides:
        copy.start()
    for copy in sides:
        copy.wait_recv()
    total = small_side[0]
    for j in range(1, tp):
        total = total + small_side[j]
    small[...] = total
    for copy in route_o:
        copy.wait_recv()
    qkv_sum.advance(3)
    qkv_sum.finish(sum_qkv)
    for copy in route_g:
        copy.wait_recv()

    @pl.when(x_bit == 1)
    def _():
        to_passer.wait_send()

    @pl.when(core_bit == 1)
    def _():
        to_core.wait_send()

    for copy in dmid_sum + dx_sum + route_o + route_g + sides:
        copy.wait_send()
    for copy in across_cores[1:]:
        copy.wait_send()
    for s in (down, down_x, gate, up, out_sum, qkv_sum):
        s.drain()


def backward_pass(grid, q_width, kv_width, *operands):
    dmid, hidden = operands[2], operands[19]
    rows, width = dmid.shape
    ff = hidden.shape[1]
    n, ctx, tp = grid.n, grid.ctx, grid.tp
    group = n * ctx
    feat = width // tp
    half = width // 2
    h = width // group
    n_pairs = q_width // 128
    qkv_width = q_width + 2 * kv_width
    stage_cols = 256 if ff % 256 == 0 else 128
    vm = pl.BlockSpec(memory_space=pltpu.VMEM)
    dma = pltpu.SemaphoreType.DMA
    V = pltpu.VMEM

    def scatter_space(cols):
        return [
            V((half, cols), BF),
            V((half, cols), BF),
            V((half, cols), BF),
            V((half // 2, cols), BF),
            V((n - 1, h, cols), BF),
        ]

    return pl.pallas_call(
        functools.partial(backward_kernel, n, ctx, tp, q_width, kv_width, stage_cols),
        in_specs=[pl.BlockSpec(memory_space=pltpu.SMEM)] + [vm] * 10 + [ANYWHERE] * 11,
        out_specs=[vm] * 8,
        out_shape=[
            shape((rows, feat), BF),
            shape((rows, feat), BF),
            shape((h, ff), F32),
            shape((h, ff), F32),
            shape((h, ff), F32),
            shape((h, q_width), F32),
            shape((h, qkv_width), F32),
            shape((8, width), F32),
        ],
        scratch_shapes=[
            V((rows, q_width), BF),
            V((rows * ctx, 2 * kv_width), BF),
            V((rows, q_width), F32),
            V((width, q_width + qkv_width), BF),
            V((rows, width), BF),
            V((width, rows), BF),
            V((2, rows, stage_cols), BF),
            V((3, half, ff), BF),
            V((2, half, ff), BF),
            V((2, half, ff), BF),
            V((3, half // 2, ff), BF),
            V((3, n - 1, h, ff), BF),
        ]
        + scatter_space(q_width)
        + scatter_space(qkv_width)
        + [
            V((rows, feat), F32),
            V((rows, width), BF),
            V((rows, q_width), BF),
            V((n_pairs, 8, 2 * rows), F32),
            V((rows, rows), F32),
            V((n_pairs, 128, 2 * rows), F32),
            V((rows * ctx, 2 * kv_width), BF),
            V((2, rows, 2 * kv_width), BF),
            V((tp - 1, rows, width), BF),
            V((tp - 1, rows, feat), BF),
            V((tp - 1, rows, feat), BF),
            V((tp - 1, rows, feat), BF),
            V((tp - 1, rows, feat), BF),
            V((rows, feat), BF),
            V((8, width), F32),
            V((group, 8, width), F32),
            V((tp, 8, width), F32),
            dma((3, tp)),
            dma((3, tp)),
            dma((2, group)),
            dma((2, group)),
            dma((2, max(group, tp))),
            dma((2, max(group, tp))),
            dma((3,)),
            dma((3,)),
            dma((3 * (ff // stage_cols) + 9,)),
            pltpu.SemaphoreType.REGULAR,
            dma((5,)),
            dma((5,)),
            dma((7,)),
            dma((7,)),
            dma((7, n)),
            dma((7, n)),
        ],
        compiler_params=pltpu.CompilerParams(
            vmem_limit_bytes=61 * 2**20, collective_id=1, has_side_effects=True
        ),
        cost_estimate=pl.CostEstimate(
            flops=20 * rows * rows * ctx * q_width, bytes_accessed=40 * 2**20, transcendentals=0
        ),
    )(*operands)


def output_kernel(
    tp, entries, place_o, place_g, send_back, gate, up, down, out, qkv, small,
    output, grad_tokens, g_query, g_key, g_value, g_out, g_gate, g_up, g_down,
    gain_a, gain_f, gain_q, gain_k, stats
):
    a, b = g_query.shape[1], g_query.shape[1] + g_key.shape[1]
    output[...] = dot(send_back[...], place_o[...], 1, 0).astype(BF)
    grad_tokens[...] = dot(send_back[...], place_g[...], 1, 0).astype(BF)
    g_query[...] = qkv[:, :a]
    g_key[...] = qkv[:, a:b]
    g_value[...] = qkv[:, b:]
    g_out[...] = out[...]
    ff = g_gate.shape[1]
    g_gate[...] = gate[:, :ff]
    g_up[...] = up[:, :ff]
    g_down[...] = down[:, :ff]
    gain_a[...] = small[0:1, :]
    gain_f[...] = small[1:2, :]

    def heads_sum(first, last):
        total = jnp.zeros((1, HEAD_SIZE), F32)
        for c in range(first, last, HEAD_SIZE):
            total = total + small[2:3, c : c + HEAD_SIZE]
        return total

    gain_q[...] = heads_sum(0, a)
    gain_k[...] = heads_sum(a, b)
    row = lanes((1, 128))
    x_sum, attn_sum, ffn_sum = (
        jnp.sum(small[3 + i : 4 + i, :], axis=1, keepdims=True) for i in range(3)
    )
    total = jnp.where(row == 0, x_sum / tp, jnp.where(row == 1, attn_sum / tp, ffn_sum))
    stats[...] = jnp.sqrt(total * (1.0 / entries))


def output_pass(grid, shapes, *operands):
    rows = operands[0].shape[0]
    entries = rows * grid.n * grid.ctx * MODEL_WIDTH
    row = lambda n: shape((1, n), F32)
    vm = pl.BlockSpec(memory_space=pltpu.VMEM)
    outs = (
        [shape(operands[0].shape, BF)] * 2
        + [shape(s, F32) for s in shapes]
        + [row(MODEL_WIDTH), row(MODEL_WIDTH), row(HEAD_SIZE), row(HEAD_SIZE), row(128)]
    )
    return pl.pallas_call(
        functools.partial(output_kernel, grid.tp, entries),
        in_specs=[vm] * len(operands),
        out_specs=[vm] * len(outs),
        out_shape=outs,
        compiler_params=pltpu.CompilerParams(vmem_limit_bytes=60 * 2**20),
    )(*operands)


def local(
    tokens,
    cotangent,
    slot_of,
    lengths,
    w_query,
    key_weight,
    value_weight,
    w_out,
    w_gate,
    w_up,
    w_down,
    gain_attn,
    gain_ffn,
    gain_query,
    gain_key,
):
    grid = Grid()
    rows, feat_len = tokens.shape
    q_heads = QUERY_HEADS // grid.tp
    key_value_heads = KEY_VALUE_HEADS // grid.tp
    q_width = q_heads * HEAD_SIZE
    kv_width = key_value_heads * HEAD_SIZE
    ff = w_gate.shape[1]
    tile = 256 if ff % 256 == 0 else 128
    head_gain = jnp.concatenate(
        [
            jnp.tile(gain_query, q_heads),
            jnp.tile(gain_key, key_value_heads),
            jnp.ones((kv_width,), F32),
        ]
    )[None, :]
    frequency = ROPE_THETA ** (-np.arange(0, HEAD_SIZE, 2, dtype=np.float64) / HEAD_SIZE)
    frequency = jnp.asarray(np.tile(frequency, 4)[None, :], F32)
    (
        sums, squares, ffn_part, d_mid_part, d_gain_ffn, take_back, send_back, cosines, sines,
        x_full, dy_full, qb, row_kv, heads, middle_own, attn_w, normed_two, hidden, d_gate, d_up,
    ) = forward_pass(
        grid,
        q_width,
        kv_width,
        tile,
        lengths,
        tokens,
        cotangent,
        slot_of.reshape(-1, 128),
        gain_attn[None, :],
        head_gain,
        gain_ffn[None, :],
        frequency,
        w_query,
        key_weight,
        value_weight,
        w_out.T,
        w_gate,
        w_up,
        w_down.T,
    )
    place_o, place_g, sum_gate, sum_up, sum_down, sum_out, sum_qkv, small = backward_pass(
        grid,
        q_width,
        kv_width,
        lengths,
        ffn_part,
        d_mid_part,
        sums,
        cosines,
        sines,
        take_back,
        gain_attn[None, :],
        head_gain,
        d_gain_ffn,
        squares,
        qb,
        row_kv,
        heads,
        attn_w,
        dy_full,
        x_full,
        middle_own,
        normed_two,
        hidden,
        d_gate,
        d_up,
    )
    weights = (w_query, key_weight, value_weight, w_out.T, w_gate, w_up, w_down.T)
    *outs, gain_a, gain_f, gain_q, gain_k, stats = output_pass(
        grid,
        [v.shape for v in weights],
        place_o,
        place_g,
        send_back,
        sum_gate,
        sum_up,
        sum_down,
        sum_out,
        sum_qkv,
        small,
    )
    outs[5], outs[8] = outs[5].T, outs[8].T
    return (*outs, gain_a[0], gain_f[0], gain_q[0], gain_k[0], stats[0, :3])


def solution(mesh):
    row = P(("fsdp", "ctx"), "tp")
    column = P("tp", ("fsdp", "ctx"))
    in_specs = (row, row, P(), P("fsdp", None), row, row, row, column, row, row, column) + (P(),) * 4
    out_specs = (row, row, row, row, row, column, row, row, column) + (P(),) * 5
    return jax.shard_map(local, mesh=mesh, in_specs=in_specs, out_specs=out_specs, check_vma=False)
```

```python
import functools

import jax
import jax.numpy as jnp
import numpy as np
from jax import lax
from jax.experimental import pallas as pl
from jax.experimental.pallas import tpu as pltpu
from jax.sharding import PartitionSpec as P

MODEL_WIDTH = 1024
QUERY_HEADS = 16
KEY_VALUE_HEADS = 8
HEAD_SIZE = 64

EPSILON = 1e-05
ROPE_THETA = 1000000.0
NEG_FILL = -1e30
BF = jnp.bfloat16
F32 = jnp.float32


class Grid:
    def __init__(self):
        self.n = lax.axis_size("fsdp")
        self.ctx = lax.axis_size("ctx")
        self.tp = lax.axis_size("tp")
        self.z = lax.axis_index("fsdp")
        self.c = lax.axis_index("ctx")
        self.t = lax.axis_index("tp")


def shape(s, t):
    return jax.ShapeDtypeStruct(s, t)


ANYWHERE = pl.BlockSpec(memory_space=pl.ANY)


def dot(a, b, ca, cb, precision=None):
    return lax.dot_general(
        a, b, (((ca,), (cb,)), ((), ())), preferred_element_type=F32, precision=precision
    )


def lanes(shape):
    return lax.broadcasted_iota(jnp.int32, shape, 1)


def half_mean(v):
    low = lanes(v.shape) < HEAD_SIZE
    first = jnp.sum(jnp.where(low, v, 0.0), axis=1, keepdims=True)
    second = jnp.sum(jnp.where(low, 0.0, v), axis=1, keepdims=True)
    return jnp.where(low, first, second) * (1.0 / HEAD_SIZE)


def half_swap(v):
    quarter = HEAD_SIZE // 2
    left = pltpu.roll(v, 128 - quarter, 1)
    right = pltpu.roll(v, quarter, 1)
    return jnp.where(lanes(v.shape) % HEAD_SIZE < quarter, left, right)


def row_scale(v):
    return lax.rsqrt(jnp.mean(v * v, axis=1, keepdims=True) + EPSILON)


def norm_back(dn, v, gain):
    scale = row_scale(v)
    unit = v * scale
    scaled = dn * gain
    grad = scale * (scaled - unit * jnp.mean(scaled * unit, axis=1, keepdims=True))
    return grad, jnp.sum(dn * unit, axis=0, keepdims=True)


def qk_forward(raw, gain, cosines, sines, is_value):
    normed = raw * lax.rsqrt(half_mean(raw * raw) + EPSILON) * gain
    turned = normed * cosines + half_swap(normed) * sines
    return jnp.where(is_value, raw, turned)


def qk_backward(grad, raw, gain, cosines, sines, is_value):
    straight = grad * cosines - half_swap(grad) * sines
    scale = lax.rsqrt(half_mean(raw * raw) + EPSILON)
    unit = raw * scale
    scaled = straight * gain
    back = scale * (scaled - unit * half_mean(scaled * unit))
    gain_grad = jnp.sum(straight * unit, axis=0, keepdims=True)
    return jnp.where(is_value, grad, back), gain_grad


def two_heads(v):
    low = lanes(v.shape) < HEAD_SIZE
    zero = jnp.zeros_like(v)
    return jnp.concatenate([jnp.where(low, v, zero), jnp.where(low, zero, v)], axis=0)


def head_gains(gain_query, gain_key, q_width, kv_width, b):
    key, value = q_width, q_width + kv_width
    parts = [
        gain_query[...]
        if c < key
        else gain_key[...]
        if c < value
        else jnp.ones((1, HEAD_SIZE), F32)
        for c in (b, b + HEAD_SIZE)
    ]
    return jnp.concatenate(parts, axis=1)


def one_row(v):
    rows = v.shape[0] // 2
    return jnp.where(lanes((rows, v.shape[1])) < HEAD_SIZE, v[:rows], v[rows:])


def twice(v, which):
    half = v[:, which * HEAD_SIZE : (which + 1) * HEAD_SIZE]
    return jnp.concatenate([half, half], axis=1)


def both_halves(v):
    return v + jnp.concatenate([v[:, HEAD_SIZE:], v[:, :HEAD_SIZE]], axis=1)


def over_key_heads(n_heads, values_from, body):
    if n_heads % 2:
        for g in range(n_heads):
            body([(g, (g // 2, g % 2), ((values_from + g) // 2, (values_from + g) % 2))])
        return

    def step(i, carry):
        body([(2 * i + e, (i, e), (values_from // 2 + i, e)) for e in range(2)])
        return carry

    lax.fori_loop(0, n_heads // 2, step, 0)


def lane_block(i):
    return block_rows(i, 128)


def segment_start(lengths, slots):
    end = lengths[0, 0]
    start = jnp.where(slots >= end, end, 0)
    for i in range(1, lengths.shape[1] - 1):
        end = end + lengths[0, i]
        start = jnp.where(slots >= end, end, start)
    return start


def sublanes(shape):
    return lax.broadcasted_iota(jnp.int32, shape, 0)


def count(mask, axis):
    return jnp.sum(mask.astype(F32), axis=axis, keepdims=True).astype(jnp.int32)


def routing(place, slots, rows, share):
    lines = rows // 128
    groups = slots.shape[0] // lines
    square = (rows, rows)

    def line(s):
        return jnp.concatenate([slots[pl.ds(s * lines + i, 1), :] for i in range(lines)], axis=1)

    row = line(place.me)
    column = jnp.broadcast_to(row.astype(F32), (128, rows)).T[:, :1].astype(jnp.int32)
    base = row // rows * rows
    rank = count((column < row) & (column >= base), 0)
    sent_row = row // rows * share + rank
    base = column // rows * rows
    rank = count((row < column) & (row >= base), 1)
    sent_column = column // rows * share + rank
    low = 32
    high = rows // low
    table = jnp.zeros((high, low), F32)
    for s in range(groups):
        r = line(s)
        left = (r // low - place.me * high) == sublanes((high, rows))
        right = r % low == sublanes((low, rows))
        table = table + dot(left.astype(BF), right.astype(BF), 1, 1) * float(s)
    spread = (lanes((low, rows)) % low == sublanes((low, rows))).astype(F32)
    pick = lanes((high, rows)) // low == sublanes((high, rows))
    from_row = jnp.sum(jnp.where(pick, dot(table, spread, 1, 0), 0.0), axis=0, keepdims=True)
    spread = (sublanes((rows, low)) % low == lanes((rows, low))).astype(F32)
    pick = sublanes((rows, high)) // low == lanes((rows, high))
    from_column = jnp.sum(jnp.where(pick, dot(spread, table, 1, 1), 0.0), axis=1, keepdims=True)
    from_row, from_column = from_row.astype(jnp.int32), from_column.astype(jnp.int32)
    same = from_row == from_column
    got_column = from_column * share + count(same & (lanes(square) < sublanes(square)), 1)
    got_row = from_row * share + count(same & (sublanes(square) < lanes(square)), 0)
    return sent_row, sent_column, got_row, got_column


class Place:
    def __init__(self, n, ctx, tp):
        self.n, self.ctx, self.tp = n, ctx, tp
        self.z = lax.axis_index("fsdp")
        self.c = lax.axis_index("ctx")
        self.t = lax.axis_index("tp")
        self.me = self.z * ctx + self.c

    def at(self, z=None, c=None, t=None):
        return (
            self.z if z is None else z,
            self.c if c is None else c,
            self.t if t is None else t,
        )

    def peer(self, j):
        p = lax.rem(self.me + j, self.n * self.ctx)
        return self.at(p // self.ctx, lax.rem(p, self.ctx))

    def up(self, j):
        return self.at(z=lax.rem(self.z + j, self.n))

    def flip(self, bit):
        if bit == 1:
            return self.c + 1 - 2 * lax.rem(self.c, 2)
        return lax.rem(self.c + 2, 4)

    def side(self, j):
        return self.at(t=lax.rem(self.t + j, self.tp))

    def owner(self, k, c):
        return lax.rem(self.z - k + self.n, self.n) * self.ctx + c

    def greet(self):
        barrier = pltpu.get_barrier_semaphore()
        group = self.n * self.ctx
        for j in range(1, group):
            pl.semaphore_signal(barrier, inc=1, device_id=self.peer(j), device_id_type=MESH)
        for j in range(1, self.tp):
            pl.semaphore_signal(barrier, inc=1, device_id=self.side(j), device_id_type=MESH)
        pl.semaphore_wait(barrier, group + self.tp - 2)


MESH = pl.DeviceIdType.MESH


def remote(src, dst, send, recv, device):
    return pltpu.make_async_remote_copy(
        src_ref=src, dst_ref=dst, send_sem=send, recv_sem=recv, device_id=device, device_id_type=MESH
    )


def block_rows(index, size):
    return pl.ds(pl.multiple_of(index * size, size), size)


class Gather:
    def __init__(self, place, whole, columns, number, sems, chip_first=False):
        z_send, z_recv, x_send, x_recv, c_send, c_recv = sems
        h = whole.shape[0] // (place.n * place.ctx)
        n = place.n
        self.n, self.chip_first = n, chip_first
        view = lambda index: whole.at[block_rows(index, h), columns]
        here, there = place.c, place.flip(2)

        def ring(lane, row):
            return [
                remote(
                    view(place.owner(k - 1, lane)),
                    view(place.owner(k - 1, lane)),
                    z_send.at[row, k],
                    z_recv.at[row, k],
                    place.up(1),
                )
                for k in range(1, n)
            ]

        self.rings = [ring(here, number)] + ([ring(there, number + 1)] if chip_first else [])
        self.chip = [
            remote(
                view(place.owner(k, here)),
                view(place.owner(k, here)),
                x_send.at[number, k],
                x_recv.at[number, k],
                place.at(c=there),
            )
            for k in range(1 if chip_first else n)
        ]
        self.core = [
            remote(
                view(place.owner(i % n, here if i < n else there)),
                view(place.owner(i % n, here if i < n else there)),
                c_send.at[number, i],
                c_recv.at[number, i],
                place.at(c=place.flip(1)),
            )
            for i in range(2 * n)
        ]

    def begin(self):
        if self.n > 1:
            self.rings[0][0].start()
        self.core[0].start()

    def begin_other(self):
        if self.n > 1:
            self.rings[1][0].start()

    def advance(self, k):
        if k >= self.n:
            return
        for r, ring in enumerate(self.rings):
            ring[k - 1].wait_recv()
            if k + 1 < self.n:
                ring[k].start()
            self.core[r * self.n + k].start()

    def to_chip(self, k):
        if k < len(self.chip):
            self.chip[k].start()

    def from_chip(self, k):
        if k < len(self.chip):
            self.chip[k].wait_recv()
            self.core[self.n + k].start()

    def finish(self):
        for copy in self.core:
            copy.wait_recv()

    def drain(self):
        for copy in sum(self.rings, []) + self.chip + self.core:
            copy.wait_send()


def forward_kernel(
    n, ctx, tp, q_width, kv_width, tile,
    lengths, tokens, cotangent, slots, gain, gain_query, gain_key, gain_ffn, frequency,
    w_query, w_key, w_value, w_out, w_gate, w_up, w_down,
    sums, squares, ffn_out, dmid, dgain, take_back, send_back, cosines, sines,
    x, dy, qb_out, kv, heads_out, mid_own, w_attn, normed_two, down_keep, d_gate, d_up,
    sent_x, sent_y, got_x, got_y, own_x, own_y, x_land, y_land, pick, qb, heads, mid,
    w, w_ffn, kv_all, part, land, bias, ffn_acc, dn_acc, acts, turned, d_keep, d_send, d_land,
    route_send, route_recv, tp_send, tp_recv, kv_send, kv_recv, out_sem, act_sem, down_send, down_recv, *gather_sems
):
    place = Place(n, ctx, tp)
    group = n * ctx
    rows = got_x.shape[0]
    share = rows // group
    feat = got_x.shape[1]
    width = x_land.shape[1]
    piece = rows
    attn = Gather(place, w, pl.ds(0, w.shape[1]), 0, gather_sems)
    tiles = w_ffn.shape[1] // (3 * tile)
    last = max(1, tiles // 9)
    cuts = [(tiles - last) * i // 3 for i in range(3)] + [tiles - last, tiles]
    first, second, third, tail = (
        Gather(
            place,
            w_ffn,
            pl.ds(cuts[i] * 3 * tile, (cuts[i + 1] - cuts[i]) * 3 * tile),
            1 + i,
            gather_sems,
            chip_first=i == 3,
        )
        for i in range(4)
    )
    groups = [first, second, third]
    stores = []

    def store(src, dst):
        copy = pltpu.make_async_copy(src, dst, out_sem.at[len(stores)])
        copy.start()
        stores.append(copy)

    def route(number, src, dst):
        return [
            remote(
                src.at[block_rows(lax.rem(place.me + j, group), share), :],
                dst.at[block_rows(place.me, share), :],
                route_send.at[number, j],
                route_recv.at[number, j],
                place.peer(j),
            )
            for j in range(1, group)
        ]

    def widen(number, src, dst):
        return [
            remote(
                src,
                dst.at[:, block_rows(place.t, feat)],
                tp_send.at[number, j],
                tp_recv.at[number, j],
                place.side(j),
            )
            for j in range(1, tp)
        ]

    def own_block(src, dst):
        at = block_rows(place.me, share)
        dst[at, :] = src[at, :]

    route_x, route_y = route(0, sent_x, got_x), route(1, sent_y, got_y)
    wide_x, wide_y = widen(0, own_x, x_land), widen(1, own_y, y_land)
    shard_rows = w_query.shape[0]
    own_shard = block_rows(place.me, shard_rows)
    column = 0
    for part_w in (w_query, w_key, w_value):
        w[own_shard, column : column + part_w.shape[1]] = part_w[...]
        column += part_w.shape[1]
    w[own_shard, column:] = w_out[...]
    place.greet()
    attn.begin()
    attn.to_chip(0)
    sent_row, sent_column, got_row, got_column = routing(place, slots, rows, share)
    for i in range(tiles):
        used = min(tile, w_gate.shape[1] - i * tile)
        cols = slice(i * tile, i * tile + used)
        for m, value in enumerate((w_gate[:, cols], w_up[:, cols], w_down[:, cols])):
            if used < tile:
                value = jnp.concatenate(
                    [value, jnp.zeros((shard_rows, tile - used), BF)], axis=1
                )
            c = (3 * i + m) * tile
            w_ffn[own_shard, c : c + tile] = value
    square = (rows, rows)
    send_pick = (sublanes(square) == sent_row).astype(BF)
    sent_x[...] = dot(send_pick, tokens[...], 1, 0).astype(BF)
    for copy in route_x:
        copy.start()
    own_block(sent_x, got_x)
    attn.advance(1)
    attn.to_chip(1)
    sent_y[...] = dot(send_pick, cotangent[...], 1, 0).astype(BF)
    own_block(sent_y, got_y)
    pick[...] = (lanes(square) == got_column).astype(BF)
    take_back[...] = (sublanes(square) == got_row).astype(BF)
    send_back[...] = (lanes(square) == sent_column).astype(BF)
    slot = place.c * piece + sublanes((rows, 128))
    start_col = segment_start(lengths, slot)
    angle = (slot - start_col).astype(F32) * frequency[...]
    start_col = start_col[:, :1]
    cosines[...] = jnp.cos(angle)
    turned_lane = lanes((rows, 128)) % HEAD_SIZE < HEAD_SIZE // 2
    sines[...] = jnp.where(turned_lane, -1.0, 1.0) * jnp.sin(angle)
    attn.from_chip(0)
    attn.advance(2)
    attn.to_chip(2)
    first.begin()
    for copy in route_x:
        copy.wait_recv()
    own_x[...] = dot(pick[...], got_x[...], 1, 0).astype(BF)
    for copy in wide_x:
        copy.start()
    x_land[:, block_rows(place.t, feat)] = own_x[...]
    attn.from_chip(1)
    attn.advance(3)
    attn.to_chip(3)
    for copy in route_y:
        copy.start()
    second.begin()
    first.to_chip(0)
    attn.from_chip(2)
    attn.from_chip(3)
    second.to_chip(0)
    for copy in wide_x:
        copy.wait_recv()
    store(x_land, x)
    v = x_land[...].astype(F32)
    normed = (v * row_scale(v) * gain[...]).astype(BF)
    attn.finish()
    store(w, w_attn)

    own_rows = block_rows(place.c, piece)
    values_from = q_width + kv_width
    for b in list(range(q_width, q_width + 2 * kv_width, 128)) + list(range(0, q_width, 128)):
        if b == 0:
            later = start_keys(place, kv_all, own_rows, kv_send, kv_recv)
        block = dot(normed, w[:, b : b + 128], 1, 0)
        is_value = lanes(block.shape) + b >= values_from
        gains = head_gains(gain_query, gain_key, q_width, kv_width, b)
        done = qk_forward(block, gains, cosines[...], sines[...], is_value)
        if b < q_width:
            qb[:, b : b + 128] = done.astype(BF)
        else:
            kv_all[own_rows, b - q_width : b - q_width + 128] = done.astype(BF)

    q_slot = place.c * piece + lax.broadcasted_iota(jnp.int32, (rows, piece), 0)
    n_pairs = q_width // 128

    def one_piece(p):
        k_slot = p * piece + lanes((rows, piece))
        open_ = (k_slot >= start_col) & (k_slot <= q_slot)
        bias[...] = jnp.where(open_, 0.0, NEG_FILL)
        at = block_rows(p, piece)

        def heads_of(members):
            for g, (kb, ke), (vb, ve) in members:
                q2 = two_heads(qb[:, lane_block(g)])
                k2 = twice(kv_all[at, lane_block(kb)], ke)
                v2 = twice(kv_all[at, lane_block(vb)], ve)
                for h in range(2):
                    part = slice(h * rows, (h + 1) * rows)
                    e = jnp.exp(dot(q2[part], k2, 1, 1) * 0.125 + bias[...])
                    part_sum = e[:, :128]
                    for b in range(128, piece, 128):
                        part_sum = part_sum + e[:, b : b + 128]
                    block = lane_block(2 * g + h)
                    acc[:, block] += dot(e.astype(BF), v2, 1, 0)
                    total[:, block] += part_sum

        over_key_heads(n_pairs, kv_width // HEAD_SIZE, heads_of)

    acc, total = ffn_acc, dn_acc
    acc[...] = jnp.zeros_like(acc)
    total[...] = jnp.zeros_like(total)
    one_piece(place.c)
    x_bit, core_bit = place.c // 2, lax.rem(place.c, 2)
    near, across, passed = later
    first.advance(1)
    second.advance(1)

    @pl.when(x_bit == 1)
    def _():
        across.wait_recv()
        passed.start()

    first.from_chip(0)
    second.from_chip(0)
    tail.to_chip(0)
    first.to_chip(1)
    for copy in route_y:
        copy.wait_recv()
    own_y[...] = dot(pick[...], got_y[...], 1, 0).astype(BF)
    for copy in wide_y:
        copy.start()
    y_land[:, block_rows(place.t, feat)] = own_y[...]

    @pl.when(core_bit == 1)
    def _():
        near.wait_recv()
        one_piece(place.c - 1)

    first.advance(2)
    second.advance(2)
    second.to_chip(1)

    @pl.when(x_bit == 1)
    def _():
        passed.wait_recv()

        def step(p, carry):
            one_piece(p)
            return carry

        lax.fori_loop(0, 2, step, 0)

    ones = jnp.ones((8, 128), F32)
    for g in range(n_pairs):
        first_head, second_head = lane_block(2 * g), lane_block(2 * g + 1)
        values, totals = (
            jnp.concatenate([v[:, first_head], v[:, second_head]], axis=0) for v in (acc, total)
        )
        row_total = jnp.sum(totals, axis=1, keepdims=True)
        heads[:, 128 * g : 128 * g + 128] = one_row(values / row_total)
        sums[g] = 1.0 / dot(ones, totals, 1, 1, lax.Precision.HIGHEST)
    part[...] = dot(heads[...].astype(BF), w[:, q_width + 2 * kv_width :], 1, 1).astype(BF)
    attention = [
        remote(part, land.at[j - 1], tp_send.at[2, j], tp_recv.at[2, j], place.side(j))
        for j in range(1, tp)
    ]
    for copy in attention:
        copy.start()
    store(qb, qb_out)
    store(heads, heads_out)
    first.from_chip(1)
    first.to_chip(2)
    first.advance(3)
    second.advance(3)
    third.begin()
    tail.from_chip(0)
    tail.begin()
    tail.begin_other()
    second.from_chip(1)
    second.to_chip(2)
    first.from_chip(2)
    first.to_chip(3)
    third.advance(1)
    second.from_chip(2)
    second.to_chip(3)
    third.to_chip(0)
    tail.advance(1)
    third.advance(2)
    first.from_chip(3)
    third.to_chip(1)
    for copy in attention:
        copy.wait_recv()
    att = part[...].astype(F32)
    for j in range(1, tp):
        att = att + land[j - 1].astype(F32)
    v = x_land[...].astype(F32)
    squares[0:1, :] = jnp.sum(v * v, axis=0, keepdims=True)
    squares[1:2, :] = jnp.sum(att * att, axis=0, keepdims=True)
    mid[...] = v + att
    store(mid.at[:, block_rows(place.t, feat)], mid_own)
    v = (v + att).astype(BF).astype(F32)
    for copy in attention:
        copy.wait_send()
    nb = part
    nb[...] = (v * row_scale(v) * gain_ffn[...]).astype(BF)
    store(nb, normed_two)
    ffn_acc[...] = jnp.zeros_like(ffn_acc)
    dn_acc[...] = jnp.zeros_like(dn_acc)
    third.to_chip(2)
    third.from_chip(0)
    for copy in wide_y:
        copy.wait_recv()
    store(y_land, dy)
    turn_blocks(place, y_land, turned)

    def one_tile(i):
        at = lambda m: block_rows(3 * i + m, tile)
        w_gate, w_up, w_down = w_ffn[:, at(0)], w_ffn[:, at(1)], w_ffn[:, at(2)]
        gate = dot(nb[...], w_gate, 1, 0)
        up = dot(nb[...], w_up, 1, 0)
        d_hidden = dot(y_land[...], w_down, 1, 0)
        sig = 1.0 / (1.0 + jnp.exp(-gate))
        silu = gate * sig
        out = block_rows(i, tile)
        hidden = (silu * up).astype(BF)
        acts[0, :, out] = (d_hidden * up * (sig * (1.0 + gate * (1.0 - sig)))).astype(BF)
        acts[1, :, out] = (d_hidden * silu).astype(BF)
        ffn_acc[...] += dot(hidden, w_down, 1, 1)
        dn_acc[...] += dot(acts[0, :, out], w_gate, 1, 1) + dot(acts[1, :, out], w_up, 1, 1)
        d_keep[:, out] = dot(turned[: width // 2, :], hidden, 1, 0).astype(BF)
        d_send[:, out] = dot(turned[width // 2 :, :], hidden, 1, 0).astype(BF)

    act_stores = []
    sides_of = [pl.ds(cuts[i] * tile, (cuts[i + 1] - cuts[i]) * tile) for i in range(4)]
    down_cores = [
        remote(
            d_send.at[:, cols],
            d_land.at[:, cols],
            down_send.at[i],
            down_recv.at[i],
            place.at(c=place.flip(1)),
        )
        for i, cols in enumerate(sides_of)
    ]

    def finish_down(i):
        core_sum(d_keep.at[:, sides_of[i]], d_land.at[:, sides_of[i]], down_cores[i])
        copy = pltpu.make_async_copy(
            d_keep.at[:, sides_of[i]], down_keep.at[:, sides_of[i]], act_sem.at[2, i]
        )
        copy.start()
        act_stores.append(copy)

    for i, g in enumerate(groups + [tail]):
        if i == 1:
            tail.advance(2)
            third.advance(3)
            third.to_chip(3)
            second.from_chip(3)
            third.from_chip(1)
        if i == 2:
            tail.advance(3)
            third.from_chip(2)
            third.from_chip(3)
        g.finish()
        repeat(cuts[i + 1] - cuts[i], lambda k, i=i: one_tile(cuts[i] + k))
        down_cores[i].start()
        if i:
            finish_down(i - 1)
        cols = sides_of[i]
        for m, out in enumerate((d_gate, d_up)):
            copy = pltpu.make_async_copy(acts.at[m, :, cols], out.at[:, cols], act_sem.at[m, i])
            copy.start()
            act_stores.append(copy)
    dgain[...] = jnp.zeros_like(dgain)

    def finish_rows(i):
        r = block_rows(i, 128)
        v = mid[r, :].astype(BF).astype(F32)
        grad, gain_sum = norm_back(dn_acc[r, :], v, gain_ffn[...])
        dgain[...] += gain_sum
        dmid[r, :] = grad.astype(BF)
        ffn_out[r, :] = ffn_acc[r, :].astype(BF)

    repeat(rows // 128, finish_rows)
    finish_down(3)

    @pl.when(core_bit == 0)
    def _():
        near.wait_send()

    @pl.when(x_bit == 0)
    def _():
        across.wait_send()

    @pl.when(x_bit == 1)
    def _():
        passed.wait_send()

    store(kv_all, kv)
    for copy in route_x + route_y + wide_x + wide_y:
        copy.wait_send()
    for g in [attn, tail] + groups:
        g.drain()
    for copy in down_cores:
        copy.wait_send()
    for copy in stores + act_stores:
        copy.wait()


def start_keys(place, kv_all, own_rows, send, recv):
    x_bit, core_bit = place.c // 2, lax.rem(place.c, 2)
    mine = kv_all.at[own_rows, :]
    near = remote(mine, mine, send.at[0], recv.at[0], place.at(c=place.flip(1)))
    across = remote(mine, mine, send.at[1], recv.at[1], place.at(c=place.flip(2)))
    from_chip = kv_all.at[block_rows(place.flip(2), own_rows.size), :]
    passed = remote(from_chip, from_chip, send.at[2], recv.at[2], place.at(c=place.flip(1)))

    @pl.when(x_bit == 0)
    def _():
        across.start()

    @pl.when(core_bit == 0)
    def _():
        near.start()

    return near, across, passed


def forward_pass(grid, q_width, kv_width, tile, *operands):
    tokens, w_query, w_key, w_gate = operands[1], operands[9], operands[10], operands[13]
    rows, feat = tokens.shape
    n, ctx, tp = grid.n, grid.ctx, grid.tp
    width = feat * tp
    n_pairs = q_width // 128
    row_len = rows * ctx
    ff = -(-w_gate.shape[1] // tile) * tile
    vm = pl.BlockSpec(memory_space=pltpu.VMEM)
    dma = pltpu.SemaphoreType.DMA
    V = pltpu.VMEM
    group = n * ctx
    attn_width = 2 * w_query.shape[1] + 2 * w_key.shape[1]
    return pl.pallas_call(
        functools.partial(forward_kernel, n, ctx, tp, q_width, kv_width, tile),
        in_specs=[pl.BlockSpec(memory_space=pltpu.SMEM)] + [vm] * 15,
        out_specs=[vm] * 9 + [ANYWHERE] * 11,
        out_shape=[
            shape((n_pairs, 8, 2 * rows), F32),
            shape((2, width), F32),
            shape((rows, width), BF),
            shape((rows, width), BF),
            shape((1, width), F32),
            shape((rows, rows), BF),
            shape((rows, rows), BF),
            shape((rows, 128), F32),
            shape((rows, 128), F32),
            shape((rows, width), BF),
            shape((rows, width), BF),
            shape((rows, q_width), BF),
            shape((row_len, 2 * kv_width), BF),
            shape((rows, q_width), F32),
            shape((rows, feat), F32),
            shape((width, attn_width), BF),
            shape((rows, width), BF),
            shape((width // 2, ff), BF),
            shape((rows, ff), BF),
            shape((rows, ff), BF),
        ],
        scratch_shapes=[V((rows, feat), BF)] * 6
        + [
            V((rows, width), BF),
            V((rows, width), BF),
            V((rows, rows), BF),
            V((rows, q_width), BF),
            V((rows, q_width), F32),
            V((rows, width), F32),
            V((width, attn_width), BF),
            V((width, 3 * ff), BF),
            V((row_len, 2 * kv_width), BF),
            V((rows, width), BF),
            V((tp - 1, rows, width), BF),
            V((rows, rows), F32),
            V((rows, width), F32),
            V((rows, width), F32),
            V((2, rows, ff), BF),
            V((width, rows), BF),
            V((width // 2, ff), BF),
            V((width // 2, ff), BF),
            V((width // 2, ff), BF),
            dma((2, group)),
            dma((2, group)),
            dma((3, tp)),
            dma((3, tp)),
            dma((3,)),
            dma((3,)),
            dma((8,)),
            dma((3, 4)),
            dma((4,)),
            dma((4,)),
            dma((6, n)),
            dma((6, n)),
            dma((5, n)),
            dma((5, n)),
            dma((5, 2 * n)),
            dma((5, 2 * n)),
        ],
        compiler_params=pltpu.CompilerParams(
            vmem_limit_bytes=61 * 2**20, collective_id=0, has_side_effects=True
        ),
        cost_estimate=pl.CostEstimate(
            flops=12 * rows * width * ff, bytes_accessed=40 * 2**20, transcendentals=0
        ),
    )(*operands)


def repeat(count, body):
    def step(i, carry):
        body(i)
        return carry

    lax.fori_loop(0, count, step, 0)


def add_into(to, more):
    step = 16

    def add(i):
        at = block_rows(i, step)
        to[at, :] = (to[at, :].astype(F32) + more[at, :].astype(F32)).astype(to.dtype)

    repeat(to.shape[0] // step, add)


def turn_blocks(place, source, turned):
    width = source.shape[1]
    n = place.n
    h = width // (n * place.ctx)
    first = lax.rem(place.c, 2) == 0

    def turn(i):
        chip = lax.rem(place.c // 2 + i // n, 2)
        pair = lax.rem(place.z - lax.rem(i, n) + n, n) * (place.ctx // 2) + chip
        block = source[:, block_rows(pair, 2 * h)].astype(F32).T.astype(turned.dtype)
        low, high = block[:h], block[h:]
        turned[block_rows(i, h), :] = jnp.where(first, low, high)
        turned[block_rows(i + 2 * n, h), :] = jnp.where(first, high, low)

    repeat(2 * n, turn)


class Scatter:
    def __init__(
        self, place, keep, columns, chip_land, line_land, number, sems, line_first=False
    ):
        x_send, x_recv, z_send, z_recv = sems
        n = place.n
        self.n, self.line_first = n, line_first
        self.h = h = keep.shape[0] // (2 * n)
        self.keep = [keep.at[pl.ds(k * h, h), columns] for k in range(2 * n)]
        land = [chip_land.at[pl.ds(k * h, h), columns] for k in range(n)]
        line = [line_land.at[k, :, columns] for k in range(n - 1)]
        there = place.at(c=place.flip(2))

        def ring(blocks, lands, row):
            return [
                remote(blocks[k], lands[k - 1], z_send.at[row, k], z_recv.at[row, k], place.up(1))
                for k in range(1, n)
            ]

        self.rings = [(ring(self.keep[:n], line, number), self.keep[:n], line)]
        if line_first:
            self.rings.append((ring(self.keep[n:], land[1:], number + 1), self.keep[n:], land[1:]))
            self.chip = remote(
                self.keep[n], land[0], x_send.at[number], x_recv.at[number], there
            )
            self.chip_land = land[:1]
        else:
            self.chip = remote(
                keep.at[pl.ds(n * h, n * h), columns],
                chip_land.at[:, columns],
                x_send.at[number],
                x_recv.at[number],
                there,
            )
            self.chip_land = land

    def to_chip(self):
        self.chip.start()

    def from_chip(self):
        self.chip.wait_recv()
        if self.line_first:
            return
        for k in list(range(1, self.n)) + [0]:
            add_into(self.keep[k], self.chip_land[k])
            if k == 1:
                self.begin()

    def begin(self):
        for ring, _, _ in self.rings:
            if ring:
                ring[0].start()

    def advance(self, k):
        if k >= self.n:
            return
        for ring, blocks, lands in self.rings:
            ring[k - 1].wait_recv()
            if k + 1 < self.n:
                add_into(blocks[k + 1], lands[k - 1])
                ring[k].start()
            elif self.line_first:
                add_into(blocks[0], lands[k - 1])

    def finish(self, out):
        last = self.chip_land[0] if self.line_first else self.rings[0][2][self.n - 2]
        step = 16

        def add(i):
            at = block_rows(i, step)
            out[at, :] = self.keep[0][at, :].astype(F32) + last[at, :].astype(F32)

        repeat(self.h // step, add)

    def drain(self, chip=True):
        if chip:
            self.chip.wait_send()
        for ring, _, _ in self.rings:
            for copy in ring:
                copy.wait_send()


def core_sum(keep, core_land, copy):
    copy.wait_recv()
    add_into(keep, core_land)


def backward_kernel(
    n, ctx, tp, q_width, kv_width, stage_cols,
    lengths, ffn, dmid, sums, cosines, sines, pick_t, gain, gain_query, gain_key,
    gain_ffn_grad, squares, qb_in, kv_in, heads_in, w_in, dy_in, x_in, mid_in, normed_two, down_in, d_gate, d_up,
    back_o, back_g, sum_gate, sum_up, sum_down, sum_out, sum_qkv, small,
    qb, kv_all, heads, w, x, turned, stage, keep, send, core_land, chip_land, line_land,
    o_keep, o_send, o_core, o_chip, o_line, a_keep, a_send, a_core, a_chip, a_line,
    d_mid_own, d_attn, dob, delta, bias, dq_t, dkv, kv_land, tp_land, ffn_away, ffn_land, dx_away, dx_land,
    sent, small_mine, small_land, small_side,
    tp_send, tp_recv, route_send, route_recv, small_send, small_recv, kv_send, kv_recv, load_sem,
    *scatter_sems
):
    place = Place(n, ctx, tp)
    group = n * ctx
    rows, width = dmid.shape
    feat = width // tp
    share = rows // group
    piece = rows
    ff = d_gate.shape[1]
    half = width // 2
    n_pairs = q_width // 128
    qkv_width = q_width + 2 * kv_width
    values_from = q_width + kv_width
    x_bit, core_bit = place.c // 2, lax.rem(place.c, 2)
    own_cols = block_rows(place.t, feat)
    c_send, c_recv, *ring_sems = scatter_sems
    everything = pl.ds(0, ff)
    lands = lambda m: (chip_land.at[m], line_land.at[m])
    cut = ff // 128 * 11 // 18 * 128
    down = Scatter(place, keep.at[0], pl.ds(0, cut), *lands(0), 0, ring_sems, True)
    down_x = Scatter(place, keep.at[0], pl.ds(cut, ff - cut), *lands(0), 6, ring_sems)
    gate = Scatter(place, keep.at[1], everything, *lands(1), 2, ring_sems)
    up = Scatter(place, keep.at[2], everything, *lands(2), 3, ring_sems)
    out_sum = Scatter(place, o_keep, pl.ds(0, q_width), o_chip, o_line, 4, ring_sems)
    qkv_sum = Scatter(place, a_keep, pl.ds(0, qkv_width), a_chip, a_line, 5, ring_sems)
    across_cores = [
        remote(src, dst, c_send.at[i], c_recv.at[i], place.at(c=place.flip(1)))
        for i, (src, dst) in enumerate(
            [(send.at[m], core_land.at[m]) for m in range(2)]
            + [(o_send, o_core), (a_send, a_core)]
        )
    ]

    def to_sides(number, src, dst):
        return [
            remote(
                src(j), dst.at[j - 1], tp_send.at[number, j], tp_recv.at[number, j], place.side(j)
            )
            for j in range(1, tp)
        ]

    def away(buffer):
        return lambda j: buffer.at[j - 1]

    def fill_away(buffer, source):
        for j in range(1, tp):
            buffer[j - 1] = source[:, block_rows(lax.rem(place.t + j, tp), feat)]

    def route(number, src, dst):
        return [
            remote(
                src.at[block_rows(lax.rem(place.me + j, group), share), :],
                dst.at[block_rows(place.me, share), :],
                route_send.at[number, j],
                route_recv.at[number, j],
                place.peer(j),
            )
            for j in range(1, group)
        ]

    dmid_sum = to_sides(0, lambda j: dmid, tp_land)
    ffn_sum = to_sides(1, away(ffn_away), ffn_land)
    dx_sum = to_sides(2, away(dx_away), dx_land)
    route_o, route_g = route(0, sent, back_o), route(1, dob, back_g)

    place.greet()
    for copy in dmid_sum:
        copy.start()

    sources = (d_gate, d_up)
    tiles = [(m, b) for m in range(2) for b in range(0, ff, stage_cols)]
    loads = [
        pltpu.make_async_copy(
            sources[m].at[:, pl.ds(b, stage_cols)], stage.at[i % 2], load_sem.at[i]
        )
        for i, (m, b) in enumerate(tiles)
    ]
    load_n = pltpu.make_async_copy(normed_two, d_attn, load_sem.at[len(tiles)])
    dy, mid = x, d_mid_own
    load_dy = pltpu.make_async_copy(dy_in, dy, load_sem.at[len(tiles) + 1])
    load_x = pltpu.make_async_copy(x_in, x, load_sem.at[len(tiles) + 2])
    load_mid = pltpu.make_async_copy(mid_in, mid, load_sem.at[len(tiles) + 3])
    load_down = pltpu.make_async_copy(down_in, keep.at[0], load_sem.at[len(tiles) + 4])
    load_down.start()
    load_n.start()
    loads[0].start()
    more_loads = [
        pltpu.make_async_copy(src, dst, load_sem.at[len(tiles) + 5 + i])
        for i, (src, dst) in enumerate(((w_in, w), (qb_in, qb), (kv_in, kv_all), (heads_in, heads)))
    ]
    for copy in [load_dy, load_mid] + more_loads:
        copy.start()
    load_down.wait()
    down.begin()
    down_x.to_chip()
    fill_away(ffn_away, ffn)
    load_n.wait()
    turn_blocks(place, d_attn, turned)
    sub = 256 if stage_cols % 256 == 0 else 128
    for i, (m, b) in enumerate(tiles):
        if i + 1 < len(tiles):
            loads[i + 1].start()
        if m == 1 and b == ff // 2 // stage_cols * stage_cols:
            core_sum(keep.at[1], core_land.at[0], across_cores[0])
            gate.to_chip()
        loads[i].wait()
        for s in range(0, stage_cols, sub):
            right = stage[i % 2, :, s : s + sub]
            cols = slice(b + s, b + s + sub)
            keep[m + 1, :, cols] = dot(turned[:half, :], right, 1, 0).astype(BF)
            send[m, :, cols] = dot(turned[half:, :], right, 1, 0).astype(BF)
        if b + stage_cols == ff:
            across_cores[m].start()
    down.advance(1)
    core_sum(keep.at[2], core_land.at[1], across_cores[1])
    load_dy.wait()

    for copy in more_loads:
        copy.wait()
    for copy in dmid_sum:
        copy.wait_recv()
    for copy in ffn_sum:
        copy.start()

    def sum_gradient(i):
        r = block_rows(i, 128)
        d_all = dy[r, :].astype(F32) + dmid[r, :].astype(F32)
        for j in range(1, tp):
            d_all = d_all + tp_land[j - 1, r, :].astype(F32)
        d_attn[r, :] = d_all.astype(BF)

    repeat(rows // 128, sum_gradient)
    dob[...] = dot(d_attn[...], w[:, qkv_width:], 1, 0).astype(BF)
    dq_t[...] = jnp.zeros_like(dq_t)
    ones = jnp.ones((8, 128), F32)

    def set_delta(g):
        both = dob[:, lane_block(g)].astype(F32) * heads[:, lane_block(g)]
        delta[g] = dot(ones, two_heads(both), 1, 1, lax.Precision.HIGHEST)

    repeat(n_pairs, set_delta)
    q_slot = place.c * piece + lanes((piece, rows))
    start_row = segment_start(lengths, place.c * piece + lanes((8, rows)))[:1]

    def one_piece(p):
        k_slot = p * piece + lax.broadcasted_iota(jnp.int32, (piece, rows), 0)
        open_ = (k_slot >= start_row) & (k_slot <= q_slot)
        bias[...] = jnp.where(open_, 0.0, NEG_FILL)
        at = block_rows(p, piece)
        def heads_of(members):
            grads = []
            for g, (kb, ke), (vb, ve) in members:
                q2 = two_heads(qb[:, lane_block(g)])
                do2 = two_heads(dob[:, lane_block(g)])
                k2 = twice(kv_all[at, lane_block(kb)], ke)
                v2 = twice(kv_all[at, lane_block(vb)], ve)
                k_t = k2.astype(F32).T.astype(BF)
                dk = jnp.zeros((piece, 128), F32)
                dv = jnp.zeros((piece, 128), F32)
                for h in range(0, 2 * rows, 256):
                    part = slice(h, h + 256)
                    open_part = slice(h % rows, h % rows + 256)
                    s = dot(k2, q2[part], 1, 1)
                    dp = dot(v2, do2[part], 1, 1)
                    pe = jnp.exp(s * 0.125 + bias[:, open_part]) * sums[g, 0:1, part]
                    ds = (pe * (dp - delta[g, 0:1, part])).astype(BF)
                    dv = dv + dot(pe.astype(BF), do2[part], 1, 0)
                    dk = dk + dot(ds, q2[part], 1, 0)
                    dq_t[g, :, part] += dot(k_t, ds, 1, 0)
                grads.append((both_halves(dk) * 0.125, both_halves(dv)))
            low = lanes((piece, 128)) < HEAD_SIZE
            kb, vb = members[0][1][0], members[0][2][0]
            if len(members) == 2:
                dkv[at, lane_block(kb)] = jnp.where(low, grads[0][0], grads[1][0]).astype(BF)
                dkv[at, lane_block(vb)] = jnp.where(low, grads[0][1], grads[1][1]).astype(BF)
            else:
                for value, (b, e) in zip(grads[0], members[0][1:]):
                    c = 128 * b + HEAD_SIZE * e
                    dkv[at, c : c + HEAD_SIZE] = value[:, :HEAD_SIZE].astype(BF)

        over_key_heads(n_pairs, kv_width // HEAD_SIZE, heads_of)

    down.advance(2)
    down_x.from_chip()

    sibling = place.at(c=place.flip(1))
    other = 1 - core_bit
    to_passer = remote(
        dkv.at[block_rows(other, piece), :], kv_land.at[0], kv_send.at[0], kv_recv.at[0], sibling
    )
    to_chip = remote(
        dkv.at[block_rows(core_bit, piece), :],
        kv_land.at[0],
        kv_send.at[1],
        kv_recv.at[1],
        place.at(c=place.flip(2)),
    )
    to_core = remote(
        dkv.at[block_rows(2 * x_bit, piece), :], kv_land.at[1], kv_send.at[2], kv_recv.at[2], sibling
    )

    @pl.when(x_bit == 1)
    def _():
        def step(p, carry):
            one_piece(p)
            return carry

        lax.fori_loop(0, 2, step, 0)
        to_passer.start()

    turn_blocks(place, d_attn, turned)
    right = heads[...].astype(BF)
    o_keep[...] = dot(turned[:half, :], right, 1, 0).astype(BF)
    o_send[...] = dot(turned[half:, :], right, 1, 0).astype(BF)
    across_cores[2].start()
    down.advance(3)
    down_x.advance(1)

    @pl.when(x_bit == 1)
    def _():
        to_passer.wait_recv()
        mine = block_rows(core_bit, piece)
        dkv[mine, :] = (dkv[mine, :].astype(F32) + kv_land[0].astype(F32)).astype(BF)
        to_chip.start()

    gate.from_chip()
    up.to_chip()
    core_sum(o_keep, o_core, across_cores[2])
    out_sum.to_chip()

    @pl.when(core_bit == 1)
    def _():
        one_piece(place.c - 1)
        to_core.start()

    for copy in ffn_sum:
        copy.wait_recv()
    small_mine[...] = jnp.zeros_like(small_mine)
    load_mid.wait()

    def finish_output(i):
        r = block_rows(i, 128)
        ffn_out = ffn[r, own_cols].astype(F32)
        for j in range(1, tp):
            ffn_out = ffn_out + ffn_land[j - 1, r, :].astype(F32)
        small_mine[5:6, :feat] += jnp.sum(ffn_out * ffn_out, axis=0, keepdims=True)
        dx_away[0, r, :] = (mid[r, :] + ffn_out).astype(BF)

    repeat(rows // 128, finish_output)
    sent[...] = dot(pick_t[...], dx_away[0], 1, 0).astype(BF)
    for copy in route_o:
        copy.start()
    own = block_rows(place.me, share)
    back_o[own, :] = sent[own, :]


    def own_gradient(i):
        r = block_rows(i, 128)
        d_own = dy[r, own_cols].astype(F32) + dmid[r, own_cols].astype(F32)
        for j in range(1, tp):
            d_own = d_own + tp_land[j - 1, r, own_cols].astype(F32)
        d_mid_own[r, :] = d_own

    repeat(rows // 128, own_gradient)
    load_x.start()
    one_piece(place.c)
    down_x.advance(2)
    gate.advance(1)
    normed = tp_land.at[0]
    load_x.wait()

    def norm_again(i):
        v = x[block_rows(i, 128), :].astype(F32)
        normed[block_rows(i, 128), :] = (v * row_scale(v) * gain[...]).astype(BF)

    repeat(rows // 128, norm_again)
    turn_blocks(place, normed, turned)
    mine = block_rows(place.c, piece)

    @pl.when(core_bit == 0)
    def _():
        to_core.wait_recv()

    @pl.when(x_bit == 0)
    def _():
        to_chip.wait_recv()

    d_qkv = d_attn.at[:, pl.ds(0, qkv_width)]
    for b in range(0, qkv_width, 128):
        if b < q_width:
            g = b // 128
            grad = one_row(dq_t[g].T) * 0.125
        else:
            cols = slice(b - q_width, b - q_width + 128)
            grad = dkv[mine, cols].astype(F32)
            grad = jnp.where(x_bit == 0, grad + kv_land[0, :, cols].astype(F32), grad)
            grad = jnp.where(core_bit == 0, grad + kv_land[1, :, cols].astype(F32), grad)
        raw = dot(normed[...], w[:, b : b + 128], 1, 0)
        is_value = lanes(grad.shape) + b >= values_from
        back, gain_grad = qk_backward(
            grad,
            raw,
            head_gains(gain_query, gain_key, q_width, kv_width, b),
            cosines[...],
            sines[...],
            is_value,
        )
        small_mine[2:3, b : b + 128] = gain_grad
        d_qkv[:, b : b + 128] = back.astype(BF)

    def finish_gradient(i):
        r = block_rows(i, 128)
        dn = dot(d_qkv[r, :], w[:, :qkv_width], 1, 1)
        dx, gain_grad = norm_back(dn, x[r, :].astype(F32), gain[...])
        normed[r, :] = dx.astype(BF)
        small_mine[0:1, :] += gain_grad

    repeat(rows // 128, finish_gradient)
    fill_away(dx_away, normed)
    for copy in dx_sum:
        copy.start()
    small_mine[1:2, :] = gain_ffn_grad[...]
    small_mine[3:5, :] = squares[...]
    for b in range(0, qkv_width, 256):
        cols = slice(b, b + 256)
        a_keep[:, cols] = dot(turned[:half, :], d_qkv[:, cols], 1, 0).astype(BF)
        a_send[:, cols] = dot(turned[half:, :], d_qkv[:, cols], 1, 0).astype(BF)
    across_cores[3].start()
    down_x.advance(3)
    gate.advance(2)
    small_out = [
        remote(
            small_mine, small_land.at[place.me], small_send.at[0, j], small_recv.at[0, j], place.peer(j)
        )
        for j in range(1, group)
    ]
    for copy in small_out:
        copy.start()
    small_land[place.me] = small_mine[...]
    core_sum(a_keep, a_core, across_cores[3])

    for copy in dx_sum:
        copy.wait_recv()
    for copy in ffn_sum:
        copy.wait_send()

    def finish_input(i):
        r = block_rows(i, 128)
        total = d_mid_own[r, :] + normed[r, own_cols].astype(F32)
        for j in range(1, tp):
            total = total + dx_land[j - 1, r, :].astype(F32)
        ffn_away[0, r, :] = total.astype(BF)

    repeat(rows // 128, finish_input)
    dob[...] = dot(pick_t[...], ffn_away[0], 1, 0).astype(BF)
    for copy in route_g:
        copy.start()
    back_g[own, :] = dob[own, :]
    up.chip.wait_send()
    qkv_sum.to_chip()
    down.to_chip()
    gate.advance(3)
    out_sum.from_chip()
    gate.finish(sum_gate)
    up.from_chip()
    out_sum.advance(1)
    up.advance(1)
    qkv_sum.from_chip()
    out_sum.advance(2)
    up.advance(2)
    qkv_sum.advance(1)
    out_sum.advance(3)
    down.from_chip()
    down.finish(sum_down.at[:, pl.ds(0, cut)])
    down_x.finish(sum_down.at[:, pl.ds(cut, ff - cut)])
    up.advance(3)
    qkv_sum.advance(2)
    out_sum.finish(sum_out)
    up.finish(sum_up)
    for copy in small_out:
        copy.wait_recv()
    total = small_land[0]
    for i in range(1, group):
        total = total + small_land[i]
    small_side[place.t] = total
    for copy in small_out:
        copy.wait_send()
    small_mine[...] = total
    sides = [
        remote(
            small_mine, small_side.at[place.t], small_send.at[1, j], small_recv.at[1, j], place.side(j)
        )
        for j in range(1, tp)
    ]
    for copy in sides:
        copy.start()
    for copy in sides:
        copy.wait_recv()
    total = small_side[0]
    for j in range(1, tp):
        total = total + small_side[j]
    small[...] = total
    for copy in route_o:
        copy.wait_recv()
    qkv_sum.advance(3)
    qkv_sum.finish(sum_qkv)
    for copy in route_g:
        copy.wait_recv()

    @pl.when(x_bit == 1)
    def _():
        to_passer.wait_send()
        to_chip.wait_send()

    @pl.when(core_bit == 1)
    def _():
        to_core.wait_send()

    for copy in dmid_sum + dx_sum + route_o + route_g + sides:
        copy.wait_send()
    for copy in across_cores:
        copy.wait_send()
    for s in (down, down_x, gate, out_sum, qkv_sum):
        s.drain()
    up.drain(chip=False)


def backward_pass(grid, q_width, kv_width, *operands):
    dmid, d_gate = operands[2], operands[21]
    rows, width = dmid.shape
    ff = d_gate.shape[1]
    n, ctx, tp = grid.n, grid.ctx, grid.tp
    group = n * ctx
    feat = width // tp
    half = width // 2
    h = width // group
    n_pairs = q_width // 128
    qkv_width = q_width + 2 * kv_width
    stage_cols = 256 if ff % 256 == 0 else 128
    vm = pl.BlockSpec(memory_space=pltpu.VMEM)
    dma = pltpu.SemaphoreType.DMA
    V = pltpu.VMEM

    def scatter_space(cols):
        return [
            V((half, cols), BF),
            V((half, cols), BF),
            V((half, cols), BF),
            V((half // 2, cols), BF),
            V((n - 1, h, cols), BF),
        ]

    return pl.pallas_call(
        functools.partial(backward_kernel, n, ctx, tp, q_width, kv_width, stage_cols),
        in_specs=[pl.BlockSpec(memory_space=pltpu.SMEM)] + [vm] * 11 + [ANYWHERE] * 11,
        out_specs=[vm] * 8,
        out_shape=[
            shape((rows, feat), BF),
            shape((rows, feat), BF),
            shape((h, ff), F32),
            shape((h, ff), F32),
            shape((h, ff), F32),
            shape((h, q_width), F32),
            shape((h, qkv_width), F32),
            shape((8, width), F32),
        ],
        scratch_shapes=[
            V((rows, q_width), BF),
            V((rows * ctx, 2 * kv_width), BF),
            V((rows, q_width), F32),
            V((width, q_width + qkv_width), BF),
            V((rows, width), BF),
            V((width, rows), BF),
            V((2, rows, stage_cols), BF),
            V((3, half, ff), BF),
            V((2, half, ff), BF),
            V((2, half, ff), BF),
            V((3, half // 2, ff), BF),
            V((3, n - 1, h, ff), BF),
        ]
        + scatter_space(q_width)
        + scatter_space(qkv_width)
        + [
            V((rows, feat), F32),
            V((rows, width), BF),
            V((rows, q_width), BF),
            V((n_pairs, 8, 2 * rows), F32),
            V((rows, rows), F32),
            V((n_pairs, 128, 2 * rows), F32),
            V((rows * ctx, 2 * kv_width), BF),
            V((2, rows, 2 * kv_width), BF),
            V((tp - 1, rows, width), BF),
            V((tp - 1, rows, feat), BF),
            V((tp - 1, rows, feat), BF),
            V((tp - 1, rows, feat), BF),
            V((tp - 1, rows, feat), BF),
            V((rows, feat), BF),
            V((8, width), F32),
            V((group, 8, width), F32),
            V((tp, 8, width), F32),
            dma((3, tp)),
            dma((3, tp)),
            dma((2, group)),
            dma((2, group)),
            dma((2, max(group, tp))),
            dma((2, max(group, tp))),
            dma((3,)),
            dma((3,)),
            dma((2 * (ff // stage_cols) + 9,)),
            dma((4,)),
            dma((4,)),
            dma((7,)),
            dma((7,)),
            dma((7, n)),
            dma((7, n)),
        ],
        compiler_params=pltpu.CompilerParams(
            vmem_limit_bytes=61 * 2**20, collective_id=1, has_side_effects=True
        ),
        cost_estimate=pl.CostEstimate(
            flops=20 * rows * rows * ctx * q_width, bytes_accessed=40 * 2**20, transcendentals=0
        ),
    )(*operands)


def output_kernel(
    tp, entries, place_o, place_g, send_back, gate, up, down, out, qkv, small,
    output, grad_tokens, g_query, g_key, g_value, g_out, g_gate, g_up, g_down,
    gain_a, gain_f, gain_q, gain_k, stats
):
    a, b = g_query.shape[1], g_query.shape[1] + g_key.shape[1]
    output[...] = dot(send_back[...], place_o[...], 1, 0).astype(BF)
    grad_tokens[...] = dot(send_back[...], place_g[...], 1, 0).astype(BF)
    g_query[...] = qkv[:, :a]
    g_key[...] = qkv[:, a:b]
    g_value[...] = qkv[:, b:]
    g_out[...] = out[...]
    ff = g_gate.shape[1]
    g_gate[...] = gate[:, :ff]
    g_up[...] = up[:, :ff]
    g_down[...] = down[:, :ff]
    gain_a[...] = small[0:1, :]
    gain_f[...] = small[1:2, :]

    def heads_sum(first, last):
        total = jnp.zeros((1, HEAD_SIZE), F32)
        for c in range(first, last, HEAD_SIZE):
            total = total + small[2:3, c : c + HEAD_SIZE]
        return total

    gain_q[...] = heads_sum(0, a)
    gain_k[...] = heads_sum(a, b)
    row = lanes((1, 128))
    x_sum, attn_sum, ffn_sum = (
        jnp.sum(small[3 + i : 4 + i, :], axis=1, keepdims=True) for i in range(3)
    )
    total = jnp.where(row == 0, x_sum / tp, jnp.where(row == 1, attn_sum / tp, ffn_sum))
    stats[...] = jnp.sqrt(total * (1.0 / entries))


def output_pass(grid, shapes, *operands):
    rows = operands[0].shape[0]
    entries = rows * grid.n * grid.ctx * MODEL_WIDTH
    row = lambda n: shape((1, n), F32)
    vm = pl.BlockSpec(memory_space=pltpu.VMEM)
    outs = (
        [shape(operands[0].shape, BF)] * 2
        + [shape(s, F32) for s in shapes]
        + [row(MODEL_WIDTH), row(MODEL_WIDTH), row(HEAD_SIZE), row(HEAD_SIZE), row(128)]
    )
    return pl.pallas_call(
        functools.partial(output_kernel, grid.tp, entries),
        in_specs=[vm] * len(operands),
        out_specs=[vm] * len(outs),
        out_shape=outs,
        compiler_params=pltpu.CompilerParams(vmem_limit_bytes=60 * 2**20),
    )(*operands)


def local(
    tokens,
    cotangent,
    slot_of,
    lengths,
    w_query,
    key_weight,
    value_weight,
    w_out,
    w_gate,
    w_up,
    w_down,
    gain_attn,
    gain_ffn,
    gain_query,
    gain_key,
):
    grid = Grid()
    rows, feat_len = tokens.shape
    q_heads = QUERY_HEADS // grid.tp
    key_value_heads = KEY_VALUE_HEADS // grid.tp
    q_width = q_heads * HEAD_SIZE
    kv_width = key_value_heads * HEAD_SIZE
    ff = w_gate.shape[1]
    tile = 256 if ff % 256 == 0 else 128
    frequency = ROPE_THETA ** (-np.arange(0, HEAD_SIZE, 2, dtype=np.float64) / HEAD_SIZE)
    frequency = jnp.asarray(np.tile(frequency, 4)[None, :], F32)
    (
        sums, squares, ffn_part, d_mid_part, d_gain_ffn, take_back, send_back, cosines, sines,
        x_full, dy_full, qb, row_kv, heads, middle_own, attn_w, normed_two, down_keep, d_gate, d_up,
    ) = forward_pass(
        grid,
        q_width,
        kv_width,
        tile,
        lengths,
        tokens,
        cotangent,
        slot_of.reshape(-1, 128),
        gain_attn[None, :],
        gain_query[None, :],
        gain_key[None, :],
        gain_ffn[None, :],
        frequency,
        w_query,
        key_weight,
        value_weight,
        w_out.T,
        w_gate,
        w_up,
        w_down.T,
    )
    place_o, place_g, sum_gate, sum_up, sum_down, sum_out, sum_qkv, small = backward_pass(
        grid,
        q_width,
        kv_width,
        lengths,
        ffn_part,
        d_mid_part,
        sums,
        cosines,
        sines,
        take_back,
        gain_attn[None, :],
        gain_query[None, :],
        gain_key[None, :],
        d_gain_ffn,
        squares,
        qb,
        row_kv,
        heads,
        attn_w,
        dy_full,
        x_full,
        middle_own,
        normed_two,
        down_keep,
        d_gate,
        d_up,
    )
    weights = (w_query, key_weight, value_weight, w_out.T, w_gate, w_up, w_down.T)
    *outs, gain_a, gain_f, gain_q, gain_k, stats = output_pass(
        grid,
        [v.shape for v in weights],
        place_o,
        place_g,
        send_back,
        sum_gate,
        sum_up,
        sum_down,
        sum_out,
        sum_qkv,
        small,
    )
    outs[5], outs[8] = outs[5].T, outs[8].T
    return (*outs, gain_a[0], gain_f[0], gain_q[0], gain_k[0], stats[0, :3])


def solution(mesh):
    row = P(("fsdp", "ctx"), "tp")
    column = P("tp", ("fsdp", "ctx"))
    in_specs = (row, row, P(), P("fsdp", None), row, row, row, column, row, row, column) + (P(),) * 4
    out_specs = (row, row, row, row, row, column, row, row, column) + (P(),) * 5
    return jax.shard_map(local, mesh=mesh, in_specs=in_specs, out_specs=out_specs, check_vma=False)
```

```python
import functools

import jax
import jax.numpy as jnp
import numpy as np
from jax import lax
from jax.experimental import pallas as pl
from jax.experimental.pallas import tpu as pltpu
from jax.sharding import PartitionSpec as P

MODEL_WIDTH = 1024
QUERY_HEADS = 16
KEY_VALUE_HEADS = 8
HEAD_SIZE = 64

EPSILON = 1e-05
ROPE_THETA = 1000000.0
NEG_FILL = -1e30
BF = jnp.bfloat16
F32 = jnp.float32


class Grid:
    def __init__(self):
        self.n = lax.axis_size("fsdp")
        self.ctx = lax.axis_size("ctx")
        self.tp = lax.axis_size("tp")
        self.z = lax.axis_index("fsdp")
        self.c = lax.axis_index("ctx")
        self.t = lax.axis_index("tp")


def shape(s, t):
    return jax.ShapeDtypeStruct(s, t)


ANYWHERE = pl.BlockSpec(memory_space=pl.ANY)


def dot(a, b, ca, cb, precision=None):
    return lax.dot_general(
        a, b, (((ca,), (cb,)), ((), ())), preferred_element_type=F32, precision=precision
    )


def lanes(shape):
    return lax.broadcasted_iota(jnp.int32, shape, 1)


def half_mean(v):
    low = lanes(v.shape) < HEAD_SIZE
    first = jnp.sum(jnp.where(low, v, 0.0), axis=1, keepdims=True)
    second = jnp.sum(jnp.where(low, 0.0, v), axis=1, keepdims=True)
    return jnp.where(low, first, second) * (1.0 / HEAD_SIZE)


def half_swap(v):
    quarter = HEAD_SIZE // 2
    left = pltpu.roll(v, 128 - quarter, 1)
    right = pltpu.roll(v, quarter, 1)
    return jnp.where(lanes(v.shape) % HEAD_SIZE < quarter, left, right)


def row_scale(v):
    return lax.rsqrt(jnp.mean(v * v, axis=1, keepdims=True) + EPSILON)


def norm_back(dn, v, gain):
    scale = row_scale(v)
    unit = v * scale
    scaled = dn * gain
    grad = scale * (scaled - unit * jnp.mean(scaled * unit, axis=1, keepdims=True))
    return grad, jnp.sum(dn * unit, axis=0, keepdims=True)


def qk_forward(raw, gain, cosines, sines, is_value):
    normed = raw * lax.rsqrt(half_mean(raw * raw) + EPSILON) * gain
    turned = normed * cosines + half_swap(normed) * sines
    return jnp.where(is_value, raw, turned)


def qk_backward(grad, raw, gain, cosines, sines, is_value):
    straight = grad * cosines - half_swap(grad) * sines
    scale = lax.rsqrt(half_mean(raw * raw) + EPSILON)
    unit = raw * scale
    scaled = straight * gain
    back = scale * (scaled - unit * half_mean(scaled * unit))
    gain_grad = jnp.sum(straight * unit, axis=0, keepdims=True)
    return jnp.where(is_value, grad, back), gain_grad


def two_heads(v):
    low = lanes(v.shape) < HEAD_SIZE
    zero = jnp.zeros_like(v)
    return jnp.concatenate([jnp.where(low, v, zero), jnp.where(low, zero, v)], axis=0)


def head_gains(gain_query, gain_key, q_width, kv_width, b):
    key, value = q_width, q_width + kv_width
    parts = [
        gain_query[...]
        if c < key
        else gain_key[...]
        if c < value
        else jnp.ones((1, HEAD_SIZE), F32)
        for c in (b, b + HEAD_SIZE)
    ]
    return jnp.concatenate(parts, axis=1)


def one_row(v):
    rows = v.shape[0] // 2
    return jnp.where(lanes((rows, v.shape[1])) < HEAD_SIZE, v[:rows], v[rows:])


def twice(v, which):
    half = v[:, which * HEAD_SIZE : (which + 1) * HEAD_SIZE]
    return jnp.concatenate([half, half], axis=1)


def both_halves(v):
    return v + jnp.concatenate([v[:, HEAD_SIZE:], v[:, :HEAD_SIZE]], axis=1)


def over_key_heads(n_heads, values_from, body):
    if n_heads % 2:
        for g in range(n_heads):
            body([(g, (g // 2, g % 2), ((values_from + g) // 2, (values_from + g) % 2))])
        return

    def step(i, carry):
        body([(2 * i + e, (i, e), (values_from // 2 + i, e)) for e in range(2)])
        return carry

    lax.fori_loop(0, n_heads // 2, step, 0)


def lane_block(i):
    return block_rows(i, 128)


def segment_start(lengths, slots):
    end = lengths[0, 0]
    start = jnp.where(slots >= end, end, 0)
    for i in range(1, lengths.shape[1] - 1):
        end = end + lengths[0, i]
        start = jnp.where(slots >= end, end, start)
    return start


def sublanes(shape):
    return lax.broadcasted_iota(jnp.int32, shape, 0)


def count(mask, axis):
    return jnp.sum(mask.astype(F32), axis=axis, keepdims=True).astype(jnp.int32)


def routing(place, slots, rows, share):
    lines = rows // 128
    groups = slots.shape[0] // lines
    square = (rows, rows)

    def line(s):
        return jnp.concatenate([slots[pl.ds(s * lines + i, 1), :] for i in range(lines)], axis=1)

    row = line(place.me)
    column = jnp.broadcast_to(row.astype(F32), (128, rows)).T[:, :1].astype(jnp.int32)
    base = row // rows * rows
    rank = count((column < row) & (column >= base), 0)
    sent_row = row // rows * share + rank
    base = column // rows * rows
    rank = count((row < column) & (row >= base), 1)
    sent_column = column // rows * share + rank
    low = 32
    high = rows // low
    table = jnp.zeros((high, low), F32)
    for s in range(groups):
        r = line(s)
        left = (r // low - place.me * high) == sublanes((high, rows))
        right = r % low == sublanes((low, rows))
        table = table + dot(left.astype(BF), right.astype(BF), 1, 1) * float(s)
    spread = (lanes((low, rows)) % low == sublanes((low, rows))).astype(F32)
    pick = lanes((high, rows)) // low == sublanes((high, rows))
    from_row = jnp.sum(jnp.where(pick, dot(table, spread, 1, 0), 0.0), axis=0, keepdims=True)
    spread = (sublanes((rows, low)) % low == lanes((rows, low))).astype(F32)
    pick = sublanes((rows, high)) // low == lanes((rows, high))
    from_column = jnp.sum(jnp.where(pick, dot(spread, table, 1, 1), 0.0), axis=1, keepdims=True)
    from_row, from_column = from_row.astype(jnp.int32), from_column.astype(jnp.int32)
    same = from_row == from_column
    got_column = from_column * share + count(same & (lanes(square) < sublanes(square)), 1)
    got_row = from_row * share + count(same & (sublanes(square) < lanes(square)), 0)
    return sent_row, sent_column, got_row, got_column


class Place:
    def __init__(self, n, ctx, tp):
        self.n, self.ctx, self.tp = n, ctx, tp
        self.z = lax.axis_index("fsdp")
        self.c = lax.axis_index("ctx")
        self.t = lax.axis_index("tp")
        self.me = self.z * ctx + self.c

    def at(self, z=None, c=None, t=None):
        return (
            self.z if z is None else z,
            self.c if c is None else c,
            self.t if t is None else t,
        )

    def peer(self, j):
        p = lax.rem(self.me + j, self.n * self.ctx)
        return self.at(p // self.ctx, lax.rem(p, self.ctx))

    def up(self, j):
        return self.at(z=lax.rem(self.z + j, self.n))

    def flip(self, bit):
        if bit == 1:
            return self.c + 1 - 2 * lax.rem(self.c, 2)
        return lax.rem(self.c + 2, 4)

    def side(self, j):
        return self.at(t=lax.rem(self.t + j, self.tp))

    def owner(self, k, c):
        return lax.rem(self.z - k + self.n, self.n) * self.ctx + c

    def greet(self):
        barrier = pltpu.get_barrier_semaphore()
        group = self.n * self.ctx
        for j in range(1, group):
            pl.semaphore_signal(barrier, inc=1, device_id=self.peer(j), device_id_type=MESH)
        for j in range(1, self.tp):
            pl.semaphore_signal(barrier, inc=1, device_id=self.side(j), device_id_type=MESH)
        pl.semaphore_wait(barrier, group + self.tp - 2)


MESH = pl.DeviceIdType.MESH


def remote(src, dst, send, recv, device):
    return pltpu.make_async_remote_copy(
        src_ref=src, dst_ref=dst, send_sem=send, recv_sem=recv, device_id=device, device_id_type=MESH
    )


def block_rows(index, size):
    return pl.ds(pl.multiple_of(index * size, size), size)


class Gather:
    def __init__(self, place, whole, columns, number, sems, chip_first=False):
        z_send, z_recv, x_send, x_recv, c_send, c_recv = sems
        h = whole.shape[0] // (place.n * place.ctx)
        n = place.n
        self.n, self.chip_first = n, chip_first
        view = lambda index: whole.at[block_rows(index, h), columns]
        here, there = place.c, place.flip(2)

        def ring(lane, row):
            return [
                remote(
                    view(place.owner(k - 1, lane)),
                    view(place.owner(k - 1, lane)),
                    z_send.at[row, k],
                    z_recv.at[row, k],
                    place.up(1),
                )
                for k in range(1, n)
            ]

        self.rings = [ring(here, number)] + ([ring(there, number + 1)] if chip_first else [])
        self.chip = [
            remote(
                view(place.owner(k, here)),
                view(place.owner(k, here)),
                x_send.at[number, k],
                x_recv.at[number, k],
                place.at(c=there),
            )
            for k in range(1 if chip_first else n)
        ]
        self.core = [
            remote(
                view(place.owner(i % n, here if i < n else there)),
                view(place.owner(i % n, here if i < n else there)),
                c_send.at[number, i],
                c_recv.at[number, i],
                place.at(c=place.flip(1)),
            )
            for i in range(2 * n)
        ]

    def begin(self):
        if self.n > 1:
            self.rings[0][0].start()
        self.core[0].start()

    def begin_other(self):
        if self.n > 1:
            self.rings[1][0].start()

    def advance(self, k):
        if k >= self.n:
            return
        for r, ring in enumerate(self.rings):
            ring[k - 1].wait_recv()
            if k + 1 < self.n:
                ring[k].start()
            self.core[r * self.n + k].start()

    def to_chip(self, k):
        if k < len(self.chip):
            self.chip[k].start()

    def from_chip(self, k):
        if k < len(self.chip):
            self.chip[k].wait_recv()
            self.core[self.n + k].start()

    def finish(self):
        for copy in self.core:
            copy.wait_recv()

    def drain(self):
        for copy in sum(self.rings, []) + self.chip + self.core:
            copy.wait_send()


def forward_kernel(
    n, ctx, tp, q_width, kv_width, tile,
    lengths, tokens, cotangent, slots, gain, gain_query, gain_key, gain_ffn, frequency,
    w_query, w_key, w_value, w_out, w_gate, w_up, w_down,
    sums, squares, ffn_out, dmid, dgain, take_back, send_back, cosines, sines,
    x, dy, qb_out, kv, heads_out, mid_own, w_attn, normed_two, down_keep, d_gate, d_up,
    sent_x, sent_y, got_x, got_y, own_x, own_y, x_land, y_land, pick, qb, heads, mid,
    w, w_ffn, kv_all, part, land, bias, ffn_acc, dn_acc, acts, turned, d_keep, d_send, d_land,
    route_send, route_recv, tp_send, tp_recv, kv_send, kv_recv, out_sem, act_sem, down_send, down_recv, *gather_sems
):
    place = Place(n, ctx, tp)
    group = n * ctx
    rows = got_x.shape[0]
    share = rows // group
    feat = got_x.shape[1]
    width = x_land.shape[1]
    piece = rows
    attn = Gather(place, w, pl.ds(0, w.shape[1]), 0, gather_sems)
    tiles = w_ffn.shape[1] // (3 * tile)
    last = max(1, tiles // 9)
    cuts = [(tiles - last) * i // 3 for i in range(3)] + [tiles - last, tiles]
    first, second, third, tail = (
        Gather(
            place,
            w_ffn,
            pl.ds(cuts[i] * 3 * tile, (cuts[i + 1] - cuts[i]) * 3 * tile),
            1 + i,
            gather_sems,
            chip_first=i == 3,
        )
        for i in range(4)
    )
    groups = [first, second, third]
    stores = []

    def store(src, dst):
        copy = pltpu.make_async_copy(src, dst, out_sem.at[len(stores)])
        copy.start()
        stores.append(copy)

    def route(number, src, dst):
        return [
            remote(
                src.at[block_rows(lax.rem(place.me + j, group), share), :],
                dst.at[block_rows(place.me, share), :],
                route_send.at[number, j],
                route_recv.at[number, j],
                place.peer(j),
            )
            for j in range(1, group)
        ]

    def widen(number, src, dst):
        return [
            remote(
                src,
                dst.at[:, block_rows(place.t, feat)],
                tp_send.at[number, j],
                tp_recv.at[number, j],
                place.side(j),
            )
            for j in range(1, tp)
        ]

    def own_block(src, dst):
        at = block_rows(place.me, share)
        dst[at, :] = src[at, :]

    route_x, route_y = route(0, sent_x, got_x), route(1, sent_y, got_y)
    wide_x, wide_y = widen(0, own_x, x_land), widen(1, own_y, y_land)
    shard_rows = w_query.shape[0]
    own_shard = block_rows(place.me, shard_rows)
    column = 0
    for part_w in (w_query, w_key, w_value):
        w[own_shard, column : column + part_w.shape[1]] = part_w[...]
        column += part_w.shape[1]
    w[own_shard, column:] = w_out[...]
    place.greet()
    attn.begin()
    attn.to_chip(0)
    sent_row, sent_column, got_row, got_column = routing(place, slots, rows, share)
    for i in range(tiles):
        used = min(tile, w_gate.shape[1] - i * tile)
        cols = slice(i * tile, i * tile + used)
        for m, value in enumerate((w_gate[:, cols], w_up[:, cols], w_down[:, cols])):
            if used < tile:
                value = jnp.concatenate(
                    [value, jnp.zeros((shard_rows, tile - used), BF)], axis=1
                )
            c = (3 * i + m) * tile
            w_ffn[own_shard, c : c + tile] = value
    square = (rows, rows)
    send_pick = (sublanes(square) == sent_row).astype(BF)
    sent_x[...] = dot(send_pick, tokens[...], 1, 0).astype(BF)
    for copy in route_x:
        copy.start()
    own_block(sent_x, got_x)
    attn.advance(1)
    attn.to_chip(1)
    sent_y[...] = dot(send_pick, cotangent[...], 1, 0).astype(BF)
    own_block(sent_y, got_y)
    pick[...] = (lanes(square) == got_column).astype(BF)
    take_back[...] = (sublanes(square) == got_row).astype(BF)
    send_back[...] = (lanes(square) == sent_column).astype(BF)
    slot = place.c * piece + sublanes((rows, 128))
    start_col = segment_start(lengths, slot)
    angle = (slot - start_col).astype(F32) * frequency[...]
    start_col = start_col[:, :1]
    cosines[...] = jnp.cos(angle)
    turned_lane = lanes((rows, 128)) % HEAD_SIZE < HEAD_SIZE // 2
    sines[...] = jnp.where(turned_lane, -1.0, 1.0) * jnp.sin(angle)
    attn.from_chip(0)
    attn.advance(2)
    attn.to_chip(2)
    first.begin()
    for copy in route_x:
        copy.wait_recv()
    own_x[...] = dot(pick[...], got_x[...], 1, 0).astype(BF)
    for copy in wide_x:
        copy.start()
    x_land[:, block_rows(place.t, feat)] = own_x[...]
    attn.from_chip(1)
    attn.advance(3)
    attn.to_chip(3)
    for copy in route_y:
        copy.start()
    second.begin()
    first.to_chip(0)
    attn.from_chip(2)
    attn.from_chip(3)
    second.to_chip(0)
    for copy in wide_x:
        copy.wait_recv()
    store(x_land, x)
    v = x_land[...].astype(F32)
    normed = (v * row_scale(v) * gain[...]).astype(BF)
    attn.finish()
    store(w, w_attn)

    own_rows = block_rows(place.c, piece)
    values_from = q_width + kv_width
    for b in list(range(q_width, q_width + 2 * kv_width, 128)) + list(range(0, q_width, 128)):
        if b == 0:
            later = start_keys(place, kv_all, own_rows, kv_send, kv_recv)
        block = dot(normed, w[:, b : b + 128], 1, 0)
        is_value = lanes(block.shape) + b >= values_from
        gains = head_gains(gain_query, gain_key, q_width, kv_width, b)
        done = qk_forward(block, gains, cosines[...], sines[...], is_value)
        if b < q_width:
            qb[:, b : b + 128] = done.astype(BF)
        else:
            kv_all[own_rows, b - q_width : b - q_width + 128] = done.astype(BF)

    q_slot = place.c * piece + lax.broadcasted_iota(jnp.int32, (rows, piece), 0)
    n_pairs = q_width // 128

    def one_piece(p):
        k_slot = p * piece + lanes((rows, piece))
        open_ = (k_slot >= start_col) & (k_slot <= q_slot)
        bias[...] = jnp.where(open_, 0.0, NEG_FILL)
        at = block_rows(p, piece)

        def heads_of(members):
            for g, (kb, ke), (vb, ve) in members:
                q2 = two_heads(qb[:, lane_block(g)])
                k2 = twice(kv_all[at, lane_block(kb)], ke)
                v2 = twice(kv_all[at, lane_block(vb)], ve)
                for h in range(2):
                    part = slice(h * rows, (h + 1) * rows)
                    e = jnp.exp(dot(q2[part], k2, 1, 1) * 0.125 + bias[...])
                    part_sum = e[:, :128]
                    for b in range(128, piece, 128):
                        part_sum = part_sum + e[:, b : b + 128]
                    block = lane_block(2 * g + h)
                    acc[:, block] += dot(e.astype(BF), v2, 1, 0)
                    total[:, block] += part_sum

        over_key_heads(n_pairs, kv_width // HEAD_SIZE, heads_of)

    acc, total = ffn_acc, dn_acc
    acc[...] = jnp.zeros_like(acc)
    total[...] = jnp.zeros_like(total)
    one_piece(place.c)
    x_bit, core_bit = place.c // 2, lax.rem(place.c, 2)
    near, across, passed = later
    first.advance(1)
    second.advance(1)

    @pl.when(x_bit == 1)
    def _():
        across.wait_recv()
        passed.start()

    first.from_chip(0)
    second.from_chip(0)
    tail.to_chip(0)
    first.to_chip(1)
    for copy in route_y:
        copy.wait_recv()
    own_y[...] = dot(pick[...], got_y[...], 1, 0).astype(BF)
    for copy in wide_y:
        copy.start()
    y_land[:, block_rows(place.t, feat)] = own_y[...]

    @pl.when(core_bit == 1)
    def _():
        near.wait_recv()
        one_piece(place.c - 1)

    first.advance(2)
    second.advance(2)
    second.to_chip(1)

    @pl.when(x_bit == 1)
    def _():
        passed.wait_recv()

        def step(p, carry):
            one_piece(p)
            return carry

        lax.fori_loop(0, 2, step, 0)

    ones = jnp.ones((8, 128), F32)
    for g in range(n_pairs):
        first_head, second_head = lane_block(2 * g), lane_block(2 * g + 1)
        values, totals = (
            jnp.concatenate([v[:, first_head], v[:, second_head]], axis=0) for v in (acc, total)
        )
        row_total = jnp.sum(totals, axis=1, keepdims=True)
        heads[:, 128 * g : 128 * g + 128] = one_row(values / row_total)
        sums[g] = 1.0 / dot(ones, totals, 1, 1, lax.Precision.HIGHEST)
    part[...] = dot(heads[...].astype(BF), w[:, q_width + 2 * kv_width :], 1, 1).astype(BF)
    attention = [
        remote(part, land.at[j - 1], tp_send.at[2, j], tp_recv.at[2, j], place.side(j))
        for j in range(1, tp)
    ]
    for copy in attention:
        copy.start()
    store(qb, qb_out)
    store(heads, heads_out)
    first.from_chip(1)
    first.to_chip(2)
    first.advance(3)
    second.advance(3)
    third.begin()
    tail.from_chip(0)
    tail.begin()
    tail.begin_other()
    second.from_chip(1)
    second.to_chip(2)
    first.from_chip(2)
    first.to_chip(3)
    third.advance(1)
    second.from_chip(2)
    second.to_chip(3)
    third.to_chip(0)
    tail.advance(1)
    third.advance(2)
    first.from_chip(3)
    third.to_chip(1)
    for copy in attention:
        copy.wait_recv()
    att = part[...].astype(F32)
    for j in range(1, tp):
        att = att + land[j - 1].astype(F32)
    v = x_land[...].astype(F32)
    squares[0:1, :] = jnp.sum(v * v, axis=0, keepdims=True)
    squares[1:2, :] = jnp.sum(att * att, axis=0, keepdims=True)
    mid[...] = v + att
    store(mid.at[:, block_rows(place.t, feat)], mid_own)
    v = (v + att).astype(BF).astype(F32)
    for copy in attention:
        copy.wait_send()
    nb = part
    nb[...] = (v * row_scale(v) * gain_ffn[...]).astype(BF)
    store(nb, normed_two)
    ffn_acc[...] = jnp.zeros_like(ffn_acc)
    dn_acc[...] = jnp.zeros_like(dn_acc)
    third.to_chip(2)
    third.from_chip(0)
    for copy in wide_y:
        copy.wait_recv()
    store(y_land, dy)
    turn_blocks(place, y_land, turned)

    def one_tile(i):
        at = lambda m: block_rows(3 * i + m, tile)
        w_gate, w_up, w_down = w_ffn[:, at(0)], w_ffn[:, at(1)], w_ffn[:, at(2)]
        gate = dot(nb[...], w_gate, 1, 0)
        up = dot(nb[...], w_up, 1, 0)
        d_hidden = dot(y_land[...], w_down, 1, 0)
        sig = 1.0 / (1.0 + jnp.exp(-gate))
        silu = gate * sig
        out = block_rows(i, tile)
        hidden = (silu * up).astype(BF)
        acts[0, :, out] = (d_hidden * up * (sig * (1.0 + gate * (1.0 - sig)))).astype(BF)
        acts[1, :, out] = (d_hidden * silu).astype(BF)
        ffn_acc[...] += dot(hidden, w_down, 1, 1)
        dn_acc[...] += dot(acts[0, :, out], w_gate, 1, 1) + dot(acts[1, :, out], w_up, 1, 1)
        d_keep[:, out] = dot(turned[: width // 2, :], hidden, 1, 0).astype(BF)
        d_send[:, out] = dot(turned[width // 2 :, :], hidden, 1, 0).astype(BF)

    act_stores = []
    sides_of = [pl.ds(cuts[i] * tile, (cuts[i + 1] - cuts[i]) * tile) for i in range(4)]
    down_cores = [
        remote(
            d_send.at[:, cols],
            d_land.at[:, cols],
            down_send.at[i],
            down_recv.at[i],
            place.at(c=place.flip(1)),
        )
        for i, cols in enumerate(sides_of)
    ]

    def finish_down(i):
        core_sum(d_keep.at[:, sides_of[i]], d_land.at[:, sides_of[i]], down_cores[i])
        copy = pltpu.make_async_copy(
            d_keep.at[:, sides_of[i]], down_keep.at[:, sides_of[i]], act_sem.at[2, i]
        )
        copy.start()
        act_stores.append(copy)

    for i, g in enumerate(groups + [tail]):
        if i == 1:
            tail.advance(2)
            third.advance(3)
            third.to_chip(3)
            second.from_chip(3)
            third.from_chip(1)
        if i == 2:
            tail.advance(3)
            third.from_chip(2)
            third.from_chip(3)
        g.finish()
        repeat(cuts[i + 1] - cuts[i], lambda k, i=i: one_tile(cuts[i] + k))
        down_cores[i].start()
        if i:
            finish_down(i - 1)
        cols = sides_of[i]
        for m, out in enumerate((d_gate, d_up)):
            copy = pltpu.make_async_copy(acts.at[m, :, cols], out.at[:, cols], act_sem.at[m, i])
            copy.start()
            act_stores.append(copy)
    dgain[...] = jnp.zeros_like(dgain)

    def finish_rows(i):
        r = block_rows(i, 128)
        v = mid[r, :].astype(BF).astype(F32)
        grad, gain_sum = norm_back(dn_acc[r, :], v, gain_ffn[...])
        dgain[...] += gain_sum
        dmid[r, :] = grad.astype(BF)
        ffn_out[r, :] = ffn_acc[r, :].astype(BF)

    repeat(rows // 128, finish_rows)
    finish_down(3)

    @pl.when(core_bit == 0)
    def _():
        near.wait_send()

    @pl.when(x_bit == 0)
    def _():
        across.wait_send()

    @pl.when(x_bit == 1)
    def _():
        passed.wait_send()

    store(kv_all, kv)
    for copy in route_x + route_y + wide_x + wide_y:
        copy.wait_send()
    for g in [attn, tail] + groups:
        g.drain()
    for copy in down_cores:
        copy.wait_send()
    for copy in stores + act_stores:
        copy.wait()


def start_keys(place, kv_all, own_rows, send, recv):
    x_bit, core_bit = place.c // 2, lax.rem(place.c, 2)
    mine = kv_all.at[own_rows, :]
    near = remote(mine, mine, send.at[0], recv.at[0], place.at(c=place.flip(1)))
    across = remote(mine, mine, send.at[1], recv.at[1], place.at(c=place.flip(2)))
    from_chip = kv_all.at[block_rows(place.flip(2), own_rows.size), :]
    passed = remote(from_chip, from_chip, send.at[2], recv.at[2], place.at(c=place.flip(1)))

    @pl.when(x_bit == 0)
    def _():
        across.start()

    @pl.when(core_bit == 0)
    def _():
        near.start()

    return near, across, passed


def forward_pass(grid, q_width, kv_width, tile, *operands):
    tokens, w_query, w_key, w_gate = operands[1], operands[9], operands[10], operands[13]
    rows, feat = tokens.shape
    n, ctx, tp = grid.n, grid.ctx, grid.tp
    width = feat * tp
    n_pairs = q_width // 128
    row_len = rows * ctx
    ff = -(-w_gate.shape[1] // tile) * tile
    vm = pl.BlockSpec(memory_space=pltpu.VMEM)
    dma = pltpu.SemaphoreType.DMA
    V = pltpu.VMEM
    group = n * ctx
    attn_width = 2 * w_query.shape[1] + 2 * w_key.shape[1]
    return pl.pallas_call(
        functools.partial(forward_kernel, n, ctx, tp, q_width, kv_width, tile),
        in_specs=[pl.BlockSpec(memory_space=pltpu.SMEM)] + [vm] * 15,
        out_specs=[vm] * 9 + [ANYWHERE] * 11,
        out_shape=[
            shape((n_pairs, 8, 2 * rows), F32),
            shape((2, width), F32),
            shape((rows, width), BF),
            shape((rows, width), BF),
            shape((1, width), F32),
            shape((rows, rows), BF),
            shape((rows, rows), BF),
            shape((rows, 128), F32),
            shape((rows, 128), F32),
            shape((rows, width), BF),
            shape((rows, width), BF),
            shape((rows, q_width), BF),
            shape((row_len, 2 * kv_width), BF),
            shape((rows, q_width), F32),
            shape((rows, feat), F32),
            shape((width, attn_width), BF),
            shape((rows, width), BF),
            shape((width // 2, ff), BF),
            shape((rows, ff), BF),
            shape((rows, ff), BF),
        ],
        scratch_shapes=[V((rows, feat), BF)] * 6
        + [
            V((rows, width), BF),
            V((rows, width), BF),
            V((rows, rows), BF),
            V((rows, q_width), BF),
            V((rows, q_width), F32),
            V((rows, width), F32),
            V((width, attn_width), BF),
            V((width, 3 * ff), BF),
            V((row_len, 2 * kv_width), BF),
            V((rows, width), BF),
            V((tp - 1, rows, width), BF),
            V((rows, rows), F32),
            V((rows, width), F32),
            V((rows, width), F32),
            V((2, rows, ff), BF),
            V((width, rows), BF),
            V((width // 2, ff), BF),
            V((width // 2, ff), BF),
            V((width // 2, ff), BF),
            dma((2, group)),
            dma((2, group)),
            dma((3, tp)),
            dma((3, tp)),
            dma((3,)),
            dma((3,)),
            dma((8,)),
            dma((3, 4)),
            dma((4,)),
            dma((4,)),
            dma((6, n)),
            dma((6, n)),
            dma((5, n)),
            dma((5, n)),
            dma((5, 2 * n)),
            dma((5, 2 * n)),
        ],
        compiler_params=pltpu.CompilerParams(
            vmem_limit_bytes=61 * 2**20, collective_id=0, has_side_effects=True
        ),
        cost_estimate=pl.CostEstimate(
            flops=12 * rows * width * ff, bytes_accessed=40 * 2**20, transcendentals=0
        ),
    )(*operands)


def repeat(count, body):
    def step(i, carry):
        body(i)
        return carry

    lax.fori_loop(0, count, step, 0)


def add_into(to, more):
    step = 16

    def add(i):
        at = block_rows(i, step)
        to[at, :] = (to[at, :].astype(F32) + more[at, :].astype(F32)).astype(to.dtype)

    repeat(to.shape[0] // step, add)


def turn_blocks(place, source, turned):
    width = source.shape[1]
    n = place.n
    h = width // (n * place.ctx)
    first = lax.rem(place.c, 2) == 0

    def turn(i):
        chip = lax.rem(place.c // 2 + i // n, 2)
        pair = lax.rem(place.z - lax.rem(i, n) + n, n) * (place.ctx // 2) + chip
        block = source[:, block_rows(pair, 2 * h)].astype(F32).T.astype(turned.dtype)
        low, high = block[:h], block[h:]
        turned[block_rows(i, h), :] = jnp.where(first, low, high)
        turned[block_rows(i + 2 * n, h), :] = jnp.where(first, high, low)

    repeat(2 * n, turn)


class Scatter:
    def __init__(
        self, place, keep, columns, chip_land, line_land, number, sems, line_first=False
    ):
        x_send, x_recv, z_send, z_recv = sems
        n = place.n
        self.n, self.line_first = n, line_first
        self.h = h = keep.shape[0] // (2 * n)
        self.keep = [keep.at[pl.ds(k * h, h), columns] for k in range(2 * n)]
        land = [chip_land.at[pl.ds(k * h, h), columns] for k in range(n)]
        line = [line_land.at[k, :, columns] for k in range(n - 1)]
        there = place.at(c=place.flip(2))

        def ring(blocks, lands, row):
            return [
                remote(blocks[k], lands[k - 1], z_send.at[row, k], z_recv.at[row, k], place.up(1))
                for k in range(1, n)
            ]

        self.rings = [(ring(self.keep[:n], line, number), self.keep[:n], line)]
        if line_first:
            self.rings.append((ring(self.keep[n:], land[1:], number + 1), self.keep[n:], land[1:]))
            self.chip = remote(
                self.keep[n], land[0], x_send.at[number], x_recv.at[number], there
            )
            self.chip_land = land[:1]
        else:
            self.chip = remote(
                keep.at[pl.ds(n * h, n * h), columns],
                chip_land.at[:, columns],
                x_send.at[number],
                x_recv.at[number],
                there,
            )
            self.chip_land = land

    def to_chip(self):
        self.chip.start()

    def from_chip(self):
        self.chip.wait_recv()
        if self.line_first:
            return
        for k in list(range(1, self.n)) + [0]:
            add_into(self.keep[k], self.chip_land[k])
            if k == 1:
                self.begin()

    def begin(self):
        for ring, _, _ in self.rings:
            if ring:
                ring[0].start()

    def advance(self, k):
        if k >= self.n:
            return
        for ring, blocks, lands in self.rings:
            ring[k - 1].wait_recv()
            if k + 1 < self.n:
                add_into(blocks[k + 1], lands[k - 1])
                ring[k].start()
            elif self.line_first:
                add_into(blocks[0], lands[k - 1])

    def finish(self, out):
        last = self.chip_land[0] if self.line_first else self.rings[0][2][self.n - 2]
        step = 16

        def add(i):
            at = block_rows(i, step)
            out[at, :] = self.keep[0][at, :].astype(F32) + last[at, :].astype(F32)

        repeat(self.h // step, add)

    def drain(self, chip=True):
        if chip:
            self.chip.wait_send()
        for ring, _, _ in self.rings:
            for copy in ring:
                copy.wait_send()


def core_sum(keep, core_land, copy):
    copy.wait_recv()
    add_into(keep, core_land)


def backward_kernel(
    n, ctx, tp, q_width, kv_width, stage_cols,
    lengths, ffn, dmid, sums, cosines, sines, pick_t, gain, gain_query, gain_key,
    gain_ffn_grad, squares, qb_in, kv_in, heads_in, w_in, dy_in, x_in, mid_in, normed_two, down_in, d_gate, d_up,
    back_o, back_g, sum_gate, sum_up, sum_down, sum_out, sum_qkv, small,
    qb, kv_all, heads, w, x, turned, stage, keep, send, core_land, chip_land, line_land,
    o_keep, o_send, o_core, o_chip, o_line, a_keep, a_send, a_core, a_chip, a_line,
    d_mid_own, d_attn, dob, delta, bias, dq_t, dkv, kv_land, tp_land, ffn_away, ffn_land, dx_away, dx_land,
    sent, small_mine, small_land, small_side,
    tp_send, tp_recv, route_send, route_recv, small_send, small_recv, kv_send, kv_recv, load_sem,
    *scatter_sems
):
    place = Place(n, ctx, tp)
    group = n * ctx
    rows, width = dmid.shape
    feat = width // tp
    share = rows // group
    piece = rows
    ff = d_gate.shape[1]
    half = width // 2
    n_pairs = q_width // 128
    qkv_width = q_width + 2 * kv_width
    values_from = q_width + kv_width
    x_bit, core_bit = place.c // 2, lax.rem(place.c, 2)
    own_cols = block_rows(place.t, feat)
    c_send, c_recv, *ring_sems = scatter_sems
    everything = pl.ds(0, ff)
    lands = lambda m: (chip_land.at[m], line_land.at[m])
    cut = ff // 128 * 16 // 18 * 128
    down = Scatter(place, keep.at[0], pl.ds(0, cut), *lands(0), 0, ring_sems, True)
    down_x = Scatter(place, keep.at[0], pl.ds(cut, ff - cut), *lands(0), 6, ring_sems)
    gate = Scatter(place, keep.at[1], everything, *lands(1), 2, ring_sems)
    mid_cut = ff // 256 * 128
    up_a = Scatter(place, keep.at[2], pl.ds(0, mid_cut), *lands(2), 3, ring_sems)
    up_b = Scatter(place, keep.at[2], pl.ds(mid_cut, ff - mid_cut), *lands(2), 7, ring_sems)
    out_sum = Scatter(place, o_keep, pl.ds(0, q_width), o_chip, o_line, 4, ring_sems)
    qkv_sum = Scatter(place, a_keep, pl.ds(0, qkv_width), a_chip, a_line, 5, ring_sems)
    across_cores = [
        remote(src, dst, c_send.at[i], c_recv.at[i], place.at(c=place.flip(1)))
        for i, (src, dst) in enumerate(
            [(send.at[m], core_land.at[m]) for m in range(2)]
            + [(o_send, o_core), (a_send, a_core)]
        )
    ]

    def to_sides(number, src, dst):
        return [
            remote(
                src(j), dst.at[j - 1], tp_send.at[number, j], tp_recv.at[number, j], place.side(j)
            )
            for j in range(1, tp)
        ]

    def away(buffer):
        return lambda j: buffer.at[j - 1]

    def fill_away(buffer, source):
        for j in range(1, tp):
            buffer[j - 1] = source[:, block_rows(lax.rem(place.t + j, tp), feat)]

    def route(number, src, dst):
        return [
            remote(
                src.at[block_rows(lax.rem(place.me + j, group), share), :],
                dst.at[block_rows(place.me, share), :],
                route_send.at[number, j],
                route_recv.at[number, j],
                place.peer(j),
            )
            for j in range(1, group)
        ]

    dmid_sum = to_sides(0, lambda j: dmid, tp_land)
    ffn_sum = to_sides(1, away(ffn_away), ffn_land)
    dx_sum = to_sides(2, away(dx_away), dx_land)
    route_o, route_g = route(0, sent, back_o), route(1, dob, back_g)

    place.greet()
    for copy in dmid_sum:
        copy.start()

    sources = (d_gate, d_up)
    tiles = [(m, b) for m in range(2) for b in range(0, ff, stage_cols)]
    loads = [
        pltpu.make_async_copy(
            sources[m].at[:, pl.ds(b, stage_cols)], stage.at[i % 2], load_sem.at[i]
        )
        for i, (m, b) in enumerate(tiles)
    ]
    load_n = pltpu.make_async_copy(normed_two, d_attn, load_sem.at[len(tiles)])
    dy, mid = x, d_mid_own
    load_dy = pltpu.make_async_copy(dy_in, dy, load_sem.at[len(tiles) + 1])
    load_x = pltpu.make_async_copy(x_in, x, load_sem.at[len(tiles) + 2])
    load_mid = pltpu.make_async_copy(mid_in, mid, load_sem.at[len(tiles) + 3])
    load_down = pltpu.make_async_copy(down_in, keep.at[0], load_sem.at[len(tiles) + 4])
    load_down.start()
    load_n.start()
    loads[0].start()
    more_loads = [
        pltpu.make_async_copy(src, dst, load_sem.at[len(tiles) + 5 + i])
        for i, (src, dst) in enumerate(((w_in, w), (qb_in, qb), (kv_in, kv_all), (heads_in, heads)))
    ]
    for copy in [load_dy, load_mid] + more_loads:
        copy.start()
    load_down.wait()
    down.begin()
    down_x.to_chip()
    fill_away(ffn_away, ffn)
    load_n.wait()
    turn_blocks(place, d_attn, turned)
    sub = 256 if stage_cols % 256 == 0 else 128
    for i, (m, b) in enumerate(tiles):
        if i + 1 < len(tiles):
            loads[i + 1].start()
        if m == 1 and b == ff // 2 // stage_cols * stage_cols:
            core_sum(keep.at[1], core_land.at[0], across_cores[0])
            gate.to_chip()
        loads[i].wait()
        for s in range(0, stage_cols, sub):
            right = stage[i % 2, :, s : s + sub]
            cols = slice(b + s, b + s + sub)
            keep[m + 1, :, cols] = dot(turned[:half, :], right, 1, 0).astype(BF)
            send[m, :, cols] = dot(turned[half:, :], right, 1, 0).astype(BF)
        if b + stage_cols == ff:
            across_cores[m].start()
    down.advance(1)
    core_sum(keep.at[2], core_land.at[1], across_cores[1])
    load_dy.wait()

    for copy in more_loads:
        copy.wait()
    for copy in dmid_sum:
        copy.wait_recv()
    for copy in ffn_sum:
        copy.start()

    def sum_gradient(i):
        r = block_rows(i, 128)
        d_all = dy[r, :].astype(F32) + dmid[r, :].astype(F32)
        for j in range(1, tp):
            d_all = d_all + tp_land[j - 1, r, :].astype(F32)
        d_attn[r, :] = d_all.astype(BF)

    repeat(rows // 128, sum_gradient)
    dob[...] = dot(d_attn[...], w[:, qkv_width:], 1, 0).astype(BF)
    dq_t[...] = jnp.zeros_like(dq_t)
    ones = jnp.ones((8, 128), F32)

    def set_delta(g):
        both = dob[:, lane_block(g)].astype(F32) * heads[:, lane_block(g)]
        delta[g] = dot(ones, two_heads(both), 1, 1, lax.Precision.HIGHEST)

    repeat(n_pairs, set_delta)
    q_slot = place.c * piece + lanes((piece, rows))
    start_row = segment_start(lengths, place.c * piece + lanes((8, rows)))[:1]

    def one_piece(p):
        k_slot = p * piece + lax.broadcasted_iota(jnp.int32, (piece, rows), 0)
        open_ = (k_slot >= start_row) & (k_slot <= q_slot)
        bias[...] = jnp.where(open_, 0.0, NEG_FILL)
        at = block_rows(p, piece)
        def heads_of(members):
            grads = []
            for g, (kb, ke), (vb, ve) in members:
                q2 = two_heads(qb[:, lane_block(g)])
                do2 = two_heads(dob[:, lane_block(g)])
                k2 = twice(kv_all[at, lane_block(kb)], ke)
                v2 = twice(kv_all[at, lane_block(vb)], ve)
                k_t = k2.astype(F32).T.astype(BF)
                dk = jnp.zeros((piece, 128), F32)
                dv = jnp.zeros((piece, 128), F32)
                for h in range(0, 2 * rows, 256):
                    part = slice(h, h + 256)
                    open_part = slice(h % rows, h % rows + 256)
                    s = dot(k2, q2[part], 1, 1)
                    dp = dot(v2, do2[part], 1, 1)
                    pe = jnp.exp(s * 0.125 + bias[:, open_part]) * sums[g, 0:1, part]
                    ds = (pe * (dp - delta[g, 0:1, part])).astype(BF)
                    dv = dv + dot(pe.astype(BF), do2[part], 1, 0)
                    dk = dk + dot(ds, q2[part], 1, 0)
                    dq_t[g, :, part] += dot(k_t, ds, 1, 0)
                grads.append((both_halves(dk) * 0.125, both_halves(dv)))
            low = lanes((piece, 128)) < HEAD_SIZE
            kb, vb = members[0][1][0], members[0][2][0]
            if len(members) == 2:
                dkv[at, lane_block(kb)] = jnp.where(low, grads[0][0], grads[1][0]).astype(BF)
                dkv[at, lane_block(vb)] = jnp.where(low, grads[0][1], grads[1][1]).astype(BF)
            else:
                for value, (b, e) in zip(grads[0], members[0][1:]):
                    c = 128 * b + HEAD_SIZE * e
                    dkv[at, c : c + HEAD_SIZE] = value[:, :HEAD_SIZE].astype(BF)

        over_key_heads(n_pairs, kv_width // HEAD_SIZE, heads_of)

    down.advance(2)
    down_x.from_chip()

    sibling = place.at(c=place.flip(1))
    other = 1 - core_bit
    to_passer = remote(
        dkv.at[block_rows(other, piece), :], kv_land.at[0], kv_send.at[0], kv_recv.at[0], sibling
    )
    to_chip = remote(
        dkv.at[block_rows(core_bit, piece), :],
        kv_land.at[0],
        kv_send.at[1],
        kv_recv.at[1],
        place.at(c=place.flip(2)),
    )
    to_core = remote(
        dkv.at[block_rows(2 * x_bit, piece), :], kv_land.at[1], kv_send.at[2], kv_recv.at[2], sibling
    )

    @pl.when(x_bit == 1)
    def _():
        def step(p, carry):
            one_piece(p)
            return carry

        lax.fori_loop(0, 2, step, 0)
        to_passer.start()

    turn_blocks(place, d_attn, turned)
    right = heads[...].astype(BF)
    o_keep[...] = dot(turned[:half, :], right, 1, 0).astype(BF)
    o_send[...] = dot(turned[half:, :], right, 1, 0).astype(BF)
    across_cores[2].start()
    down.advance(3)
    down_x.advance(1)

    @pl.when(x_bit == 1)
    def _():
        to_passer.wait_recv()
        mine = block_rows(core_bit, piece)
        dkv[mine, :] = (dkv[mine, :].astype(F32) + kv_land[0].astype(F32)).astype(BF)
        to_chip.start()

    gate.from_chip()
    up_a.to_chip()
    core_sum(o_keep, o_core, across_cores[2])
    out_sum.to_chip()

    @pl.when(core_bit == 1)
    def _():
        one_piece(place.c - 1)
        to_core.start()

    for copy in ffn_sum:
        copy.wait_recv()
    small_mine[...] = jnp.zeros_like(small_mine)
    load_mid.wait()

    def finish_output(i):
        r = block_rows(i, 128)
        ffn_out = ffn[r, own_cols].astype(F32)
        for j in range(1, tp):
            ffn_out = ffn_out + ffn_land[j - 1, r, :].astype(F32)
        small_mine[5:6, :feat] += jnp.sum(ffn_out * ffn_out, axis=0, keepdims=True)
        dx_away[0, r, :] = (mid[r, :] + ffn_out).astype(BF)

    repeat(rows // 128, finish_output)
    sent[...] = dot(pick_t[...], dx_away[0], 1, 0).astype(BF)
    for copy in route_o:
        copy.start()
    own = block_rows(place.me, share)
    back_o[own, :] = sent[own, :]


    def own_gradient(i):
        r = block_rows(i, 128)
        d_own = dy[r, own_cols].astype(F32) + dmid[r, own_cols].astype(F32)
        for j in range(1, tp):
            d_own = d_own + tp_land[j - 1, r, own_cols].astype(F32)
        d_mid_own[r, :] = d_own

    repeat(rows // 128, own_gradient)
    load_x.start()
    one_piece(place.c)
    up_b.to_chip()
    down_x.advance(2)
    gate.advance(1)
    normed = tp_land.at[0]
    load_x.wait()

    def norm_again(i):
        v = x[block_rows(i, 128), :].astype(F32)
        normed[block_rows(i, 128), :] = (v * row_scale(v) * gain[...]).astype(BF)

    repeat(rows // 128, norm_again)
    turn_blocks(place, normed, turned)
    mine = block_rows(place.c, piece)

    @pl.when(core_bit == 0)
    def _():
        to_core.wait_recv()

    @pl.when(x_bit == 0)
    def _():
        to_chip.wait_recv()

    d_qkv = d_attn.at[:, pl.ds(0, qkv_width)]
    for b in range(0, qkv_width, 128):
        if b < q_width:
            g = b // 128
            grad = one_row(dq_t[g].T) * 0.125
        else:
            cols = slice(b - q_width, b - q_width + 128)
            grad = dkv[mine, cols].astype(F32)
            grad = jnp.where(x_bit == 0, grad + kv_land[0, :, cols].astype(F32), grad)
            grad = jnp.where(core_bit == 0, grad + kv_land[1, :, cols].astype(F32), grad)
        raw = dot(normed[...], w[:, b : b + 128], 1, 0)
        is_value = lanes(grad.shape) + b >= values_from
        back, gain_grad = qk_backward(
            grad,
            raw,
            head_gains(gain_query, gain_key, q_width, kv_width, b),
            cosines[...],
            sines[...],
            is_value,
        )
        small_mine[2:3, b : b + 128] = gain_grad
        d_qkv[:, b : b + 128] = back.astype(BF)

    def finish_gradient(i):
        r = block_rows(i, 128)
        dn = dot(d_qkv[r, :], w[:, :qkv_width], 1, 1)
        dx, gain_grad = norm_back(dn, x[r, :].astype(F32), gain[...])
        normed[r, :] = dx.astype(BF)
        small_mine[0:1, :] += gain_grad

    repeat(rows // 128, finish_gradient)
    fill_away(dx_away, normed)
    for copy in dx_sum:
        copy.start()
    small_mine[1:2, :] = gain_ffn_grad[...]
    small_mine[3:5, :] = squares[...]
    for b in range(0, qkv_width, 256):
        cols = slice(b, b + 256)
        a_keep[:, cols] = dot(turned[:half, :], d_qkv[:, cols], 1, 0).astype(BF)
        a_send[:, cols] = dot(turned[half:, :], d_qkv[:, cols], 1, 0).astype(BF)
    across_cores[3].start()
    down_x.advance(3)
    gate.advance(2)
    small_out = [
        remote(
            small_mine, small_land.at[place.me], small_send.at[0, j], small_recv.at[0, j], place.peer(j)
        )
        for j in range(1, group)
    ]
    for copy in small_out:
        copy.start()
    small_land[place.me] = small_mine[...]
    core_sum(a_keep, a_core, across_cores[3])
    up_a.from_chip()

    for copy in dx_sum:
        copy.wait_recv()
    for copy in ffn_sum:
        copy.wait_send()

    def finish_input(i):
        r = block_rows(i, 128)
        total = d_mid_own[r, :] + normed[r, own_cols].astype(F32)
        for j in range(1, tp):
            total = total + dx_land[j - 1, r, :].astype(F32)
        ffn_away[0, r, :] = total.astype(BF)

    repeat(rows // 128, finish_input)
    dob[...] = dot(pick_t[...], ffn_away[0], 1, 0).astype(BF)
    for copy in route_g:
        copy.start()
    back_g[own, :] = dob[own, :]
    up_a.advance(1)
    up_b.chip.wait_send()
    qkv_sum.to_chip()
    down.to_chip()
    gate.advance(3)
    out_sum.from_chip()
    up_a.advance(2)
    gate.finish(sum_gate)
    up_b.from_chip()
    out_sum.advance(1)
    up_a.advance(3)
    up_b.advance(1)
    qkv_sum.from_chip()
    out_sum.advance(2)
    up_b.advance(2)
    qkv_sum.advance(1)
    out_sum.advance(3)
    down.from_chip()
    down.finish(sum_down.at[:, pl.ds(0, cut)])
    down_x.finish(sum_down.at[:, pl.ds(cut, ff - cut)])
    up_a.finish(sum_up.at[:, pl.ds(0, mid_cut)])
    up_b.advance(3)
    qkv_sum.advance(2)
    out_sum.finish(sum_out)
    up_b.finish(sum_up.at[:, pl.ds(mid_cut, ff - mid_cut)])
    for copy in small_out:
        copy.wait_recv()
    total = small_land[0]
    for i in range(1, group):
        total = total + small_land[i]
    small_side[place.t] = total
    for copy in small_out:
        copy.wait_send()
    small_mine[...] = total
    sides = [
        remote(
            small_mine, small_side.at[place.t], small_send.at[1, j], small_recv.at[1, j], place.side(j)
        )
        for j in range(1, tp)
    ]
    for copy in sides:
        copy.start()
    for copy in sides:
        copy.wait_recv()
    total = small_side[0]
    for j in range(1, tp):
        total = total + small_side[j]
    small[...] = total
    for copy in route_o:
        copy.wait_recv()
    qkv_sum.advance(3)
    qkv_sum.finish(sum_qkv)
    for copy in route_g:
        copy.wait_recv()

    @pl.when(x_bit == 1)
    def _():
        to_passer.wait_send()
        to_chip.wait_send()

    @pl.when(core_bit == 1)
    def _():
        to_core.wait_send()

    for copy in dmid_sum + dx_sum + route_o + route_g + sides:
        copy.wait_send()
    for copy in across_cores:
        copy.wait_send()
    for s in (down, down_x, gate, up_a, out_sum, qkv_sum):
        s.drain()
    up_b.drain(chip=False)


def backward_pass(grid, q_width, kv_width, *operands):
    dmid, d_gate = operands[2], operands[21]
    rows, width = dmid.shape
    ff = d_gate.shape[1]
    n, ctx, tp = grid.n, grid.ctx, grid.tp
    group = n * ctx
    feat = width // tp
    half = width // 2
    h = width // group
    n_pairs = q_width // 128
    qkv_width = q_width + 2 * kv_width
    stage_cols = 256 if ff % 256 == 0 else 128
    vm = pl.BlockSpec(memory_space=pltpu.VMEM)
    dma = pltpu.SemaphoreType.DMA
    V = pltpu.VMEM

    def scatter_space(cols):
        return [
            V((half, cols), BF),
            V((half, cols), BF),
            V((half, cols), BF),
            V((half // 2, cols), BF),
            V((n - 1, h, cols), BF),
        ]

    return pl.pallas_call(
        functools.partial(backward_kernel, n, ctx, tp, q_width, kv_width, stage_cols),
        in_specs=[pl.BlockSpec(memory_space=pltpu.SMEM)] + [vm] * 11 + [ANYWHERE] * 11,
        out_specs=[vm] * 8,
        out_shape=[
            shape((rows, feat), BF),
            shape((rows, feat), BF),
            shape((h, ff), F32),
            shape((h, ff), F32),
            shape((h, ff), F32),
            shape((h, q_width), F32),
            shape((h, qkv_width), F32),
            shape((8, width), F32),
        ],
        scratch_shapes=[
            V((rows, q_width), BF),
            V((rows * ctx, 2 * kv_width), BF),
            V((rows, q_width), F32),
            V((width, q_width + qkv_width), BF),
            V((rows, width), BF),
            V((width, rows), BF),
            V((2, rows, stage_cols), BF),
            V((3, half, ff), BF),
            V((2, half, ff), BF),
            V((2, half, ff), BF),
            V((3, half // 2, ff), BF),
            V((3, n - 1, h, ff), BF),
        ]
        + scatter_space(q_width)
        + scatter_space(qkv_width)
        + [
            V((rows, feat), F32),
            V((rows, width), BF),
            V((rows, q_width), BF),
            V((n_pairs, 8, 2 * rows), F32),
            V((rows, rows), F32),
            V((n_pairs, 128, 2 * rows), F32),
            V((rows * ctx, 2 * kv_width), BF),
            V((2, rows, 2 * kv_width), BF),
            V((tp - 1, rows, width), BF),
            V((tp - 1, rows, feat), BF),
            V((tp - 1, rows, feat), BF),
            V((tp - 1, rows, feat), BF),
            V((tp - 1, rows, feat), BF),
            V((rows, feat), BF),
            V((8, width), F32),
            V((group, 8, width), F32),
            V((tp, 8, width), F32),
            dma((3, tp)),
            dma((3, tp)),
            dma((2, group)),
            dma((2, group)),
            dma((2, max(group, tp))),
            dma((2, max(group, tp))),
            dma((3,)),
            dma((3,)),
            dma((2 * (ff // stage_cols) + 9,)),
            dma((4,)),
            dma((4,)),
            dma((8,)),
            dma((8,)),
            dma((8, n)),
            dma((8, n)),
        ],
        compiler_params=pltpu.CompilerParams(
            vmem_limit_bytes=61 * 2**20, collective_id=1, has_side_effects=True
        ),
        cost_estimate=pl.CostEstimate(
            flops=20 * rows * rows * ctx * q_width, bytes_accessed=40 * 2**20, transcendentals=0
        ),
    )(*operands)


def output_kernel(
    tp, entries, place_o, place_g, send_back, gate, up, down, out, qkv, small,
    output, grad_tokens, g_query, g_key, g_value, g_out, g_gate, g_up, g_down,
    gain_a, gain_f, gain_q, gain_k, stats
):
    a, b = g_query.shape[1], g_query.shape[1] + g_key.shape[1]
    output[...] = dot(send_back[...], place_o[...], 1, 0).astype(BF)
    grad_tokens[...] = dot(send_back[...], place_g[...], 1, 0).astype(BF)
    g_query[...] = qkv[:, :a]
    g_key[...] = qkv[:, a:b]
    g_value[...] = qkv[:, b:]
    g_out[...] = out[...]
    ff = g_gate.shape[1]
    g_gate[...] = gate[:, :ff]
    g_up[...] = up[:, :ff]
    g_down[...] = down[:, :ff]
    gain_a[...] = small[0:1, :]
    gain_f[...] = small[1:2, :]

    def heads_sum(first, last):
        total = jnp.zeros((1, HEAD_SIZE), F32)
        for c in range(first, last, HEAD_SIZE):
            total = total + small[2:3, c : c + HEAD_SIZE]
        return total

    gain_q[...] = heads_sum(0, a)
    gain_k[...] = heads_sum(a, b)
    row = lanes((1, 128))
    x_sum, attn_sum, ffn_sum = (
        jnp.sum(small[3 + i : 4 + i, :], axis=1, keepdims=True) for i in range(3)
    )
    total = jnp.where(row == 0, x_sum / tp, jnp.where(row == 1, attn_sum / tp, ffn_sum))
    stats[...] = jnp.sqrt(total * (1.0 / entries))


def output_pass(grid, shapes, *operands):
    rows = operands[0].shape[0]
    entries = rows * grid.n * grid.ctx * MODEL_WIDTH
    row = lambda n: shape((1, n), F32)
    vm = pl.BlockSpec(memory_space=pltpu.VMEM)
    outs = (
        [shape(operands[0].shape, BF)] * 2
        + [shape(s, F32) for s in shapes]
        + [row(MODEL_WIDTH), row(MODEL_WIDTH), row(HEAD_SIZE), row(HEAD_SIZE), row(128)]
    )
    return pl.pallas_call(
        functools.partial(output_kernel, grid.tp, entries),
        in_specs=[vm] * len(operands),
        out_specs=[vm] * len(outs),
        out_shape=outs,
        compiler_params=pltpu.CompilerParams(vmem_limit_bytes=60 * 2**20),
    )(*operands)


def local(
    tokens,
    cotangent,
    slot_of,
    lengths,
    w_query,
    key_weight,
    value_weight,
    w_out,
    w_gate,
    w_up,
    w_down,
    gain_attn,
    gain_ffn,
    gain_query,
    gain_key,
):
    grid = Grid()
    rows, feat_len = tokens.shape
    q_heads = QUERY_HEADS // grid.tp
    key_value_heads = KEY_VALUE_HEADS // grid.tp
    q_width = q_heads * HEAD_SIZE
    kv_width = key_value_heads * HEAD_SIZE
    ff = w_gate.shape[1]
    tile = 256 if ff % 256 == 0 else 128
    frequency = ROPE_THETA ** (-np.arange(0, HEAD_SIZE, 2, dtype=np.float64) / HEAD_SIZE)
    frequency = jnp.asarray(np.tile(frequency, 4)[None, :], F32)
    (
        sums, squares, ffn_part, d_mid_part, d_gain_ffn, take_back, send_back, cosines, sines,
        x_full, dy_full, qb, row_kv, heads, middle_own, attn_w, normed_two, down_keep, d_gate, d_up,
    ) = forward_pass(
        grid,
        q_width,
        kv_width,
        tile,
        lengths,
        tokens,
        cotangent,
        slot_of.reshape(-1, 128),
        gain_attn[None, :],
        gain_query[None, :],
        gain_key[None, :],
        gain_ffn[None, :],
        frequency,
        w_query,
        key_weight,
        value_weight,
        w_out.T,
        w_gate,
        w_up,
        w_down.T,
    )
    place_o, place_g, sum_gate, sum_up, sum_down, sum_out, sum_qkv, small = backward_pass(
        grid,
        q_width,
        kv_width,
        lengths,
        ffn_part,
        d_mid_part,
        sums,
        cosines,
        sines,
        take_back,
        gain_attn[None, :],
        gain_query[None, :],
        gain_key[None, :],
        d_gain_ffn,
        squares,
        qb,
        row_kv,
        heads,
        attn_w,
        dy_full,
        x_full,
        middle_own,
        normed_two,
        down_keep,
        d_gate,
        d_up,
    )
    weights = (w_query, key_weight, value_weight, w_out.T, w_gate, w_up, w_down.T)
    *outs, gain_a, gain_f, gain_q, gain_k, stats = output_pass(
        grid,
        [v.shape for v in weights],
        place_o,
        place_g,
        send_back,
        sum_gate,
        sum_up,
        sum_down,
        sum_out,
        sum_qkv,
        small,
    )
    outs[5], outs[8] = outs[5].T, outs[8].T
    return (*outs, gain_a[0], gain_f[0], gain_q[0], gain_k[0], stats[0, :3])


def solution(mesh):
    row = P(("fsdp", "ctx"), "tp")
    column = P("tp", ("fsdp", "ctx"))
    in_specs = (row, row, P(), P("fsdp", None), row, row, row, column, row, row, column) + (P(),) * 4
    out_specs = (row, row, row, row, row, column, row, row, column) + (P(),) * 5
    return jax.shard_map(local, mesh=mesh, in_specs=in_specs, out_specs=out_specs, check_vma=False)
```
